32 devices in a mesh: dp: 8 (over y, x, core), seq: 4 (over z).
Axes of the slice: x: 2, y: 2, z: 4, core: 2. Of those that a mesh axis runs over, the one named last changes fastest.
Arguments:
- tokens: bfloat16 [16384, 768], P(('dp', 'seq')), may hold values from -6 to 6
- w_qkv: bfloat16 [768, 2304], P(('dp', 'seq')), may hold values from -0.21875 to 0.21875
- w_out: bfloat16 [768, 768], P(('dp', 'seq')), may hold values from -1.75 to 1.75
- attn_gain: bfloat16 [768], P(('dp', 'seq')), may hold values from 0.5 to 1.5
- mlp_gain: bfloat16 [768], P(('dp', 'seq')), may hold values from 0.5 to 1.5
- w_in: bfloat16 [768, 2, 1152], P('dp', None, 'seq'), may hold values from -0.21875 to 0.21875
- w_down: bfloat16 [1152, 768], P('seq', 'dp'), may hold values from -0.1875 to 0.1875
- grad_out: bfloat16 [16384, 768], P(('dp', 'seq')), may hold values from -6 to 6
Outputs:
- out_block: bfloat16 [16384, 768], P(('dp', 'seq'))
- grad_tokens: bfloat16 [16384, 768], P(('dp', 'seq'))
- grad_w_qkv: float32 [768, 2304], P(('dp', 'seq'))
- grad_w_out: float32 [768, 768], P(('dp', 'seq'))
- grad_attn_gain: float32 [768], P(('dp', 'seq'))
- grad_mlp_gain: float32 [768], P(('dp', 'seq'))
- grad_w_in: float32 [768, 2, 1152], P('dp', None, 'seq')
- grad_w_down: float32 [1152, 768], P('seq', 'dp')
The draws below stay inside these ranges and needn't reach their ends.
All inputs are finite; a program needn't handle non-finite values.
Results may differ from the reference program's by a relative error of at most 0.028.
Values may be sent and summed in bfloat16 or wider, within the bound.
A program may use at most 128 MiB of HBM per device.

```python
import jax
import jax.numpy as jnp
from jax import lax

D = 768
HEADS = 12
HEAD_DIM = 64
FF = 1152
DOC_LEN = 2048
DOCS = 8
TOKENS = 16384


def level_of(key, extent, pieces, low, high):
    def one(dim, blocks):
        heights = jax.random.uniform(jax.random.fold_in(jax.random.fold_in(key, 6), dim), (blocks,), jnp.float32, low / len(pieces), high / len(pieces))
        return jnp.repeat(jnp.exp(heights), extent[dim] // blocks).reshape((-1,) + (1,) * (len(extent) - dim - 1))

    loudness = one(*pieces[0])
    for cut in pieces[1:]:
        loudness = loudness * one(*cut)
    return loudness


def bell_draw(own_key, extent, scale, bound, shards=(), held_as=jnp.bfloat16):
    loudness = level_of(own_key, extent, shards, -0.22, 0.18) if shards else 1.0
    values = jax.random.normal(own_key, extent, jnp.float32) * scale * loudness
    return jnp.minimum(jnp.maximum(values, -bound), bound).astype(held_as)


def setup_inputs(seed: int = 0) -> dict:
    keys = jax.random.split(jax.random.key(seed), 9)
    tokens = bell_draw(keys[0], (TOKENS, D), 1.0, 6.0, ((0, 32),))
    w_qkv = bell_draw(keys[1], (D, 3 * D), D ** -0.5, 0.21875, ((0, 32),))
    w_out = bell_draw(keys[2], (D, D), (max(1, D * 32 // DOC_LEN)) ** -0.5, 1.75, ((0, 32),))
    attn_gain = jnp.clip(1.0 + 0.1 * jax.random.normal(keys[3], (D,), jnp.float32), 0.5, 1.5).astype(jnp.bfloat16)
    mlp_gain = jnp.clip(1.0 + 0.1 * jax.random.normal(keys[4], (D,), jnp.float32), 0.5, 1.5).astype(jnp.bfloat16)
    w_in = bell_draw(keys[5], (D, 2, FF), D ** -0.5, 0.21875, ((0, 8), (2, 4)))
    w_down = bell_draw(keys[6], (FF, D), FF ** -0.5, 0.1875, ((0, 4), (1, 8)))
    grad_out = bell_draw(keys[7], (TOKENS, D), 1.0, 6.0, ((0, 32),))
    return {"tokens": tokens, "w_qkv": w_qkv, "w_out": w_out, "attn_gain": attn_gain, "mlp_gain": mlp_gain, "w_in": w_in, "w_down": w_down, "grad_out": grad_out}


NORM_EPS = 1e-05
ROPE_THETA = 160000.0

@jax.custom_vjp
def low(v):
    return lax.optimization_barrier(v.astype(jnp.bfloat16)).astype(jnp.float32)

@jax.custom_vjp
def low_back(v):
    return v

def low_keep(v):
    return (low(v), None)

def low_pass(kept, grad):
    return (grad,)

def back_keep(v):
    return (v, None)

def back_low(kept, grad):
    return (low(grad),)
low.defvjp(low_keep, low_pass)
low_back.defvjp(back_keep, back_low)

def layer_norm(values, gain):
    mean_row = lax.optimization_barrier(jnp.mean(values, -1, keepdims=True))
    centred = values - mean_row
    inv_std = lax.rsqrt(lax.optimization_barrier(jnp.mean(centred * centred, -1, keepdims=True)) + NORM_EPS)
    return centred * inv_std * gain

def rotary_tables(first_pos, pos_count, head_size):
    position = (first_pos + jnp.arange(pos_count)).astype(jnp.float32)
    half_dim = head_size // 2
    inv_freq = ROPE_THETA ** (-jnp.arange(half_dim).astype(jnp.float32) * 2.0 / head_size)
    angle_tab = position[:, None] * inv_freq[None, :]
    angle_tab = jnp.concatenate([angle_tab, angle_tab], -1)
    return (jnp.cos(angle_tab), jnp.sin(angle_tab))

def rotate(values, cos_tab, sine_tab):
    half_dim = values.shape[-1] // 2
    turned = jnp.concatenate([-values[..., half_dim:], values[..., :half_dim]], -1)
    return values * cos_tab[:, None, :] + turned * sine_tab[:, None, :]

def attend_block(query_blk, key_all, value_all):
    scale_qk = HEAD_DIM ** (-0.5)
    scores = low_back(jnp.einsum('qhd,khd->hqk', query_blk, key_all, precision=lax.Precision.HIGHEST) * scale_qk)
    row_top = lax.optimization_barrier(jnp.max(scores, -1, keepdims=True))
    expo_vals = jnp.exp(scores - row_top)
    prob_vals = low(expo_vals / lax.optimization_barrier(jnp.sum(expo_vals, -1, keepdims=True)))
    return jnp.einsum('hqk,khd->qhd', prob_vals, value_all, precision=lax.Precision.HIGHEST)

def doc_forward(doc_tokens, w_qkv, w_out, attn_gain, mlp_gain, w_in, w_down):
    length = doc_tokens.shape[0]
    high = lax.Precision.HIGHEST
    first_in = low(layer_norm(doc_tokens, attn_gain))
    projected = low_back(jnp.dot(first_in, w_qkv, precision=high, preferred_element_type=jnp.float32))
    cos_tab, sine_tab = rotary_tables(0, length, HEAD_DIM)
    query = low(rotate(projected[:, :D].reshape(length, HEADS, HEAD_DIM), cos_tab, sine_tab))
    key_all = low(rotate(projected[:, D:2 * D].reshape(length, HEADS, HEAD_DIM), cos_tab, sine_tab))
    value_all = low(projected[:, 2 * D:].reshape(length, HEADS, HEAD_DIM))
    block_rows = min(512, length)
    blocks = query.reshape(length // block_rows, block_rows, HEADS, HEAD_DIM)
    mixed_out = lax.map(jax.checkpoint(lambda query_blk: attend_block(query_blk, key_all, value_all)), blocks)
    mixed_out = low(low_back(mixed_out.reshape(length, D)))
    resid_mid = doc_tokens + low_back(jnp.dot(mixed_out, w_out, precision=high, preferred_element_type=jnp.float32))
    second_in = low(layer_norm(resid_mid, mlp_gain))
    gate_up = low_back(jnp.einsum('td,dgf->tgf', second_in, w_in, precision=high))
    hidden = low(jax.nn.gelu(gate_up[:, 0], approximate=False) * gate_up[:, 1])
    return resid_mid + jnp.dot(hidden, w_down, precision=high, preferred_element_type=jnp.float32)

def reference(tokens, w_qkv, w_out, attn_gain, mlp_gain, w_in, w_down, grad_out):

    def forward(tok_all, wq, wo, gain_a, gain_m, wi, wd):
        doc_rows = tok_all.reshape(DOCS, DOC_LEN, D)
        outputs = lax.map(lambda doc_tokens: doc_forward(doc_tokens, wq, wo, gain_a, gain_m, wi, wd), doc_rows)
        return outputs.reshape(TOKENS, D)
    inputs = (tokens, w_qkv, w_out, attn_gain, mlp_gain, w_in, w_down)
    inputs = tuple((item.astype(jnp.float32) for item in inputs))
    result, pull = jax.vjp(forward, *inputs)
    grads = pull(grad_out.astype(jnp.float32))
    return (result.astype(jnp.bfloat16), grads[0].astype(jnp.bfloat16), grads[1], grads[2], grads[3], grads[4], grads[5], grads[6])
```

```python
import functools
import math

import jax
import jax.numpy as jnp
import numpy as np
from jax import lax
from jax.experimental import pallas as pl
from jax.experimental.pallas import tpu as pltpu
from jax.sharding import PartitionSpec as P

HEADS = 12
HEAD_DIM = 64
NORM_EPS = 1e-05
ROPE_THETA = 160000.0

F32 = jnp.float32
BF = jnp.bfloat16
MESH = pl.DeviceIdType.MESH
NT = (((1,), (1,)), ((), ()))
NN = (((1,), (0,)), ((), ()))
TN = (((0,), (0,)), ((), ()))

WIDTH = 768
PAIRS = HEADS // 2
UNITS = 1152
GROUPS = 8
LINE = 4
BAND = WIDTH // GROUPS
SLIVER = BAND // LINE
SHARE = UNITS // LINE
MAIN = 256
REST = SHARE - MAIN
LOG2E = math.log2(math.e)
SCALE = HEAD_DIM**-0.5


def dot(a, b, dims):
    return lax.dot_general(a, b, dims, preferred_element_type=F32)


def lanes_of(tile, width=128):
    return pl.ds(pl.multiple_of(tile * width, width), width)


def lane_iota():
    return lax.broadcasted_iota(jnp.int32, (1, 128), 1)


def swap_halves(u):
    low = lax.rem(lane_iota(), 64) < 32
    return jnp.where(low, pltpu.roll(u, 96, 1), pltpu.roll(u, 32, 1))


def rope(u, cos, sine):
    return u * cos + swap_halves(u) * sine


def rope_back(u, cos, sine):
    return u * cos - swap_halves(u) * sine


def rope_tables(rows):
    position = np.arange(rows, dtype=np.float32)
    half = HEAD_DIM // 2
    freq = (ROPE_THETA ** (-np.arange(half) * 2.0 / HEAD_DIM)).astype(np.float32)
    angle = (position[:, None] * freq[None, :]).astype(np.float64)
    cos, sine = np.cos(angle), np.sin(angle)
    cos = np.concatenate([cos] * 4, 1).astype(np.float32)
    sine = np.concatenate([-sine, sine] * 2, 1).astype(np.float32)
    return cos, sine


def normed(x):
    centred = x - jnp.mean(x, -1, keepdims=True)
    inv = lax.rsqrt(jnp.mean(centred * centred, -1, keepdims=True) + NORM_EPS)
    return centred * inv, inv


def norm_back(dy, gain, hat, inv):
    d = dy * gain
    return inv * (d - jnp.mean(d, -1, keepdims=True) - hat * jnp.mean(d * hat, -1, keepdims=True))


def chunk_at(z, t, nz):
    both = jnp.minimum(z, nz - 1 - z)
    near = jnp.where(lax.rem(t, 2) == 1, z - (t + 1) // 2, z + (t + 1) // 2)
    far = jnp.where(z < nz - 1 - z, z + t - both, z - t + both)
    return jnp.where(t <= 2 * both, near, far)


def remote(src, dst, send, recv, device):
    return pltpu.make_async_remote_copy(src, dst, send, recv, device_id=device, device_id_type=MESH)


def greet(z, nz, dp, masks):
    bar = pltpu.get_barrier_semaphore()
    for o in range(1, nz):
        pl.semaphore_signal(bar, inc=1, device_id={"seq": lax.rem(z + o, nz)}, device_id_type=MESH)
    for m in masks:
        pl.semaphore_signal(bar, inc=1, device_id={"dp": dp ^ m}, device_id_type=MESH)
    pl.semaphore_wait(bar, nz - 1 + len(masks))


class Gather:
    COPIES = 9

    def __init__(self, src, out, cut, nz, masks, send, recv):
        self.src, self.out, self.cut, self.nz, self.masks = src, out, cut, nz, masks
        self.send, self.recv = send, recv
        self.dp, self.z = lax.axis_index("dp"), lax.axis_index("seq")
        self.started = []

    @staticmethod
    def sems(nz):
        return Gather.COPIES * nz + nz

    def key(self, o, k):
        return o * self.COPIES + k

    def copy(self, src, dst, device, k):
        return remote(src, dst, self.send.at[k], self.recv.at[k], device)

    def begin(self, src, dst, device, k):
        c = self.copy(src, dst, device, k)
        c.start()
        self.started.append(c)

    def arrived(self, ref, k):
        self.copy(ref, ref, {"dp": self.dp ^ self.masks[0]}, k).wait_recv()

    def slot(self, o):
        return lax.rem(self.z + self.nz - o, self.nz)

    def part(self, ref, p):
        if p is None:
            return ref
        width = self.out.shape[-1]
        return ref.at[:, pl.ds(0, self.cut)] if p == 0 else ref.at[:, pl.ds(self.cut, width - self.cut)]

    def along(self):
        for o in range(1, self.nz):
            k = self.COPIES * self.nz + o
            self.begin(self.src, self.out.at[self.dp, self.z], {"seq": lax.rem(self.z + o, self.nz)}, k)

    def forward(self, src, d, s, mask, k, p=None):
        dst = self.out.at[d, s]
        self.begin(self.part(src, p), self.part(dst, p), {"dp": self.dp ^ mask}, k)

    def first(self, o):
        my, mx, mc = self.masks
        s = self.slot(o)
        src = self.src
        if o:
            src = self.out.at[self.dp, s]
            self.arrived(src, self.COPIES * self.nz + o)
        self.forward(src, self.dp, s, my, self.key(o, 0))
        self.forward(src, self.dp, s, mx, self.key(o, 1))
        self.forward(src, self.dp, s, mc, self.key(o, 2))

    def second(self, o):
        my, mx, mc = self.masks
        s = self.slot(o)
        for m, k, k2, kc, p, m2 in ((my, 0, 3, 4, 0, mx), (mx, 1, 5, 6, 1, my)):
            ref = self.out.at[self.dp ^ m, s]
            self.arrived(ref, self.key(o, k))
            self.forward(ref, self.dp ^ m, s, m2, self.key(o, k2), p)
            self.forward(ref, self.dp ^ m, s, mc, self.key(o, kc))

    def third(self, o):
        my, mx, mc = self.masks
        s = self.slot(o)
        d = self.dp ^ my ^ mx
        for p, k, kc in ((0, 3, 7), (1, 5, 8)):
            ref = self.out.at[d, s]
            self.arrived(self.part(ref, p), self.key(o, k))
            self.forward(ref, d, s, mc, self.key(o, kc), p)

    def finish(self, o):
        my, mx, mc = self.masks
        s = self.slot(o)
        for k, d in ((2, mc), (4, mc ^ my), (6, mc ^ mx)):
            self.arrived(self.out.at[self.dp ^ d, s], self.key(o, k))
        for k, p in ((7, 0), (8, 1)):
            self.arrived(self.part(self.out.at[self.dp ^ mc ^ my ^ mx, s], p), self.key(o, k))

    def done(self):
        for c in self.started:
            c.wait_send()


def half_lanes(width):
    return (width // 256) * 128


def front_kernel(nz, masks, rows, *refs):
    fused = masks is not None
    if fused:
        (tok, pq, po, pm, cos, sine, mixed, lse, query, keys, values, firsts, wqkv, gain, po_all, pm_all, tok_all, pq_all,
         gcol, acc, top, total, tsend, trecv, qs, qr, os_, or_, ms, mr, loc) = refs
    else:
        (tok, pq_all, cos, sine, mixed, lse, query, keys, values, firsts, wqkv, gain, tok_all,
         gcol, acc, top, total, tsend, trecv, loc) = refs
    dp, z = lax.axis_index("dp"), lax.axis_index("seq")

    own = pltpu.make_async_copy(tok, tok_all.at[z], loc.at[0])
    own.start()
    if fused:
        locals_ = []
        for i, (src, out) in enumerate(((pq, pq_all), (po, po_all), (pm, pm_all))):
            c = pltpu.make_async_copy(src, out.at[dp, z], loc.at[1 + i])
            c.start()
            locals_.append(c)
        greet(z, nz, dp, masks)
        packs = [
            Gather(pq, pq_all, half_lanes(pq.shape[-1]), nz, masks, qs, qr),
            Gather(po, po_all, half_lanes(po.shape[-1]), nz, masks, os_, or_),
            Gather(pm, pm_all, half_lanes(pm.shape[-1]), nz, masks, ms, mr),
        ]
        first, *later = packs
        first.along()
        first.first(0)
    else:
        bar = pltpu.get_barrier_semaphore()
        for o in range(1, nz):
            pl.semaphore_signal(bar, inc=1, device_id={"seq": lax.rem(z + o, nz)}, device_id_type=MESH)
        pl.semaphore_wait(bar, nz - 1)

    def hop(src, c, left):
        to = z - 1 if left else z + 1
        k = nz if left else c
        if src is None:
            src = tok_all.at[c]
            k = c
        return remote(src, tok_all.at[c], tsend.at[k], trecv.at[c], {"seq": to})

    @pl.when(z + 1 < nz)
    def _():
        hop(tok, z, False).start()

    @pl.when(z > 0)
    def _():
        hop(tok, z, True).start()

    if fused:
        for g in later:
            g.along()
        first.second(0)
        for o in range(1, nz):
            first.first(o)
        for o in range(1, nz):
            first.second(o)
        for o in range(nz):
            first.third(o)
        for g in later:
            for o in range(nz):
                g.first(o)
        for o in range(nz):
            first.finish(o)
        for c in locals_:
            c.wait()
    own.wait()

    half = 1152

    def build(g, _):
        slabs = [pq_all[g, s].astype(F32) for s in range(LINE)]
        band = pl.ds(pl.multiple_of(g * BAND, BAND), BAND)
        wqkv[band, :half] = jnp.concatenate([x[:SLIVER, :half] for x in slabs], 0).astype(BF)
        wqkv[band, half:] = jnp.concatenate([x[SLIVER:, :half] for x in slabs], 0).astype(BF)
        gcol[band, :] = jnp.concatenate([x[:SLIVER, half:] for x in slabs], 0)
        return 0

    lax.fori_loop(0, GROUPS, build, 0)
    gain[...] = gcol[...].T[:8]

    def norm_chunk(c):
        def block(i, _):
            at = pl.ds(pl.multiple_of(i * 64, 64), 64)
            hat, _ = normed(tok_all[c, at, :].astype(F32))
            firsts[c, at, :] = (hat * gain[0:1, :]).astype(BF)
            return 0

        lax.fori_loop(0, rows // 64, block, 0)

    def project(c, j, base):
        return dot(firsts[c], wqkv[:, base + 256 * j : base + 256 * j + 256], NN)

    norm_chunk(z)
    for j in range(3):
        u = project(z, j, 0)
        for i in range(2):
            tile = rope(u[:, 128 * i : 128 * i + 128], cos[z], sine[z])
            query[:, 256 * j + 128 * i : 256 * j + 128 * i + 128] = (tile * (SCALE * LOG2E)).astype(BF)
    acc[...] = jnp.zeros_like(acc)
    total[...] = jnp.zeros_like(total)
    top[...] = jnp.full_like(top, -1e30)

    def visit(t, _):
        c = chunk_at(z, t, nz)

        @pl.when(t > 0)
        def _():
            remote(tok_all.at[c], tok_all.at[c], tsend.at[c], trecv.at[c], {"seq": lax.rem(z + 1, nz)}).wait_recv()

            @pl.when((c < z) & (z + 1 < nz))
            def _():
                hop(None, c, False).start()

            @pl.when((c > z) & (z > 0))
            def _():
                hop(None, c, True).start()

            norm_chunk(c)

        for j in range(3):
            u = project(c, j, WIDTH)
            for i in range(2):
                at = 256 * j + 128 * i
                keys[c, :, at : at + 128] = rope(u[:, 128 * i : 128 * i + 128], cos[c], sine[c]).astype(BF)
            values[c, :, 256 * j : 256 * j + 256] = project(c, j, 2 * WIDTH).astype(BF)

        def pair(hp, _):
            q, k, v = query[:, lanes_of(hp)], keys[c, :, lanes_of(hp)], values[c, :, lanes_of(hp)]
            for h in range(2):
                mask = (lane_iota() < 64) if h == 0 else (lane_iota() >= 64)
                s = dot(k, jnp.where(mask, q, jnp.zeros_like(q)), NT)
                at = pl.ds(hp * 2 + h, 1)
                old = top[at, :]
                new = jnp.maximum(old, jnp.max(s, 0, keepdims=True))
                p = jnp.exp2(s - new)
                fade = jnp.exp2(old - new)
                top[at, :] = new
                total[at, :] = total[at, :] * fade + jnp.sum(p, 0, keepdims=True)
                band = pl.ds(pl.multiple_of(hp * 128 + h * 64, 64), 64)
                acc[band, :] = acc[band, :] * fade + dot(v[:, h * 64 : h * 64 + 64], p.astype(BF), TN)
            return 0

        lax.fori_loop(0, PAIRS, pair, 0)
        return 0

    lax.fori_loop(0, nz, visit, 0)

    for hp in range(PAIRS):
        parts = [
            acc[128 * hp + 64 * h : 128 * hp + 64 * h + 64, :] / total[2 * hp + h : 2 * hp + h + 1, :] for h in range(2)
        ]
        mixed[:, 128 * hp : 128 * hp + 128] = jnp.concatenate(parts, 0).T.astype(BF)
    lse[...] = top[...] + jnp.log(jnp.maximum(total[...], 1e-30)) * LOG2E

    if fused:
        for g in later:
            for o in range(nz):
                g.second(o)
        for g in later:
            for o in range(nz):
                g.third(o)
        for g in later:
            for o in range(nz):
                g.finish(o)
        for g in packs:
            g.done()

    @pl.when(z + 1 < nz)
    def _():
        hop(tok, z, False).wait_send()

    @pl.when(z > 0)
    def _():
        hop(tok, z, True).wait_send()

    for t in range(1, nz):
        c = chunk_at(z, t, nz)

        @pl.when(((c < z) & (z + 1 < nz)) | ((c > z) & (z > 0)))
        def _(c=c):
            hop(None, c, False).wait_send()


def front(tok, packs, cos, sine, nz, masks):
    rows = tok.shape[0]
    fused = masks is not None
    vmem, anyspace = pl.BlockSpec(memory_space=pltpu.VMEM), pl.BlockSpec(memory_space=pl.ANY)
    shape = jax.ShapeDtypeStruct
    outs = [
        shape((rows, WIDTH), BF),
        shape((16, rows), F32),
        shape((rows, WIDTH), BF),
        shape((nz, rows, WIDTH), BF),
        shape((nz, rows, WIDTH), BF),
        shape((nz, rows, WIDTH), BF),
        shape((WIDTH, 3 * WIDTH), BF),
        shape((8, WIDTH), F32),
    ]
    out_specs = [vmem] * 8
    scratch = [pltpu.VMEM((nz, rows, WIDTH), BF)]
    if fused:
        pq, po, pm = packs
        outs += [shape((GROUPS, nz) + po.shape, BF), shape((GROUPS, nz) + pm.shape, BF)]
        out_specs += [anyspace] * 2
        in_specs = [anyspace] * 4 + [vmem] * 2
        scratch += [pltpu.VMEM((GROUPS, nz) + pq.shape, BF)]
    else:
        in_specs = [anyspace] + [vmem] * 3
    scratch += [
        pltpu.VMEM((WIDTH, 128), F32),
        pltpu.VMEM((WIDTH, rows), F32),
        pltpu.VMEM((16, rows), F32),
        pltpu.VMEM((16, rows), F32),
        pltpu.SemaphoreType.DMA((nz + 1,)),
        pltpu.SemaphoreType.DMA((nz,)),
    ]
    if fused:
        scratch += [pltpu.SemaphoreType.DMA((Gather.sems(nz),)) for _ in range(6)]
    scratch += [pltpu.SemaphoreType.DMA((4,))]
    return pl.pallas_call(
        functools.partial(front_kernel, nz, masks, rows),
        out_shape=outs,
        in_specs=in_specs,
        out_specs=out_specs,
        scratch_shapes=scratch,
        compiler_params=pltpu.CompilerParams(collective_id=0, has_side_effects=True, vmem_limit_bytes=58 << 20),
        cost_estimate=pl.CostEstimate(flops=14_000_000_000, bytes_accessed=40_000_000, transcendentals=13_000_000),
        name="front",
    )(tok, *packs, cos, sine)


def middle_kernel(rows, tok, mixed, gout, po_all, pm_all, out, gmid, gmixed, delta, po_g, pm_g,
                  wout, wg, wu, wd, gcol, gain, resid, hat, inv, second, hidden, ggate, gup, gsec, gattn, dwout):
    lane = lane_iota()

    def build(g, _):
        band = pl.ds(pl.multiple_of(g * BAND, BAND), BAND)
        slabs = [po_all[g, s].astype(F32) for s in range(LINE)]
        wout[band, :384] = jnp.concatenate([x[:SLIVER, :384] for x in slabs], 0).astype(BF)
        wout[band, 384:] = jnp.concatenate([x[SLIVER:, :384] for x in slabs], 0).astype(BF)
        gcol[band, :] = jnp.concatenate([x[:SLIVER, 384:] for x in slabs], 0)
        for i, w in enumerate((wg, wu, wd)):
            tail = jnp.zeros((BAND, 128), F32)
            for s in range(LINE):
                w[band, MAIN * s : MAIN * s + MAIN] = pm_all[g, s, :, MAIN * i : MAIN * i + MAIN]
                rest = pm_all[g, s, :, 3 * MAIN :].astype(F32)
                turn = (REST * (s - i)) % 128
                rest = pltpu.roll(rest, turn, 1) if turn else rest
                tail = jnp.where((lane >= REST * s) & (lane < REST * (s + 1)), rest, tail)
            w[band, MAIN * LINE :] = tail.astype(BF)
        return 0

    lax.fori_loop(0, GROUPS, build, 0)
    gain[...] = gcol[...].T[:8]

    for j in range(3):
        at = slice(256 * j, 256 * j + 256)
        resid[:, at] = tok[:, at].astype(F32) + dot(mixed[...], wout[:, at], NN)

    def norm_block(i, _):
        at = pl.ds(pl.multiple_of(i * 64, 64), 64)
        h, r = normed(resid[at, :])
        hat[at, :] = h
        inv[at, :] = jnp.broadcast_to(r, (64, 128))
        second[at, :] = (h * gain[0:1, :]).astype(BF)
        return 0

    lax.fori_loop(0, rows // 64, norm_block, 0)

    def units(start, width):
        at = pl.ds(start, width)
        gate, up, gh = dot(second[...], wg[:, at], NN), dot(second[...], wu[:, at], NN), dot(gout[...], wd[:, at], NN)
        cdf = 0.5 + 0.5 * lax.erf(gate * math.sqrt(0.5))
        pdf = jnp.exp2(gate * gate * (-0.5 * LOG2E)) * (1.0 / math.sqrt(2.0 * math.pi))
        act = gate * cdf
        hidden[:, at] = (act * up).astype(BF)
        gup[:, at] = (gh * act).astype(BF)
        ggate[:, at] = (gh * up * (cdf + gate * pdf)).astype(BF)

    def unit_block(i, _):
        units(pl.multiple_of(i * 128, 128), 128)
        return 0

    lax.fori_loop(0, UNITS // 128, unit_block, 0)

    for j in range(3):
        at = slice(256 * j, 256 * j + 256)
        out[:, at] = (resid[:, at] + dot(hidden[...], wd[at, :], NT)).astype(BF)
        gsec[:, at] = dot(ggate[...], wg[at, :], NT) + dot(gup[...], wu[at, :], NT)

    def back_block(i, dgain):
        at = pl.ds(pl.multiple_of(i * 64, 64), 64)
        dy, h = gsec[at, :], hat[at, :]
        gm = gout[at, :].astype(F32) + norm_back(dy, gain[0:1, :], h, inv[at, 0:1])
        gmid[at, :] = gm
        gattn[at, :] = gm.astype(BF)
        return dgain + jnp.sum(dy * h, 0, keepdims=True)

    dgain = lax.fori_loop(0, rows // 64, back_block, jnp.zeros((1, WIDTH), F32))

    heads = lax.broadcasted_iota(jnp.int32, (16, 256), 0)
    for j in range(3):
        at = slice(256 * j, 256 * j + 256)
        gmx = dot(gattn[...], wout[at, :], NT).astype(BF)
        gmixed[:, at] = gmx
        prod = gmx.astype(F32) * mixed[:, at].astype(F32)
        high = prod.astype(BF)
        low = (prod - high.astype(F32)).astype(BF)
        pick = ((lax.broadcasted_iota(jnp.int32, (16, 256), 1) + 256 * j) // HEAD_DIM == heads).astype(BF)
        part = dot(pick, high, NT) + dot(pick, low, NT)
        delta[...] = part if j == 0 else delta[...] + part

    for j in range(2):
        at = slice(384 * j, 384 * j + 384)
        dwout[at, :] = dot(mixed[:, at], gattn[...], TN)
    row = lax.broadcasted_iota(jnp.int32, (128, WIDTH), 0)
    gcol[...] = jnp.where(row == 0, dgain, 0.0).T

    def pack_out(g, _):
        for s in range(LINE):
            at = pl.ds(pl.multiple_of(g * BAND + s * SLIVER, 8), SLIVER)
            x, c = dwout[at, :], gcol[at, :]
            po_g[g, s, :, :384] = jnp.concatenate([x[:, :384], x[:, 384:]], 0).astype(BF)
            po_g[g, s, :, 384:] = jnp.concatenate([c, jnp.zeros_like(c)], 0).astype(BF)
        return 0

    lax.fori_loop(0, GROUPS, pack_out, 0)

    for j in range(2):
        at = slice(384 * j, 384 * j + 384)
        tails = []
        for i, (a, b) in enumerate(((second, ggate), (second, gup), (gout, hidden))):
            for s in range(LINE):
                x = dot(a[:, at], b[:, MAIN * s : MAIN * s + MAIN], TN).astype(BF)
                for g in range(4):
                    pm_g[4 * j + g, s, :, MAIN * i : MAIN * i + MAIN] = x[BAND * g : BAND * g + BAND]
            tails.append(dot(a[:, at], b[:, MAIN * LINE :], TN))
        for s in range(LINE):
            y = jnp.zeros((384, 128), F32)
            for i, tail in enumerate(tails):
                turn = (REST * (i - s)) % 128
                tail = pltpu.roll(tail, turn, 1) if turn else tail
                y = jnp.where((lane >= REST * i) & (lane < REST * (i + 1)), tail, y)
            y = y.astype(BF)
            for g in range(4):
                pm_g[4 * j + g, s, :, 3 * MAIN :] = y[BAND * g : BAND * g + BAND]


def middle(tok, mixed, gout, po_all, pm_all):
    rows = tok.shape[0]
    shape, vm = jax.ShapeDtypeStruct, pltpu.VMEM
    vmem = pl.BlockSpec(memory_space=pltpu.VMEM)
    return pl.pallas_call(
        functools.partial(middle_kernel, rows),
        out_shape=[
            shape((rows, WIDTH), BF),
            shape((rows, WIDTH), F32),
            shape((rows, WIDTH), BF),
            shape((16, rows), F32),
            shape(po_all.shape, BF),
            shape(pm_all.shape, BF),
        ],
        in_specs=[vmem] * 5,
        out_specs=[vmem] * 6,
        scratch_shapes=[
            vm((WIDTH, WIDTH), BF),
            vm((WIDTH, UNITS), BF),
            vm((WIDTH, UNITS), BF),
            vm((WIDTH, UNITS), BF),
            vm((WIDTH, 128), F32),
            vm((8, WIDTH), F32),
            vm((rows, WIDTH), F32),
            vm((rows, WIDTH), F32),
            vm((rows, 128), F32),
            vm((rows, WIDTH), BF),
            vm((rows, UNITS), BF),
            vm((rows, UNITS), BF),
            vm((rows, UNITS), BF),
            vm((rows, WIDTH), F32),
            vm((rows, WIDTH), BF),
            vm((WIDTH, WIDTH), F32),
        ],
        compiler_params=pltpu.CompilerParams(vmem_limit_bytes=58 << 20),
        cost_estimate=pl.CostEstimate(flops=11_000_000_000, bytes_accessed=25_000_000, transcendentals=1_200_000),
        name="middle",
    )(tok, mixed, gout, po_all, pm_all)


def back_kernel(nz, rows, tok, gmid, query, keys, values, firsts, wqkv, gain, gmixed, lse, delta, cos, sine,
                gtok, pq_g, dq, dkv, dx, dw, posted, landed, gcol, send, recv):
    z = lax.axis_index("seq")
    bar = pltpu.get_barrier_semaphore()
    for o in range(1, nz):
        pl.semaphore_signal(bar, inc=1, device_id={"seq": lax.rem(z + o, nz)}, device_id_type=MESH)
    pl.semaphore_wait(bar, nz - 1)
    dq[...] = jnp.zeros_like(dq)
    dw[...] = jnp.zeros_like(dw)

    def post(c):
        k = lax.rem(z - c + nz, nz) - 1
        return remote(posted.at[k], landed.at[k], send.at[k], recv.at[k], {"seq": c})

    def visit(t, _):
        c = chunk_at(z, nz - 1 - t, nz)

        def pair(hp, _):
            at = lanes_of(hp)
            q, g, k, v = query[:, at], gmixed[:, at], keys[c, :, at], values[c, :, at]
            dk = dv = None
            for h in range(2):
                mask = (lane_iota() < 64) if h == 0 else (lane_iota() >= 64)
                qh, gh = jnp.where(mask, q, jnp.zeros_like(q)), jnp.where(mask, g, jnp.zeros_like(g))
                head = pl.ds(hp * 2 + h, 1)
                p = jnp.exp2(dot(k, qh, NT) - lse[head, :])
                ds = (p * (dot(v, gh, NT) - delta[head, :])).astype(BF)
                a = dot(p.astype(BF), gh, NN)
                dv = a if dv is None else dv + a
                a = dot(ds, qh, NN)
                dk = a if dk is None else dk + a
                band = pl.ds(pl.multiple_of(hp * 128 + h * 64, 64), 64)
                dq[band, :] += dot(k[:, h * 64 : h * 64 + 64], ds, TN)
            dkv[:, at] = rope_back(dk * (1.0 / LOG2E), cos[c], sine[c]).astype(BF)
            dkv[:, lanes_of(hp + PAIRS)] = dv.astype(BF)
            return 0

        lax.fori_loop(0, PAIRS, pair, 0)

        for j in range(3):
            at = slice(256 * j, 256 * j + 256)
            x = dot(dkv[...], wqkv[at, WIDTH:], NT)
            dx[:, at] = x

        @pl.when(c != z)
        def _():
            k = lax.rem(z - c + nz, nz) - 1
            posted[k] = dx[...].astype(BF)
            post(c).start()

        def weigh(i, _):
            at, to = lanes_of(i, 256), lanes_of(i + 3, 256)
            for j in range(2):
                r = slice(384 * j, 384 * j + 384)
                dw[r, to] += dot(firsts[c, :, r], dkv[:, at], TN)
            return 0

        lax.fori_loop(0, 6, weigh, 0)
        return 0

    lax.fori_loop(0, nz, visit, 0)

    for hp in range(PAIRS):
        at = slice(128 * hp, 128 * hp + 128)
        u = dq[at, :].T * SCALE
        dkv[:, at] = rope_back(u, cos[z], sine[z]).astype(BF)
    for j in range(3):
        at = slice(256 * j, 256 * j + 256)
        dx[:, at] += dot(dkv[:, :WIDTH], wqkv[at, :WIDTH], NT)
        for i in range(2):
            r = slice(384 * i, 384 * i + 384)
            dw[r, at] = dot(firsts[z, :, r], dkv[:, at], TN)

    for o in range(1, nz):
        post(lax.rem(z + nz - o, nz)).wait_recv()

    def norm_block(i, dgain):
        at = pl.ds(pl.multiple_of(i * 64, 64), 64)
        dy = dx[at, :]
        for k in range(nz - 1):
            dy = dy + landed[k, at, :].astype(F32)
        h, r = normed(tok[at, :].astype(F32))
        gtok[at, :] = (gmid[at, :] + norm_back(dy, gain[0:1, :], h, r)).astype(BF)
        return dgain + jnp.sum(dy * h, 0, keepdims=True)

    dgain = lax.fori_loop(0, rows // 64, norm_block, jnp.zeros((1, WIDTH), F32))
    row = lax.broadcasted_iota(jnp.int32, (128, WIDTH), 0)
    gcol[...] = jnp.where(row == 0, dgain, 0.0).T

    def pack(g, _):
        for s in range(LINE):
            at = pl.ds(pl.multiple_of(g * BAND + s * SLIVER, 8), SLIVER)
            x, c = dw[at, :], gcol[at, :]
            pq_g[g, s, :, :1152] = jnp.concatenate([x[:, :1152], x[:, 1152:]], 0).astype(BF)
            pq_g[g, s, :, 1152:] = jnp.concatenate([c, jnp.zeros_like(c)], 0).astype(BF)
        return 0

    lax.fori_loop(0, GROUPS, pack, 0)
    for o in range(1, nz):
        post(lax.rem(z + nz - o, nz)).wait_send()


def back(tok, gmid, query, keys, values, firsts, wqkv, gain, gmixed, lse, delta, cos, sine, nz):
    rows = tok.shape[0]
    shape, vm = jax.ShapeDtypeStruct, pltpu.VMEM
    vmem = pl.BlockSpec(memory_space=pltpu.VMEM)
    return pl.pallas_call(
        functools.partial(back_kernel, nz, rows),
        out_shape=[shape((rows, WIDTH), BF), shape((GROUPS, LINE, 2 * SLIVER, 1280), BF)],
        in_specs=[vmem] * 13,
        out_specs=[vmem] * 2,
        scratch_shapes=[
            vm((WIDTH, rows), F32),
            vm((rows, 2 * WIDTH), BF),
            vm((rows, WIDTH), F32),
            vm((WIDTH, 3 * WIDTH), F32),
            vm((nz - 1, rows, WIDTH), BF),
            vm((nz - 1, rows, WIDTH), BF),
            vm((WIDTH, 128), F32),
            pltpu.SemaphoreType.DMA((nz - 1,)),
            pltpu.SemaphoreType.DMA((nz - 1,)),
        ],
        compiler_params=pltpu.CompilerParams(collective_id=1, has_side_effects=True, vmem_limit_bytes=58 << 20),
        cost_estimate=pl.CostEstimate(flops=24_000_000_000, bytes_accessed=40_000_000, transcendentals=13_000_000),
        name="back",
    )(tok, gmid, query, keys, values, firsts, wqkv, gain, gmixed, lse, delta, cos, sine)


class Reduce:
    COPIES = 10

    def __init__(self, src, total, cut, nz, masks, bufs, send, recv, loc):
        self.src, self.total, self.cut, self.nz, self.masks = src, total, cut, nz, masks
        self.mine, self.near, self.side0, self.side1, self.far = bufs
        self.send, self.recv, self.loc = send, recv, loc
        self.dp, self.z = lax.axis_index("dp"), lax.axis_index("seq")
        my, mx, mc = masks
        self.turns = (0, my, mx, my ^ mx)
        self.started = []

    @staticmethod
    def scratch(shape, cut, nz):
        r, c = shape
        return [
            pltpu.VMEM((4, nz, r, c), BF),
            pltpu.VMEM((4, nz, r, c), BF),
            pltpu.VMEM((3, nz, r, cut), BF),
            pltpu.VMEM((3, nz, r, c - cut), BF),
            pltpu.VMEM((nz - 1, r, c), BF),
        ], [
            pltpu.SemaphoreType.DMA((Reduce.COPIES * nz + nz,)),
            pltpu.SemaphoreType.DMA((Reduce.COPIES * nz + nz,)),
            pltpu.SemaphoreType.DMA((4 * nz,)),
        ]

    def begin(self, src, dst, device, k):
        c = remote(src, dst, self.send.at[k], self.recv.at[k], device)
        c.start()
        self.started.append(c)

    def arrived(self, ref, k):
        remote(ref, ref, self.send.at[k], self.recv.at[k], {"dp": self.dp ^ self.masks[2]}).wait_recv()

    def seat(self, o):
        return lax.rem(self.z + o, self.nz)

    def local(self, i, o):
        s = self.seat(o)
        return pltpu.make_async_copy(self.src.at[self.dp ^ self.turns[i], s], self.mine.at[i, s], self.loc.at[4 * o + i])

    def zero(self, o):
        s, mc = self.seat(o), self.masks[2]
        for i in (3, 1, 2, 0):
            self.local(i, o).start()
            self.begin(self.src.at[self.dp ^ mc ^ self.turns[i], s], self.near.at[i, s], {"dp": self.dp ^ mc}, self.COPIES * o + i)

    def add(self, ref, other):
        ref[...] = (ref[...].astype(F32) + other[...].astype(F32)).astype(BF)

    def p0(self, i, s):
        return self.mine.at[i, s, :, pl.ds(0, self.cut)]

    def p1(self, i, s):
        return self.mine.at[i, s, :, pl.ds(self.cut, self.mine.shape[-1] - self.cut)]

    def one(self, o):
        my, mx, _ = self.masks
        s, k = self.seat(o), self.COPIES * o
        for i in (3, 1, 2, 0):
            self.local(i, o).wait()
            self.arrived(self.near.at[i, s], k + i)
            self.add(self.mine.at[i, s], self.near.at[i, s])
            if i == 3:
                self.begin(self.p0(3, s), self.side0.at[1, s], {"dp": self.dp ^ my}, k + 4)
                self.begin(self.p1(3, s), self.side1.at[1, s], {"dp": self.dp ^ mx}, k + 5)
            if i == 1:
                self.begin(self.p0(1, s), self.side0.at[0, s], {"dp": self.dp ^ my}, k + 6)
            if i == 2:
                self.begin(self.p1(2, s), self.side1.at[0, s], {"dp": self.dp ^ mx}, k + 7)

    def two(self, o):
        my, mx, _ = self.masks
        s, k = self.seat(o), self.COPIES * o
        self.arrived(self.side0.at[1, s], k + 4)
        self.add(self.p0(2, s), self.side0.at[1, s])
        self.begin(self.p0(2, s), self.side0.at[2, s], {"dp": self.dp ^ mx}, k + 8)
        self.arrived(self.side1.at[1, s], k + 5)
        self.add(self.p1(1, s), self.side1.at[1, s])
        self.begin(self.p1(1, s), self.side1.at[2, s], {"dp": self.dp ^ my}, k + 9)

    def three(self, o):
        s, k = self.seat(o), self.COPIES * o
        for ref, side, k1, k2 in ((self.p0(0, s), self.side0, k + 6, k + 8), (self.p1(0, s), self.side1, k + 7, k + 9)):
            self.arrived(side.at[0, s], k1)
            self.arrived(side.at[2, s], k2)
            ref[...] = (ref[...].astype(F32) + side[0, s].astype(F32) + side[2, s].astype(F32)).astype(BF)
        if o:
            self.begin(self.mine.at[0, s], self.far.at[o - 1], {"seq": s}, self.COPIES * self.nz + o)

    def four(self):
        out = self.mine[0, self.z].astype(F32)
        for o in range(1, self.nz):
            self.arrived(self.far.at[o - 1], self.COPIES * self.nz + o)
            out = out + self.far[o - 1].astype(F32)
        self.total[...] = out

    def done(self):
        for c in self.started:
            c.wait_send()


def reduce_kernel(nz, masks, n, *refs):
    srcs, totals, rest = refs[:n], refs[n : 2 * n], refs[2 * n :]
    dp, z = lax.axis_index("dp"), lax.axis_index("seq")
    greet(z, nz, dp, masks)
    jobs = []
    for i in range(n):
        part = rest[8 * i : 8 * i + 8]
        jobs.append(Reduce(srcs[i], totals[i], half_lanes(srcs[i].shape[-1]), nz, masks, part[:5], *part[5:]))
    order = list(range(1, nz)) + [0]
    for step in ("zero", "one", "two", "three"):
        for j in jobs:
            for o in order:
                getattr(j, step)(o)
    for j in jobs:
        j.four()
    for j in jobs:
        j.done()


def reduced(packs, nz, masks):
    scratch = []
    for p in packs:
        bufs, sems = Reduce.scratch(p.shape[-2:], half_lanes(p.shape[-1]), nz)
        scratch += bufs + sems
    return pl.pallas_call(
        functools.partial(reduce_kernel, nz, masks, len(packs)),
        out_shape=[jax.ShapeDtypeStruct(p.shape[-2:], F32) for p in packs],
        in_specs=[pl.BlockSpec(memory_space=pl.ANY)] * len(packs),
        out_specs=[pl.BlockSpec(memory_space=pltpu.VMEM)] * len(packs),
        scratch_shapes=scratch,
        compiler_params=pltpu.CompilerParams(collective_id=2, has_side_effects=True, vmem_limit_bytes=58 << 20),
        name="sum_packs",
    )(*packs)


def pack_qkv(w_qkv, gain):
    r = w_qkv.shape[0]
    body = jnp.concatenate([w_qkv[:, :1152], w_qkv[:, 1152:]], 0)
    return jnp.concatenate([body, jnp.pad(gain[:, None], ((0, r), (0, 127)))], 1)


def pack_out(w_out, gain):
    r = w_out.shape[0]
    body = jnp.concatenate([w_out[:, :384], w_out[:, 384:]], 0)
    return jnp.concatenate([body, jnp.pad(gain[:, None], ((0, r), (0, 127)))], 1)


def unpack_rows(total):
    r, c = total.shape[0] // 2, total.shape[1] - 128
    return jnp.concatenate([total[:r, :c], total[r:, :c]], 1), total[:r, c]


def pack_mlp(w_in, w_down):
    parts = (w_in[:, 0], w_in[:, 1], w_down.T)
    pads = jnp.zeros((w_in.shape[0], 128 - 3 * REST), BF)
    return jnp.concatenate([x[:, :MAIN] for x in parts] + [x[:, MAIN:] for x in parts] + [pads], 1)


def unpack_mlp(total):
    gate, up, down = [
        jnp.concatenate([total[:, MAIN * i : MAIN * i + MAIN], total[:, 3 * MAIN + REST * i : 3 * MAIN + REST * i + REST]], 1)
        for i in range(3)
    ]
    return jnp.stack([gate, up], 1), down.T


def whole_packs(w_qkv, w_out, attn_gain, mlp_gain, w_in, w_down):
    both = ("dp", "seq")

    def rows_of(w, gain, pack):
        w, gain = lax.all_gather(w, both, axis=0, tiled=True), lax.all_gather(gain, both, axis=0, tiled=True)
        shards = jax.vmap(pack)(w.reshape(GROUPS * LINE, SLIVER, -1), gain.reshape(GROUPS * LINE, SLIVER))
        return shards.reshape((GROUPS, LINE) + shards.shape[1:])

    mlp = pack_mlp(lax.all_gather(w_in, "dp", axis=0, tiled=True), lax.all_gather(w_down, "dp", axis=1, tiled=True))
    mlp = lax.all_gather(mlp, "seq", axis=0, tiled=False)
    mlp = mlp.reshape(LINE, GROUPS, BAND, -1).transpose(1, 0, 2, 3)
    return rows_of(w_qkv, attn_gain, pack_qkv), rows_of(w_out, mlp_gain, pack_out), mlp


def whole_sums(pq_g, po_g, pm_g):
    both = ("dp", "seq")
    found = []
    for pack in (pq_g, po_g):
        w, gain = jax.vmap(unpack_rows)(pack.reshape((GROUPS * LINE,) + pack.shape[2:]).astype(F32))
        found.append(lax.psum_scatter(w.reshape(WIDTH, -1), both, scatter_dimension=0, tiled=True))
        found.append(lax.psum_scatter(gain.reshape(WIDTH), both, scatter_dimension=0, tiled=True))
    mlp = pm_g.astype(F32).transpose(1, 0, 2, 3).reshape(LINE, WIDTH, -1)
    mlp = lax.psum_scatter(mlp, "seq", scatter_dimension=0, tiled=False)
    mlp = lax.psum_scatter(mlp, "dp", scatter_dimension=0, tiled=True)
    return found + list(unpack_mlp(mlp))


def on_device(tokens, w_qkv, w_out, attn_gain, mlp_gain, w_in, w_down, grad_out, *, dp, nz):
    rows = tokens.shape[0]
    masks = (dp // 2, dp // 4, 1) if dp == GROUPS and nz == LINE else None
    cos, sine = [jnp.asarray(t).reshape(nz, rows, 128) for t in rope_tables(nz * rows)]
    if masks:
        packs = [pack_qkv(w_qkv, attn_gain), pack_out(w_out, mlp_gain), pack_mlp(w_in, w_down)]
        mixed, lse, query, keys, values, firsts, wqkv, gain, po_all, pm_all = front(tokens, packs, cos, sine, nz, masks)
    else:
        pq_all, po_all, pm_all = whole_packs(w_qkv, w_out, attn_gain, mlp_gain, w_in, w_down)
        mixed, lse, query, keys, values, firsts, wqkv, gain = front(tokens, [pq_all], cos, sine, nz, None)
    out, gmid, gmixed, delta, po_g, pm_g = middle(tokens, mixed, grad_out, po_all, pm_all)
    gtok, pq_g = back(tokens, gmid, query, keys, values, firsts, wqkv, gain, gmixed, lse, delta, cos, sine, nz)
    if masks:
        sq, so, sm = reduced([pq_g, po_g, pm_g], nz, masks)
        g_qkv, g_gain_a = unpack_rows(sq)
        g_out, g_gain_m = unpack_rows(so)
        g_in, g_down = unpack_mlp(sm)
    else:
        g_qkv, g_gain_a, g_out, g_gain_m, g_in, g_down = whole_sums(pq_g, po_g, pm_g)
    return out, gtok, g_qkv, g_out, g_gain_a, g_gain_m, g_in, g_down


def solution(mesh):
    both = P(("dp", "seq"), None)
    vector = P(("dp", "seq"))
    w_in, w_down = P("dp", None, "seq"), P("seq", "dp")
    step = functools.partial(on_device, dp=mesh.shape["dp"], nz=mesh.shape["seq"])
    return jax.shard_map(
        step,
        mesh=mesh,
        in_specs=(both, both, both, vector, vector, w_in, w_down, both),
        out_specs=(both, both, both, both, vector, vector, w_in, w_down),
        check_vma=False,
    )
```

```python
import functools
import math

import jax
import jax.numpy as jnp
import numpy as np
from jax import lax
from jax.experimental import pallas as pl
from jax.experimental.pallas import tpu as pltpu
from jax.sharding import PartitionSpec as P

HEADS = 12
HEAD_DIM = 64
NORM_EPS = 1e-05
ROPE_THETA = 160000.0

F32 = jnp.float32
BF = jnp.bfloat16
MESH = pl.DeviceIdType.MESH
NT = (((1,), (1,)), ((), ()))
NN = (((1,), (0,)), ((), ()))
TN = (((0,), (0,)), ((), ()))

WIDTH = 768
PAIRS = HEADS // 2
UNITS = 1152
GROUPS = 8
LINE = 4
BAND = WIDTH // GROUPS
SLIVER = BAND // LINE
SHARE = UNITS // LINE
MAIN = 256
REST = SHARE - MAIN
LOG2E = math.log2(math.e)
SCALE = HEAD_DIM**-0.5


def dot(a, b, dims):
    return lax.dot_general(a, b, dims, preferred_element_type=F32)


def lanes_of(tile, width=128):
    return pl.ds(pl.multiple_of(tile * width, width), width)


def lane_iota():
    return lax.broadcasted_iota(jnp.int32, (1, 128), 1)


def swap_halves(u):
    low = lax.rem(lane_iota(), 64) < 32
    return jnp.where(low, pltpu.roll(u, 96, 1), pltpu.roll(u, 32, 1))


def rope(u, cos, sine):
    return u * cos + swap_halves(u) * sine


def rope_back(u, cos, sine):
    return u * cos - swap_halves(u) * sine


def rope_tables(rows):
    position = np.arange(rows, dtype=np.float32)
    half = HEAD_DIM // 2
    freq = (ROPE_THETA ** (-np.arange(half) * 2.0 / HEAD_DIM)).astype(np.float32)
    angle = (position[:, None] * freq[None, :]).astype(np.float64)
    cos, sine = np.cos(angle), np.sin(angle)
    cos = np.concatenate([cos] * 4, 1).astype(np.float32)
    sine = np.concatenate([-sine, sine] * 2, 1).astype(np.float32)
    return cos, sine


def normed(x):
    centred = x - jnp.mean(x, -1, keepdims=True)
    inv = lax.rsqrt(jnp.mean(centred * centred, -1, keepdims=True) + NORM_EPS)
    return centred * inv, inv


def norm_back(dy, gain, hat, inv):
    d = dy * gain
    return inv * (d - jnp.mean(d, -1, keepdims=True) - hat * jnp.mean(d * hat, -1, keepdims=True))


def remote(src, dst, send, recv, device):
    return pltpu.make_async_remote_copy(src, dst, send, recv, device_id=device, device_id_type=MESH)


class Place:
    def __init__(self, nz):
        self.dp, self.z = lax.axis_index("dp"), lax.axis_index("seq")
        self.nz = nz
        upper = self.z // (nz // 2)
        self.moves = lax.rem(self.dp, 2) != upper
        self.stays = lax.rem(self.dp, 2) == upper
        self.shard = jnp.where(self.moves, nz - 1 - self.z, self.z)
        self.opposite = {"dp": self.dp ^ 1, "seq": nz - 1 - self.z}
        self.twin = {"dp": self.dp ^ 1}
        self.beside = {"seq": self.z ^ 1}

    def greet(self, masks):
        bar = pltpu.get_barrier_semaphore()

        def hello(device):
            pl.semaphore_signal(bar, inc=1, device_id=device, device_id_type=MESH)

        for o in range(1, self.nz):
            hello({"seq": lax.rem(self.z + o, self.nz)})
        for m in masks:
            hello({"dp": self.dp ^ m})
        hello(self.opposite)
        pl.semaphore_wait(bar, self.nz + len(masks))


class Gather:
    COPIES = 9

    def __init__(self, src, out, cut, nz, masks, send, recv):
        self.src, self.out, self.cut, self.nz, self.masks = src, out, cut, nz, masks
        self.send, self.recv = send, recv
        self.dp, self.z = lax.axis_index("dp"), lax.axis_index("seq")
        self.started = []

    @staticmethod
    def sems(nz):
        return Gather.COPIES * nz + nz

    def key(self, o, k):
        return o * self.COPIES + k

    def copy(self, src, dst, device, k):
        return remote(src, dst, self.send.at[k], self.recv.at[k], device)

    def begin(self, src, dst, device, k, p=None):
        self.copy(src, dst, device, k).start()
        self.started.append((k, p))

    def arrived(self, ref, k):
        self.copy(ref, ref, {"dp": self.dp ^ self.masks[0]}, k).wait_recv()

    def slot(self, o):
        return lax.rem(self.z + self.nz - o, self.nz)

    def part(self, ref, p):
        if p is None:
            return ref
        width = self.out.shape[-1]
        return ref.at[:, pl.ds(0, self.cut)] if p == 0 else ref.at[:, pl.ds(self.cut, width - self.cut)]

    def along(self):
        for o in range(1, self.nz):
            k = self.COPIES * self.nz + o
            self.begin(self.src, self.out.at[self.dp, self.z], {"seq": lax.rem(self.z + o, self.nz)}, k)

    def forward(self, src, d, s, mask, k, p=None):
        dst = self.out.at[d, s]
        self.begin(self.part(src, p), self.part(dst, p), {"dp": self.dp ^ mask}, k, p)

    def first(self, o):
        my, mx, mc = self.masks
        s = self.slot(o)
        src = self.src
        if o:
            src = self.out.at[self.dp, s]
            self.arrived(src, self.COPIES * self.nz + o)
        self.forward(src, self.dp, s, my, self.key(o, 0))
        self.forward(src, self.dp, s, mx, self.key(o, 1))
        self.forward(src, self.dp, s, mc, self.key(o, 2))

    def second(self, o):
        my, mx, mc = self.masks
        s = self.slot(o)
        for m, k, k2, kc, p, m2 in ((my, 0, 3, 4, 0, mx), (mx, 1, 5, 6, 1, my)):
            ref = self.out.at[self.dp ^ m, s]
            self.arrived(ref, self.key(o, k))
            self.forward(ref, self.dp ^ m, s, m2, self.key(o, k2), p)
            self.forward(ref, self.dp ^ m, s, mc, self.key(o, kc))

    def third(self, o):
        my, mx, mc = self.masks
        s = self.slot(o)
        d = self.dp ^ my ^ mx
        for p, k, kc in ((0, 3, 7), (1, 5, 8)):
            ref = self.out.at[d, s]
            self.arrived(self.part(ref, p), self.key(o, k))
            self.forward(ref, d, s, mc, self.key(o, kc), p)

    def finish(self, o):
        my, mx, mc = self.masks
        s = self.slot(o)
        for k, d in ((2, mc), (4, mc ^ my), (6, mc ^ mx)):
            self.arrived(self.out.at[self.dp ^ d, s], self.key(o, k))
        for k, p in ((7, 0), (8, 1)):
            self.arrived(self.part(self.out.at[self.dp ^ mc ^ my ^ mx, s], p), self.key(o, k))

    def done(self):
        for k, p in self.started:
            ref = self.part(self.out.at[self.dp, self.z], p)
            self.copy(ref, ref, {"dp": self.dp ^ self.masks[0]}, k).wait_send()


def half_lanes(width):
    return (width // 256) * 128


def front_kernel(nz, masks, rows, *refs):
    fused = masks is not None
    if fused:
        (tok, gout, pq, po, pm, cos, sine, mixed, lse, query, gain, tok_own, gout_own, keys, values, firsts, wqkv, po_all, pm_all,
         tok_all, kb, vb, fb, wq, gcol, acc, top, total, tsend, trecv, loc, pq_all, qs, qr, os_, or_, ms, mr) = refs
    else:
        (tok, gout, pq_all, cos, sine, mixed, lse, query, gain, tok_own, gout_own, keys, values, firsts, wqkv,
         tok_all, kb, vb, fb, wq, gcol, acc, top, total, tsend, trecv, loc) = refs
    me = Place(nz)
    own = me.shard

    def here(src, dst, k):
        return pltpu.make_async_copy(src, dst, loc.at[k])

    def there(src, dst, device, k):
        return remote(src, dst, tsend.at[k], trecv.at[k], device)

    @pl.when(me.stays)
    def _():
        here(tok, tok_all.at[own], 0).start()
        here(gout, gout_own, 1).start()

    if fused:
        locals_ = [here(src, out.at[me.dp, me.z], 2 + i) for i, (src, out) in enumerate(((pq, pq_all), (po, po_all), (pm, pm_all)))]
        for c in locals_:
            c.start()
    me.greet(masks or (1,))
    if fused:
        packs = [
            Gather(pq, pq_all, half_lanes(pq.shape[-1]), nz, masks, qs, qr),
            Gather(po, po_all, half_lanes(po.shape[-1]), nz, masks, os_, or_),
            Gather(pm, pm_all, half_lanes(pm.shape[-1]), nz, masks, ms, mr),
        ]
        first, *later = packs
        first.along()
        first.first(0)

    @pl.when(me.stays)
    def _():
        there(tok, tok_all.at[own], me.twin, 1).start()
        there(tok, tok_all.at[own], me.beside, 2).start()

    @pl.when(me.moves)
    def _():
        there(tok, tok_all.at[me.z], me.opposite, 0).start()

    if fused:
        first.second(0)
        for o in range(1, nz):
            first.first(o)
        for o in range(1, nz):
            first.second(o)
        for o in range(nz):
            first.third(o)

    @pl.when(me.moves)
    def _():
        there(tok, tok_all.at[own], me.opposite, 0).wait_recv()
        there(tok_all.at[own], tok_all.at[own], me.twin, 1).start()
        there(tok_all.at[own], tok_all.at[own], me.beside, 2).start()
        there(gout, gout_own, me.opposite, 4).start()

    @pl.when(me.stays)
    def _():
        here(tok, tok_all.at[own], 0).wait()

    here(tok_all.at[own], tok_own, 5).start()
    if fused:
        for g in later:
            g.along()
            g.first(0)
        locals_[0].wait()
        for o in range(nz):
            first.finish(o)

    half = 1152

    def build(g, _):
        slabs = [pq_all[g, s].astype(F32) for s in range(LINE)]
        band = pl.ds(pl.multiple_of(g * BAND, BAND), BAND)
        wq[band, :half] = jnp.concatenate([x[:SLIVER, :half] for x in slabs], 0).astype(BF)
        wq[band, half:] = jnp.concatenate([x[SLIVER:, :half] for x in slabs], 0).astype(BF)
        gcol[band, :] = jnp.concatenate([x[:SLIVER, half:] for x in slabs], 0)
        return 0

    lax.fori_loop(0, GROUPS, build, 0)
    here(wq, wqkv, 6).start()
    gain[...] = gcol[...].T[:8]

    def norm_chunk(c):
        def block(i, _):
            at = pl.ds(pl.multiple_of(i * 64, 64), 64)
            hat, _ = normed(tok_all[c, at, :].astype(F32))
            fb[c, at, :] = (hat * gain[0:1, :]).astype(BF)
            return 0

        lax.fori_loop(0, rows // 64, block, 0)
        here(fb.at[c], firsts.at[c], 7 + c).start()

    def project(c, j, base):
        return dot(fb[c], wq[:, base + 256 * j : base + 256 * j + 256], NN)

    norm_chunk(own)
    for j in range(3):
        u = project(own, j, 0)
        for i in range(2):
            tile = rope(u[:, 128 * i : 128 * i + 128], cos[own], sine[own])
            query[:, 256 * j + 128 * i : 256 * j + 128 * i + 128] = (tile * (SCALE * LOG2E)).astype(BF)
    acc[...] = jnp.zeros_like(acc)
    total[...] = jnp.zeros_like(total)
    top[...] = jnp.full_like(top, -1e30)

    def visit(t, _):
        c = jnp.where(t == 0, own, jnp.where(t == 1, own ^ 3, jnp.where(t == 2, own ^ 1, own ^ 2)))

        @pl.when(t > 0)
        def _():
            there(tok_all.at[c], tok_all.at[c], me.twin, t).wait_recv()

            @pl.when(t == 2)
            def _():
                there(tok_all.at[c], tok_all.at[c], me.twin, 3).start()

            norm_chunk(c)

        for j in range(3):
            u = project(c, j, WIDTH)
            for i in range(2):
                at = 256 * j + 128 * i
                kb[c, :, at : at + 128] = rope(u[:, 128 * i : 128 * i + 128], cos[c], sine[c]).astype(BF)
            vb[c, :, 256 * j : 256 * j + 256] = project(c, j, 2 * WIDTH).astype(BF)
        here(kb.at[c], keys.at[c], 7 + nz + c).start()
        here(vb.at[c], values.at[c], 7 + 2 * nz + c).start()

        def pair(hp, _):
            q, k, v = query[:, lanes_of(hp)], kb[c, :, lanes_of(hp)], vb[c, :, lanes_of(hp)]
            for h in range(2):
                mask = (lane_iota() < 64) if h == 0 else (lane_iota() >= 64)
                s = dot(k, jnp.where(mask, q, jnp.zeros_like(q)), NT)
                at = pl.ds(hp * 2 + h, 1)
                old = top[at, :]
                new = jnp.maximum(old, jnp.max(s, 0, keepdims=True))
                p = jnp.exp2(s - new)
                fade = jnp.exp2(old - new)
                top[at, :] = new
                total[at, :] = total[at, :] * fade + jnp.sum(p, 0, keepdims=True)
                band = pl.ds(pl.multiple_of(hp * 128 + h * 64, 64), 64)
                acc[band, :] = acc[band, :] * fade + dot(v[:, h * 64 : h * 64 + 64], p.astype(BF), TN)
            return 0

        lax.fori_loop(0, PAIRS, pair, 0)
        if fused:

            @pl.when(t == 1)
            def _():
                for g in later:
                    for o in range(1, nz):
                        g.first(o)

            @pl.when(t == 2)
            def _():
                for g in later:
                    for o in range(nz):
                        g.second(o)

            @pl.when(t == 3)
            def _():
                for g in later:
                    for o in range(nz):
                        g.third(o)

        return 0

    lax.fori_loop(0, nz, visit, 0)

    for hp in range(PAIRS):
        parts = [
            acc[128 * hp + 64 * h : 128 * hp + 64 * h + 64, :] / total[2 * hp + h : 2 * hp + h + 1, :] for h in range(2)
        ]
        mixed[:, 128 * hp : 128 * hp + 128] = jnp.concatenate(parts, 0).T.astype(BF)
    lse[...] = top[...] + jnp.log(jnp.maximum(total[...], 1e-30)) * LOG2E

    if fused:
        for g in later:
            for o in range(nz):
                g.finish(o)
        for g in packs:
            g.done()
        for c in locals_[1:]:
            c.wait()
    there(tok, tok_all.at[own], me.twin, 1).wait_send()
    there(tok, tok_all.at[own], me.beside, 2).wait_send()
    there(tok_all.at[own], tok_all.at[own], me.twin, 3).wait_send()

    @pl.when(me.moves)
    def _():
        there(tok, tok_all.at[me.z], me.opposite, 0).wait_send()
        there(gout, gout_own, me.opposite, 4).wait()

    @pl.when(me.stays)
    def _():
        here(gout, gout_own, 1).wait()

    here(tok_all.at[own], tok_own, 5).wait()
    here(wq, wqkv, 6).wait()
    for c in range(nz):
        for i, (buf, dst) in enumerate(((fb, firsts), (kb, keys), (vb, values))):
            here(buf.at[c], dst.at[c], 7 + nz * i + c).wait()


def front(tok, gout, packs, cos, sine, nz, masks):
    rows = tok.shape[0]
    fused = masks is not None
    vmem, anyspace = pl.BlockSpec(memory_space=pltpu.VMEM), pl.BlockSpec(memory_space=pl.ANY)
    shape, vm = jax.ShapeDtypeStruct, pltpu.VMEM
    outs = [shape((rows, WIDTH), BF), shape((16, rows), F32), shape((rows, WIDTH), BF), shape((8, WIDTH), F32)]
    outs += [shape((rows, WIDTH), BF)] * 2 + [shape((nz, rows, WIDTH), BF)] * 3 + [shape((WIDTH, 3 * WIDTH), BF)]
    out_specs = [vmem] * 4 + [anyspace] * 6
    scratch = [vm((nz, rows, WIDTH), BF)] * 4 + [
        vm((WIDTH, 3 * WIDTH), BF),
        vm((WIDTH, 128), F32),
        vm((WIDTH, rows), F32),
        vm((16, rows), F32),
        vm((16, rows), F32),
        pltpu.SemaphoreType.DMA((5,)),
        pltpu.SemaphoreType.DMA((5,)),
        pltpu.SemaphoreType.DMA((7 + 3 * nz,)),
    ]
    if fused:
        pq, po, pm = packs
        outs += [shape((GROUPS, nz) + po.shape, BF), shape((GROUPS, nz) + pm.shape, BF)]
        out_specs += [anyspace] * 2
        in_specs = [anyspace] * 5 + [vmem] * 2
        scratch += [vm((GROUPS, nz) + pq.shape, BF)] + [pltpu.SemaphoreType.DMA((Gather.sems(nz),)) for _ in range(6)]
    else:
        in_specs = [anyspace] * 2 + [vmem] * 3
    return pl.pallas_call(
        functools.partial(front_kernel, nz, masks, rows),
        out_shape=outs,
        in_specs=in_specs,
        out_specs=out_specs,
        scratch_shapes=scratch,
        compiler_params=pltpu.CompilerParams(collective_id=0, has_side_effects=True, vmem_limit_bytes=58 << 20),
        cost_estimate=pl.CostEstimate(flops=14_000_000_000, bytes_accessed=40_000_000, transcendentals=13_000_000),
        name="front",
    )(tok, gout, *packs, cos, sine)


def middle_kernel(rows, tok, mixed, gout, po_all, pm_all, out, gmid, gmixed, delta, po_g, pm_g,
                  wout, wg, wu, wd, gcol, gain, resid, hat, inv, second, hidden, ggate, gup, gsec, gattn, dwout):
    lane = lane_iota()

    def build(g, _):
        band = pl.ds(pl.multiple_of(g * BAND, BAND), BAND)
        slabs = [po_all[g, s].astype(F32) for s in range(LINE)]
        wout[band, :384] = jnp.concatenate([x[:SLIVER, :384] for x in slabs], 0).astype(BF)
        wout[band, 384:] = jnp.concatenate([x[SLIVER:, :384] for x in slabs], 0).astype(BF)
        gcol[band, :] = jnp.concatenate([x[:SLIVER, 384:] for x in slabs], 0)
        for i, w in enumerate((wg, wu, wd)):
            tail = jnp.zeros((BAND, 128), F32)
            for s in range(LINE):
                w[band, MAIN * s : MAIN * s + MAIN] = pm_all[g, s, :, MAIN * i : MAIN * i + MAIN]
                rest = pm_all[g, s, :, 3 * MAIN :].astype(F32)
                turn = (REST * (s - i)) % 128
                rest = pltpu.roll(rest, turn, 1) if turn else rest
                tail = jnp.where((lane >= REST * s) & (lane < REST * (s + 1)), rest, tail)
            w[band, MAIN * LINE :] = tail.astype(BF)
        return 0

    lax.fori_loop(0, GROUPS, build, 0)
    gain[...] = gcol[...].T[:8]

    for j in range(3):
        at = slice(256 * j, 256 * j + 256)
        resid[:, at] = tok[:, at].astype(F32) + dot(mixed[...], wout[:, at], NN)

    def norm_block(i, _):
        at = pl.ds(pl.multiple_of(i * 64, 64), 64)
        h, r = normed(resid[at, :])
        hat[at, :] = h
        inv[at, :] = jnp.broadcast_to(r, (64, 128))
        second[at, :] = (h * gain[0:1, :]).astype(BF)
        return 0

    lax.fori_loop(0, rows // 64, norm_block, 0)

    def units(start, width):
        at = pl.ds(start, width)
        gate, up, gh = dot(second[...], wg[:, at], NN), dot(second[...], wu[:, at], NN), dot(gout[...], wd[:, at], NN)
        cdf = 0.5 + 0.5 * lax.erf(gate * math.sqrt(0.5))
        pdf = jnp.exp2(gate * gate * (-0.5 * LOG2E)) * (1.0 / math.sqrt(2.0 * math.pi))
        act = gate * cdf
        hidden[:, at] = (act * up).astype(BF)
        gup[:, at] = (gh * act).astype(BF)
        ggate[:, at] = (gh * up * (cdf + gate * pdf)).astype(BF)

    def unit_block(i, _):
        units(pl.multiple_of(i * 128, 128), 128)
        return 0

    lax.fori_loop(0, UNITS // 128, unit_block, 0)

    for j in range(3):
        at = slice(256 * j, 256 * j + 256)
        out[:, at] = (resid[:, at] + dot(hidden[...], wd[at, :], NT)).astype(BF)
        gsec[:, at] = dot(ggate[...], wg[at, :], NT) + dot(gup[...], wu[at, :], NT)

    def back_block(i, dgain):
        at = pl.ds(pl.multiple_of(i * 64, 64), 64)
        dy, h = gsec[at, :], hat[at, :]
        gm = gout[at, :].astype(F32) + norm_back(dy, gain[0:1, :], h, inv[at, 0:1])
        gmid[at, :] = gm
        gattn[at, :] = gm.astype(BF)
        return dgain + jnp.sum(dy * h, 0, keepdims=True)

    dgain = lax.fori_loop(0, rows // 64, back_block, jnp.zeros((1, WIDTH), F32))

    heads = lax.broadcasted_iota(jnp.int32, (16, 256), 0)
    for j in range(3):
        at = slice(256 * j, 256 * j + 256)
        gmx = dot(gattn[...], wout[at, :], NT).astype(BF)
        gmixed[:, at] = gmx
        prod = gmx.astype(F32) * mixed[:, at].astype(F32)
        high = prod.astype(BF)
        low = (prod - high.astype(F32)).astype(BF)
        pick = ((lax.broadcasted_iota(jnp.int32, (16, 256), 1) + 256 * j) // HEAD_DIM == heads).astype(BF)
        part = dot(pick, high, NT) + dot(pick, low, NT)
        delta[...] = part if j == 0 else delta[...] + part

    for j in range(2):
        at = slice(384 * j, 384 * j + 384)
        dwout[at, :] = dot(mixed[:, at], gattn[...], TN)
    row = lax.broadcasted_iota(jnp.int32, (128, WIDTH), 0)
    gcol[...] = jnp.where(row == 0, dgain, 0.0).T

    def pack_out(g, _):
        for s in range(LINE):
            at = pl.ds(pl.multiple_of(g * BAND + s * SLIVER, 8), SLIVER)
            x, c = dwout[at, :], gcol[at, :]
            po_g[g, s, :, :384] = jnp.concatenate([x[:, :384], x[:, 384:]], 0).astype(BF)
            po_g[g, s, :, 384:] = jnp.concatenate([c, jnp.zeros_like(c)], 0).astype(BF)
        return 0

    lax.fori_loop(0, GROUPS, pack_out, 0)

    for j in range(2):
        at = slice(384 * j, 384 * j + 384)
        tails = []
        for i, (a, b) in enumerate(((second, ggate), (second, gup), (gout, hidden))):
            for s in range(LINE):
                x = dot(a[:, at], b[:, MAIN * s : MAIN * s + MAIN], TN).astype(BF)
                for g in range(4):
                    pm_g[4 * j + g, s, :, MAIN * i : MAIN * i + MAIN] = x[BAND * g : BAND * g + BAND]
            tails.append(dot(a[:, at], b[:, MAIN * LINE :], TN))
        for s in range(LINE):
            y = jnp.zeros((384, 128), F32)
            for i, tail in enumerate(tails):
                turn = (REST * (i - s)) % 128
                tail = pltpu.roll(tail, turn, 1) if turn else tail
                y = jnp.where((lane >= REST * i) & (lane < REST * (i + 1)), tail, y)
            y = y.astype(BF)
            for g in range(4):
                pm_g[4 * j + g, s, :, 3 * MAIN :] = y[BAND * g : BAND * g + BAND]


def middle(tok, mixed, gout, po_all, pm_all):
    rows = tok.shape[0]
    shape, vm = jax.ShapeDtypeStruct, pltpu.VMEM
    vmem = pl.BlockSpec(memory_space=pltpu.VMEM)
    return pl.pallas_call(
        functools.partial(middle_kernel, rows),
        out_shape=[
            shape((rows, WIDTH), BF),
            shape((rows, WIDTH), F32),
            shape((rows, WIDTH), BF),
            shape((16, rows), F32),
            shape(po_all.shape, BF),
            shape(pm_all.shape, BF),
        ],
        in_specs=[vmem] * 5,
        out_specs=[vmem] * 6,
        scratch_shapes=[
            vm((WIDTH, WIDTH), BF),
            vm((WIDTH, UNITS), BF),
            vm((WIDTH, UNITS), BF),
            vm((WIDTH, UNITS), BF),
            vm((WIDTH, 128), F32),
            vm((8, WIDTH), F32),
            vm((rows, WIDTH), F32),
            vm((rows, WIDTH), F32),
            vm((rows, 128), F32),
            vm((rows, WIDTH), BF),
            vm((rows, UNITS), BF),
            vm((rows, UNITS), BF),
            vm((rows, UNITS), BF),
            vm((rows, WIDTH), F32),
            vm((rows, WIDTH), BF),
            vm((WIDTH, WIDTH), F32),
        ],
        compiler_params=pltpu.CompilerParams(vmem_limit_bytes=58 << 20),
        cost_estimate=pl.CostEstimate(flops=11_000_000_000, bytes_accessed=25_000_000, transcendentals=1_200_000),
        name="middle",
    )(tok, mixed, gout, po_all, pm_all)


class Reduce:
    COPIES = 10

    def __init__(self, src, total, cut, nz, masks, bufs, send, recv, loc=None):
        self.src, self.total, self.cut, self.nz, self.masks = src, total, cut, nz, masks
        self.near, self.side0, self.side1, self.far, *mine = bufs
        self.mine = mine[0] if mine else None
        self.send, self.recv, self.loc = send, recv, loc
        self.dp, self.z = lax.axis_index("dp"), lax.axis_index("seq")
        my, mx, mc = masks
        self.turns = (0, my, mx, my ^ mx)
        self.started = []

    @staticmethod
    def scratch(shape, nz, held):
        r, c = shape
        cut = half_lanes(c)
        bufs = [
            pltpu.VMEM((4, nz, r, c), BF),
            pltpu.VMEM((3, nz, r, cut), BF),
            pltpu.VMEM((3, nz, r, c - cut), BF),
            pltpu.VMEM((nz - 1, r, c), BF),
        ]
        sems = [pltpu.SemaphoreType.DMA((Reduce.COPIES * nz + nz,))] * 2
        if not held:
            bufs += [pltpu.VMEM((4, nz, r, c), BF)]
            sems += [pltpu.SemaphoreType.DMA((4 * nz,))]
        return bufs, sems

    def begin(self, src, dst, device, k):
        remote(src, dst, self.send.at[k], self.recv.at[k], device).start()
        self.started.append((k, src.shape[-1]))

    def arrived(self, ref, k):
        remote(ref, ref, self.send.at[k], self.recv.at[k], {"dp": self.dp ^ self.masks[2]}).wait_recv()

    def seat(self, o):
        return lax.rem(self.z + o, self.nz)

    def held(self, i, s):
        return self.mine.at[i, s] if self.mine is not None else self.src.at[self.dp ^ self.turns[i], s]

    def local(self, i, o):
        s = self.seat(o)
        return pltpu.make_async_copy(self.src.at[self.dp ^ self.turns[i], s], self.mine.at[i, s], self.loc.at[4 * o + i])

    def zero(self, o):
        s, mc = self.seat(o), self.masks[2]
        for i in (3, 1, 2, 0):
            if self.mine is not None:
                self.local(i, o).start()
            self.begin(self.src.at[self.dp ^ mc ^ self.turns[i], s], self.near.at[i, s], {"dp": self.dp ^ mc}, self.COPIES * o + i)

    def add(self, ref, other):
        ref[...] = (ref[...].astype(F32) + other[...].astype(F32)).astype(BF)

    def p0(self, i, s):
        return self.held(i, s).at[:, pl.ds(0, self.cut)]

    def p1(self, i, s):
        return self.held(i, s).at[:, pl.ds(self.cut, self.src.shape[-1] - self.cut)]

    def one(self, o):
        my, mx, _ = self.masks
        s, k = self.seat(o), self.COPIES * o
        for i in (3, 1, 2, 0):
            if self.mine is not None:
                self.local(i, o).wait()
            self.arrived(self.near.at[i, s], k + i)
            self.add(self.held(i, s), self.near.at[i, s])
            if i == 3:
                self.begin(self.p0(3, s), self.side0.at[1, s], {"dp": self.dp ^ my}, k + 4)
                self.begin(self.p1(3, s), self.side1.at[1, s], {"dp": self.dp ^ mx}, k + 5)
            if i == 1:
                self.begin(self.p0(1, s), self.side0.at[0, s], {"dp": self.dp ^ my}, k + 6)
            if i == 2:
                self.begin(self.p1(2, s), self.side1.at[0, s], {"dp": self.dp ^ mx}, k + 7)

    def two(self, o):
        my, mx, _ = self.masks
        s, k = self.seat(o), self.COPIES * o
        self.arrived(self.side0.at[1, s], k + 4)
        self.add(self.p0(2, s), self.side0.at[1, s])
        self.begin(self.p0(2, s), self.side0.at[2, s], {"dp": self.dp ^ mx}, k + 8)
        self.arrived(self.side1.at[1, s], k + 5)
        self.add(self.p1(1, s), self.side1.at[1, s])
        self.begin(self.p1(1, s), self.side1.at[2, s], {"dp": self.dp ^ my}, k + 9)

    def three(self, o):
        s, k = self.seat(o), self.COPIES * o
        for ref, side, k1, k2 in ((self.p0(0, s), self.side0, k + 6, k + 8), (self.p1(0, s), self.side1, k + 7, k + 9)):
            self.arrived(side.at[0, s], k1)
            self.arrived(side.at[2, s], k2)
            ref[...] = (ref[...].astype(F32) + side[0, s].astype(F32) + side[2, s].astype(F32)).astype(BF)
        if o:
            self.begin(self.held(0, s), self.far.at[o - 1], {"seq": s}, self.COPIES * self.nz + o)

    def four(self):
        out = self.held(0, self.z)[...].astype(F32)
        for o in range(1, self.nz):
            self.arrived(self.far.at[o - 1], self.COPIES * self.nz + o)
            out = out + self.far[o - 1].astype(F32)
        self.total[...] = out

    def done(self):
        for k, width in self.started:
            whole = width == self.src.shape[-1]
            ref = self.near.at[0, 0] if whole else (self.side0 if k % self.COPIES in (4, 6, 8) else self.side1).at[0, 0]
            remote(ref, ref, self.send.at[k], self.recv.at[k], {"dp": self.dp ^ self.masks[2]}).wait_send()


def back_kernel(nz, masks, rows, *refs):
    fused = masks is not None
    (tok, gmid, out_own, query, keys, values, firsts, wqkv, gain, gmixed, lse, delta, cos, sine), refs = refs[:14], refs[14:]
    if fused:
        (po_g, pm_g, gtok, out, sq, so, sm), refs = refs[:7], refs[7:]
    else:
        (gtok, out, pq_g), refs = refs[:3], refs[3:]
    (kb, vb, fb, ft, wq, dq, dkv, dx, dw, sent, landed, gown, gcol, send, recv, loc), refs = refs[:16], refs[16:]
    me = Place(nz)
    own = me.shard
    me.greet(masks or (1,))

    def here(src, dst, k):
        return pltpu.make_async_copy(src, dst, loc.at[k])

    def there(src, dst, device, k):
        return remote(src, dst, send.at[k], recv.at[k], device)

    def chunk(t):
        return jnp.where(t == 0, own ^ 2, jnp.where(t == 1, own ^ 1, jnp.where(t == 2, own ^ 3, own)))

    def fetch(t):
        c, slot = chunk(t), lax.rem(t, 2)
        return [here(src.at[c], buf.at[slot], 3 * slot + i) for i, (src, buf) in enumerate(((keys, kb), (values, vb), (firsts, fb)))]

    for c in fetch(0):
        c.start()
    here(wqkv, wq, 6).start()
    jobs = []
    if fused:
        pq_g, refs = refs[0], refs[1:]
        last = Reduce(pq_g, sq, half_lanes(pq_g.shape[-1]), nz, masks, refs[:4], *refs[4:6])
        refs = refs[6:]
        for src, total in ((po_g, so), (pm_g, sm)):
            jobs.append(Reduce(src, total, half_lanes(src.shape[-1]), nz, masks, refs[:5], *refs[5:8]))
            refs = refs[8:]
    order = list(range(1, nz)) + [0]

    def advance(which, step):
        for j in which:
            for o in order:
                getattr(j, step)(o)

    advance(jobs, "zero")

    @pl.when(me.moves)
    def _():
        there(out_own, out, me.opposite, 3).start()

    @pl.when(me.stays)
    def _():
        here(out_own, out, 7).start()

    dq[...] = jnp.zeros_like(dq)
    dw[...] = jnp.zeros_like(dw)

    def visit(t, _):
        c, slot = chunk(t), lax.rem(t, 2)
        for f in fetch(t):
            f.wait()

        @pl.when(t + 1 < nz)
        def _():
            for f in fetch(t + 1):
                f.start()

        def pair(hp, _):
            at = lanes_of(hp)
            q, g, k, v = query[:, at], gmixed[:, at], kb[slot, :, at], vb[slot, :, at]
            dk = dv = None
            for h in range(2):
                mask = (lane_iota() < 64) if h == 0 else (lane_iota() >= 64)
                qh, gh = jnp.where(mask, q, jnp.zeros_like(q)), jnp.where(mask, g, jnp.zeros_like(g))
                head = pl.ds(hp * 2 + h, 1)
                p = jnp.exp2(dot(k, qh, NT) - lse[head, :])
                ds = (p * (dot(v, gh, NT) - delta[head, :])).astype(BF)
                a = dot(p.astype(BF), gh, NN)
                dv = a if dv is None else dv + a
                a = dot(ds, qh, NN)
                dk = a if dk is None else dk + a
                band = pl.ds(pl.multiple_of(hp * 128 + h * 64, 64), 64)
                dq[band, :] += dot(k[:, h * 64 : h * 64 + 64], ds, TN)
            dkv[:, at] = rope_back(dk * (1.0 / LOG2E), cos[c], sine[c]).astype(BF)
            dkv[:, lanes_of(hp + PAIRS)] = dv.astype(BF)
            return 0

        lax.fori_loop(0, PAIRS, pair, 0)

        @pl.when(t == 0)
        def _():
            here(wqkv, wq, 6).wait()

        for j in range(3):
            at = slice(256 * j, 256 * j + 256)
            dx[:, at] = dot(dkv[...], wq[at, WIDTH:], NT)

        @pl.when(lax.rem(t, 2) == 0)
        def _():
            sent[t] = dx[...].astype(BF)
            there(sent.at[t], landed.at[t], me.twin, t).start()

        @pl.when(t == 1)
        def _():
            there(sent.at[0], landed.at[0], me.twin, 0).wait_recv()
            sent[1] = (dx[...] + landed[0].astype(F32)).astype(BF)
            there(sent.at[1], landed.at[1], me.beside, 1).start()

        for j in range(6):
            ft[128 * j : 128 * j + 128, :] = fb[slot, :, 128 * j : 128 * j + 128].T

        def weigh(i, _):
            at, to = lanes_of(i, 256), lanes_of(i + 3, 256)
            for j in range(2):
                r = slice(384 * j, 384 * j + 384)
                dw[r, to] += dot(ft[r, :], dkv[:, at], NN)
            return 0

        lax.fori_loop(0, 6, weigh, 0)
        if fused:
            for k, step in enumerate(("one", "two", "three")):

                @pl.when(t == k)
                def _(step=step):
                    advance(jobs, step)

        return 0

    lax.fori_loop(0, nz, visit, 0)

    for hp in range(PAIRS):
        at = slice(128 * hp, 128 * hp + 128)
        u = dq[at, :].T * SCALE
        dkv[:, at] = rope_back(u, cos[own], sine[own]).astype(BF)
    for j in range(3):
        at = slice(256 * j, 256 * j + 256)
        dx[:, at] += dot(dkv[:, :WIDTH], wq[at, :WIDTH], NT)
        for i in range(2):
            r = slice(384 * i, 384 * i + 384)
            dw[r, at] = dot(ft[r, :], dkv[:, at], NN)

    there(sent.at[1], landed.at[1], me.beside, 1).wait_recv()
    there(sent.at[2], landed.at[2], me.twin, 2).wait_recv()

    def norm_block(i, dgain):
        at = pl.ds(pl.multiple_of(i * 64, 64), 64)
        dy = dx[at, :] + landed[1, at, :].astype(F32) + landed[2, at, :].astype(F32)
        h, r = normed(tok[at, :].astype(F32))
        gown[at, :] = (gmid[at, :] + norm_back(dy, gain[0:1, :], h, r)).astype(BF)
        return dgain + jnp.sum(dy * h, 0, keepdims=True)

    dgain = lax.fori_loop(0, rows // 64, norm_block, jnp.zeros((1, WIDTH), F32))

    @pl.when(me.moves)
    def _():
        there(gown, gtok, me.opposite, 4).start()

    @pl.when(me.stays)
    def _():
        here(gown, gtok, 8).start()

    row = lax.broadcasted_iota(jnp.int32, (128, WIDTH), 0)
    gcol[...] = jnp.where(row == 0, dgain, 0.0).T

    def pack(g, _):
        for s in range(LINE):
            at = pl.ds(pl.multiple_of(g * BAND + s * SLIVER, 8), SLIVER)
            x, c = dw[at, :], gcol[at, :]
            pq_g[g, s, :, :1152] = jnp.concatenate([x[:, :1152], x[:, 1152:]], 0).astype(BF)
            pq_g[g, s, :, 1152:] = jnp.concatenate([c, jnp.zeros_like(c)], 0).astype(BF)
        return 0

    lax.fori_loop(0, GROUPS, pack, 0)
    if fused:
        advance([last], "zero")
        for j in jobs:
            j.four()
        for step in ("one", "two", "three"):
            advance([last], step)
        last.four()
        for j in jobs + [last]:
            j.done()
    for k, device in ((0, me.twin), (1, me.beside), (2, me.twin)):
        there(sent.at[k], landed.at[k], device, k).wait_send()

    @pl.when(me.moves)
    def _():
        there(out_own, out, me.opposite, 3).wait()
        there(gown, gtok, me.opposite, 4).wait()

    @pl.when(me.stays)
    def _():
        here(out_own, out, 7).wait()
        here(gown, gtok, 8).wait()


def back(tok, gmid, out_own, query, keys, values, firsts, wqkv, gain, gmixed, lse, delta, cos, sine, packs, nz, masks):
    rows = tok.shape[0]
    shape, vm = jax.ShapeDtypeStruct, pltpu.VMEM
    vmem, anyspace = pl.BlockSpec(memory_space=pltpu.VMEM), pl.BlockSpec(memory_space=pl.ANY)
    in_specs = [vmem, vmem, anyspace, vmem, anyspace, anyspace, anyspace, anyspace] + [vmem] * 6
    slab = (2 * SLIVER, 1280)
    outs, out_specs = [shape((rows, WIDTH), BF)] * 2, [anyspace] * 2
    scratch = [vm((2, rows, WIDTH), BF)] * 3 + [
        vm((WIDTH, rows), BF),
        vm((WIDTH, 3 * WIDTH), BF),
        vm((WIDTH, rows), F32),
        vm((rows, 2 * WIDTH), BF),
        vm((rows, WIDTH), F32),
        vm((WIDTH, 3 * WIDTH), F32),
        vm((3, rows, WIDTH), BF),
        vm((3, rows, WIDTH), BF),
        vm((rows, WIDTH), BF),
        vm((WIDTH, 128), F32),
        pltpu.SemaphoreType.DMA((5,)),
        pltpu.SemaphoreType.DMA((5,)),
        pltpu.SemaphoreType.DMA((9,)),
    ]
    if masks:
        in_specs += [anyspace] * 2
        outs += [shape(s, F32) for s in (slab, packs[0].shape[-2:], packs[1].shape[-2:])]
        out_specs += [vmem] * 3
        scratch += [vm((GROUPS, LINE) + slab, BF)]
        for s, held in ((slab, True), (packs[0].shape[-2:], False), (packs[1].shape[-2:], False)):
            bufs, sems = Reduce.scratch(s, nz, held)
            scratch += bufs + sems
    else:
        outs += [shape((GROUPS, LINE) + slab, BF)]
        out_specs += [vmem]
        packs = []
    return pl.pallas_call(
        functools.partial(back_kernel, nz, masks, rows),
        out_shape=outs,
        in_specs=in_specs,
        out_specs=out_specs,
        scratch_shapes=scratch,
        compiler_params=pltpu.CompilerParams(collective_id=1, has_side_effects=True, vmem_limit_bytes=60 << 20),
        cost_estimate=pl.CostEstimate(flops=24_000_000_000, bytes_accessed=40_000_000, transcendentals=13_000_000),
        name="back",
    )(tok, gmid, out_own, query, keys, values, firsts, wqkv, gain, gmixed, lse, delta, cos, sine, *packs)


def pack_qkv(w_qkv, gain):
    r = w_qkv.shape[0]
    body = jnp.concatenate([w_qkv[:, :1152], w_qkv[:, 1152:]], 0)
    return jnp.concatenate([body, jnp.pad(gain[:, None], ((0, r), (0, 127)))], 1)


def pack_out(w_out, gain):
    r = w_out.shape[0]
    body = jnp.concatenate([w_out[:, :384], w_out[:, 384:]], 0)
    return jnp.concatenate([body, jnp.pad(gain[:, None], ((0, r), (0, 127)))], 1)


def unpack_rows(total):
    r, c = total.shape[0] // 2, total.shape[1] - 128
    return jnp.concatenate([total[:r, :c], total[r:, :c]], 1), total[:r, c]


def pack_mlp(w_in, w_down):
    parts = (w_in[:, 0], w_in[:, 1], w_down.T)
    pads = jnp.zeros((w_in.shape[0], 128 - 3 * REST), BF)
    return jnp.concatenate([x[:, :MAIN] for x in parts] + [x[:, MAIN:] for x in parts] + [pads], 1)


def unpack_mlp(total):
    gate, up, down = [
        jnp.concatenate([total[:, MAIN * i : MAIN * i + MAIN], total[:, 3 * MAIN + REST * i : 3 * MAIN + REST * i + REST]], 1)
        for i in range(3)
    ]
    return jnp.stack([gate, up], 1), down.T


def whole_packs(w_qkv, w_out, attn_gain, mlp_gain, w_in, w_down):
    both = ("dp", "seq")

    def rows_of(w, gain, pack):
        w, gain = lax.all_gather(w, both, axis=0, tiled=True), lax.all_gather(gain, both, axis=0, tiled=True)
        shards = jax.vmap(pack)(w.reshape(GROUPS * LINE, SLIVER, -1), gain.reshape(GROUPS * LINE, SLIVER))
        return shards.reshape((GROUPS, LINE) + shards.shape[1:])

    mlp = pack_mlp(lax.all_gather(w_in, "dp", axis=0, tiled=True), lax.all_gather(w_down, "dp", axis=1, tiled=True))
    mlp = lax.all_gather(mlp, "seq", axis=0, tiled=False)
    mlp = mlp.reshape(LINE, GROUPS, BAND, -1).transpose(1, 0, 2, 3)
    return rows_of(w_qkv, attn_gain, pack_qkv), rows_of(w_out, mlp_gain, pack_out), mlp


def whole_sums(pq_g, po_g, pm_g):
    both = ("dp", "seq")
    found = []
    for pack in (pq_g, po_g):
        w, gain = jax.vmap(unpack_rows)(pack.reshape((GROUPS * LINE,) + pack.shape[2:]).astype(F32))
        found.append(lax.psum_scatter(w.reshape(WIDTH, -1), both, scatter_dimension=0, tiled=True))
        found.append(lax.psum_scatter(gain.reshape(WIDTH), both, scatter_dimension=0, tiled=True))
    mlp = pm_g.astype(F32).transpose(1, 0, 2, 3).reshape(LINE, WIDTH, -1)
    mlp = lax.psum_scatter(mlp, "seq", scatter_dimension=0, tiled=False)
    mlp = lax.psum_scatter(mlp, "dp", scatter_dimension=0, tiled=True)
    return found + list(unpack_mlp(mlp))


def on_device(tokens, w_qkv, w_out, attn_gain, mlp_gain, w_in, w_down, grad_out, *, dp, nz):
    rows = tokens.shape[0]
    masks = (dp // 2, dp // 4, 1) if dp == GROUPS and nz == LINE else None
    cos, sine = [jnp.asarray(t).reshape(nz, rows, 128) for t in rope_tables(nz * rows)]
    if masks:
        packs = [pack_qkv(w_qkv, attn_gain), pack_out(w_out, mlp_gain), pack_mlp(w_in, w_down)]
        got = front(tokens, grad_out, packs, cos, sine, nz, masks)
        po_all, pm_all = got[-2:]
    else:
        pq_all, po_all, pm_all = whole_packs(w_qkv, w_out, attn_gain, mlp_gain, w_in, w_down)
        got = front(tokens, grad_out, [pq_all], cos, sine, nz, None)
    mixed, lse, query, gain, tok_own, gout_own, keys, values, firsts, wqkv = got[:10]
    out_own, gmid, gmixed, delta, po_g, pm_g = middle(tok_own, mixed, gout_own, po_all, pm_all)
    found = back(
        tok_own, gmid, out_own, query, keys, values, firsts, wqkv, gain, gmixed, lse, delta, cos, sine, [po_g, pm_g], nz, masks
    )
    gtok, out = found[:2]
    if masks:
        sq, so, sm = found[2:]
        g_qkv, g_gain_a = unpack_rows(sq)
        g_out, g_gain_m = unpack_rows(so)
        g_in, g_down = unpack_mlp(sm)
    else:
        g_qkv, g_gain_a, g_out, g_gain_m, g_in, g_down = whole_sums(found[2], po_g, pm_g)
    return out, gtok, g_qkv, g_out, g_gain_a, g_gain_m, g_in, g_down


def solution(mesh):
    both = P(("dp", "seq"), None)
    vector = P(("dp", "seq"))
    w_in, w_down = P("dp", None, "seq"), P("seq", "dp")
    step = functools.partial(on_device, dp=mesh.shape["dp"], nz=mesh.shape["seq"])
    return jax.shard_map(
        step,
        mesh=mesh,
        in_specs=(both, both, both, vector, vector, w_in, w_down, both),
        out_specs=(both, both, both, both, vector, vector, w_in, w_down),
        check_vma=False,
    )
```

```python
import functools
import math

import jax
import jax.numpy as jnp
import numpy as np
from jax import lax
from jax.experimental import pallas as pl
from jax.experimental.pallas import tpu as pltpu
from jax.sharding import PartitionSpec as P

HEADS = 12
HEAD_DIM = 64
NORM_EPS = 1e-05
ROPE_THETA = 160000.0

F32 = jnp.float32
BF = jnp.bfloat16
MESH = pl.DeviceIdType.MESH
NT = (((1,), (1,)), ((), ()))
NN = (((1,), (0,)), ((), ()))
TN = (((0,), (0,)), ((), ()))

WIDTH = 768
PAIRS = HEADS // 2
UNITS = 1152
GROUPS = 8
LINE = 4
BAND = WIDTH // GROUPS
SLIVER = BAND // LINE
SHARE = UNITS // LINE
MAIN = 256
REST = SHARE - MAIN
LINKED = (0, 1, 3, 2)
HALF = WIDTH // 2
CUTS = {640: 256, 512: 256, 896: 384}
LOG2E = math.log2(math.e)
SCALE = HEAD_DIM**-0.5


def dot(a, b, dims):
    return lax.dot_general(a, b, dims, preferred_element_type=F32)


def lanes_of(tile, width=128):
    return pl.ds(pl.multiple_of(tile * width, width), width)


def lane_iota():
    return lax.broadcasted_iota(jnp.int32, (1, 128), 1)


def swap_halves(u):
    low = lax.rem(lane_iota(), 64) < 32
    return jnp.where(low, pltpu.roll(u, 96, 1), pltpu.roll(u, 32, 1))


def rope(u, cos, sine):
    return u * cos + swap_halves(u) * sine


def rope_back(u, cos, sine):
    return u * cos - swap_halves(u) * sine


def rope_tables(rows):
    position = np.arange(rows, dtype=np.float32)
    half = HEAD_DIM // 2
    freq = (ROPE_THETA ** (-np.arange(half) * 2.0 / HEAD_DIM)).astype(np.float32)
    angle = (position[:, None] * freq[None, :]).astype(np.float64)
    cos, sine = np.cos(angle), np.sin(angle)
    cos = np.concatenate([cos] * 4, 1).astype(np.float32)
    sine = np.concatenate([-sine, sine] * 2, 1).astype(np.float32)
    return cos, sine


def normed(x):
    centred = x - jnp.mean(x, -1, keepdims=True)
    inv = lax.rsqrt(jnp.mean(centred * centred, -1, keepdims=True) + NORM_EPS)
    return centred * inv, inv


def norm_back(dy, gain, hat, inv):
    d = dy * gain
    return inv * (d - jnp.mean(d, -1, keepdims=True) - hat * jnp.mean(d * hat, -1, keepdims=True))


def remote(src, dst, send, recv, device):
    return pltpu.make_async_remote_copy(src, dst, send, recv, device_id=device, device_id_type=MESH)


class Place:
    def __init__(self, nz):
        self.dp, self.z = lax.axis_index("dp"), lax.axis_index("seq")
        self.nz = nz
        upper = self.z // (nz // 2)
        self.moves = lax.rem(self.dp, 2) != upper
        self.stays = lax.rem(self.dp, 2) == upper
        self.shard = jnp.where(self.moves, nz - 1 - self.z, self.z)
        self.opposite = {"dp": self.dp ^ 1, "seq": nz - 1 - self.z}
        self.twin = {"dp": self.dp ^ 1}
        self.beside = {"seq": self.z ^ 1}

    def greet(self, masks):
        bar = pltpu.get_barrier_semaphore()

        def hello(device):
            pl.semaphore_signal(bar, inc=1, device_id=device, device_id_type=MESH)

        for o in range(1, self.nz):
            hello({"seq": lax.rem(self.z + o, self.nz)})
        for m in masks:
            hello({"dp": self.dp ^ m})
        hello(self.opposite)
        pl.semaphore_wait(bar, self.nz + len(masks))


class Gather:
    COPIES = 9

    def __init__(self, src, out, cut, nz, masks, send, recv):
        self.src, self.out, self.cut, self.nz, self.masks = src, out, cut, nz, masks
        self.send, self.recv = send, recv
        self.dp, self.z = lax.axis_index("dp"), lax.axis_index("seq")
        self.started = []
        self.relayed = None

    @staticmethod
    def sems(nz):
        return Gather.COPIES * nz + nz

    def key(self, o, k):
        return o * self.COPIES + k

    def copy(self, src, dst, device, k):
        return remote(src, dst, self.send.at[k], self.recv.at[k], device)

    def begin(self, src, dst, device, k, p=None):
        self.copy(src, dst, device, k).start()
        self.started.append((k, p))

    def arrived(self, ref, k):
        self.copy(ref, ref, {"dp": self.dp ^ self.masks[0]}, k).wait_recv()

    def slot(self, o):
        return self.z ^ LINKED[o]

    def part(self, ref, p):
        if p is None:
            return ref
        width = self.out.shape[-1]
        return ref.at[:, pl.ds(0, self.cut)] if p == 0 else ref.at[:, pl.ds(self.cut, width - self.cut)]

    def along(self, o):
        self.begin(self.src, self.out.at[self.dp, self.z], {"seq": self.z ^ LINKED[o]}, self.COPIES * self.nz + o)

    def relay(self, o):
        ref = self.out.at[self.dp, self.slot(o)]
        self.arrived(ref, self.COPIES * self.nz + o)
        self.relayed = o
        self.begin(ref, ref, {"seq": self.z ^ 1}, self.COPIES * self.nz + 3)

    def forward(self, src, d, s, mask, k, p=None):
        dst = self.out.at[d, s]
        self.begin(self.part(src, p), self.part(dst, p), {"dp": self.dp ^ mask}, k, p)

    def first(self, o):
        my, mx, mc = self.masks
        s = self.slot(o)
        src = self.src
        if o:
            src = self.out.at[self.dp, s]
            if o != self.relayed:
                self.arrived(src, self.COPIES * self.nz + o)
        self.forward(src, self.dp, s, my, self.key(o, 0))
        self.forward(src, self.dp, s, mx, self.key(o, 1))
        self.forward(src, self.dp, s, mc, self.key(o, 2))

    def second(self, o):
        my, mx, mc = self.masks
        s = self.slot(o)
        for m, k, k2, kc, p, m2 in ((my, 0, 3, 4, 0, mx), (mx, 1, 5, 6, 1, my)):
            ref = self.out.at[self.dp ^ m, s]
            self.arrived(ref, self.key(o, k))
            self.forward(ref, self.dp ^ m, s, m2, self.key(o, k2), p)
            self.forward(ref, self.dp ^ m, s, mc, self.key(o, kc))

    def third(self, o):
        my, mx, mc = self.masks
        s = self.slot(o)
        d = self.dp ^ my ^ mx
        for p, k, kc in ((0, 3, 7), (1, 5, 8)):
            ref = self.out.at[d, s]
            self.arrived(self.part(ref, p), self.key(o, k))
            self.forward(ref, d, s, mc, self.key(o, kc), p)

    def finish(self, o):
        my, mx, mc = self.masks
        s = self.slot(o)
        for k, d in ((2, mc), (4, mc ^ my), (6, mc ^ mx)):
            self.arrived(self.out.at[self.dp ^ d, s], self.key(o, k))
        for k, p in ((7, 0), (8, 1)):
            self.arrived(self.part(self.out.at[self.dp ^ mc ^ my ^ mx, s], p), self.key(o, k))

    def done(self):
        for k, p in self.started:
            ref = self.part(self.out.at[self.dp, self.z], p)
            self.copy(ref, ref, {"dp": self.dp ^ self.masks[0]}, k).wait_send()


def pack_group(w, tile, i):
    q, k, v = [w[:, WIDTH * j + HALF * i : WIDTH * j + HALF * i + HALF] for j in range(3)]
    return jnp.concatenate([jnp.concatenate([q, v[:, :256]], 1), jnp.concatenate([k, v[:, 256:], tile], 1)], 0)


def unpack_group(total):
    r = total.shape[0] // 2
    upper, lower = total[:r], total[r:]
    return upper[:, :HALF], lower[:, :HALF], upper[:, HALF:], lower[:, HALF : HALF + 128], lower[:, HALF + 128 :]


def pack_out(w, tile):
    return jnp.concatenate([jnp.concatenate([w[:, :HALF], w[:, HALF:]], 0), jnp.concatenate([tile, jnp.zeros_like(tile)], 0)], 1)


def pack_mlp(gate, up, down):
    parts = (gate, up, down)
    pads = jnp.zeros((gate.shape[0], 128 - 3 * REST), gate.dtype)
    return jnp.concatenate([x[:, :MAIN] for x in parts] + [x[:, MAIN:] for x in parts] + [pads], 1)


def unpack_mlp(total):
    return [
        jnp.concatenate([total[:, MAIN * i : MAIN * i + MAIN], total[:, 3 * MAIN + REST * i : 3 * MAIN + REST * i + REST]], 1)
        for i in range(3)
    ]


def front_kernel(nz, masks, rows, *refs):
    fused = masks is not None
    if fused:
        (tok, gout, w_qkv, w_out, gains, w_in, w_down, cos_in, sine_in), refs = refs[:9], refs[9:]
    else:
        (tok, gout, g0_all, g1_all, cos_in, sine_in), refs = refs[:6], refs[6:]
    (mixed, lse, query, gain, tok_own, gout_own, kv, firsts, wqkv), refs = refs[:9], refs[9:]
    if fused:
        (po_all, pm_all), refs = refs[:2], refs[2:]
    (tok_all, kvb, fb, wq, cos, sine, gcol, acc, top, total, tsend, trecv, loc), refs = refs[:13], refs[13:]
    me = Place(nz)
    own = me.shard

    def here(src, dst, k):
        return pltpu.make_async_copy(src, dst, loc.at[k])

    def there(src, dst, device, k):
        return remote(src, dst, tsend.at[k], trecv.at[k], device)

    @pl.when(me.stays)
    def _():
        here(tok, tok_all.at[own], 0).start()
        here(gout, gout_own, 1).start()

    here(cos_in, cos, 2).start()
    here(sine_in, sine, 3).start()
    groups, later = [], []
    every, rest = range(nz), (2, 1, 3)
    if fused:
        p0, p1, po, pm, g0_all, g1_all, *sems = refs
        row = lax.broadcasted_iota(jnp.int32, (128, 128), 0)

        def tile_of(i):
            return jnp.where(row == 0, gains[i : i + 1, :], 0.0).T[:SLIVER]

        p0[...] = pack_group(w_qkv[...].astype(F32), tile_of(0), 0).astype(BF)
        g0_all[me.dp, me.z] = p0[...]
    me.greet(masks or (1,))
    if fused:
        shapes = ((p0, g0_all), (p1, g1_all), (po, po_all), (pm, pm_all))
        packs = [
            Gather(src, dst, CUTS[src.shape[-1]], nz, masks, sems[2 * i], sems[2 * i + 1]) for i, (src, dst) in enumerate(shapes)
        ]
        groups, later = packs[:2], packs[2:]
        for o in rest:
            groups[0].along(o)
        groups[0].first(0)

    @pl.when(me.stays)
    def _():
        there(tok, tok_all.at[own], me.twin, 1).start()
        there(tok, tok_all.at[own], me.beside, 2).start()

    @pl.when(me.moves)
    def _():
        there(tok, tok_all.at[me.z], me.opposite, 0).start()

    if fused:
        w = w_qkv[...].astype(F32)
        p1[...] = pack_group(w, jnp.zeros((SLIVER, 128), F32), 1).astype(BF)
        g1_all[me.dp, me.z] = p1[...]
        po[...] = pack_out(w_out[...].astype(F32), tile_of(1)).astype(BF)
        w = w_in[...].astype(F32)
        pm[...] = pack_mlp(w[:, :SHARE], w[:, SHARE:], w_down[...].astype(F32).T).astype(BF)
        here(po, po_all.at[me.dp, me.z], 4).start()
        here(pm, pm_all.at[me.dp, me.z], 5).start()
        for o in rest:
            groups[1].along(o)
        groups[1].first(0)
        groups[0].second(0)
        for o in rest:
            groups[0].first(o)
        for o in rest:
            groups[0].second(o)
        for o in rest:
            groups[1].first(o)
        for g in later:
            g.along(1)
            g.first(0)

    @pl.when(me.moves)
    def _():
        there(tok, tok_all.at[own], me.opposite, 0).wait_recv()
        there(tok_all.at[own], tok_all.at[own], me.twin, 1).start()
        there(tok_all.at[own], tok_all.at[own], me.beside, 2).start()

    @pl.when(me.stays)
    def _():
        here(tok, tok_all.at[own], 0).wait()

    here(tok_all.at[own], tok_own, 6).start()
    if fused:
        for g in later:
            g.along(2)
        for o in range(nz):
            groups[0].third(o)
        for o in range(nz):
            groups[0].finish(o)

    @pl.when(me.moves)
    def _():
        there(gout, gout_own, me.opposite, 4).start()

    here(cos_in, cos, 2).wait()
    here(sine_in, sine, 3).wait()

    def build(i, whole):
        def band_of(g, _):
            slabs = [unpack_group(whole[g, s].astype(F32)) for s in range(LINE)]
            band = pl.ds(pl.multiple_of(g * BAND, BAND), BAND)
            q, k, v0, v1, t = [jnp.concatenate([x[j] for x in slabs], 0) for j in range(5)]
            at = WIDTH * i
            wq[band, at : at + HALF] = k.astype(BF)
            wq[band, at + HALF : at + HALF + 256] = v0.astype(BF)
            wq[band, at + HALF + 256 : at + WIDTH] = v1.astype(BF)
            wq[band, 2 * WIDTH + HALF * i : 2 * WIDTH + HALF * i + HALF] = q.astype(BF)
            if i == 0:
                gcol[band, :] = t
            return 0

        lax.fori_loop(0, GROUPS, band_of, 0)

    def norm_chunk(c):
        def block(i, _):
            at = pl.ds(pl.multiple_of(i * 64, 64), 64)
            hat, _ = normed(tok_all[c, at, :].astype(F32))
            fb[c, at, :] = (hat * gain[0:1, :]).astype(BF)
            return 0

        lax.fori_loop(0, rows // 64, block, 0)
        here(fb.at[c], firsts.at[c], 8 + c).start()

    def queries(i):
        u = dot(fb[own], wq[:, 2 * WIDTH + HALF * i : 2 * WIDTH + HALF * i + HALF], NN)
        for j in range(3):
            tile = rope(u[:, 128 * j : 128 * j + 128], cos[own], sine[own])
            query[:, HALF * i + 128 * j : HALF * i + 128 * j + 128] = (tile * (SCALE * LOG2E)).astype(BF)

    def visits(grp, steps):
        def visit(t, _):
            c = jnp.where(t == 0, own, jnp.where(t == 1, own ^ 3, jnp.where(t == 2, own ^ 1, own ^ 2)))
            if grp == 0:

                @pl.when(t > 0)
                def _():
                    there(tok_all.at[c], tok_all.at[c], me.twin, t).wait_recv()

                    @pl.when(t == 2)
                    def _():
                        there(tok_all.at[c], tok_all.at[c], me.twin, 3).start()

                    norm_chunk(c)

            for j in range(3):
                u = dot(fb[c], wq[:, WIDTH * grp + 256 * j : WIDTH * grp + 256 * j + 256], NN)
                for i in range(2):
                    n = 2 * j + i
                    x = u[:, 128 * i : 128 * i + 128]
                    x = rope(x, cos[c], sine[c]) if n < 3 else x
                    kvb[grp, c, :, 128 * n : 128 * n + 128] = x.astype(BF)
            here(kvb.at[grp, c], kv.at[grp, c], 8 + nz * (1 + grp) + c).start()
            jobs = [(i, h) for i in range(3) for h in range(2)]

            def score(i, h):
                q = query[:, HALF * grp + 128 * i : HALF * grp + 128 * i + 128]
                mask = (lane_iota() < 64) if h == 0 else (lane_iota() >= 64)
                return dot(kvb[grp, c, :, 128 * i : 128 * i + 128], jnp.where(mask, q, jnp.zeros_like(q)), NT)

            ready = [score(*j) for j in jobs[:2]]
            for n, (i, h) in enumerate(jobs):
                if h == 0:
                    vt = kvb[grp, c, :, HALF + 128 * i : HALF + 128 * i + 128].T
                s = ready[n]
                if n + 2 < len(jobs):
                    ready.append(score(*jobs[n + 2]))
                head = 6 * grp + n
                old = top[head : head + 1, :]
                new = jnp.maximum(old, jnp.max(s, 0, keepdims=True))
                p = jnp.exp2(s - new)
                fade = jnp.exp2(old - new)
                top[head : head + 1, :] = new
                lhs = jnp.concatenate([vt[h * 64 : h * 64 + 64], jnp.ones((16, rows), BF)], 0)
                oo = dot(lhs, p.astype(BF), NN)
                total[head : head + 1, :] = total[head : head + 1, :] * fade + oo[64:65]
                acc[64 * head : 64 * head + 64, :] = acc[64 * head : 64 * head + 64, :] * fade + oo[:64]
            if fused:
                for k, step in steps.items():

                    @pl.when(t == k)
                    def _(step=step):
                        for which, name, order in step:
                            for g in which:
                                for o in order:
                                    getattr(g, name)(o)

            return 0

        lax.fori_loop(0, nz, visit, 0)

    build(0, g0_all)
    gain[...] = gcol[...].T[:8]
    norm_chunk(own)
    queries(0)
    acc[...] = jnp.zeros_like(acc)
    total[...] = jnp.zeros_like(total)
    top[...] = jnp.full_like(top, -1e30)
    one = groups[1:]
    visits(0, {0: [(one, "second", every), (later, "first", (1,))], 1: [(one, "third", every)], 2: [(later, "relay", (2,)), (later, "first", (2,))], 3: [(one, "finish", every), (later, "second", (0, 1))]})
    build(1, g1_all)
    here(wq, wqkv, 7).start()
    queries(1)
    visits(1, {0: [(later, "first", (3,))], 1: [(later, "second", (2,))], 2: [(later, "second", (3,))], 3: [(later, "third", every)]})

    for hp in range(PAIRS):
        parts = [
            acc[128 * hp + 64 * h : 128 * hp + 64 * h + 64, :] / total[2 * hp + h : 2 * hp + h + 1, :] for h in range(2)
        ]
        mixed[:, 128 * hp : 128 * hp + 128] = jnp.concatenate(parts, 0).T.astype(BF)
    lse[...] = top[...] + jnp.log(jnp.maximum(total[...], 1e-30)) * LOG2E

    if fused:
        for g in later:
            for o in range(nz):
                g.finish(o)
        for g in packs:
            g.done()
        here(po, po_all.at[me.dp, me.z], 4).wait()
        here(pm, pm_all.at[me.dp, me.z], 5).wait()
    there(tok, tok_all.at[own], me.twin, 1).wait_send()
    there(tok, tok_all.at[own], me.beside, 2).wait_send()
    there(tok_all.at[own], tok_all.at[own], me.twin, 3).wait_send()

    @pl.when(me.moves)
    def _():
        there(tok, tok_all.at[me.z], me.opposite, 0).wait_send()
        there(gout, gout_own, me.opposite, 4).wait()

    @pl.when(me.stays)
    def _():
        here(gout, gout_own, 1).wait()

    here(tok_all.at[own], tok_own, 6).wait()
    here(wq, wqkv, 7).wait()
    for c in range(nz):
        here(fb.at[c], firsts.at[c], 8 + c).wait()
        for grp in range(2):
            here(kvb.at[grp, c], kv.at[grp, c], 8 + nz * (1 + grp) + c).wait()


def front(tok, gout, weights, cos, sine, nz, masks):
    rows = tok.shape[0]
    vmem, anyspace = pl.BlockSpec(memory_space=pltpu.VMEM), pl.BlockSpec(memory_space=pl.ANY)
    shape, vm = jax.ShapeDtypeStruct, pltpu.VMEM
    outs = [shape((rows, WIDTH), BF), shape((16, rows), F32), shape((rows, WIDTH), BF), shape((8, WIDTH), F32)]
    outs += [shape((rows, WIDTH), BF)] * 2
    outs += [shape((2, nz, rows, WIDTH), BF), shape((nz, rows, WIDTH), BF), shape((WIDTH, 3 * WIDTH), BF)]
    out_specs = [vmem] * 4 + [anyspace, vmem] + [anyspace] * 3
    scratch = [
        vm((nz, rows, WIDTH), BF),
        vm((2, nz, rows, WIDTH), BF),
        vm((nz, rows, WIDTH), BF),
        vm((WIDTH, 3 * WIDTH), BF),
        vm((nz, rows, 128), F32),
        vm((nz, rows, 128), F32),
        vm((WIDTH, 128), F32),
        vm((WIDTH, rows), F32),
        vm((16, rows), F32),
        vm((16, rows), F32),
        pltpu.SemaphoreType.DMA((5,)),
        pltpu.SemaphoreType.DMA((5,)),
        pltpu.SemaphoreType.DMA((8 + 3 * nz,)),
    ]
    if masks:
        grp, out, mlp = (2 * SLIVER, 640), (2 * SLIVER, 512), (BAND, 896)
        outs += [shape((GROUPS, nz) + out, BF), shape((GROUPS, nz) + mlp, BF)]
        out_specs += [anyspace] * 2
        scratch += [vm(x, BF) for x in (grp, grp, out, mlp)] + [vm((GROUPS, nz) + grp, BF)] * 2
        scratch += [pltpu.SemaphoreType.DMA((Gather.sems(nz),)) for _ in range(8)]
    return pl.pallas_call(
        functools.partial(front_kernel, nz, masks, rows),
        out_shape=outs,
        in_specs=[anyspace] * 2 + [vmem] * len(weights) + [anyspace] * 2,
        out_specs=out_specs,
        scratch_shapes=scratch,
        compiler_params=pltpu.CompilerParams(collective_id=0, has_side_effects=True, vmem_limit_bytes=60 << 20),
        cost_estimate=pl.CostEstimate(flops=14_000_000_000, bytes_accessed=40_000_000, transcendentals=13_000_000),
        name="front",
    )(tok, gout, *weights, cos, sine)


def middle_kernel(rows, tok, mixed, gout, po_all, pm_all, out, gmid, gmixed, delta, po_g, pm_g,
                  wout, wg, wu, wd, gcol, gain, resid, hat, inv, second, hidden, ggate, gup, gsec, gattn, dwout):
    lane = lane_iota()

    def build(g, _):
        band = pl.ds(pl.multiple_of(g * BAND, BAND), BAND)
        slabs = [po_all[g, s].astype(F32) for s in range(LINE)]
        wout[band, :384] = jnp.concatenate([x[:SLIVER, :384] for x in slabs], 0).astype(BF)
        wout[band, 384:] = jnp.concatenate([x[SLIVER:, :384] for x in slabs], 0).astype(BF)
        gcol[band, :] = jnp.concatenate([x[:SLIVER, 384:] for x in slabs], 0)
        for i, w in enumerate((wg, wu, wd)):
            tail = jnp.zeros((BAND, 128), F32)
            for s in range(LINE):
                w[band, MAIN * s : MAIN * s + MAIN] = pm_all[g, s, :, MAIN * i : MAIN * i + MAIN]
                rest = pm_all[g, s, :, 3 * MAIN :].astype(F32)
                turn = (REST * (s - i)) % 128
                rest = pltpu.roll(rest, turn, 1) if turn else rest
                tail = jnp.where((lane >= REST * s) & (lane < REST * (s + 1)), rest, tail)
            w[band, MAIN * LINE :] = tail.astype(BF)
        return 0

    lax.fori_loop(0, GROUPS, build, 0)
    gain[...] = gcol[...].T[:8]

    for j in range(3):
        at = slice(256 * j, 256 * j + 256)
        resid[:, at] = tok[:, at].astype(F32) + dot(mixed[...], wout[:, at], NN)

    def norm_block(i, _):
        at = pl.ds(pl.multiple_of(i * 64, 64), 64)
        h, r = normed(resid[at, :])
        hat[at, :] = h
        inv[at, :] = jnp.broadcast_to(r, (64, 128))
        second[at, :] = (h * gain[0:1, :]).astype(BF)
        return 0

    lax.fori_loop(0, rows // 64, norm_block, 0)

    def units(start, width):
        at = pl.ds(start, width)
        gate, up, gh = dot(second[...], wg[:, at], NN), dot(second[...], wu[:, at], NN), dot(gout[...], wd[:, at], NN)
        cdf = 0.5 + 0.5 * lax.erf(gate * math.sqrt(0.5))
        pdf = jnp.exp2(gate * gate * (-0.5 * LOG2E)) * (1.0 / math.sqrt(2.0 * math.pi))
        act = gate * cdf
        hidden[:, at] = (act * up).astype(BF)
        gup[:, at] = (gh * act).astype(BF)
        ggate[:, at] = (gh * up * (cdf + gate * pdf)).astype(BF)

    def unit_block(i, _):
        units(pl.multiple_of(i * 128, 128), 128)
        return 0

    lax.fori_loop(0, UNITS // 128, unit_block, 0)

    for j in range(3):
        at = slice(256 * j, 256 * j + 256)
        out[:, at] = (resid[:, at] + dot(hidden[...], wd[at, :], NT)).astype(BF)
        gsec[:, at] = dot(ggate[...], wg[at, :], NT) + dot(gup[...], wu[at, :], NT)

    def back_block(i, dgain):
        at = pl.ds(pl.multiple_of(i * 64, 64), 64)
        dy, h = gsec[at, :], hat[at, :]
        gm = gout[at, :].astype(F32) + norm_back(dy, gain[0:1, :], h, inv[at, 0:1])
        gmid[at, :] = gm
        gattn[at, :] = gm.astype(BF)
        return dgain + jnp.sum(dy * h, 0, keepdims=True)

    dgain = lax.fori_loop(0, rows // 64, back_block, jnp.zeros((1, WIDTH), F32))

    heads = lax.broadcasted_iota(jnp.int32, (16, 256), 0)
    for j in range(3):
        at = slice(256 * j, 256 * j + 256)
        gmx = dot(gattn[...], wout[at, :], NT).astype(BF)
        gmixed[:, at] = gmx
        prod = gmx.astype(F32) * mixed[:, at].astype(F32)
        high = prod.astype(BF)
        low = (prod - high.astype(F32)).astype(BF)
        pick = ((lax.broadcasted_iota(jnp.int32, (16, 256), 1) + 256 * j) // HEAD_DIM == heads).astype(BF)
        part = dot(pick, high, NT) + dot(pick, low, NT)
        delta[...] = part if j == 0 else delta[...] + part

    for j in range(2):
        at = slice(384 * j, 384 * j + 384)
        dwout[at, :] = dot(mixed[:, at], gattn[...], TN)
    row = lax.broadcasted_iota(jnp.int32, (128, WIDTH), 0)
    gcol[...] = jnp.where(row == 0, dgain, 0.0).T

    def pack_out(g, _):
        for s in range(LINE):
            at = pl.ds(pl.multiple_of(g * BAND + s * SLIVER, 8), SLIVER)
            x, c = dwout[at, :], gcol[at, :]
            po_g[g, s, :, :384] = jnp.concatenate([x[:, :384], x[:, 384:]], 0).astype(BF)
            po_g[g, s, :, 384:] = jnp.concatenate([c, jnp.zeros_like(c)], 0).astype(BF)
        return 0

    lax.fori_loop(0, GROUPS, pack_out, 0)

    for j in range(2):
        at = slice(384 * j, 384 * j + 384)
        tails = []
        for i, (a, b) in enumerate(((second, ggate), (second, gup), (gout, hidden))):
            for s in range(LINE):
                x = dot(a[:, at], b[:, MAIN * s : MAIN * s + MAIN], TN).astype(BF)
                for g in range(4):
                    pm_g[4 * j + g, s, :, MAIN * i : MAIN * i + MAIN] = x[BAND * g : BAND * g + BAND]
            tails.append(dot(a[:, at], b[:, MAIN * LINE :], TN))
        for s in range(LINE):
            y = jnp.zeros((384, 128), F32)
            for i, tail in enumerate(tails):
                turn = (REST * (i - s)) % 128
                tail = pltpu.roll(tail, turn, 1) if turn else tail
                y = jnp.where((lane >= REST * i) & (lane < REST * (i + 1)), tail, y)
            y = y.astype(BF)
            for g in range(4):
                pm_g[4 * j + g, s, :, 3 * MAIN :] = y[BAND * g : BAND * g + BAND]


def middle(tok, mixed, gout, po_all, pm_all):
    rows = tok.shape[0]
    shape, vm = jax.ShapeDtypeStruct, pltpu.VMEM
    vmem = pl.BlockSpec(memory_space=pltpu.VMEM)
    return pl.pallas_call(
        functools.partial(middle_kernel, rows),
        out_shape=[
            shape((rows, WIDTH), BF),
            shape((rows, WIDTH), F32),
            shape((rows, WIDTH), BF),
            shape((16, rows), F32),
            shape(po_all.shape, BF),
            shape(pm_all.shape, BF),
        ],
        in_specs=[vmem] * 5,
        out_specs=[vmem] * 6,
        scratch_shapes=[
            vm((WIDTH, WIDTH), BF),
            vm((WIDTH, UNITS), BF),
            vm((WIDTH, UNITS), BF),
            vm((WIDTH, UNITS), BF),
            vm((WIDTH, 128), F32),
            vm((8, WIDTH), F32),
            vm((rows, WIDTH), F32),
            vm((rows, WIDTH), F32),
            vm((rows, 128), F32),
            vm((rows, WIDTH), BF),
            vm((rows, UNITS), BF),
            vm((rows, UNITS), BF),
            vm((rows, UNITS), BF),
            vm((rows, WIDTH), F32),
            vm((rows, WIDTH), BF),
            vm((WIDTH, WIDTH), F32),
        ],
        compiler_params=pltpu.CompilerParams(vmem_limit_bytes=58 << 20),
        cost_estimate=pl.CostEstimate(flops=11_000_000_000, bytes_accessed=25_000_000, transcendentals=1_200_000),
        name="middle",
    )(tok, mixed, gout, po_all, pm_all)


class Reduce:
    COPIES = 10

    def __init__(self, src, total, cut, nz, masks, bufs, send, recv, loc=None):
        self.src, self.total, self.cut, self.nz, self.masks = src, total, cut, nz, masks
        self.near, self.side0, self.side1, self.far, *mine = bufs
        self.mine = mine[0] if mine else None
        self.send, self.recv, self.loc = send, recv, loc
        self.dp, self.z = lax.axis_index("dp"), lax.axis_index("seq")
        my, mx, mc = masks
        self.turns = (0, my, mx, my ^ mx)
        self.started = []

    @staticmethod
    def scratch(shape, nz, held):
        r, c = shape
        cut = CUTS[c]
        bufs = [
            pltpu.VMEM((4, nz, r, c), BF),
            pltpu.VMEM((3, nz, r, cut), BF),
            pltpu.VMEM((3, nz, r, c - cut), BF),
            pltpu.VMEM((nz - 1, r, c), BF),
        ]
        sems = [pltpu.SemaphoreType.DMA((Reduce.COPIES * nz + nz,))] * 2
        if not held:
            bufs += [pltpu.VMEM((4, nz, r, c), BF)]
            sems += [pltpu.SemaphoreType.DMA((4 * nz,))]
        return bufs, sems

    def begin(self, src, dst, device, k):
        remote(src, dst, self.send.at[k], self.recv.at[k], device).start()
        self.started.append((k, src.shape[-1]))

    def arrived(self, ref, k):
        remote(ref, ref, self.send.at[k], self.recv.at[k], {"dp": self.dp ^ self.masks[2]}).wait_recv()

    def seat(self, o):
        return self.z ^ LINKED[o]

    def held(self, i, s):
        return self.mine.at[i, s] if self.mine is not None else self.src.at[self.dp ^ self.turns[i], s]

    def local(self, i, o):
        s = self.seat(o)
        return pltpu.make_async_copy(self.src.at[self.dp ^ self.turns[i], s], self.mine.at[i, s], self.loc.at[4 * o + i])

    def zero(self, o):
        s, mc = self.seat(o), self.masks[2]
        for i in (3, 1, 2, 0):
            if self.mine is not None:
                self.local(i, o).start()
            self.begin(self.src.at[self.dp ^ mc ^ self.turns[i], s], self.near.at[i, s], {"dp": self.dp ^ mc}, self.COPIES * o + i)

    def add(self, ref, other):
        ref[...] = (ref[...].astype(F32) + other[...].astype(F32)).astype(BF)

    def p0(self, i, s):
        return self.held(i, s).at[:, pl.ds(0, self.cut)]

    def p1(self, i, s):
        return self.held(i, s).at[:, pl.ds(self.cut, self.src.shape[-1] - self.cut)]

    def one(self, o):
        my, mx, _ = self.masks
        s, k = self.seat(o), self.COPIES * o
        for i in (3, 1, 2, 0):
            if self.mine is not None:
                self.local(i, o).wait()
            self.arrived(self.near.at[i, s], k + i)
            self.add(self.held(i, s), self.near.at[i, s])
            if i == 3:
                self.begin(self.p0(3, s), self.side0.at[1, s], {"dp": self.dp ^ my}, k + 4)
                self.begin(self.p1(3, s), self.side1.at[1, s], {"dp": self.dp ^ mx}, k + 5)
            if i == 1:
                self.begin(self.p0(1, s), self.side0.at[0, s], {"dp": self.dp ^ my}, k + 6)
            if i == 2:
                self.begin(self.p1(2, s), self.side1.at[0, s], {"dp": self.dp ^ mx}, k + 7)

    def two(self, o):
        my, mx, _ = self.masks
        s, k = self.seat(o), self.COPIES * o
        self.arrived(self.side0.at[1, s], k + 4)
        self.add(self.p0(2, s), self.side0.at[1, s])
        self.begin(self.p0(2, s), self.side0.at[2, s], {"dp": self.dp ^ mx}, k + 8)
        self.arrived(self.side1.at[1, s], k + 5)
        self.add(self.p1(1, s), self.side1.at[1, s])
        self.begin(self.p1(1, s), self.side1.at[2, s], {"dp": self.dp ^ my}, k + 9)

    def three(self, o):
        s, k = self.seat(o), self.COPIES * o
        for ref, side, k1, k2 in ((self.p0(0, s), self.side0, k + 6, k + 8), (self.p1(0, s), self.side1, k + 7, k + 9)):
            self.arrived(side.at[0, s], k1)
            self.arrived(side.at[2, s], k2)
            ref[...] = (ref[...].astype(F32) + side[0, s].astype(F32) + side[2, s].astype(F32)).astype(BF)
        if o:
            self.begin(self.held(0, s), self.far.at[o - 1], {"seq": s}, self.COPIES * self.nz + o)

    def four(self):
        out = self.held(0, self.z)[...].astype(F32)
        for o in range(1, self.nz):
            self.arrived(self.far.at[o - 1], self.COPIES * self.nz + o)
            out = out + self.far[o - 1].astype(F32)
        self.total[...] = out

    def done(self):
        for k, width in self.started:
            whole = width == self.src.shape[-1]
            ref = self.near.at[0, 0] if whole else (self.side0 if k % self.COPIES in (4, 6, 8) else self.side1).at[0, 0]
            remote(ref, ref, self.send.at[k], self.recv.at[k], {"dp": self.dp ^ self.masks[2]}).wait_send()


def back_kernel(nz, masks, rows, *refs):
    fused = masks is not None
    (tok, gmid, out_own, query, kv, firsts, wqkv, gain, gmixed, lse, delta, cos_in, sine_in), refs = refs[:13], refs[13:]
    if fused:
        (po_g, pm_g, gtok, out, s0, s1, so, sm), refs = refs[:8], refs[8:]
    else:
        (gtok, out, p0_g, p1_g), refs = refs[:4], refs[4:]
    (kvb, fb, ft, wq, cos, sine, dq, dqb, dkv, dx, dw, sent, landed, gown, gcol, send, recv, loc), refs = refs[:18], refs[18:]
    me = Place(nz)
    own = me.shard

    def here(src, dst, k):
        return pltpu.make_async_copy(src, dst, loc.at[k])

    def there(src, dst, device, k):
        return remote(src, dst, send.at[k], recv.at[k], device)

    def chunk(t):
        return jnp.where(t == 0, own ^ 2, jnp.where(t == 1, own ^ 1, jnp.where(t == 2, own ^ 3, own)))

    def fetch(grp, t):
        c, slot = chunk(t), lax.rem(t, 2)
        found = [here(kv.at[grp, c], kvb.at[slot], slot)]
        if grp == 0:
            found.append(here(firsts.at[c], fb.at[slot], 2 + slot))
        return found

    for c in fetch(0, 0):
        c.start()
    whole = [here(wqkv, wq, 4), here(cos_in, cos, 5), here(sine_in, sine, 6)]
    for c in whole:
        c.start()
    me.greet(masks or (1,))
    jobs, sums = [], []
    if fused:
        (p0_g, p1_g), refs = refs[:2], refs[2:]
        for src, total in ((p0_g, s0), (p1_g, s1)):
            sums.append(Reduce(src, total, CUTS[src.shape[-1]], nz, masks, refs[:4], *refs[4:6]))
            refs = refs[6:]
        for src, total in ((po_g, so), (pm_g, sm)):
            jobs.append(Reduce(src, total, CUTS[src.shape[-1]], nz, masks, refs[:5], *refs[5:8]))
            refs = refs[8:]
    order = (3, 2, 1, 0)

    def advance(which, step):
        for j in which:
            for o in order:
                getattr(j, step)(o)

    def wave(which):
        for i in range(nz + 2):
            for k, step in enumerate(("one", "two", "three")):
                if 0 <= i - k < nz:
                    for j in which:
                        getattr(j, step)(order[i - k])

    advance(jobs, "zero")

    @pl.when(me.moves)
    def _():
        there(out_own, out, me.opposite, 3).start()

    @pl.when(me.stays)
    def _():
        here(out_own, out, 7).start()

    dq[...] = jnp.zeros_like(dq)
    for c in whole:
        c.wait()

    def visits(grp, steps):
        def visit(t, _):
            c, slot = chunk(t), lax.rem(t, 2)
            for f in fetch(grp, t):
                f.wait()

            @pl.when(t + 1 < nz)
            def _():
                for f in fetch(grp, t + 1):
                    f.start()

            if grp == 0:

                @pl.when(t + 1 == nz)
                def _():
                    for f in fetch(1, 0):
                        f.start()

            band = pl.ds(pl.multiple_of(t * rows, rows), rows)
            todo = [(i, h) for i in range(3) for h in range(2)]

            def pick(ref, i, h):
                x = ref[:, HALF * grp + 128 * i : HALF * grp + 128 * i + 128]
                mask = (lane_iota() < 64) if h == 0 else (lane_iota() >= 64)
                return jnp.where(mask, x, jnp.zeros_like(x))

            def score(i, h):
                qh, gh = pick(query, i, h), pick(gmixed, i, h)
                k, v = kvb[slot, :, 128 * i : 128 * i + 128], kvb[slot, :, HALF + 128 * i : HALF + 128 * i + 128]
                return dot(k, qh, NT), dot(v, gh, NT), qh, gh

            ready = [score(*todo[0])]
            dk = dv = None
            for n, (i, h) in enumerate(todo):
                s, dp, qh, gh = ready[n]
                if n + 1 < len(todo):
                    ready.append(score(*todo[n + 1]))
                if h == 0:
                    kt = kvb[slot, :, 128 * i : 128 * i + 128].T
                head = 6 * grp + n
                p = jnp.exp2(s - lse[head : head + 1, :])
                ds = (p * (dp - delta[head : head + 1, :])).astype(BF)
                a = dot(p.astype(BF), gh, NN)
                dv = a if h == 0 else dv + a
                a = dot(ds, qh, NN)
                dk = a if h == 0 else dk + a
                dq[64 * head : 64 * head + 64, :] += dot(kt[h * 64 : h * 64 + 64], ds, NN)
                if h == 1:
                    at = WIDTH * grp + 128 * i
                    dkv[band, at : at + 128] = rope_back(dk * (1.0 / LOG2E), cos[c], sine[c]).astype(BF)
                    dkv[band, at + HALF : at + HALF + 128] = dv.astype(BF)

            if grp == 0:
                for j in range(6):
                    ft[128 * j : 128 * j + 128, band] = fb[slot, :, 128 * j : 128 * j + 128].T
            else:
                for j in range(3):
                    at = slice(256 * j, 256 * j + 256)
                    dx[:, at] = dot(dkv[band, :], wq[at, : 2 * WIDTH], NT)

                @pl.when(lax.rem(t, 2) == 0)
                def _():
                    sent[t] = dx[...].astype(BF)
                    there(sent.at[t], landed.at[t], me.twin, t).start()

                @pl.when(t == 1)
                def _():
                    there(sent.at[0], landed.at[0], me.twin, 0).wait_recv()
                    sent[1] = (dx[...] + landed[0].astype(F32)).astype(BF)
                    there(sent.at[1], landed.at[1], me.beside, 1).start()

            if fused:
                for k, step in steps.items():

                    @pl.when(t == k)
                    def _(step=step):
                        for which, name in step:
                            if name == "four":
                                for j in which:
                                    j.four()
                            else:
                                advance(which, name)

            return 0

        lax.fori_loop(0, nz, visit, 0)
        for i in range(3 * grp, 3 * grp + 3):
            at = slice(128 * i, 128 * i + 128)
            dqb[:, at] = rope_back(dq[at, :].T * SCALE, cos[own], sine[own]).astype(BF)

    def weigh(grp):
        for r in (slice(0, HALF), slice(HALF, WIDTH)):
            for j in range(3):
                at = WIDTH * grp + 256 * j
                dw[r, HALF + 256 * j : HALF + 256 * j + 256] = dot(ft[r, :], dkv[:, at : at + 256], NN)
            dw[r, :HALF] = dot(ft[r, (nz - 1) * rows :], dqb[:, HALF * grp : HALF * grp + HALF], NN)

    def pack(grp, dst):
        def band_of(g, _):
            for s in range(LINE):
                at = pl.ds(pl.multiple_of(g * BAND + s * SLIVER, 8), SLIVER)
                q, k, v0, v1 = dw[at, :HALF], dw[at, HALF:WIDTH], dw[at, WIDTH : WIDTH + 256], dw[at, WIDTH + 256 :]
                tile = gcol[at, :] if grp else jnp.zeros((SLIVER, 128), F32)
                dst[g, s] = jnp.concatenate(
                    [jnp.concatenate([q, v0], 1), jnp.concatenate([k, v1, tile], 1)], 0
                ).astype(BF)
            return 0

        lax.fori_loop(0, GROUPS, band_of, 0)

    visits(0, {0: [(jobs, "one")]})
    weigh(0)
    pack(0, p0_g)
    early = sums[:1]
    advance(early, "zero")
    visits(1, {0: [(jobs, "two"), (early, "one")], 2: [(jobs, "three")], 3: [(early, "two"), (early, "three")]})
    for j in range(3):
        at = slice(256 * j, 256 * j + 256)
        dx[:, at] += dot(dqb[...], wq[at, 2 * WIDTH :], NT)
    weigh(1)
    there(sent.at[1], landed.at[1], me.beside, 1).wait_recv()
    there(sent.at[2], landed.at[2], me.twin, 2).wait_recv()

    def norm_block(i, dgain):
        at = pl.ds(pl.multiple_of(i * 64, 64), 64)
        dy = dx[at, :] + landed[1, at, :].astype(F32) + landed[2, at, :].astype(F32)
        h, r = normed(tok[at, :].astype(F32))
        gown[at, :] = (gmid[at, :] + norm_back(dy, gain[0:1, :], h, r)).astype(BF)
        return dgain + jnp.sum(dy * h, 0, keepdims=True)

    dgain = lax.fori_loop(0, rows // 64, norm_block, jnp.zeros((1, WIDTH), F32))

    @pl.when(me.moves)
    def _():
        there(gown, gtok, me.opposite, 4).start()

    @pl.when(me.stays)
    def _():
        here(gown, gtok, 8).start()

    row = lax.broadcasted_iota(jnp.int32, (128, WIDTH), 0)
    gcol[...] = jnp.where(row == 0, dgain, 0.0).T
    pack(1, p1_g)
    if fused:
        advance(sums[1:], "zero")
        for j in jobs + early:
            j.four()
        wave(sums[1:])
        sums[1].four()
        for j in jobs + sums:
            j.done()
    for k, device in ((0, me.twin), (1, me.beside), (2, me.twin)):
        there(sent.at[k], landed.at[k], device, k).wait_send()

    @pl.when(me.moves)
    def _():
        there(out_own, out, me.opposite, 3).wait()
        there(gown, gtok, me.opposite, 4).wait()

    @pl.when(me.stays)
    def _():
        here(out_own, out, 7).wait()
        here(gown, gtok, 8).wait()


def back(tok, gmid, out_own, query, kv, firsts, wqkv, gain, gmixed, lse, delta, cos, sine, packs, nz, masks):
    rows = tok.shape[0]
    shape, vm = jax.ShapeDtypeStruct, pltpu.VMEM
    vmem, anyspace = pl.BlockSpec(memory_space=pltpu.VMEM), pl.BlockSpec(memory_space=pl.ANY)
    in_specs = [vmem] * 4 + [anyspace] * 3 + [vmem] * 4 + [anyspace] * 2
    slab = (2 * SLIVER, 640)
    outs, out_specs = [shape((rows, WIDTH), BF)] * 2, [vmem] * 2
    scratch = [
        vm((2, rows, WIDTH), BF),
        vm((2, rows, WIDTH), BF),
        vm((WIDTH, nz * rows), BF),
        vm((WIDTH, 3 * WIDTH), BF),
        vm((nz, rows, 128), F32),
        vm((nz, rows, 128), F32),
        vm((WIDTH, rows), F32),
        vm((rows, WIDTH), BF),
        vm((nz * rows, 2 * WIDTH), BF),
        vm((rows, WIDTH), F32),
        vm((WIDTH, 3 * HALF), F32),
        vm((3, rows, WIDTH), BF),
        vm((3, rows, WIDTH), BF),
        vm((rows, WIDTH), BF),
        vm((WIDTH, 128), F32),
        pltpu.SemaphoreType.DMA((5,)),
        pltpu.SemaphoreType.DMA((5,)),
        pltpu.SemaphoreType.DMA((9,)),
    ]
    if masks:
        in_specs += [anyspace] * 2
        outs += [shape(s, F32) for s in (slab, slab, packs[0].shape[-2:], packs[1].shape[-2:])]
        out_specs += [vmem] * 4
        scratch += [vm((GROUPS, LINE) + slab, BF)] * 2
        for s, held in ((slab, True), (slab, True), (packs[0].shape[-2:], False), (packs[1].shape[-2:], False)):
            bufs, sems = Reduce.scratch(s, nz, held)
            scratch += bufs + sems
    else:
        outs += [shape((GROUPS, LINE) + slab, BF)] * 2
        out_specs += [vmem] * 2
        packs = []
    return pl.pallas_call(
        functools.partial(back_kernel, nz, masks, rows),
        out_shape=outs,
        in_specs=in_specs,
        out_specs=out_specs,
        scratch_shapes=scratch,
        compiler_params=pltpu.CompilerParams(collective_id=1, has_side_effects=True, vmem_limit_bytes=62 << 20),
        cost_estimate=pl.CostEstimate(flops=24_000_000_000, bytes_accessed=40_000_000, transcendentals=13_000_000),
        name="back",
    )(tok, gmid, out_own, query, kv, firsts, wqkv, gain, gmixed, lse, delta, cos, sine, *packs)


def finish_kernel(out, gtok, s0, s1, so, sm, out_o, gtok_o, qkv_o, w_out_o, gains_o, gate_o, down_o):
    out_o[...] = out[...]
    gtok_o[...] = gtok[...]
    for i, total in enumerate((s0, s1)):
        q, k, v0, v1, tile = unpack_group(total[...])
        for j, x in enumerate((q, k)):
            qkv_o[:, WIDTH * j + HALF * i : WIDTH * j + HALF * i + HALF] = x
        at = 2 * WIDTH + HALF * i
        qkv_o[:, at : at + 256] = v0
        qkv_o[:, at + 256 : at + HALF] = v1
    w_out_o[:, :HALF] = so[:SLIVER, :HALF]
    w_out_o[:, HALF:] = so[SLIVER:, :HALF]
    zeros = jnp.zeros((128 - SLIVER, 128), F32)
    for i, col in enumerate((tile, so[:SLIVER, HALF:])):
        gains_o[i : i + 1, :] = jnp.concatenate([col, zeros], 0).T[:1]
    gate, up, down = unpack_mlp(sm[...])
    gate_o[:, :SHARE] = gate
    gate_o[:, SHARE:] = up
    down_o[...] = down.T


def finish(out, gtok, s0, s1, so, sm):
    shape = jax.ShapeDtypeStruct
    vmem = pl.BlockSpec(memory_space=pltpu.VMEM)
    return pl.pallas_call(
        finish_kernel,
        out_shape=[
            shape(out.shape, BF),
            shape(gtok.shape, BF),
            shape((SLIVER, 3 * WIDTH), F32),
            shape((SLIVER, WIDTH), F32),
            shape((8, 128), F32),
            shape((BAND, 2 * SHARE), F32),
            shape((SHARE, BAND), F32),
        ],
        in_specs=[vmem] * 6,
        out_specs=[vmem] * 7,
        compiler_params=pltpu.CompilerParams(vmem_limit_bytes=40 << 20),
        name="finish",
    )(out, gtok, s0, s1, so, sm)


def whole_packs(w_qkv, w_out, attn_gain, mlp_gain, w_in, w_down):
    both = ("dp", "seq")

    def shards_of(w):
        w = lax.all_gather(w, both, axis=0, tiled=True)
        return w.reshape(GROUPS * LINE, SLIVER, -1)

    def slabs(pack, w, gain):
        found = jax.vmap(pack)(w, jnp.pad(gain, ((0, 0), (0, 0), (0, 127))))
        return found.reshape((GROUPS, LINE) + found.shape[1:])

    qkv, gain_a, gain_m = shards_of(w_qkv), shards_of(attn_gain), shards_of(mlp_gain)
    groups = [slabs(lambda w, t, i=i: pack_group(w, t, i), qkv, gain_a) for i in range(2)]
    w_in, w_down = lax.all_gather(w_in, "dp", axis=0, tiled=True), lax.all_gather(w_down, "dp", axis=1, tiled=True)
    mlp = lax.all_gather(pack_mlp(w_in[:, 0], w_in[:, 1], w_down.T), "seq", axis=0, tiled=False)
    mlp = mlp.reshape(LINE, GROUPS, BAND, -1).transpose(1, 0, 2, 3)
    return groups, slabs(pack_out, shards_of(w_out), gain_m), mlp


def whole_sums(p0_g, p1_g, po_g, pm_g):
    both = ("dp", "seq")

    def scattered(x):
        return lax.psum_scatter(x.reshape(WIDTH, -1), both, scatter_dimension=0, tiled=True)

    parts = [jax.vmap(unpack_group)(p.reshape((GROUPS * LINE,) + p.shape[2:]).astype(F32)) for p in (p0_g, p1_g)]
    columns = [parts[0][0], parts[1][0], parts[0][1], parts[1][1], parts[0][2], parts[0][3], parts[1][2], parts[1][3]]
    g_qkv, gain_a = scattered(jnp.concatenate(columns, -1)), scattered(parts[1][4][..., :1])[:, 0]
    po = po_g.reshape(GROUPS * LINE, 2 * SLIVER, -1).astype(F32)
    g_out = scattered(jnp.concatenate([po[:, :SLIVER, :HALF], po[:, SLIVER:, :HALF]], -1))
    gain_m = scattered(po[:, :SLIVER, HALF : HALF + 1])[:, 0]
    mlp = pm_g.astype(F32).transpose(1, 0, 2, 3).reshape(LINE, WIDTH, -1)
    mlp = lax.psum_scatter(mlp, "seq", scatter_dimension=0, tiled=False)
    gate, up, down = unpack_mlp(lax.psum_scatter(mlp, "dp", scatter_dimension=0, tiled=True))
    return g_qkv, g_out, gain_a, gain_m, jnp.stack([gate, up], 1), down.T


def on_device(tokens, w_qkv, w_out, attn_gain, mlp_gain, w_in, w_down, grad_out, *, dp, nz):
    rows = tokens.shape[0]
    masks = (dp // 2, dp // 4, 1) if dp == GROUPS else None
    cos, sine = [jnp.asarray(t).reshape(nz, rows, 128) for t in rope_tables(nz * rows)]
    if masks:
        gains = jnp.pad(jnp.stack([attn_gain, mlp_gain]).astype(F32), ((0, 6), (0, 128 - SLIVER)))
        weights = [w_qkv, w_out, gains, w_in.reshape(w_in.shape[0], -1), w_down]
        got = front(tokens, grad_out, weights, cos, sine, nz, masks)
        po_all, pm_all = got[-2:]
    else:
        groups, po_all, pm_all = whole_packs(w_qkv, w_out, attn_gain, mlp_gain, w_in, w_down)
        got = front(tokens, grad_out, groups, cos, sine, nz, None)
    mixed, lse, query, gain, tok_own, gout_own, kv, firsts, wqkv = got[:9]
    out_own, gmid, gmixed, delta, po_g, pm_g = middle(tok_own, mixed, gout_own, po_all, pm_all)
    found = back(tok_own, gmid, out_own, query, kv, firsts, wqkv, gain, gmixed, lse, delta, cos, sine, [po_g, pm_g], nz, masks)
    gtok, out, *sums = found
    if not masks:
        return (out, gtok, *whole_sums(*sums, po_g, pm_g))
    out, gtok, g_qkv, g_out, gains, g_in, g_down = finish(out, gtok, *sums)
    g_in = g_in.reshape(g_in.shape[0], 2, SHARE)
    return out, gtok, g_qkv, g_out, gains[0, :SLIVER], gains[1, :SLIVER], g_in, g_down


def solution(mesh):
    both = P(("dp", "seq"), None)
    vector = P(("dp", "seq"))
    w_in, w_down = P("dp", None, "seq"), P("seq", "dp")
    step = functools.partial(on_device, dp=mesh.shape["dp"], nz=mesh.shape["seq"])
    return jax.shard_map(
        step,
        mesh=mesh,
        in_specs=(both, both, both, vector, vector, w_in, w_down, both),
        out_specs=(both, both, both, both, vector, vector, w_in, w_down),
        check_vma=False,
    )
```

```python
import functools
import math

import jax
import jax.numpy as jnp
import numpy as np
from jax import lax
from jax.experimental import pallas as pl
from jax.experimental.pallas import tpu as pltpu
from jax.sharding import PartitionSpec as P

HEADS = 12
HEAD_DIM = 64
NORM_EPS = 1e-05
ROPE_THETA = 160000.0

F32 = jnp.float32
BF = jnp.bfloat16
MESH = pl.DeviceIdType.MESH
NT = (((1,), (1,)), ((), ()))
NN = (((1,), (0,)), ((), ()))
TN = (((0,), (0,)), ((), ()))

WIDTH = 768
PAIRS = HEADS // 2
UNITS = 1152
GROUPS = 8
LINE = 4
BAND = WIDTH // GROUPS
SLIVER = BAND // LINE
SHARE = UNITS // LINE
MAIN = 256
REST = SHARE - MAIN
LINKED = (0, 1, 3, 2)
HALF = WIDTH // 2
CUTS = {640: 256, 512: 256, 896: 384}
LOG2E = math.log2(math.e)
SCALE = HEAD_DIM**-0.5


def dot(a, b, dims):
    return lax.dot_general(a, b, dims, preferred_element_type=F32)


def lanes_of(tile, width=128):
    return pl.ds(pl.multiple_of(tile * width, width), width)


def lane_iota():
    return lax.broadcasted_iota(jnp.int32, (1, 128), 1)


def swap_halves(u):
    low = lax.rem(lane_iota(), 64) < 32
    return jnp.where(low, pltpu.roll(u, 96, 1), pltpu.roll(u, 32, 1))


def rope(u, cos, sine):
    return u * cos + swap_halves(u) * sine


def rope_back(u, cos, sine):
    return u * cos - swap_halves(u) * sine


def rope_tables(rows):
    position = np.arange(rows, dtype=np.float32)
    half = HEAD_DIM // 2
    freq = (ROPE_THETA ** (-np.arange(half) * 2.0 / HEAD_DIM)).astype(np.float32)
    angle = (position[:, None] * freq[None, :]).astype(np.float64)
    cos, sine = np.cos(angle), np.sin(angle)
    cos = np.concatenate([cos] * 4, 1).astype(np.float32)
    sine = np.concatenate([-sine, sine] * 2, 1).astype(np.float32)
    return cos, sine


def normed(x):
    centred = x - jnp.mean(x, -1, keepdims=True)
    inv = lax.rsqrt(jnp.mean(centred * centred, -1, keepdims=True) + NORM_EPS)
    return centred * inv, inv


def norm_back(dy, gain, hat, inv):
    d = dy * gain
    return inv * (d - jnp.mean(d, -1, keepdims=True) - hat * jnp.mean(d * hat, -1, keepdims=True))


def remote(src, dst, send, recv, device):
    return pltpu.make_async_remote_copy(src, dst, send, recv, device_id=device, device_id_type=MESH)


class Place:
    def __init__(self, nz):
        self.dp, self.z = lax.axis_index("dp"), lax.axis_index("seq")
        self.nz = nz
        upper = self.z // (nz // 2)
        self.moves = lax.rem(self.dp, 2) != upper
        self.stays = lax.rem(self.dp, 2) == upper
        self.shard = jnp.where(self.moves, nz - 1 - self.z, self.z)
        self.opposite = {"dp": self.dp ^ 1, "seq": nz - 1 - self.z}
        self.twin = {"dp": self.dp ^ 1}
        self.beside = {"seq": self.z ^ 1}

    def greet(self, masks):
        bar = pltpu.get_barrier_semaphore()

        def hello(device):
            pl.semaphore_signal(bar, inc=1, device_id=device, device_id_type=MESH)

        for o in range(1, self.nz):
            hello({"seq": lax.rem(self.z + o, self.nz)})
        for m in masks:
            hello({"dp": self.dp ^ m})
        hello(self.opposite)
        pl.semaphore_wait(bar, self.nz + len(masks))


class Gather:
    COPIES = 9

    def __init__(self, src, out, cut, nz, masks, send, recv):
        self.src, self.out, self.cut, self.nz, self.masks = src, out, cut, nz, masks
        self.send, self.recv = send, recv
        self.dp, self.z = lax.axis_index("dp"), lax.axis_index("seq")
        self.started = []
        self.relayed = None

    @staticmethod
    def sems(nz):
        return Gather.COPIES * nz + nz

    def key(self, o, k):
        return o * self.COPIES + k

    def copy(self, src, dst, device, k):
        return remote(src, dst, self.send.at[k], self.recv.at[k], device)

    def begin(self, src, dst, device, k, p=None):
        self.copy(src, dst, device, k).start()
        self.started.append((k, p))

    def arrived(self, ref, k):
        self.copy(ref, ref, {"dp": self.dp ^ self.masks[0]}, k).wait_recv()

    def slot(self, o):
        return self.z ^ LINKED[o]

    def part(self, ref, p):
        if p is None:
            return ref
        width = self.out.shape[-1]
        return ref.at[:, pl.ds(0, self.cut)] if p == 0 else ref.at[:, pl.ds(self.cut, width - self.cut)]

    def along(self, o):
        self.begin(self.src, self.out.at[self.dp, self.z], {"seq": self.z ^ LINKED[o]}, self.COPIES * self.nz + o)

    def relay(self, o):
        ref = self.out.at[self.dp, self.slot(o)]
        self.arrived(ref, self.COPIES * self.nz + o)
        self.relayed = o
        self.begin(ref, ref, {"seq": self.z ^ 1}, self.COPIES * self.nz + 3)

    def forward(self, src, d, s, mask, k, p=None):
        dst = self.out.at[d, s]
        self.begin(self.part(src, p), self.part(dst, p), {"dp": self.dp ^ mask}, k, p)

    def first(self, o):
        my, mx, mc = self.masks
        s = self.slot(o)
        src = self.src
        if o:
            src = self.out.at[self.dp, s]
            if o != self.relayed:
                self.arrived(src, self.COPIES * self.nz + o)
        self.forward(src, self.dp, s, my, self.key(o, 0))
        self.forward(src, self.dp, s, mx, self.key(o, 1))
        self.forward(src, self.dp, s, mc, self.key(o, 2))

    def second(self, o):
        my, mx, mc = self.masks
        s = self.slot(o)
        for m, k, k2, kc, p, m2 in ((my, 0, 3, 4, 0, mx), (mx, 1, 5, 6, 1, my)):
            ref = self.out.at[self.dp ^ m, s]
            self.arrived(ref, self.key(o, k))
            self.forward(ref, self.dp ^ m, s, m2, self.key(o, k2), p)
            self.forward(ref, self.dp ^ m, s, mc, self.key(o, kc))

    def third(self, o):
        my, mx, mc = self.masks
        s = self.slot(o)
        d = self.dp ^ my ^ mx
        for p, k, kc in ((0, 3, 7), (1, 5, 8)):
            ref = self.out.at[d, s]
            self.arrived(self.part(ref, p), self.key(o, k))
            self.forward(ref, d, s, mc, self.key(o, kc), p)

    def finish(self, o):
        my, mx, mc = self.masks
        s = self.slot(o)
        for k, d in ((2, mc), (4, mc ^ my), (6, mc ^ mx)):
            self.arrived(self.out.at[self.dp ^ d, s], self.key(o, k))
        for k, p in ((7, 0), (8, 1)):
            self.arrived(self.part(self.out.at[self.dp ^ mc ^ my ^ mx, s], p), self.key(o, k))

    def done(self):
        for k, p in self.started:
            ref = self.part(self.out.at[self.dp, self.z], p)
            self.copy(ref, ref, {"dp": self.dp ^ self.masks[0]}, k).wait_send()


def pack_group(w, tile, i):
    q, k, v = [w[:, WIDTH * j + HALF * i : WIDTH * j + HALF * i + HALF] for j in range(3)]
    return jnp.concatenate([jnp.concatenate([q, v[:, :256]], 1), jnp.concatenate([k, v[:, 256:], tile], 1)], 0)


def unpack_group(total):
    r = total.shape[0] // 2
    upper, lower = total[:r], total[r:]
    return upper[:, :HALF], lower[:, :HALF], upper[:, HALF:], lower[:, HALF : HALF + 128], lower[:, HALF + 128 :]


def pack_out(w, tile):
    return jnp.concatenate([jnp.concatenate([w[:, :HALF], w[:, HALF:]], 0), jnp.concatenate([tile, jnp.zeros_like(tile)], 0)], 1)


def pack_mlp(gate, up, down):
    parts = (gate, up, down)
    pads = jnp.zeros((gate.shape[0], 128 - 3 * REST), gate.dtype)
    return jnp.concatenate([x[:, :MAIN] for x in parts] + [x[:, MAIN:] for x in parts] + [pads], 1)


def unpack_mlp(total):
    return [
        jnp.concatenate([total[:, MAIN * i : MAIN * i + MAIN], total[:, 3 * MAIN + REST * i : 3 * MAIN + REST * i + REST]], 1)
        for i in range(3)
    ]


def front_kernel(nz, masks, rows, *refs):
    fused = masks is not None
    if fused:
        (tok, gout, w_qkv, w_out, gains, w_in, w_down, cos_in, sine_in), refs = refs[:9], refs[9:]
    else:
        (tok, gout, g0_all, g1_all, cos_in, sine_in), refs = refs[:6], refs[6:]
    (mixed, lse, query, gain, tok_own, gout_own, kv, firsts, wqkv), refs = refs[:9], refs[9:]
    if fused:
        (po_all, pm_all), refs = refs[:2], refs[2:]
    (tok_all, kvb, fb, wq, cos, sine, gcol, acc, top, total, tsend, trecv, loc), refs = refs[:13], refs[13:]
    me = Place(nz)
    own = me.shard

    def here(src, dst, k):
        return pltpu.make_async_copy(src, dst, loc.at[k])

    def there(src, dst, device, k):
        return remote(src, dst, tsend.at[k], trecv.at[k], device)

    def rows_to(src, c, device, k, i):
        at = pl.ds(i * (rows // 2), rows // 2)
        src = tok_all.at[c] if src is None else src
        return there(src.at[at], tok_all.at[c, at], device, k + 5 * i)

    @pl.when(me.stays)
    def _():
        here(tok, tok_all.at[own], 0).start()
        here(gout, gout_own, 1).start()

    here(cos_in, cos, 2).start()
    here(sine_in, sine, 3).start()
    groups, later = [], []
    every, rest = range(nz), (2, 1, 3)
    if fused:
        p0, p1, po, pm, g0_all, g1_all, *sems = refs
        row = lax.broadcasted_iota(jnp.int32, (128, 128), 0)

        def tile_of(i):
            return jnp.where(row == 0, gains[i : i + 1, :], 0.0).T[:SLIVER]

        p0[...] = pack_group(w_qkv[...].astype(F32), tile_of(0), 0).astype(BF)
        g0_all[me.dp, me.z] = p0[...]
    me.greet(masks or (1,))
    if fused:
        shapes = ((p0, g0_all), (p1, g1_all), (po, po_all), (pm, pm_all))
        packs = [
            Gather(src, dst, CUTS[src.shape[-1]], nz, masks, sems[2 * i], sems[2 * i + 1]) for i, (src, dst) in enumerate(shapes)
        ]
        groups, later = packs[:2], packs[2:]
        for o in rest:
            groups[0].along(o)
        groups[0].first(0)

    @pl.when(me.stays)
    def _():
        for i in range(2):
            rows_to(tok, own, me.twin, 1, i).start()
            rows_to(tok, own, me.beside, 2, i).start()

    @pl.when(me.moves)
    def _():
        for i in range(2):
            rows_to(tok, me.z, me.opposite, 0, i).start()

    def swapped(i):
        @pl.when(me.moves)
        def _():
            rows_to(None, own, me.opposite, 0, i).wait_recv()
            rows_to(None, own, me.beside, 2, i).start()
            rows_to(None, own, me.twin, 1, i).start()

    if fused:
        w = w_qkv[...].astype(F32)
        p1[...] = pack_group(w, jnp.zeros((SLIVER, 128), F32), 1).astype(BF)
        g1_all[me.dp, me.z] = p1[...]
        po[...] = pack_out(w_out[...].astype(F32), tile_of(1)).astype(BF)
        w = w_in[...].astype(F32)
        pm[...] = pack_mlp(w[:, :SHARE], w[:, SHARE:], w_down[...].astype(F32).T).astype(BF)
        here(po, po_all.at[me.dp, me.z], 4).start()
        here(pm, pm_all.at[me.dp, me.z], 5).start()
        for o in rest:
            groups[1].along(o)
        groups[1].first(0)
        groups[0].second(0)
        for o in rest:
            groups[0].first(o)
        swapped(0)
        for o in rest:
            groups[0].second(o)
        for o in rest:
            groups[1].first(o)
        for g in later:
            g.along(1)
            g.first(0)

    if not fused:
        swapped(0)
    swapped(1)

    @pl.when(me.stays)
    def _():
        here(tok, tok_all.at[own], 0).wait()

    here(tok_all.at[own], tok_own, 6).start()
    if fused:
        for g in later:
            g.along(2)
        for o in range(nz):
            groups[0].third(o)
        for o in range(nz):
            groups[0].finish(o)

    @pl.when(me.moves)
    def _():
        there(gout, gout_own, me.opposite, 4).start()

    here(cos_in, cos, 2).wait()
    here(sine_in, sine, 3).wait()

    def build(i, whole):
        def band_of(g, _):
            slabs = [unpack_group(whole[g, s].astype(F32)) for s in range(LINE)]
            band = pl.ds(pl.multiple_of(g * BAND, BAND), BAND)
            q, k, v0, v1, t = [jnp.concatenate([x[j] for x in slabs], 0) for j in range(5)]
            at = WIDTH * i
            wq[band, at : at + HALF] = k.astype(BF)
            wq[band, at + HALF : at + HALF + 256] = v0.astype(BF)
            wq[band, at + HALF + 256 : at + WIDTH] = v1.astype(BF)
            wq[band, 2 * WIDTH + HALF * i : 2 * WIDTH + HALF * i + HALF] = q.astype(BF)
            if i == 0:
                gcol[band, :] = t
            return 0

        lax.fori_loop(0, GROUPS, band_of, 0)

    def norm_chunk(c):
        def block(i, _):
            at = pl.ds(pl.multiple_of(i * 64, 64), 64)
            hat, _ = normed(tok_all[c, at, :].astype(F32))
            fb[c, at, :] = (hat * gain[0:1, :]).astype(BF)
            return 0

        lax.fori_loop(0, rows // 64, block, 0)
        here(fb.at[c], firsts.at[c], 8 + c).start()

    def queries(i):
        u = dot(fb[own], wq[:, 2 * WIDTH + HALF * i : 2 * WIDTH + HALF * i + HALF], NN)
        for j in range(3):
            tile = rope(u[:, 128 * j : 128 * j + 128], cos[own], sine[own])
            query[:, HALF * i + 128 * j : HALF * i + 128 * j + 128] = (tile * (SCALE * LOG2E)).astype(BF)

    def visits(grp, steps):
        def visit(t, _):
            stay = jnp.where(t == 1, 1, jnp.where(t == 2, 3, 2))
            move = jnp.where(t == 1, 3, jnp.where(t == 2, 2, 1))
            turn = jnp.where(me.stays, stay, move)
            c = jnp.where(t == 0, own, own ^ turn)
            if grp == 0:

                @pl.when(t > 0)
                def _():
                    for i in range(2):
                        rows_to(None, c, me.twin, jnp.where(turn == 1, 2, jnp.where(turn == 3, 1, 3)), i).wait_recv()

                        @pl.when(turn == 1)
                        def _(i=i):
                            rows_to(None, c, me.twin, 3, i).start()

                    norm_chunk(c)

            for j in range(3):
                u = dot(fb[c], wq[:, WIDTH * grp + 256 * j : WIDTH * grp + 256 * j + 256], NN)
                for i in range(2):
                    n = 2 * j + i
                    x = u[:, 128 * i : 128 * i + 128]
                    x = rope(x, cos[c], sine[c]) if n < 3 else x
                    kvb[grp, c, :, 128 * n : 128 * n + 128] = x.astype(BF)
            here(kvb.at[grp, c], kv.at[grp, c], 8 + nz * (1 + grp) + c).start()
            jobs = [(i, h) for i in range(3) for h in range(2)]

            def score(i, h):
                q = query[:, HALF * grp + 128 * i : HALF * grp + 128 * i + 128]
                mask = (lane_iota() < 64) if h == 0 else (lane_iota() >= 64)
                return dot(kvb[grp, c, :, 128 * i : 128 * i + 128], jnp.where(mask, q, jnp.zeros_like(q)), NT)

            ready = [score(*j) for j in jobs[:2]]
            for n, (i, h) in enumerate(jobs):
                if h == 0:
                    vt = kvb[grp, c, :, HALF + 128 * i : HALF + 128 * i + 128].T
                s = ready[n]
                if n + 2 < len(jobs):
                    ready.append(score(*jobs[n + 2]))
                head = 6 * grp + n
                old = top[head : head + 1, :]
                new = jnp.maximum(old, jnp.max(s, 0, keepdims=True))
                p = jnp.exp2(s - new)
                fade = jnp.exp2(old - new)
                top[head : head + 1, :] = new
                lhs = jnp.concatenate([vt[h * 64 : h * 64 + 64], jnp.ones((16, rows), BF)], 0)
                oo = dot(lhs, p.astype(BF), NN)
                total[head : head + 1, :] = total[head : head + 1, :] * fade + oo[64:65]
                acc[64 * head : 64 * head + 64, :] = acc[64 * head : 64 * head + 64, :] * fade + oo[:64]
            if fused:
                for k, step in steps.items():

                    @pl.when(t == k)
                    def _(step=step):
                        for which, name, order in step:
                            for g in which:
                                for o in order:
                                    getattr(g, name)(o)

            return 0

        lax.fori_loop(0, nz, visit, 0)

    build(0, g0_all)
    gain[...] = gcol[...].T[:8]
    norm_chunk(own)
    queries(0)
    acc[...] = jnp.zeros_like(acc)
    total[...] = jnp.zeros_like(total)
    top[...] = jnp.full_like(top, -1e30)
    one = groups[1:]
    visits(0, {0: [(one, "second", every), (later, "first", (1,))], 1: [(one, "third", every)], 2: [(later, "relay", (2,)), (later, "first", (2,))], 3: [(one, "finish", every), (later, "second", (0, 1))]})
    build(1, g1_all)
    here(wq, wqkv, 7).start()
    queries(1)
    visits(1, {0: [(later, "first", (3,))], 1: [(later, "second", (2,))], 2: [(later, "second", (3,))], 3: [(later, "third", every)]})

    for hp in range(PAIRS):
        parts = [
            acc[128 * hp + 64 * h : 128 * hp + 64 * h + 64, :] / total[2 * hp + h : 2 * hp + h + 1, :] for h in range(2)
        ]
        mixed[:, 128 * hp : 128 * hp + 128] = jnp.concatenate(parts, 0).T.astype(BF)
    lse[...] = top[...] + jnp.log(jnp.maximum(total[...], 1e-30)) * LOG2E

    if fused:
        for g in later:
            for o in range(nz):
                g.finish(o)
        for g in packs:
            g.done()
        here(po, po_all.at[me.dp, me.z], 4).wait()
        here(pm, pm_all.at[me.dp, me.z], 5).wait()
    for i in range(2):
        for k in (1, 2, 3):
            rows_to(None, own, me.twin, k, i).wait_send()

    @pl.when(me.moves)
    def _():
        for i in range(2):
            rows_to(None, own, me.opposite, 0, i).wait_send()
        there(gout, gout_own, me.opposite, 4).wait()

    @pl.when(me.stays)
    def _():
        here(gout, gout_own, 1).wait()

    here(tok_all.at[own], tok_own, 6).wait()
    here(wq, wqkv, 7).wait()
    for c in range(nz):
        here(fb.at[c], firsts.at[c], 8 + c).wait()
        for grp in range(2):
            here(kvb.at[grp, c], kv.at[grp, c], 8 + nz * (1 + grp) + c).wait()


def front(tok, gout, weights, cos, sine, nz, masks):
    rows = tok.shape[0]
    vmem, anyspace = pl.BlockSpec(memory_space=pltpu.VMEM), pl.BlockSpec(memory_space=pl.ANY)
    shape, vm = jax.ShapeDtypeStruct, pltpu.VMEM
    outs = [shape((rows, WIDTH), BF), shape((16, rows), F32), shape((rows, WIDTH), BF), shape((8, WIDTH), F32)]
    outs += [shape((rows, WIDTH), BF)] * 2
    outs += [shape((2, nz, rows, WIDTH), BF), shape((nz, rows, WIDTH), BF), shape((WIDTH, 3 * WIDTH), BF)]
    out_specs = [vmem] * 4 + [anyspace, vmem] + [anyspace] * 3
    scratch = [
        vm((nz, rows, WIDTH), BF),
        vm((2, nz, rows, WIDTH), BF),
        vm((nz, rows, WIDTH), BF),
        vm((WIDTH, 3 * WIDTH), BF),
        vm((nz, rows, 128), F32),
        vm((nz, rows, 128), F32),
        vm((WIDTH, 128), F32),
        vm((WIDTH, rows), F32),
        vm((16, rows), F32),
        vm((16, rows), F32),
        pltpu.SemaphoreType.DMA((9,)),
        pltpu.SemaphoreType.DMA((9,)),
        pltpu.SemaphoreType.DMA((8 + 3 * nz,)),
    ]
    if masks:
        grp, out, mlp = (2 * SLIVER, 640), (2 * SLIVER, 512), (BAND, 896)
        outs += [shape((GROUPS, nz) + out, BF), shape((GROUPS, nz) + mlp, BF)]
        out_specs += [anyspace] * 2
        scratch += [vm(x, BF) for x in (grp, grp, out, mlp)] + [vm((GROUPS, nz) + grp, BF)] * 2
        scratch += [pltpu.SemaphoreType.DMA((Gather.sems(nz),)) for _ in range(8)]
    return pl.pallas_call(
        functools.partial(front_kernel, nz, masks, rows),
        out_shape=outs,
        in_specs=[anyspace] * 2 + [vmem] * len(weights) + [anyspace] * 2,
        out_specs=out_specs,
        scratch_shapes=scratch,
        compiler_params=pltpu.CompilerParams(collective_id=0, has_side_effects=True, vmem_limit_bytes=60 << 20),
        cost_estimate=pl.CostEstimate(flops=14_000_000_000, bytes_accessed=40_000_000, transcendentals=13_000_000),
        name="front",
    )(tok, gout, *weights, cos, sine)


def middle_kernel(rows, tok, mixed, gout, po_all, pm_all, out, gmid, gmixed, delta, po_g, pm_g,
                  wout, wg, wu, wd, gcol, gain, resid, hat, inv, second, hidden, ggate, gup, gsec, gattn, dwout):
    lane = lane_iota()

    def build(g, _):
        band = pl.ds(pl.multiple_of(g * BAND, BAND), BAND)
        slabs = [po_all[g, s].astype(F32) for s in range(LINE)]
        wout[band, :384] = jnp.concatenate([x[:SLIVER, :384] for x in slabs], 0).astype(BF)
        wout[band, 384:] = jnp.concatenate([x[SLIVER:, :384] for x in slabs], 0).astype(BF)
        gcol[band, :] = jnp.concatenate([x[:SLIVER, 384:] for x in slabs], 0)
        for i, w in enumerate((wg, wu, wd)):
            tail = jnp.zeros((BAND, 128), F32)
            for s in range(LINE):
                w[band, MAIN * s : MAIN * s + MAIN] = pm_all[g, s, :, MAIN * i : MAIN * i + MAIN]
                rest = pm_all[g, s, :, 3 * MAIN :].astype(F32)
                turn = (REST * (s - i)) % 128
                rest = pltpu.roll(rest, turn, 1) if turn else rest
                tail = jnp.where((lane >= REST * s) & (lane < REST * (s + 1)), rest, tail)
            w[band, MAIN * LINE :] = tail.astype(BF)
        return 0

    lax.fori_loop(0, GROUPS, build, 0)
    gain[...] = gcol[...].T[:8]

    for j in range(3):
        at = slice(256 * j, 256 * j + 256)
        resid[:, at] = tok[:, at].astype(F32) + dot(mixed[...], wout[:, at], NN)

    def norm_block(i, _):
        at = pl.ds(pl.multiple_of(i * 64, 64), 64)
        h, r = normed(resid[at, :])
        hat[at, :] = h
        inv[at, :] = jnp.broadcast_to(r, (64, 128))
        second[at, :] = (h * gain[0:1, :]).astype(BF)
        return 0

    lax.fori_loop(0, rows // 64, norm_block, 0)

    def units(start, width):
        at = pl.ds(start, width)
        gate, up, gh = dot(second[...], wg[:, at], NN), dot(second[...], wu[:, at], NN), dot(gout[...], wd[:, at], NN)
        cdf = 0.5 + 0.5 * lax.erf(gate * math.sqrt(0.5))
        pdf = jnp.exp2(gate * gate * (-0.5 * LOG2E)) * (1.0 / math.sqrt(2.0 * math.pi))
        act = gate * cdf
        hidden[:, at] = (act * up).astype(BF)
        gup[:, at] = (gh * act).astype(BF)
        ggate[:, at] = (gh * up * (cdf + gate * pdf)).astype(BF)

    for start in range(0, UNITS, 256):
        units(start, min(256, UNITS - start))

    for j in range(3):
        at = slice(256 * j, 256 * j + 256)
        out[:, at] = (resid[:, at] + dot(hidden[...], wd[at, :], NT)).astype(BF)
        gsec[:, at] = dot(ggate[...], wg[at, :], NT) + dot(gup[...], wu[at, :], NT)

    def back_block(i, dgain):
        at = pl.ds(pl.multiple_of(i * 64, 64), 64)
        dy, h = gsec[at, :], hat[at, :]
        gm = gout[at, :].astype(F32) + norm_back(dy, gain[0:1, :], h, inv[at, 0:1])
        gmid[at, :] = gm
        gattn[at, :] = gm.astype(BF)
        return dgain + jnp.sum(dy * h, 0, keepdims=True)

    dgain = lax.fori_loop(0, rows // 64, back_block, jnp.zeros((1, WIDTH), F32))

    heads = lax.broadcasted_iota(jnp.int32, (16, 256), 0)
    for j in range(3):
        at = slice(256 * j, 256 * j + 256)
        gmx = dot(gattn[...], wout[at, :], NT).astype(BF)
        gmixed[:, at] = gmx
        prod = gmx.astype(F32) * mixed[:, at].astype(F32)
        high = prod.astype(BF)
        low = (prod - high.astype(F32)).astype(BF)
        pick = ((lax.broadcasted_iota(jnp.int32, (16, 256), 1) + 256 * j) // HEAD_DIM == heads).astype(BF)
        part = dot(pick, high, NT) + dot(pick, low, NT)
        delta[...] = part if j == 0 else delta[...] + part

    for j in range(2):
        at = slice(384 * j, 384 * j + 384)
        dwout[at, :] = dot(mixed[:, at], gattn[...], TN)
    row = lax.broadcasted_iota(jnp.int32, (128, WIDTH), 0)
    gcol[...] = jnp.where(row == 0, dgain, 0.0).T

    def pack_out(g, _):
        for s in range(LINE):
            at = pl.ds(pl.multiple_of(g * BAND + s * SLIVER, 8), SLIVER)
            x, c = dwout[at, :], gcol[at, :]
            po_g[g, s, :, :384] = jnp.concatenate([x[:, :384], x[:, 384:]], 0).astype(BF)
            po_g[g, s, :, 384:] = jnp.concatenate([c, jnp.zeros_like(c)], 0).astype(BF)
        return 0

    lax.fori_loop(0, GROUPS, pack_out, 0)

    for j in range(2):
        at = slice(384 * j, 384 * j + 384)
        tails = []
        for i, (a, b) in enumerate(((second, ggate), (second, gup), (gout, hidden))):
            for s in range(LINE):
                x = dot(a[:, at], b[:, MAIN * s : MAIN * s + MAIN], TN).astype(BF)
                for g in range(4):
                    pm_g[4 * j + g, s, :, MAIN * i : MAIN * i + MAIN] = x[BAND * g : BAND * g + BAND]
            tails.append(dot(a[:, at], b[:, MAIN * LINE :], TN))
        for s in range(LINE):
            y = jnp.zeros((384, 128), F32)
            for i, tail in enumerate(tails):
                turn = (REST * (i - s)) % 128
                tail = pltpu.roll(tail, turn, 1) if turn else tail
                y = jnp.where((lane >= REST * i) & (lane < REST * (i + 1)), tail, y)
            y = y.astype(BF)
            for g in range(4):
                pm_g[4 * j + g, s, :, 3 * MAIN :] = y[BAND * g : BAND * g + BAND]


def middle(tok, mixed, gout, po_all, pm_all):
    rows = tok.shape[0]
    shape, vm = jax.ShapeDtypeStruct, pltpu.VMEM
    vmem = pl.BlockSpec(memory_space=pltpu.VMEM)
    return pl.pallas_call(
        functools.partial(middle_kernel, rows),
        out_shape=[
            shape((rows, WIDTH), BF),
            shape((rows, WIDTH), F32),
            shape((rows, WIDTH), BF),
            shape((16, rows), F32),
            shape(po_all.shape, BF),
            shape(pm_all.shape, BF),
        ],
        in_specs=[vmem] * 5,
        out_specs=[vmem] * 6,
        scratch_shapes=[
            vm((WIDTH, WIDTH), BF),
            vm((WIDTH, UNITS), BF),
            vm((WIDTH, UNITS), BF),
            vm((WIDTH, UNITS), BF),
            vm((WIDTH, 128), F32),
            vm((8, WIDTH), F32),
            vm((rows, WIDTH), F32),
            vm((rows, WIDTH), F32),
            vm((rows, 128), F32),
            vm((rows, WIDTH), BF),
            vm((rows, UNITS), BF),
            vm((rows, UNITS), BF),
            vm((rows, UNITS), BF),
            vm((rows, WIDTH), F32),
            vm((rows, WIDTH), BF),
            vm((WIDTH, WIDTH), F32),
        ],
        compiler_params=pltpu.CompilerParams(vmem_limit_bytes=58 << 20),
        cost_estimate=pl.CostEstimate(flops=11_000_000_000, bytes_accessed=25_000_000, transcendentals=1_200_000),
        name="middle",
    )(tok, mixed, gout, po_all, pm_all)


class Reduce:
    COPIES = 10

    def __init__(self, src, total, cut, nz, masks, bufs, send, recv, loc=None):
        self.src, self.total, self.cut, self.nz, self.masks = src, total, cut, nz, masks
        self.near, self.side0, self.side1, self.far, *mine = bufs
        self.mine = mine[0] if mine else None
        self.send, self.recv, self.loc = send, recv, loc
        self.dp, self.z = lax.axis_index("dp"), lax.axis_index("seq")
        my, mx, mc = masks
        self.turns = (0, my, mx, my ^ mx)
        self.started = []

    @staticmethod
    def scratch(shape, nz, held):
        r, c = shape
        cut = CUTS[c]
        bufs = [
            pltpu.VMEM((4, nz, r, c), BF),
            pltpu.VMEM((3, nz, r, cut), BF),
            pltpu.VMEM((3, nz, r, c - cut), BF),
            pltpu.VMEM((nz - 1, r, c), BF),
        ]
        sems = [pltpu.SemaphoreType.DMA((Reduce.COPIES * nz + nz,))] * 2
        if not held:
            bufs += [pltpu.VMEM((4, nz, r, c), BF)]
            sems += [pltpu.SemaphoreType.DMA((4 * nz,))]
        return bufs, sems

    def begin(self, src, dst, device, k):
        remote(src, dst, self.send.at[k], self.recv.at[k], device).start()
        self.started.append((k, src.shape[-1]))

    def arrived(self, ref, k):
        remote(ref, ref, self.send.at[k], self.recv.at[k], {"dp": self.dp ^ self.masks[2]}).wait_recv()

    def seat(self, o):
        return self.z ^ LINKED[o]

    def held(self, i, s):
        return self.mine.at[i, s] if self.mine is not None else self.src.at[self.dp ^ self.turns[i], s]

    def local(self, i, o):
        s = self.seat(o)
        return pltpu.make_async_copy(self.src.at[self.dp ^ self.turns[i], s], self.mine.at[i, s], self.loc.at[4 * o + i])

    def zero(self, o):
        s, mc = self.seat(o), self.masks[2]
        for i in (3, 1, 2, 0):
            if self.mine is not None:
                self.local(i, o).start()
            self.begin(self.src.at[self.dp ^ mc ^ self.turns[i], s], self.near.at[i, s], {"dp": self.dp ^ mc}, self.COPIES * o + i)

    def add(self, ref, other):
        ref[...] = (ref[...].astype(F32) + other[...].astype(F32)).astype(BF)

    def p0(self, i, s):
        return self.held(i, s).at[:, pl.ds(0, self.cut)]

    def p1(self, i, s):
        return self.held(i, s).at[:, pl.ds(self.cut, self.src.shape[-1] - self.cut)]

    def one(self, o):
        my, mx, _ = self.masks
        s, k = self.seat(o), self.COPIES * o
        for i in (3, 1, 2, 0):
            if self.mine is not None:
                self.local(i, o).wait()
            self.arrived(self.near.at[i, s], k + i)
            self.add(self.held(i, s), self.near.at[i, s])
            if i == 3:
                self.begin(self.p0(3, s), self.side0.at[1, s], {"dp": self.dp ^ my}, k + 4)
                self.begin(self.p1(3, s), self.side1.at[1, s], {"dp": self.dp ^ mx}, k + 5)
            if i == 1:
                self.begin(self.p0(1, s), self.side0.at[0, s], {"dp": self.dp ^ my}, k + 6)
            if i == 2:
                self.begin(self.p1(2, s), self.side1.at[0, s], {"dp": self.dp ^ mx}, k + 7)

    def two(self, o):
        my, mx, _ = self.masks
        s, k = self.seat(o), self.COPIES * o
        self.arrived(self.side0.at[1, s], k + 4)
        self.add(self.p0(2, s), self.side0.at[1, s])
        self.begin(self.p0(2, s), self.side0.at[2, s], {"dp": self.dp ^ mx}, k + 8)
        self.arrived(self.side1.at[1, s], k + 5)
        self.add(self.p1(1, s), self.side1.at[1, s])
        self.begin(self.p1(1, s), self.side1.at[2, s], {"dp": self.dp ^ my}, k + 9)

    def three(self, o):
        s, k = self.seat(o), self.COPIES * o
        for ref, side, k1, k2 in ((self.p0(0, s), self.side0, k + 6, k + 8), (self.p1(0, s), self.side1, k + 7, k + 9)):
            self.arrived(side.at[0, s], k1)
            self.arrived(side.at[2, s], k2)
            ref[...] = (ref[...].astype(F32) + side[0, s].astype(F32) + side[2, s].astype(F32)).astype(BF)
        if o:
            self.begin(self.held(0, s), self.far.at[o - 1], {"seq": s}, self.COPIES * self.nz + o)

    def four(self):
        out = self.held(0, self.z)[...].astype(F32)
        for o in range(1, self.nz):
            self.arrived(self.far.at[o - 1], self.COPIES * self.nz + o)
            out = out + self.far[o - 1].astype(F32)
        self.total[...] = out

    def done(self):
        for k, width in self.started:
            whole = width == self.src.shape[-1]
            ref = self.near.at[0, 0] if whole else (self.side0 if k % self.COPIES in (4, 6, 8) else self.side1).at[0, 0]
            remote(ref, ref, self.send.at[k], self.recv.at[k], {"dp": self.dp ^ self.masks[2]}).wait_send()


def back_kernel(nz, masks, rows, *refs):
    fused = masks is not None
    (tok, gmid, out_own, query, kv, firsts, wqkv, gain, gmixed, lse, delta, cos_in, sine_in), refs = refs[:13], refs[13:]
    if fused:
        (po_g, pm_g, gtok, out, s0, s1, so, sm), refs = refs[:8], refs[8:]
    else:
        (gtok, out, p0_g, p1_g), refs = refs[:4], refs[4:]
    (kvb, fb, ft, wq, cos, sine, dq, dqb, dkv, dx, dw, sent, landed, gown, gcol, send, recv, loc), refs = refs[:18], refs[18:]
    me = Place(nz)
    own = me.shard

    def here(src, dst, k):
        return pltpu.make_async_copy(src, dst, loc.at[k])

    def there(src, dst, device, k):
        return remote(src, dst, send.at[k], recv.at[k], device)

    def chunk(t):
        return jnp.where(t == 0, own ^ 2, jnp.where(t == 1, own ^ 1, jnp.where(t == 2, own ^ 3, own)))

    def fetch(grp, t):
        c, slot = chunk(t), lax.rem(t, 2)
        found = [here(kv.at[grp, c], kvb.at[slot], slot)]
        if grp == 0:
            found.append(here(firsts.at[c], fb.at[slot], 2 + slot))
        return found

    for c in fetch(0, 0):
        c.start()
    whole = [here(wqkv, wq, 4), here(cos_in, cos, 5), here(sine_in, sine, 6)]
    for c in whole:
        c.start()
    me.greet(masks or (1,))
    jobs, sums = [], []
    if fused:
        (p0_g, p1_g), refs = refs[:2], refs[2:]
        for src, total in ((p0_g, s0), (p1_g, s1)):
            sums.append(Reduce(src, total, CUTS[src.shape[-1]], nz, masks, refs[:4], *refs[4:6]))
            refs = refs[6:]
        for src, total in ((po_g, so), (pm_g, sm)):
            jobs.append(Reduce(src, total, CUTS[src.shape[-1]], nz, masks, refs[:5], *refs[5:8]))
            refs = refs[8:]
    order = (3, 2, 1, 0)

    def advance(which, step):
        for j in which:
            for o in order:
                getattr(j, step)(o)

    def wave(which):
        for i in range(nz + 2):
            for k, step in enumerate(("one", "two", "three")):
                if 0 <= i - k < nz:
                    for j in which:
                        getattr(j, step)(order[i - k])

    advance(jobs, "zero")

    @pl.when(me.moves)
    def _():
        there(out_own, out, me.opposite, 3).start()

    @pl.when(me.stays)
    def _():
        here(out_own, out, 7).start()

    dq[...] = jnp.zeros_like(dq)
    for c in whole:
        c.wait()

    def visits(grp, steps):
        def visit(t, _):
            c, slot = chunk(t), lax.rem(t, 2)
            for f in fetch(grp, t):
                f.wait()

            @pl.when(t + 1 < nz)
            def _():
                for f in fetch(grp, t + 1):
                    f.start()

            if grp == 0:

                @pl.when(t + 1 == nz)
                def _():
                    for f in fetch(1, 0):
                        f.start()

            band = pl.ds(pl.multiple_of(t * rows, rows), rows)
            todo = [(i, h) for i in range(3) for h in range(2)]

            def pick(ref, i, h):
                x = ref[:, HALF * grp + 128 * i : HALF * grp + 128 * i + 128]
                mask = (lane_iota() < 64) if h == 0 else (lane_iota() >= 64)
                return jnp.where(mask, x, jnp.zeros_like(x))

            def score(i, h):
                qh, gh = pick(query, i, h), pick(gmixed, i, h)
                k, v = kvb[slot, :, 128 * i : 128 * i + 128], kvb[slot, :, HALF + 128 * i : HALF + 128 * i + 128]
                return dot(k, qh, NT), dot(v, gh, NT), qh, gh

            ready = [score(*todo[0])]
            dk = dv = None
            for n, (i, h) in enumerate(todo):
                s, dp, qh, gh = ready[n]
                if n + 1 < len(todo):
                    ready.append(score(*todo[n + 1]))
                if h == 0:
                    kt = kvb[slot, :, 128 * i : 128 * i + 128].T
                head = 6 * grp + n
                p = jnp.exp2(s - lse[head : head + 1, :])
                ds = (p * (dp - delta[head : head + 1, :])).astype(BF)
                a = dot(p.astype(BF), gh, NN)
                dv = a if h == 0 else dv + a
                a = dot(ds, qh, NN)
                dk = a if h == 0 else dk + a
                dq[64 * head : 64 * head + 64, :] += dot(kt[h * 64 : h * 64 + 64], ds, NN)
                if h == 1:
                    at = WIDTH * grp + 128 * i
                    dkv[band, at : at + 128] = rope_back(dk * (1.0 / LOG2E), cos[c], sine[c]).astype(BF)
                    dkv[band, at + HALF : at + HALF + 128] = dv.astype(BF)

            if grp == 0:
                for j in range(6):
                    ft[128 * j : 128 * j + 128, band] = fb[slot, :, 128 * j : 128 * j + 128].T
            else:
                for j in range(3):
                    at = slice(256 * j, 256 * j + 256)
                    dx[:, at] = dot(dkv[band, :], wq[at, : 2 * WIDTH], NT)

                @pl.when(lax.rem(t, 2) == 0)
                def _():
                    sent[t] = dx[...].astype(BF)
                    there(sent.at[t], landed.at[t], me.twin, t).start()

                @pl.when(t == 1)
                def _():
                    there(sent.at[0], landed.at[0], me.twin, 0).wait_recv()
                    sent[1] = (dx[...] + landed[0].astype(F32)).astype(BF)
                    there(sent.at[1], landed.at[1], me.beside, 1).start()

            if fused:
                for k, step in steps.items():

                    @pl.when(t == k)
                    def _(step=step):
                        for which, name in step:
                            if name == "four":
                                for j in which:
                                    j.four()
                            else:
                                advance(which, name)

            return 0

        lax.fori_loop(0, nz, visit, 0)
        for i in range(3 * grp, 3 * grp + 3):
            at = slice(128 * i, 128 * i + 128)
            dqb[:, at] = rope_back(dq[at, :].T * SCALE, cos[own], sine[own]).astype(BF)

    def weigh(grp):
        for r in (slice(0, HALF), slice(HALF, WIDTH)):
            for j in range(3):
                at = WIDTH * grp + 256 * j
                dw[r, HALF + 256 * j : HALF + 256 * j + 256] = dot(ft[r, :], dkv[:, at : at + 256], NN)
            dw[r, :HALF] = dot(ft[r, (nz - 1) * rows :], dqb[:, HALF * grp : HALF * grp + HALF], NN)

    def pack(grp, dst):
        def band_of(g, _):
            for s in range(LINE):
                at = pl.ds(pl.multiple_of(g * BAND + s * SLIVER, 8), SLIVER)
                q, k, v0, v1 = dw[at, :HALF], dw[at, HALF:WIDTH], dw[at, WIDTH : WIDTH + 256], dw[at, WIDTH + 256 :]
                tile = gcol[at, :] if grp else jnp.zeros((SLIVER, 128), F32)
                dst[g, s] = jnp.concatenate(
                    [jnp.concatenate([q, v0], 1), jnp.concatenate([k, v1, tile], 1)], 0
                ).astype(BF)
            return 0

        lax.fori_loop(0, GROUPS, band_of, 0)

    visits(0, {0: [(jobs, "one")]})
    weigh(0)
    pack(0, p0_g)
    early = sums[:1]
    advance(early, "zero")
    visits(1, {0: [(jobs, "two"), (early, "one")], 2: [(jobs, "three")], 3: [(early, "two"), (early, "three")]})
    for j in range(3):
        at = slice(256 * j, 256 * j + 256)
        dx[:, at] += dot(dqb[...], wq[at, 2 * WIDTH :], NT)
    there(sent.at[1], landed.at[1], me.beside, 1).wait_recv()
    there(sent.at[2], landed.at[2], me.twin, 2).wait_recv()

    def norm_block(i, dgain):
        at = pl.ds(pl.multiple_of(i * 64, 64), 64)
        dy = dx[at, :] + landed[1, at, :].astype(F32) + landed[2, at, :].astype(F32)
        h, r = normed(tok[at, :].astype(F32))
        gown[at, :] = (gmid[at, :] + norm_back(dy, gain[0:1, :], h, r)).astype(BF)
        return dgain + jnp.sum(dy * h, 0, keepdims=True)

    dgain = lax.fori_loop(0, rows // 64, norm_block, jnp.zeros((1, WIDTH), F32))

    @pl.when(me.moves)
    def _():
        there(gown, gtok, me.opposite, 4).start()

    @pl.when(me.stays)
    def _():
        here(gown, gtok, 8).start()

    row = lax.broadcasted_iota(jnp.int32, (128, WIDTH), 0)
    gcol[...] = jnp.where(row == 0, dgain, 0.0).T
    weigh(1)
    pack(1, p1_g)
    if fused:
        advance(sums[1:], "zero")
        wave(sums[1:])
        for j in jobs + sums:
            j.four()
        for j in jobs + sums:
            j.done()
    for k, device in ((0, me.twin), (1, me.beside), (2, me.twin)):
        there(sent.at[k], landed.at[k], device, k).wait_send()

    @pl.when(me.moves)
    def _():
        there(out_own, out, me.opposite, 3).wait()
        there(gown, gtok, me.opposite, 4).wait()

    @pl.when(me.stays)
    def _():
        here(out_own, out, 7).wait()
        here(gown, gtok, 8).wait()


def back(tok, gmid, out_own, query, kv, firsts, wqkv, gain, gmixed, lse, delta, cos, sine, packs, nz, masks):
    rows = tok.shape[0]
    shape, vm = jax.ShapeDtypeStruct, pltpu.VMEM
    vmem, anyspace = pl.BlockSpec(memory_space=pltpu.VMEM), pl.BlockSpec(memory_space=pl.ANY)
    in_specs = [vmem] * 4 + [anyspace] * 3 + [vmem] * 4 + [anyspace] * 2
    slab = (2 * SLIVER, 640)
    outs, out_specs = [shape((rows, WIDTH), BF)] * 2, [vmem] * 2
    scratch = [
        vm((2, rows, WIDTH), BF),
        vm((2, rows, WIDTH), BF),
        vm((WIDTH, nz * rows), BF),
        vm((WIDTH, 3 * WIDTH), BF),
        vm((nz, rows, 128), F32),
        vm((nz, rows, 128), F32),
        vm((WIDTH, rows), F32),
        vm((rows, WIDTH), BF),
        vm((nz * rows, 2 * WIDTH), BF),
        vm((rows, WIDTH), F32),
        vm((WIDTH, 3 * HALF), F32),
        vm((3, rows, WIDTH), BF),
        vm((3, rows, WIDTH), BF),
        vm((rows, WIDTH), BF),
        vm((WIDTH, 128), F32),
        pltpu.SemaphoreType.DMA((5,)),
        pltpu.SemaphoreType.DMA((5,)),
        pltpu.SemaphoreType.DMA((9,)),
    ]
    if masks:
        in_specs += [anyspace] * 2
        outs += [shape(s, F32) for s in (slab, slab, packs[0].shape[-2:], packs[1].shape[-2:])]
        out_specs += [vmem] * 4
        scratch += [vm((GROUPS, LINE) + slab, BF)] * 2
        for s, held in ((slab, True), (slab, True), (packs[0].shape[-2:], False), (packs[1].shape[-2:], False)):
            bufs, sems = Reduce.scratch(s, nz, held)
            scratch += bufs + sems
    else:
        outs += [shape((GROUPS, LINE) + slab, BF)] * 2
        out_specs += [vmem] * 2
        packs = []
    return pl.pallas_call(
        functools.partial(back_kernel, nz, masks, rows),
        out_shape=outs,
        in_specs=in_specs,
        out_specs=out_specs,
        scratch_shapes=scratch,
        compiler_params=pltpu.CompilerParams(collective_id=1, has_side_effects=True, vmem_limit_bytes=62 << 20),
        cost_estimate=pl.CostEstimate(flops=24_000_000_000, bytes_accessed=40_000_000, transcendentals=13_000_000),
        name="back",
    )(tok, gmid, out_own, query, kv, firsts, wqkv, gain, gmixed, lse, delta, cos, sine, *packs)


def finish_kernel(out, gtok, s0, s1, so, sm, out_o, gtok_o, qkv_o, w_out_o, gains_o, gate_o, down_o):
    out_o[...] = out[...]
    gtok_o[...] = gtok[...]
    for i, total in enumerate((s0, s1)):
        q, k, v0, v1, tile = unpack_group(total[...])
        for j, x in enumerate((q, k)):
            qkv_o[:, WIDTH * j + HALF * i : WIDTH * j + HALF * i + HALF] = x
        at = 2 * WIDTH + HALF * i
        qkv_o[:, at : at + 256] = v0
        qkv_o[:, at + 256 : at + HALF] = v1
    w_out_o[:, :HALF] = so[:SLIVER, :HALF]
    w_out_o[:, HALF:] = so[SLIVER:, :HALF]
    zeros = jnp.zeros((128 - SLIVER, 128), F32)
    for i, col in enumerate((tile, so[:SLIVER, HALF:])):
        gains_o[i : i + 1, :] = jnp.concatenate([col, zeros], 0).T[:1]
    gate, up, down = unpack_mlp(sm[...])
    gate_o[:, :SHARE] = gate
    gate_o[:, SHARE:] = up
    down_o[...] = down.T


def finish(out, gtok, s0, s1, so, sm):
    shape = jax.ShapeDtypeStruct
    vmem = pl.BlockSpec(memory_space=pltpu.VMEM)
    return pl.pallas_call(
        finish_kernel,
        out_shape=[
            shape(out.shape, BF),
            shape(gtok.shape, BF),
            shape((SLIVER, 3 * WIDTH), F32),
            shape((SLIVER, WIDTH), F32),
            shape((8, 128), F32),
            shape((BAND, 2 * SHARE), F32),
            shape((SHARE, BAND), F32),
        ],
        in_specs=[vmem] * 6,
        out_specs=[vmem] * 7,
        compiler_params=pltpu.CompilerParams(vmem_limit_bytes=40 << 20),
        name="finish",
    )(out, gtok, s0, s1, so, sm)


def whole_packs(w_qkv, w_out, attn_gain, mlp_gain, w_in, w_down):
    both = ("dp", "seq")

    def shards_of(w):
        w = lax.all_gather(w, both, axis=0, tiled=True)
        return w.reshape(GROUPS * LINE, SLIVER, -1)

    def slabs(pack, w, gain):
        found = jax.vmap(pack)(w, jnp.pad(gain, ((0, 0), (0, 0), (0, 127))))
        return found.reshape((GROUPS, LINE) + found.shape[1:])

    qkv, gain_a, gain_m = shards_of(w_qkv), shards_of(attn_gain), shards_of(mlp_gain)
    groups = [slabs(lambda w, t, i=i: pack_group(w, t, i), qkv, gain_a) for i in range(2)]
    w_in, w_down = lax.all_gather(w_in, "dp", axis=0, tiled=True), lax.all_gather(w_down, "dp", axis=1, tiled=True)
    mlp = lax.all_gather(pack_mlp(w_in[:, 0], w_in[:, 1], w_down.T), "seq", axis=0, tiled=False)
    mlp = mlp.reshape(LINE, GROUPS, BAND, -1).transpose(1, 0, 2, 3)
    return groups, slabs(pack_out, shards_of(w_out), gain_m), mlp


def whole_sums(p0_g, p1_g, po_g, pm_g):
    both = ("dp", "seq")

    def scattered(x):
        return lax.psum_scatter(x.reshape(WIDTH, -1), both, scatter_dimension=0, tiled=True)

    parts = [jax.vmap(unpack_group)(p.reshape((GROUPS * LINE,) + p.shape[2:]).astype(F32)) for p in (p0_g, p1_g)]
    columns = [parts[0][0], parts[1][0], parts[0][1], parts[1][1], parts[0][2], parts[0][3], parts[1][2], parts[1][3]]
    g_qkv, gain_a = scattered(jnp.concatenate(columns, -1)), scattered(parts[1][4][..., :1])[:, 0]
    po = po_g.reshape(GROUPS * LINE, 2 * SLIVER, -1).astype(F32)
    g_out = scattered(jnp.concatenate([po[:, :SLIVER, :HALF], po[:, SLIVER:, :HALF]], -1))
    gain_m = scattered(po[:, :SLIVER, HALF : HALF + 1])[:, 0]
    mlp = pm_g.astype(F32).transpose(1, 0, 2, 3).reshape(LINE, WIDTH, -1)
    mlp = lax.psum_scatter(mlp, "seq", scatter_dimension=0, tiled=False)
    gate, up, down = unpack_mlp(lax.psum_scatter(mlp, "dp", scatter_dimension=0, tiled=True))
    return g_qkv, g_out, gain_a, gain_m, jnp.stack([gate, up], 1), down.T


def on_device(tokens, w_qkv, w_out, attn_gain, mlp_gain, w_in, w_down, grad_out, *, dp, nz):
    rows = tokens.shape[0]
    masks = (dp // 2, dp // 4, 1) if dp == GROUPS else None
    cos, sine = [jnp.asarray(t).reshape(nz, rows, 128) for t in rope_tables(nz * rows)]
    if masks:
        gains = jnp.pad(jnp.stack([attn_gain, mlp_gain]).astype(F32), ((0, 6), (0, 128 - SLIVER)))
        weights = [w_qkv, w_out, gains, w_in.reshape(w_in.shape[0], -1), w_down]
        got = front(tokens, grad_out, weights, cos, sine, nz, masks)
        po_all, pm_all = got[-2:]
    else:
        groups, po_all, pm_all = whole_packs(w_qkv, w_out, attn_gain, mlp_gain, w_in, w_down)
        got = front(tokens, grad_out, groups, cos, sine, nz, None)
    mixed, lse, query, gain, tok_own, gout_own, kv, firsts, wqkv = got[:9]
    out_own, gmid, gmixed, delta, po_g, pm_g = middle(tok_own, mixed, gout_own, po_all, pm_all)
    found = back(tok_own, gmid, out_own, query, kv, firsts, wqkv, gain, gmixed, lse, delta, cos, sine, [po_g, pm_g], nz, masks)
    gtok, out, *sums = found
    if not masks:
        return (out, gtok, *whole_sums(*sums, po_g, pm_g))
    out, gtok, g_qkv, g_out, gains, g_in, g_down = finish(out, gtok, *sums)
    g_in = g_in.reshape(g_in.shape[0], 2, SHARE)
    return out, gtok, g_qkv, g_out, gains[0, :SLIVER], gains[1, :SLIVER], g_in, g_down


def solution(mesh):
    both = P(("dp", "seq"), None)
    vector = P(("dp", "seq"))
    w_in, w_down = P("dp", None, "seq"), P("seq", "dp")
    step = functools.partial(on_device, dp=mesh.shape["dp"], nz=mesh.shape["seq"])
    return jax.shard_map(
        step,
        mesh=mesh,
        in_specs=(both, both, both, vector, vector, w_in, w_down, both),
        out_specs=(both, both, both, both, vector, vector, w_in, w_down),
        check_vma=False,
    )
```

```python
import functools
import math

import jax
import jax.numpy as jnp
import numpy as np
from jax import lax
from jax.experimental import pallas as pl
from jax.experimental.pallas import tpu as pltpu
from jax.sharding import PartitionSpec as P

HEADS = 12
HEAD_DIM = 64
NORM_EPS = 1e-05
ROPE_THETA = 160000.0

F32 = jnp.float32
BF = jnp.bfloat16
MESH = pl.DeviceIdType.MESH
NT = (((1,), (1,)), ((), ()))
NN = (((1,), (0,)), ((), ()))
TN = (((0,), (0,)), ((), ()))

WIDTH = 768
PAIRS = HEADS // 2
UNITS = 1152
GROUPS = 8
LINE = 4
BAND = WIDTH // GROUPS
SLIVER = BAND // LINE
SHARE = UNITS // LINE
MAIN = 256
REST = SHARE - MAIN
LINKED = (0, 1, 3, 2)
HALF = WIDTH // 2
CUTS = {640: 256, 512: 256, 896: 384}
LOG2E = math.log2(math.e)
SCALE = HEAD_DIM**-0.5


def dot(a, b, dims):
    return lax.dot_general(a, b, dims, preferred_element_type=F32)


def lanes_of(tile, width=128):
    return pl.ds(pl.multiple_of(tile * width, width), width)


def tiles(start, width):
    return pl.ds(pl.multiple_of(start, width if width < 128 else 128), width)


def lane_iota():
    return lax.broadcasted_iota(jnp.int32, (1, 128), 1)


def swap_halves(u):
    low = lax.rem(lane_iota(), 64) < 32
    return jnp.where(low, pltpu.roll(u, 96, 1), pltpu.roll(u, 32, 1))


def rope(u, cos, sine):
    return u * cos + swap_halves(u) * sine


def rope_back(u, cos, sine):
    return u * cos - swap_halves(u) * sine


def rope_tables(rows):
    position = np.arange(rows, dtype=np.float32)
    half = HEAD_DIM // 2
    freq = (ROPE_THETA ** (-np.arange(half) * 2.0 / HEAD_DIM)).astype(np.float32)
    angle = (position[:, None] * freq[None, :]).astype(np.float64)
    cos, sine = np.cos(angle), np.sin(angle)
    return np.concatenate([cos, cos, -sine, sine], 1).astype(np.float32)


def spread_tables(cos, sine):
    low = lane_iota() < 64

    def chunk(c, _):
        both = cos[c]
        other = pltpu.roll(both, 64, 1)
        cos[c] = jnp.where(low, both, other)
        sine[c] = jnp.where(low, other, both)
        return 0

    lax.fori_loop(0, cos.shape[0], chunk, 0)


def normed(x):
    centred = x - jnp.mean(x, -1, keepdims=True)
    inv = lax.rsqrt(jnp.mean(centred * centred, -1, keepdims=True) + NORM_EPS)
    return centred * inv, inv


def norm_back(dy, gain, hat, inv):
    d = dy * gain
    return inv * (d - jnp.mean(d, -1, keepdims=True) - hat * jnp.mean(d * hat, -1, keepdims=True))


def remote(src, dst, send, recv, device):
    return pltpu.make_async_remote_copy(src, dst, send, recv, device_id=device, device_id_type=MESH)


class Place:
    def __init__(self, nz):
        self.dp, self.z = lax.axis_index("dp"), lax.axis_index("seq")
        self.nz = nz
        upper = self.z // (nz // 2)
        self.moves = lax.rem(self.dp, 2) != upper
        self.stays = lax.rem(self.dp, 2) == upper
        self.shard = jnp.where(self.moves, nz - 1 - self.z, self.z)
        self.opposite = {"dp": self.dp ^ 1, "seq": nz - 1 - self.z}
        self.twin = {"dp": self.dp ^ 1}
        self.beside = {"seq": self.z ^ 1}

    def greet(self, masks):
        bar = pltpu.get_barrier_semaphore()

        def hello(device):
            pl.semaphore_signal(bar, inc=1, device_id=device, device_id_type=MESH)

        for o in range(1, self.nz):
            hello({"seq": lax.rem(self.z + o, self.nz)})
        for m in masks:
            hello({"dp": self.dp ^ m})
        hello(self.opposite)
        pl.semaphore_wait(bar, self.nz + len(masks))


class Gather:
    COPIES = 9

    def __init__(self, src, out, cut, nz, masks, send, recv):
        self.src, self.out, self.cut, self.nz, self.masks = src, out, cut, nz, masks
        self.send, self.recv = send, recv
        self.dp, self.z = lax.axis_index("dp"), lax.axis_index("seq")
        self.started = []
        self.relayed = None

    @staticmethod
    def sems(nz):
        return Gather.COPIES * nz + nz

    def key(self, o, k):
        return o * self.COPIES + k

    def copy(self, src, dst, device, k):
        return remote(src, dst, self.send.at[k], self.recv.at[k], device)

    def begin(self, src, dst, device, k, p=None):
        self.copy(src, dst, device, k).start()
        self.started.append((k, p))

    def arrived(self, ref, k):
        self.copy(ref, ref, {"dp": self.dp ^ self.masks[0]}, k).wait_recv()

    def slot(self, o):
        return self.z ^ LINKED[o]

    def part(self, ref, p):
        if p is None:
            return ref
        width = self.out.shape[-1]
        return ref.at[:, pl.ds(0, self.cut)] if p == 0 else ref.at[:, pl.ds(self.cut, width - self.cut)]

    def along(self, o):
        self.begin(self.src, self.out.at[self.dp, self.z], {"seq": self.z ^ LINKED[o]}, self.COPIES * self.nz + o)

    def relay(self, o):
        ref = self.out.at[self.dp, self.slot(o)]
        self.arrived(ref, self.COPIES * self.nz + o)
        self.relayed = o
        self.begin(ref, ref, {"seq": self.z ^ 1}, self.COPIES * self.nz + 3)

    def forward(self, src, d, s, mask, k, p=None):
        dst = self.out.at[d, s]
        self.begin(self.part(src, p), self.part(dst, p), {"dp": self.dp ^ mask}, k, p)

    def first(self, o):
        my, mx, mc = self.masks
        s = self.slot(o)
        src = self.src
        if o:
            src = self.out.at[self.dp, s]
            if o != self.relayed:
                self.arrived(src, self.COPIES * self.nz + o)
        self.forward(src, self.dp, s, my, self.key(o, 0))
        self.forward(src, self.dp, s, mx, self.key(o, 1))
        self.forward(src, self.dp, s, mc, self.key(o, 2))

    def second(self, o):
        my, mx, mc = self.masks
        s = self.slot(o)
        for m, k, k2, kc, p, m2 in ((my, 0, 3, 4, 0, mx), (mx, 1, 5, 6, 1, my)):
            ref = self.out.at[self.dp ^ m, s]
            self.arrived(ref, self.key(o, k))
            self.forward(ref, self.dp ^ m, s, m2, self.key(o, k2), p)
            self.forward(ref, self.dp ^ m, s, mc, self.key(o, kc))

    def third(self, o):
        my, mx, mc = self.masks
        s = self.slot(o)
        d = self.dp ^ my ^ mx
        for p, k, kc in ((0, 3, 7), (1, 5, 8)):
            ref = self.out.at[d, s]
            self.arrived(self.part(ref, p), self.key(o, k))
            self.forward(ref, d, s, mc, self.key(o, kc), p)

    def finish(self, o):
        my, mx, mc = self.masks
        s = self.slot(o)
        for k, d in ((2, mc), (4, mc ^ my), (6, mc ^ mx)):
            self.arrived(self.out.at[self.dp ^ d, s], self.key(o, k))
        for k, p in ((7, 0), (8, 1)):
            self.arrived(self.part(self.out.at[self.dp ^ mc ^ my ^ mx, s], p), self.key(o, k))

    def done(self):
        for k, p in self.started:
            ref = self.part(self.out.at[self.dp, self.z], p)
            self.copy(ref, ref, {"dp": self.dp ^ self.masks[0]}, k).wait_send()


def pack_group(w, tile, i):
    q, k, v = [w[:, WIDTH * j + HALF * i : WIDTH * j + HALF * i + HALF] for j in range(3)]
    return jnp.concatenate([jnp.concatenate([q, v[:, :256]], 1), jnp.concatenate([k, v[:, 256:], tile], 1)], 0)


def unpack_group(total):
    r = total.shape[0] // 2
    upper, lower = total[:r], total[r:]
    return upper[:, :HALF], lower[:, :HALF], upper[:, HALF:], lower[:, HALF : HALF + 128], lower[:, HALF + 128 :]


def pack_out(w, tile):
    return jnp.concatenate([jnp.concatenate([w[:, :HALF], w[:, HALF:]], 0), jnp.concatenate([tile, jnp.zeros_like(tile)], 0)], 1)


def pack_mlp(gate, up, down):
    parts = (gate, up, down)
    pads = jnp.zeros((gate.shape[0], 128 - 3 * REST), gate.dtype)
    return jnp.concatenate([x[:, :MAIN] for x in parts] + [x[:, MAIN:] for x in parts] + [pads], 1)


def unpack_mlp(total):
    return [
        jnp.concatenate([total[:, MAIN * i : MAIN * i + MAIN], total[:, 3 * MAIN + REST * i : 3 * MAIN + REST * i + REST]], 1)
        for i in range(3)
    ]


def front_kernel(nz, masks, rows, *refs):
    fused = masks is not None
    if fused:
        (tok, gout, w_qkv, w_out, gains, w_in, w_down, cos_in), refs = refs[:8], refs[8:]
    else:
        (tok, gout, g0_all, g1_all, cos_in), refs = refs[:5], refs[5:]
    (mixed, lse, query, gain, tok_own, gout_own, kv, firsts, wqkv), refs = refs[:9], refs[9:]
    if fused:
        (po_all, pm_all), refs = refs[:2], refs[2:]
    (tok_all, kvb, fb, wq, cos, sine, gcol, acc, top, total, tsend, trecv, loc), refs = refs[:13], refs[13:]
    me = Place(nz)
    own = me.shard

    def here(src, dst, k):
        return pltpu.make_async_copy(src, dst, loc.at[k])

    def there(src, dst, device, k):
        return remote(src, dst, tsend.at[k], trecv.at[k], device)

    def rows_to(src, c, device, k, i):
        at = pl.ds(i * (rows // 2), rows // 2)
        src = tok_all.at[c] if src is None else src
        return there(src.at[at], tok_all.at[c, at], device, k + 5 * i)

    @pl.when(me.stays)
    def _():
        here(tok, tok_all.at[own], 0).start()
        here(gout, gout_own, 1).start()

    here(cos_in, cos, 2).start()
    groups, later = [], []
    every, rest = range(nz), (2, 1, 3)
    if fused:
        p0, p1, po, pm, g0_all, g1_all, *sems = refs
        row = lax.broadcasted_iota(jnp.int32, (128, 128), 0)

        def tile_of(i):
            return jnp.where(row == 0, gains[i : i + 1, :], 0.0).T[:SLIVER]

        p0[...] = pack_group(w_qkv[...].astype(F32), tile_of(0), 0).astype(BF)
        g0_all[me.dp, me.z] = p0[...]
    me.greet(masks or (1,))
    if fused:
        shapes = ((p0, g0_all), (p1, g1_all), (po, po_all), (pm, pm_all))
        packs = [
            Gather(src, dst, CUTS[src.shape[-1]], nz, masks, sems[2 * i], sems[2 * i + 1]) for i, (src, dst) in enumerate(shapes)
        ]
        groups, later = packs[:2], packs[2:]
        for o in rest:
            groups[0].along(o)
        groups[0].first(0)

    @pl.when(me.stays)
    def _():
        for i in range(2):
            rows_to(tok, own, me.twin, 1, i).start()
            rows_to(tok, own, me.beside, 2, i).start()

    @pl.when(me.moves)
    def _():
        for i in range(2):
            rows_to(tok, me.z, me.opposite, 0, i).start()

    def swapped(i):
        @pl.when(me.moves)
        def _():
            rows_to(None, own, me.opposite, 0, i).wait_recv()
            rows_to(None, own, me.beside, 2, i).start()
            rows_to(None, own, me.twin, 1, i).start()

    if fused:
        w = w_qkv[...].astype(F32)
        p1[...] = pack_group(w, jnp.zeros((SLIVER, 128), F32), 1).astype(BF)
        g1_all[me.dp, me.z] = p1[...]
        po[...] = pack_out(w_out[...].astype(F32), tile_of(1)).astype(BF)
        w = w_in[...].astype(F32)
        pm[...] = pack_mlp(w[:, :SHARE], w[:, SHARE:], w_down[...].astype(F32).T).astype(BF)
        here(po, po_all.at[me.dp, me.z], 4).start()
        here(pm, pm_all.at[me.dp, me.z], 5).start()
        for o in rest:
            groups[1].along(o)
        groups[1].first(0)
        groups[0].second(0)
        for o in rest:
            groups[0].first(o)
        swapped(0)
        for o in rest:
            groups[0].second(o)
        for o in rest:
            groups[1].first(o)
        for g in later:
            g.along(1)
            g.first(0)

    if not fused:
        swapped(0)
    swapped(1)

    @pl.when(me.stays)
    def _():
        here(tok, tok_all.at[own], 0).wait()

    here(tok_all.at[own], tok_own, 6).start()
    if fused:
        for g in later:
            g.along(2)
        for o in range(nz):
            groups[0].third(o)
        for o in range(nz):
            groups[0].finish(o)

    @pl.when(me.moves)
    def _():
        there(gout, gout_own, me.opposite, 4).start()

    here(cos_in, cos, 2).wait()
    spread_tables(cos, sine)

    def build(i, whole):
        def band_of(g, _):
            slabs = [unpack_group(whole[g, s].astype(F32)) for s in range(LINE)]
            band = pl.ds(pl.multiple_of(g * BAND, BAND), BAND)
            q, k, v0, v1, t = [jnp.concatenate([x[j] for x in slabs], 0) for j in range(5)]
            at = WIDTH * i
            wq[band, at : at + HALF] = k.astype(BF)
            wq[band, at + HALF : at + HALF + 256] = v0.astype(BF)
            wq[band, at + HALF + 256 : at + WIDTH] = v1.astype(BF)
            wq[band, 2 * WIDTH + HALF * i : 2 * WIDTH + HALF * i + HALF] = q.astype(BF)
            if i == 0:
                gcol[band, :] = t
            return 0

        lax.fori_loop(0, GROUPS, band_of, 0)

    def norm_chunk(c):
        def block(i, _):
            at = pl.ds(pl.multiple_of(i * 64, 64), 64)
            hat, _ = normed(tok_all[c, at, :].astype(F32))
            fb[c, at, :] = (hat * gain[0:1, :]).astype(BF)
            return 0

        lax.fori_loop(0, rows // 64, block, 0)
        here(fb.at[c], firsts.at[c], 8 + c).start()

    def queries(i):
        u = dot(fb[own], wq[:, 2 * WIDTH + HALF * i : 2 * WIDTH + HALF * i + HALF], NN)
        for j in range(3):
            tile = rope(u[:, 128 * j : 128 * j + 128], cos[own], sine[own])
            query[:, HALF * i + 128 * j : HALF * i + 128 * j + 128] = (tile * (SCALE * LOG2E)).astype(BF)

    def visits(steps):
        def visit(n, _):
            t, grp = lax.rem(n, nz), n // nz
            stay = jnp.where(t == 1, 1, jnp.where(t == 2, 3, 2))
            move = jnp.where(t == 1, 3, jnp.where(t == 2, 2, 1))
            turn = jnp.where(me.stays, stay, move)
            c = jnp.where(t == 0, own, own ^ turn)
            @pl.when((n > 0) & (n < nz))
            def _():
                for i in range(2):
                    rows_to(None, c, me.twin, jnp.where(turn == 1, 2, jnp.where(turn == 3, 1, 3)), i).wait_recv()

                    @pl.when(turn == 1)
                    def _(i=i):
                        rows_to(None, c, me.twin, 3, i).start()

                norm_chunk(c)

            for j in range(3):
                u = dot(fb[c], wq[:, tiles(WIDTH * grp + 256 * j, 256)], NN)
                for i in range(2):
                    tile = 2 * j + i
                    x = u[:, 128 * i : 128 * i + 128]
                    x = rope(x, cos[c], sine[c]) if tile < 3 else x
                    kvb[grp, c, :, 128 * tile : 128 * tile + 128] = x.astype(BF)
            here(kvb.at[grp, c], kv.at[grp, c], 8 + nz * (1 + grp) + c).start()
            jobs = [(i, h) for i in range(3) for h in range(2)]

            def score(i, h):
                q = query[:, tiles(HALF * grp + 128 * i, 128)]
                mask = (lane_iota() < 64) if h == 0 else (lane_iota() >= 64)
                return dot(kvb[grp, c, :, 128 * i : 128 * i + 128], jnp.where(mask, q, jnp.zeros_like(q)), NT)

            ready = [score(*j) for j in jobs[:2]]
            for m, (i, h) in enumerate(jobs):
                if h == 0:
                    vt = kvb[grp, c, :, HALF + 128 * i : HALF + 128 * i + 128].T
                s = ready[m]
                if m + 2 < len(jobs):
                    ready.append(score(*jobs[m + 2]))
                head = pl.ds(6 * grp + m, 1)
                band = tiles(64 * (6 * grp + m), 64)
                old = top[head, :]
                new = jnp.maximum(old, jnp.max(s, 0, keepdims=True))
                p = jnp.exp2(s - new)
                fade = jnp.exp2(old - new)
                top[head, :] = new
                lhs = jnp.concatenate([vt[h * 64 : h * 64 + 64], jnp.ones((16, rows), BF)], 0)
                oo = dot(lhs, p.astype(BF), NN)
                total[head, :] = total[head, :] * fade + oo[64:65]
                acc[band, :] = acc[band, :] * fade + oo[:64]
            for k, step in steps.items():

                @pl.when(n == k)
                def _(k=k, step=step):
                    for which, name, order in step:
                        for g in which:
                            for o in order:
                                getattr(g, name)(o)
                    if k == nz - 1:
                        build(1, g1_all)
                        here(wq, wqkv, 7).start()
                        queries(1)

            return 0

        lax.fori_loop(0, 2 * nz, visit, 0)

    build(0, g0_all)
    gain[...] = gcol[...].T[:8]
    norm_chunk(own)
    queries(0)
    acc[...] = jnp.zeros_like(acc)
    total[...] = jnp.zeros_like(total)
    top[...] = jnp.full_like(top, -1e30)
    one = groups[1:]
    visits({
        0: [(one, "second", every), (later, "first", (1,))],
        1: [(one, "third", every)],
        2: [(later, "relay", (2,)), (later, "first", (2,))],
        3: [(one, "finish", every), (later, "second", (0, 1))],
        4: [(later, "first", (3,))],
        5: [(later, "second", (2,))],
        6: [(later, "second", (3,))],
        7: [(later, "third", every)],
    })

    for hp in range(PAIRS):
        parts = [
            acc[128 * hp + 64 * h : 128 * hp + 64 * h + 64, :] / total[2 * hp + h : 2 * hp + h + 1, :] for h in range(2)
        ]
        mixed[:, 128 * hp : 128 * hp + 128] = jnp.concatenate(parts, 0).T.astype(BF)
    lse[...] = top[...] + jnp.log(jnp.maximum(total[...], 1e-30)) * LOG2E

    if fused:
        for g in later:
            for o in range(nz):
                g.finish(o)
        for g in packs:
            g.done()
        here(po, po_all.at[me.dp, me.z], 4).wait()
        here(pm, pm_all.at[me.dp, me.z], 5).wait()
    for i in range(2):
        for k in (1, 2, 3):
            rows_to(None, own, me.twin, k, i).wait_send()

    @pl.when(me.moves)
    def _():
        for i in range(2):
            rows_to(None, own, me.opposite, 0, i).wait_send()
        there(gout, gout_own, me.opposite, 4).wait()

    @pl.when(me.stays)
    def _():
        here(gout, gout_own, 1).wait()

    here(tok_all.at[own], tok_own, 6).wait()
    here(wq, wqkv, 7).wait()
    for c in range(nz):
        here(fb.at[c], firsts.at[c], 8 + c).wait()
        for grp in range(2):
            here(kvb.at[grp, c], kv.at[grp, c], 8 + nz * (1 + grp) + c).wait()


def front(tok, gout, weights, tables, nz, masks):
    rows = tok.shape[0]
    vmem, anyspace = pl.BlockSpec(memory_space=pltpu.VMEM), pl.BlockSpec(memory_space=pl.ANY)
    shape, vm = jax.ShapeDtypeStruct, pltpu.VMEM
    outs = [shape((rows, WIDTH), BF), shape((16, rows), F32), shape((rows, WIDTH), BF), shape((8, WIDTH), F32)]
    outs += [shape((rows, WIDTH), BF)] * 2
    outs += [shape((2, nz, rows, WIDTH), BF), shape((nz, rows, WIDTH), BF), shape((WIDTH, 3 * WIDTH), BF)]
    out_specs = [vmem] * 4 + [anyspace, vmem] + [anyspace] * 3
    scratch = [
        vm((nz, rows, WIDTH), BF),
        vm((2, nz, rows, WIDTH), BF),
        vm((nz, rows, WIDTH), BF),
        vm((WIDTH, 3 * WIDTH), BF),
        vm((nz, rows, 128), F32),
        vm((nz, rows, 128), F32),
        vm((WIDTH, 128), F32),
        vm((WIDTH, rows), F32),
        vm((16, rows), F32),
        vm((16, rows), F32),
        pltpu.SemaphoreType.DMA((9,)),
        pltpu.SemaphoreType.DMA((9,)),
        pltpu.SemaphoreType.DMA((8 + 3 * nz,)),
    ]
    if masks:
        grp, out, mlp = (2 * SLIVER, 640), (2 * SLIVER, 512), (BAND, 896)
        outs += [shape((GROUPS, nz) + out, BF), shape((GROUPS, nz) + mlp, BF)]
        out_specs += [anyspace] * 2
        scratch += [vm(x, BF) for x in (grp, grp, out, mlp)] + [vm((GROUPS, nz) + grp, BF)] * 2
        scratch += [pltpu.SemaphoreType.DMA((Gather.sems(nz),)) for _ in range(8)]
    return pl.pallas_call(
        functools.partial(front_kernel, nz, masks, rows),
        out_shape=outs,
        in_specs=[anyspace] * 2 + [vmem] * len(weights) + [anyspace],
        out_specs=out_specs,
        scratch_shapes=scratch,
        compiler_params=pltpu.CompilerParams(collective_id=0, has_side_effects=True, vmem_limit_bytes=60 << 20),
        cost_estimate=pl.CostEstimate(flops=14_000_000_000, bytes_accessed=40_000_000, transcendentals=13_000_000),
        name="front",
    )(tok, gout, *weights, tables)


def middle_kernel(rows, tok, mixed, gout, po_all, pm_all, out, gmid, gmixed, delta, po_g, pm_g,
                  wout, wg, wu, wd, gcol, gain, resid, hat, inv, second, hidden, ggate, gup, gsec, gattn, dwout):
    lane = lane_iota()

    def build(g, _):
        band = pl.ds(pl.multiple_of(g * BAND, BAND), BAND)
        slabs = [po_all[g, s].astype(F32) for s in range(LINE)]
        wout[band, :384] = jnp.concatenate([x[:SLIVER, :384] for x in slabs], 0).astype(BF)
        wout[band, 384:] = jnp.concatenate([x[SLIVER:, :384] for x in slabs], 0).astype(BF)
        gcol[band, :] = jnp.concatenate([x[:SLIVER, 384:] for x in slabs], 0)
        for i, w in enumerate((wg, wu, wd)):
            tail = jnp.zeros((BAND, 128), F32)
            for s in range(LINE):
                w[band, MAIN * s : MAIN * s + MAIN] = pm_all[g, s, :, MAIN * i : MAIN * i + MAIN]
                rest = pm_all[g, s, :, 3 * MAIN :].astype(F32)
                turn = (REST * (s - i)) % 128
                rest = pltpu.roll(rest, turn, 1) if turn else rest
                tail = jnp.where((lane >= REST * s) & (lane < REST * (s + 1)), rest, tail)
            w[band, MAIN * LINE :] = tail.astype(BF)
        return 0

    lax.fori_loop(0, GROUPS, build, 0)
    gain[...] = gcol[...].T[:8]

    for j in range(3):
        at = slice(256 * j, 256 * j + 256)
        resid[:, at] = tok[:, at].astype(F32) + dot(mixed[...], wout[:, at], NN)

    def norm_block(i, _):
        at = pl.ds(pl.multiple_of(i * 64, 64), 64)
        h, r = normed(resid[at, :])
        hat[at, :] = h
        inv[at, :] = jnp.broadcast_to(r, (64, 128))
        second[at, :] = (h * gain[0:1, :]).astype(BF)
        return 0

    lax.fori_loop(0, rows // 64, norm_block, 0)

    def units(start, width):
        at = pl.ds(start, width)
        gate, up, gh = dot(second[...], wg[:, at], NN), dot(second[...], wu[:, at], NN), dot(gout[...], wd[:, at], NN)
        cdf = 0.5 + 0.5 * lax.erf(gate * math.sqrt(0.5))
        pdf = jnp.exp2(gate * gate * (-0.5 * LOG2E)) * (1.0 / math.sqrt(2.0 * math.pi))
        act = gate * cdf
        hidden[:, at] = (act * up).astype(BF)
        gup[:, at] = (gh * act).astype(BF)
        ggate[:, at] = (gh * up * (cdf + gate * pdf)).astype(BF)

    for start in range(0, UNITS, 256):
        units(start, min(256, UNITS - start))

    for j in range(3):
        at = slice(256 * j, 256 * j + 256)
        out[:, at] = (resid[:, at] + dot(hidden[...], wd[at, :], NT)).astype(BF)
        gsec[:, at] = dot(ggate[...], wg[at, :], NT) + dot(gup[...], wu[at, :], NT)

    def back_block(i, dgain):
        at = pl.ds(pl.multiple_of(i * 64, 64), 64)
        dy, h = gsec[at, :], hat[at, :]
        gm = gout[at, :].astype(F32) + norm_back(dy, gain[0:1, :], h, inv[at, 0:1])
        gmid[at, :] = gm
        gattn[at, :] = gm.astype(BF)
        return dgain + jnp.sum(dy * h, 0, keepdims=True)

    dgain = lax.fori_loop(0, rows // 64, back_block, jnp.zeros((1, WIDTH), F32))

    heads = lax.broadcasted_iota(jnp.int32, (16, 256), 0)
    for j in range(3):
        at = slice(256 * j, 256 * j + 256)
        gmx = dot(gattn[...], wout[at, :], NT).astype(BF)
        gmixed[:, at] = gmx
        prod = gmx.astype(F32) * mixed[:, at].astype(F32)
        high = prod.astype(BF)
        low = (prod - high.astype(F32)).astype(BF)
        pick = ((lax.broadcasted_iota(jnp.int32, (16, 256), 1) + 256 * j) // HEAD_DIM == heads).astype(BF)
        part = dot(pick, high, NT) + dot(pick, low, NT)
        delta[...] = part if j == 0 else delta[...] + part

    for j in range(2):
        at = slice(384 * j, 384 * j + 384)
        dwout[at, :] = dot(mixed[:, at], gattn[...], TN)
    row = lax.broadcasted_iota(jnp.int32, (128, WIDTH), 0)
    gcol[...] = jnp.where(row == 0, dgain, 0.0).T

    def pack_out(g, _):
        for s in range(LINE):
            at = pl.ds(pl.multiple_of(g * BAND + s * SLIVER, 8), SLIVER)
            x, c = dwout[at, :], gcol[at, :]
            po_g[g, s, :, :384] = jnp.concatenate([x[:, :384], x[:, 384:]], 0).astype(BF)
            po_g[g, s, :, 384:] = jnp.concatenate([c, jnp.zeros_like(c)], 0).astype(BF)
        return 0

    lax.fori_loop(0, GROUPS, pack_out, 0)

    for j in range(2):
        at = slice(384 * j, 384 * j + 384)
        tails = []
        for i, (a, b) in enumerate(((second, ggate), (second, gup), (gout, hidden))):
            for s in range(LINE):
                x = dot(a[:, at], b[:, MAIN * s : MAIN * s + MAIN], TN).astype(BF)
                for g in range(4):
                    pm_g[4 * j + g, s, :, MAIN * i : MAIN * i + MAIN] = x[BAND * g : BAND * g + BAND]
            tails.append(dot(a[:, at], b[:, MAIN * LINE :], TN))
        for s in range(LINE):
            y = jnp.zeros((384, 128), F32)
            for i, tail in enumerate(tails):
                turn = (REST * (i - s)) % 128
                tail = pltpu.roll(tail, turn, 1) if turn else tail
                y = jnp.where((lane >= REST * i) & (lane < REST * (i + 1)), tail, y)
            y = y.astype(BF)
            for g in range(4):
                pm_g[4 * j + g, s, :, 3 * MAIN :] = y[BAND * g : BAND * g + BAND]


def middle(tok, mixed, gout, po_all, pm_all):
    rows = tok.shape[0]
    shape, vm = jax.ShapeDtypeStruct, pltpu.VMEM
    vmem = pl.BlockSpec(memory_space=pltpu.VMEM)
    return pl.pallas_call(
        functools.partial(middle_kernel, rows),
        out_shape=[
            shape((rows, WIDTH), BF),
            shape((rows, WIDTH), F32),
            shape((rows, WIDTH), BF),
            shape((16, rows), F32),
            shape(po_all.shape, BF),
            shape(pm_all.shape, BF),
        ],
        in_specs=[vmem] * 5,
        out_specs=[vmem] * 6,
        scratch_shapes=[
            vm((WIDTH, WIDTH), BF),
            vm((WIDTH, UNITS), BF),
            vm((WIDTH, UNITS), BF),
            vm((WIDTH, UNITS), BF),
            vm((WIDTH, 128), F32),
            vm((8, WIDTH), F32),
            vm((rows, WIDTH), F32),
            vm((rows, WIDTH), F32),
            vm((rows, 128), F32),
            vm((rows, WIDTH), BF),
            vm((rows, UNITS), BF),
            vm((rows, UNITS), BF),
            vm((rows, UNITS), BF),
            vm((rows, WIDTH), F32),
            vm((rows, WIDTH), BF),
            vm((WIDTH, WIDTH), F32),
        ],
        compiler_params=pltpu.CompilerParams(vmem_limit_bytes=58 << 20),
        cost_estimate=pl.CostEstimate(flops=11_000_000_000, bytes_accessed=25_000_000, transcendentals=1_200_000),
        name="middle",
    )(tok, mixed, gout, po_all, pm_all)


class Reduce:
    COPIES = 10

    def __init__(self, src, total, cut, nz, masks, bufs, send, recv, loc=None):
        self.src, self.total, self.cut, self.nz, self.masks = src, total, cut, nz, masks
        self.near, self.side0, self.side1, self.far, *mine = bufs
        self.mine = mine[0] if mine else None
        self.send, self.recv, self.loc = send, recv, loc
        self.dp, self.z = lax.axis_index("dp"), lax.axis_index("seq")
        my, mx, mc = masks
        self.turns = (0, my, mx, my ^ mx)
        self.started = []

    @staticmethod
    def scratch(shape, nz, held):
        r, c = shape
        cut = CUTS[c]
        bufs = [
            pltpu.VMEM((4, nz, r, c), BF),
            pltpu.VMEM((3, nz, r, cut), BF),
            pltpu.VMEM((3, nz, r, c - cut), BF),
            pltpu.VMEM((nz - 1, r, c), BF),
        ]
        sems = [pltpu.SemaphoreType.DMA((Reduce.COPIES * nz + nz,))] * 2
        if not held:
            bufs += [pltpu.VMEM((4, nz, r, c), BF)]
            sems += [pltpu.SemaphoreType.DMA((4 * nz,))]
        return bufs, sems

    def begin(self, src, dst, device, k):
        remote(src, dst, self.send.at[k], self.recv.at[k], device).start()
        self.started.append((k, src.shape[-1]))

    def arrived(self, ref, k):
        remote(ref, ref, self.send.at[k], self.recv.at[k], {"dp": self.dp ^ self.masks[2]}).wait_recv()

    def seat(self, o):
        return self.z ^ LINKED[o]

    def held(self, i, s):
        return self.mine.at[i, s] if self.mine is not None else self.src.at[self.dp ^ self.turns[i], s]

    def local(self, i, o):
        s = self.seat(o)
        return pltpu.make_async_copy(self.src.at[self.dp ^ self.turns[i], s], self.mine.at[i, s], self.loc.at[4 * o + i])

    def zero(self, o):
        s, mc = self.seat(o), self.masks[2]
        for i in (3, 1, 2, 0):
            if self.mine is not None:
                self.local(i, o).start()
            self.begin(self.src.at[self.dp ^ mc ^ self.turns[i], s], self.near.at[i, s], {"dp": self.dp ^ mc}, self.COPIES * o + i)

    def add(self, ref, other):
        ref[...] = (ref[...].astype(F32) + other[...].astype(F32)).astype(BF)

    def p0(self, i, s):
        return self.held(i, s).at[:, pl.ds(0, self.cut)]

    def p1(self, i, s):
        return self.held(i, s).at[:, pl.ds(self.cut, self.src.shape[-1] - self.cut)]

    def one(self, o):
        my, mx, _ = self.masks
        s, k = self.seat(o), self.COPIES * o
        for i in (3, 1, 2, 0):
            if self.mine is not None:
                self.local(i, o).wait()
            self.arrived(self.near.at[i, s], k + i)
            self.add(self.held(i, s), self.near.at[i, s])
            if i == 3:
                self.begin(self.p0(3, s), self.side0.at[1, s], {"dp": self.dp ^ my}, k + 4)
                self.begin(self.p1(3, s), self.side1.at[1, s], {"dp": self.dp ^ mx}, k + 5)
            if i == 1:
                self.begin(self.p0(1, s), self.side0.at[0, s], {"dp": self.dp ^ my}, k + 6)
            if i == 2:
                self.begin(self.p1(2, s), self.side1.at[0, s], {"dp": self.dp ^ mx}, k + 7)

    def two(self, o):
        my, mx, _ = self.masks
        s, k = self.seat(o), self.COPIES * o
        self.arrived(self.side0.at[1, s], k + 4)
        self.add(self.p0(2, s), self.side0.at[1, s])
        self.begin(self.p0(2, s), self.side0.at[2, s], {"dp": self.dp ^ mx}, k + 8)
        self.arrived(self.side1.at[1, s], k + 5)
        self.add(self.p1(1, s), self.side1.at[1, s])
        self.begin(self.p1(1, s), self.side1.at[2, s], {"dp": self.dp ^ my}, k + 9)

    def three(self, o):
        s, k = self.seat(o), self.COPIES * o
        for ref, side, k1, k2 in ((self.p0(0, s), self.side0, k + 6, k + 8), (self.p1(0, s), self.side1, k + 7, k + 9)):
            self.arrived(side.at[0, s], k1)
            self.arrived(side.at[2, s], k2)
            ref[...] = (ref[...].astype(F32) + side[0, s].astype(F32) + side[2, s].astype(F32)).astype(BF)
        if o:
            self.begin(self.held(0, s), self.far.at[o - 1], {"seq": s}, self.COPIES * self.nz + o)

    def four(self):
        out = self.held(0, self.z)[...].astype(F32)
        for o in range(1, self.nz):
            self.arrived(self.far.at[o - 1], self.COPIES * self.nz + o)
            out = out + self.far[o - 1].astype(F32)
        self.total[...] = out

    def done(self):
        for k, width in self.started:
            whole = width == self.src.shape[-1]
            ref = self.near.at[0, 0] if whole else (self.side0 if k % self.COPIES in (4, 6, 8) else self.side1).at[0, 0]
            remote(ref, ref, self.send.at[k], self.recv.at[k], {"dp": self.dp ^ self.masks[2]}).wait_send()


def back_kernel(nz, masks, rows, *refs):
    fused = masks is not None
    (tok, gmid, out_own, query, kv, firsts, wqkv, gain, gmixed, lse, delta, cos_in), refs = refs[:12], refs[12:]
    if fused:
        (po_g, pm_g, gtok, out, s0, s1, so, sm), refs = refs[:8], refs[8:]
    else:
        (gtok, out, p0_g, p1_g), refs = refs[:4], refs[4:]
    (kvb, fb, ft, wq, cos, sine, dq, dqb, dkv, dx, dw, sent, landed, gown, gcol, send, recv, loc), refs = refs[:18], refs[18:]
    me = Place(nz)
    own = me.shard

    def here(src, dst, k):
        return pltpu.make_async_copy(src, dst, loc.at[k])

    def there(src, dst, device, k):
        return remote(src, dst, send.at[k], recv.at[k], device)

    def chunk(t):
        return jnp.where(t == 0, own ^ 2, jnp.where(t == 1, own ^ 1, jnp.where(t == 2, own ^ 3, own)))

    def fetch(n):
        return here(kv.at[n // nz, chunk(lax.rem(n, nz))], kvb.at[lax.rem(n, 2)], lax.rem(n, 2))

    def fetch_first(t):
        return here(firsts.at[chunk(t)], fb.at[lax.rem(t, 2)], 2 + lax.rem(t, 2))

    fetch(0).start()
    fetch_first(0).start()
    whole = [here(wqkv, wq, 4), here(cos_in, cos, 5)]
    for c in whole:
        c.start()
    me.greet(masks or (1,))
    jobs, sums = [], []
    if fused:
        (p0_g, p1_g), refs = refs[:2], refs[2:]
        for src, total in ((p0_g, s0), (p1_g, s1)):
            sums.append(Reduce(src, total, CUTS[src.shape[-1]], nz, masks, refs[:4], *refs[4:6]))
            refs = refs[6:]
        for src, total in ((po_g, so), (pm_g, sm)):
            jobs.append(Reduce(src, total, CUTS[src.shape[-1]], nz, masks, refs[:5], *refs[5:8]))
            refs = refs[8:]
    order = (3, 2, 1, 0)

    def advance(which, step):
        for j in which:
            for o in order:
                getattr(j, step)(o)

    def wave(which):
        for i in range(nz + 2):
            for k, step in enumerate(("one", "two", "three")):
                if 0 <= i - k < nz:
                    for j in which:
                        getattr(j, step)(order[i - k])

    advance(jobs, "zero")

    @pl.when(me.moves)
    def _():
        there(out_own, out, me.opposite, 3).start()

    @pl.when(me.stays)
    def _():
        here(out_own, out, 7).start()

    dq[...] = jnp.zeros_like(dq)
    for c in whole:
        c.wait()
    spread_tables(cos, sine)

    def visits(steps):
        def visit(n, _):
            t, grp = lax.rem(n, nz), n // nz
            c, slot = chunk(t), lax.rem(t, 2)
            fetch(n).wait()

            @pl.when(n < nz)
            def _():
                fetch_first(t).wait()

            @pl.when(n + 1 < 2 * nz)
            def _():
                fetch(n + 1).start()

            @pl.when(n + 1 < nz)
            def _():
                fetch_first(n + 1).start()

            band = pl.ds(pl.multiple_of(t * rows, rows), rows)
            todo = [(i, h) for i in range(3) for h in range(2)]

            def pick(ref, i, h):
                x = ref[:, tiles(HALF * grp + 128 * i, 128)]
                mask = (lane_iota() < 64) if h == 0 else (lane_iota() >= 64)
                return jnp.where(mask, x, jnp.zeros_like(x))

            def score(i, h):
                qh, gh = pick(query, i, h), pick(gmixed, i, h)
                k, v = kvb[slot, :, 128 * i : 128 * i + 128], kvb[slot, :, HALF + 128 * i : HALF + 128 * i + 128]
                return dot(k, qh, NT), dot(v, gh, NT), qh, gh

            ready = [score(*todo[0])]
            dk = dv = None
            for m, (i, h) in enumerate(todo):
                s, dp, qh, gh = ready[m]
                if m + 1 < len(todo):
                    ready.append(score(*todo[m + 1]))
                if h == 0:
                    kt = kvb[slot, :, 128 * i : 128 * i + 128].T
                head = pl.ds(6 * grp + m, 1)
                rows_of = tiles(64 * (6 * grp + m), 64)
                p = jnp.exp2(s - lse[head, :])
                ds = (p * (dp - delta[head, :])).astype(BF)
                a = dot(p.astype(BF), gh, NN)
                dv = a if h == 0 else dv + a
                a = dot(ds, qh, NN)
                dk = a if h == 0 else dk + a
                dq[rows_of, :] += dot(kt[h * 64 : h * 64 + 64], ds, NN)
                if h == 1:
                    at = WIDTH * grp + 128 * i
                    dkv[band, tiles(at, 128)] = rope_back(dk * (1.0 / LOG2E), cos[c], sine[c]).astype(BF)
                    dkv[band, tiles(at + HALF, 128)] = dv.astype(BF)

            @pl.when(n < nz)
            def _():
                for j in range(6):
                    ft[128 * j : 128 * j + 128, band] = fb[slot, :, 128 * j : 128 * j + 128].T
            @pl.when(n >= nz)
            def _():
                for j in range(3):
                    at = slice(256 * j, 256 * j + 256)
                    dx[:, at] = dot(dkv[band, :], wq[at, : 2 * WIDTH], NT)

                @pl.when(lax.rem(t, 2) == 0)
                def _():
                    sent[t] = dx[...].astype(BF)
                    there(sent.at[t], landed.at[t], me.twin, t).start()

                @pl.when(t == 1)
                def _():
                    there(sent.at[0], landed.at[0], me.twin, 0).wait_recv()
                    sent[1] = (dx[...] + landed[0].astype(F32)).astype(BF)
                    there(sent.at[1], landed.at[1], me.beside, 1).start()

            for k, step in steps.items():

                @pl.when(n == k)
                def _(k=k, step=step):
                    if k == nz - 1:
                        close(0)
                        weigh(0)
                        pack(0, p0_g)
                    for which, name in step:
                        advance(which, name)

            return 0

        lax.fori_loop(0, 2 * nz, visit, 0)

    def close(grp):
        for i in range(3 * grp, 3 * grp + 3):
            at = slice(128 * i, 128 * i + 128)
            dqb[:, at] = rope_back(dq[at, :].T * SCALE, cos[own], sine[own]).astype(BF)

    def weigh(grp):
        for r in (slice(0, HALF), slice(HALF, WIDTH)):
            for j in range(3):
                at = WIDTH * grp + 256 * j
                dw[r, HALF + 256 * j : HALF + 256 * j + 256] = dot(ft[r, :], dkv[:, at : at + 256], NN)
            dw[r, :HALF] = dot(ft[r, (nz - 1) * rows :], dqb[:, HALF * grp : HALF * grp + HALF], NN)

    def pack(grp, dst):
        def band_of(g, _):
            for s in range(LINE):
                at = pl.ds(pl.multiple_of(g * BAND + s * SLIVER, 8), SLIVER)
                q, k, v0, v1 = dw[at, :HALF], dw[at, HALF:WIDTH], dw[at, WIDTH : WIDTH + 256], dw[at, WIDTH + 256 :]
                tile = gcol[at, :] if grp else jnp.zeros((SLIVER, 128), F32)
                dst[g, s] = jnp.concatenate(
                    [jnp.concatenate([q, v0], 1), jnp.concatenate([k, v1, tile], 1)], 0
                ).astype(BF)
            return 0

        lax.fori_loop(0, GROUPS, band_of, 0)

    early = sums[:1]
    visits({
        0: [(jobs, "one")],
        3: [(early, "zero")],
        4: [(jobs, "two"), (early, "one")],
        6: [(jobs, "three")],
        7: [(early, "two"), (early, "three")],
    })
    close(1)
    for j in range(3):
        at = slice(256 * j, 256 * j + 256)
        dx[:, at] += dot(dqb[...], wq[at, 2 * WIDTH :], NT)
    there(sent.at[1], landed.at[1], me.beside, 1).wait_recv()
    there(sent.at[2], landed.at[2], me.twin, 2).wait_recv()

    def norm_block(i, dgain):
        at = pl.ds(pl.multiple_of(i * 64, 64), 64)
        dy = dx[at, :] + landed[1, at, :].astype(F32) + landed[2, at, :].astype(F32)
        h, r = normed(tok[at, :].astype(F32))
        gown[at, :] = (gmid[at, :] + norm_back(dy, gain[0:1, :], h, r)).astype(BF)
        return dgain + jnp.sum(dy * h, 0, keepdims=True)

    dgain = lax.fori_loop(0, rows // 64, norm_block, jnp.zeros((1, WIDTH), F32))

    @pl.when(me.moves)
    def _():
        there(gown, gtok, me.opposite, 4).start()

    @pl.when(me.stays)
    def _():
        here(gown, gtok, 8).start()

    row = lax.broadcasted_iota(jnp.int32, (128, WIDTH), 0)
    gcol[...] = jnp.where(row == 0, dgain, 0.0).T
    weigh(1)
    pack(1, p1_g)
    if fused:
        advance(sums[1:], "zero")
        wave(sums[1:])
        for j in jobs + sums:
            j.four()
        for j in jobs + sums:
            j.done()
    for k, device in ((0, me.twin), (1, me.beside), (2, me.twin)):
        there(sent.at[k], landed.at[k], device, k).wait_send()

    @pl.when(me.moves)
    def _():
        there(out_own, out, me.opposite, 3).wait()
        there(gown, gtok, me.opposite, 4).wait()

    @pl.when(me.stays)
    def _():
        here(out_own, out, 7).wait()
        here(gown, gtok, 8).wait()


def back(tok, gmid, out_own, query, kv, firsts, wqkv, gain, gmixed, lse, delta, tables, packs, nz, masks):
    rows = tok.shape[0]
    shape, vm = jax.ShapeDtypeStruct, pltpu.VMEM
    vmem, anyspace = pl.BlockSpec(memory_space=pltpu.VMEM), pl.BlockSpec(memory_space=pl.ANY)
    in_specs = [vmem] * 4 + [anyspace] * 3 + [vmem] * 4 + [anyspace]
    slab = (2 * SLIVER, 640)
    outs, out_specs = [shape((rows, WIDTH), BF)] * 2, [vmem] * 2
    scratch = [
        vm((2, rows, WIDTH), BF),
        vm((2, rows, WIDTH), BF),
        vm((WIDTH, nz * rows), BF),
        vm((WIDTH, 3 * WIDTH), BF),
        vm((nz, rows, 128), F32),
        vm((nz, rows, 128), F32),
        vm((WIDTH, rows), F32),
        vm((rows, WIDTH), BF),
        vm((nz * rows, 2 * WIDTH), BF),
        vm((rows, WIDTH), F32),
        vm((WIDTH, 3 * HALF), F32),
        vm((3, rows, WIDTH), BF),
        vm((3, rows, WIDTH), BF),
        vm((rows, WIDTH), BF),
        vm((WIDTH, 128), F32),
        pltpu.SemaphoreType.DMA((5,)),
        pltpu.SemaphoreType.DMA((5,)),
        pltpu.SemaphoreType.DMA((9,)),
    ]
    if masks:
        in_specs += [anyspace] * 2
        outs += [shape(s, F32) for s in (slab, slab, packs[0].shape[-2:], packs[1].shape[-2:])]
        out_specs += [vmem] * 4
        scratch += [vm((GROUPS, LINE) + slab, BF)] * 2
        for s, held in ((slab, True), (slab, True), (packs[0].shape[-2:], False), (packs[1].shape[-2:], False)):
            bufs, sems = Reduce.scratch(s, nz, held)
            scratch += bufs + sems
    else:
        outs += [shape((GROUPS, LINE) + slab, BF)] * 2
        out_specs += [vmem] * 2
        packs = []
    return pl.pallas_call(
        functools.partial(back_kernel, nz, masks, rows),
        out_shape=outs,
        in_specs=in_specs,
        out_specs=out_specs,
        scratch_shapes=scratch,
        compiler_params=pltpu.CompilerParams(collective_id=1, has_side_effects=True, vmem_limit_bytes=62 << 20),
        cost_estimate=pl.CostEstimate(flops=24_000_000_000, bytes_accessed=40_000_000, transcendentals=13_000_000),
        name="back",
    )(tok, gmid, out_own, query, kv, firsts, wqkv, gain, gmixed, lse, delta, tables, *packs)


def finish_kernel(out, gtok, s0, s1, so, sm, out_o, gtok_o, qkv_o, w_out_o, gains_o, gate_o, down_o):
    out_o[...] = out[...]
    gtok_o[...] = gtok[...]
    for i, total in enumerate((s0, s1)):
        q, k, v0, v1, tile = unpack_group(total[...])
        for j, x in enumerate((q, k)):
            qkv_o[:, WIDTH * j + HALF * i : WIDTH * j + HALF * i + HALF] = x
        at = 2 * WIDTH + HALF * i
        qkv_o[:, at : at + 256] = v0
        qkv_o[:, at + 256 : at + HALF] = v1
    w_out_o[:, :HALF] = so[:SLIVER, :HALF]
    w_out_o[:, HALF:] = so[SLIVER:, :HALF]
    zeros = jnp.zeros((128 - SLIVER, 128), F32)
    for i, col in enumerate((tile, so[:SLIVER, HALF:])):
        gains_o[i : i + 1, :] = jnp.concatenate([col, zeros], 0).T[:1]
    gate, up, down = unpack_mlp(sm[...])
    gate_o[:, :SHARE] = gate
    gate_o[:, SHARE:] = up
    down_o[...] = down.T


def finish(out, gtok, s0, s1, so, sm):
    shape = jax.ShapeDtypeStruct
    vmem = pl.BlockSpec(memory_space=pltpu.VMEM)
    return pl.pallas_call(
        finish_kernel,
        out_shape=[
            shape(out.shape, BF),
            shape(gtok.shape, BF),
            shape((SLIVER, 3 * WIDTH), F32),
            shape((SLIVER, WIDTH), F32),
            shape((8, 128), F32),
            shape((BAND, 2 * SHARE), F32),
            shape((SHARE, BAND), F32),
        ],
        in_specs=[vmem] * 6,
        out_specs=[vmem] * 7,
        compiler_params=pltpu.CompilerParams(vmem_limit_bytes=40 << 20),
        name="finish",
    )(out, gtok, s0, s1, so, sm)


def whole_packs(w_qkv, w_out, attn_gain, mlp_gain, w_in, w_down):
    both = ("dp", "seq")

    def shards_of(w):
        w = lax.all_gather(w, both, axis=0, tiled=True)
        return w.reshape(GROUPS * LINE, SLIVER, -1)

    def slabs(pack, w, gain):
        found = jax.vmap(pack)(w, jnp.pad(gain, ((0, 0), (0, 0), (0, 127))))
        return found.reshape((GROUPS, LINE) + found.shape[1:])

    qkv, gain_a, gain_m = shards_of(w_qkv), shards_of(attn_gain), shards_of(mlp_gain)
    groups = [slabs(lambda w, t, i=i: pack_group(w, t, i), qkv, gain_a) for i in range(2)]
    w_in, w_down = lax.all_gather(w_in, "dp", axis=0, tiled=True), lax.all_gather(w_down, "dp", axis=1, tiled=True)
    mlp = lax.all_gather(pack_mlp(w_in[:, 0], w_in[:, 1], w_down.T), "seq", axis=0, tiled=False)
    mlp = mlp.reshape(LINE, GROUPS, BAND, -1).transpose(1, 0, 2, 3)
    return groups, slabs(pack_out, shards_of(w_out), gain_m), mlp


def whole_sums(p0_g, p1_g, po_g, pm_g):
    both = ("dp", "seq")

    def scattered(x):
        return lax.psum_scatter(x.reshape(WIDTH, -1), both, scatter_dimension=0, tiled=True)

    parts = [jax.vmap(unpack_group)(p.reshape((GROUPS * LINE,) + p.shape[2:]).astype(F32)) for p in (p0_g, p1_g)]
    columns = [parts[0][0], parts[1][0], parts[0][1], parts[1][1], parts[0][2], parts[0][3], parts[1][2], parts[1][3]]
    g_qkv, gain_a = scattered(jnp.concatenate(columns, -1)), scattered(parts[1][4][..., :1])[:, 0]
    po = po_g.reshape(GROUPS * LINE, 2 * SLIVER, -1).astype(F32)
    g_out = scattered(jnp.concatenate([po[:, :SLIVER, :HALF], po[:, SLIVER:, :HALF]], -1))
    gain_m = scattered(po[:, :SLIVER, HALF : HALF + 1])[:, 0]
    mlp = pm_g.astype(F32).transpose(1, 0, 2, 3).reshape(LINE, WIDTH, -1)
    mlp = lax.psum_scatter(mlp, "seq", scatter_dimension=0, tiled=False)
    gate, up, down = unpack_mlp(lax.psum_scatter(mlp, "dp", scatter_dimension=0, tiled=True))
    return g_qkv, g_out, gain_a, gain_m, jnp.stack([gate, up], 1), down.T


def on_device(tokens, w_qkv, w_out, attn_gain, mlp_gain, w_in, w_down, grad_out, *, dp, nz):
    rows = tokens.shape[0]
    masks = (dp // 2, dp // 4, 1) if dp == GROUPS else None
    tables = jnp.asarray(rope_tables(nz * rows)).reshape(nz, rows, 128)
    if masks:
        gains = jnp.pad(jnp.stack([attn_gain, mlp_gain]).astype(F32), ((0, 6), (0, 128 - SLIVER)))
        weights = [w_qkv, w_out, gains, w_in.reshape(w_in.shape[0], -1), w_down]
        got = front(tokens, grad_out, weights, tables, nz, masks)
        po_all, pm_all = got[-2:]
    else:
        groups, po_all, pm_all = whole_packs(w_qkv, w_out, attn_gain, mlp_gain, w_in, w_down)
        got = front(tokens, grad_out, groups, tables, nz, None)
    mixed, lse, query, gain, tok_own, gout_own, kv, firsts, wqkv = got[:9]
    out_own, gmid, gmixed, delta, po_g, pm_g = middle(tok_own, mixed, gout_own, po_all, pm_all)
    found = back(tok_own, gmid, out_own, query, kv, firsts, wqkv, gain, gmixed, lse, delta, tables, [po_g, pm_g], nz, masks)
    gtok, out, *sums = found
    if not masks:
        return (out, gtok, *whole_sums(*sums, po_g, pm_g))
    out, gtok, g_qkv, g_out, gains, g_in, g_down = finish(out, gtok, *sums)
    g_in = g_in.reshape(g_in.shape[0], 2, SHARE)
    return out, gtok, g_qkv, g_out, gains[0, :SLIVER], gains[1, :SLIVER], g_in, g_down


def solution(mesh):
    both = P(("dp", "seq"), None)
    vector = P(("dp", "seq"))
    w_in, w_down = P("dp", None, "seq"), P("seq", "dp")
    step = functools.partial(on_device, dp=mesh.shape["dp"], nz=mesh.shape["seq"])
    return jax.shard_map(
        step,
        mesh=mesh,
        in_specs=(both, both, both, vector, vector, w_in, w_down, both),
        out_specs=(both, both, both, both, vector, vector, w_in, w_down),
        check_vma=False,
    )
```

```python
import functools
import math

import jax
import jax.numpy as jnp
import numpy as np
from jax import lax
from jax.experimental import pallas as pl
from jax.experimental.pallas import tpu as pltpu
from jax.sharding import PartitionSpec as P

HEADS = 12
HEAD_DIM = 64
NORM_EPS = 1e-05
ROPE_THETA = 160000.0

F32 = jnp.float32
BF = jnp.bfloat16
MESH = pl.DeviceIdType.MESH
NT = (((1,), (1,)), ((), ()))
NN = (((1,), (0,)), ((), ()))
TN = (((0,), (0,)), ((), ()))

WIDTH = 768
PAIRS = HEADS // 2
UNITS = 1152
GROUPS = 8
LINE = 4
BAND = WIDTH // GROUPS
SLIVER = BAND // LINE
SHARE = UNITS // LINE
MAIN = 256
REST = SHARE - MAIN
LINKED = (0, 1, 3, 2)
HALF = WIDTH // 2
CUTS = {640: 256, 512: 256, 896: 384}
LOG2E = math.log2(math.e)
SCALE = HEAD_DIM**-0.5


def dot(a, b, dims):
    return lax.dot_general(a, b, dims, preferred_element_type=F32)


def lanes_of(tile, width=128):
    return pl.ds(pl.multiple_of(tile * width, width), width)


def tiles(start, width):
    return pl.ds(pl.multiple_of(start, width if width < 128 else 128), width)


def lane_iota():
    return lax.broadcasted_iota(jnp.int32, (1, 128), 1)


def swap_halves(u):
    low = lax.rem(lane_iota(), 64) < 32
    return jnp.where(low, pltpu.roll(u, 96, 1), pltpu.roll(u, 32, 1))


def rope(u, cos, sine):
    return u * cos + swap_halves(u) * sine


def rope_back(u, cos, sine):
    return u * cos - swap_halves(u) * sine


def rope_tables(rows):
    position = np.arange(rows, dtype=np.float32)
    half = HEAD_DIM // 2
    freq = (ROPE_THETA ** (-np.arange(half) * 2.0 / HEAD_DIM)).astype(np.float32)
    angle = (position[:, None] * freq[None, :]).astype(np.float64)
    cos, sine = np.cos(angle), np.sin(angle)
    return np.concatenate([cos, cos, -sine, sine], 1).astype(np.float32)


def spread_tables(cos, sine):
    low = lane_iota() < 64

    def chunk(c, _):
        both = cos[c]
        other = pltpu.roll(both, 64, 1)
        cos[c] = jnp.where(low, both, other)
        sine[c] = jnp.where(low, other, both)
        return 0

    lax.fori_loop(0, cos.shape[0], chunk, 0)


def normed(x):
    centred = x - jnp.mean(x, -1, keepdims=True)
    inv = lax.rsqrt(jnp.mean(centred * centred, -1, keepdims=True) + NORM_EPS)
    return centred * inv, inv


def norm_back(dy, gain, hat, inv):
    d = dy * gain
    return inv * (d - jnp.mean(d, -1, keepdims=True) - hat * jnp.mean(d * hat, -1, keepdims=True))


def remote(src, dst, send, recv, device):
    return pltpu.make_async_remote_copy(src, dst, send, recv, device_id=device, device_id_type=MESH)


class Place:
    def __init__(self, nz):
        self.dp, self.z = lax.axis_index("dp"), lax.axis_index("seq")
        self.nz = nz
        upper = self.z // (nz // 2)
        self.moves = lax.rem(self.dp, 2) != upper
        self.stays = lax.rem(self.dp, 2) == upper
        self.shard = jnp.where(self.moves, nz - 1 - self.z, self.z)
        self.opposite = {"dp": self.dp ^ 1, "seq": nz - 1 - self.z}
        self.twin = {"dp": self.dp ^ 1}
        self.beside = {"seq": self.z ^ 1}

    def greet(self, masks):
        bar = pltpu.get_barrier_semaphore()

        def hello(device):
            pl.semaphore_signal(bar, inc=1, device_id=device, device_id_type=MESH)

        for o in range(1, self.nz):
            hello({"seq": lax.rem(self.z + o, self.nz)})
        for m in masks:
            hello({"dp": self.dp ^ m})
        hello(self.opposite)
        pl.semaphore_wait(bar, self.nz + len(masks))


class Gather:
    COPIES = 9

    def __init__(self, src, out, cut, nz, masks, send, recv):
        self.src, self.out, self.cut, self.nz, self.masks = src, out, cut, nz, masks
        self.send, self.recv = send, recv
        self.dp, self.z = lax.axis_index("dp"), lax.axis_index("seq")
        self.started = []
        self.relayed = None

    @staticmethod
    def sems(nz):
        return Gather.COPIES * nz + nz

    def key(self, o, k):
        return o * self.COPIES + k

    def copy(self, src, dst, device, k):
        return remote(src, dst, self.send.at[k], self.recv.at[k], device)

    def begin(self, src, dst, device, k, p=None):
        self.copy(src, dst, device, k).start()
        self.started.append((k, p))

    def arrived(self, ref, k):
        self.copy(ref, ref, {"dp": self.dp ^ self.masks[0]}, k).wait_recv()

    def slot(self, o):
        return self.z ^ LINKED[o]

    def part(self, ref, p):
        if p is None:
            return ref
        width = self.out.shape[-1]
        return ref.at[:, pl.ds(0, self.cut)] if p == 0 else ref.at[:, pl.ds(self.cut, width - self.cut)]

    def along(self, o):
        self.begin(self.src, self.out.at[self.dp, self.z], {"seq": self.z ^ LINKED[o]}, self.COPIES * self.nz + o)

    def relay(self, o):
        ref = self.out.at[self.dp, self.slot(o)]
        self.arrived(ref, self.COPIES * self.nz + o)
        self.relayed = o
        self.begin(ref, ref, {"seq": self.z ^ 1}, self.COPIES * self.nz + 3)

    def forward(self, src, d, s, mask, k, p=None):
        dst = self.out.at[d, s]
        self.begin(self.part(src, p), self.part(dst, p), {"dp": self.dp ^ mask}, k, p)

    def first(self, o):
        my, mx, mc = self.masks
        s = self.slot(o)
        src = self.src
        if o:
            src = self.out.at[self.dp, s]
            if o != self.relayed:
                self.arrived(src, self.COPIES * self.nz + o)
        self.forward(src, self.dp, s, my, self.key(o, 0))
        self.forward(src, self.dp, s, mx, self.key(o, 1))
        self.forward(src, self.dp, s, mc, self.key(o, 2))

    def second(self, o):
        my, mx, mc = self.masks
        s = self.slot(o)
        for m, k, k2, kc, p, m2 in ((my, 0, 3, 4, 0, mx), (mx, 1, 5, 6, 1, my)):
            ref = self.out.at[self.dp ^ m, s]
            self.arrived(ref, self.key(o, k))
            self.forward(ref, self.dp ^ m, s, m2, self.key(o, k2), p)
            self.forward(ref, self.dp ^ m, s, mc, self.key(o, kc))

    def third(self, o):
        my, mx, mc = self.masks
        s = self.slot(o)
        d = self.dp ^ my ^ mx
        for p, k, kc in ((0, 3, 7), (1, 5, 8)):
            ref = self.out.at[d, s]
            self.arrived(self.part(ref, p), self.key(o, k))
            self.forward(ref, d, s, mc, self.key(o, kc), p)

    def finish(self, o):
        my, mx, mc = self.masks
        s = self.slot(o)
        for k, d in ((2, mc), (4, mc ^ my), (6, mc ^ mx)):
            self.arrived(self.out.at[self.dp ^ d, s], self.key(o, k))
        for k, p in ((7, 0), (8, 1)):
            self.arrived(self.part(self.out.at[self.dp ^ mc ^ my ^ mx, s], p), self.key(o, k))

    def done(self):
        for k, p in self.started:
            ref = self.part(self.out.at[self.dp, self.z], p)
            self.copy(ref, ref, {"dp": self.dp ^ self.masks[0]}, k).wait_send()


def pack_group(w, tile, i):
    q, k, v = [w[:, WIDTH * j + HALF * i : WIDTH * j + HALF * i + HALF] for j in range(3)]
    return jnp.concatenate([jnp.concatenate([q, v[:, :256]], 1), jnp.concatenate([k, v[:, 256:], tile], 1)], 0)


def unpack_group(total):
    r = total.shape[0] // 2
    upper, lower = total[:r], total[r:]
    return upper[:, :HALF], lower[:, :HALF], upper[:, HALF:], lower[:, HALF : HALF + 128], lower[:, HALF + 128 :]


def pack_out(w, tile):
    return jnp.concatenate([jnp.concatenate([w[:, :HALF], w[:, HALF:]], 0), jnp.concatenate([tile, jnp.zeros_like(tile)], 0)], 1)


def pack_mlp(gate, up, down):
    parts = (gate, up, down)
    pads = jnp.zeros((gate.shape[0], 128 - 3 * REST), gate.dtype)
    return jnp.concatenate([x[:, :MAIN] for x in parts] + [x[:, MAIN:] for x in parts] + [pads], 1)


def unpack_mlp(total):
    return [
        jnp.concatenate([total[:, MAIN * i : MAIN * i + MAIN], total[:, 3 * MAIN + REST * i : 3 * MAIN + REST * i + REST]], 1)
        for i in range(3)
    ]


def front_kernel(nz, masks, rows, *refs):
    fused = masks is not None
    if fused:
        (tok, gout, w_qkv, w_out, gain_a, gain_m, w_in, w_down, cos_in), refs = refs[:9], refs[9:]
    else:
        (tok, gout, g0_all, g1_all, cos_in), refs = refs[:5], refs[5:]
    (mixed, lse, query, gain, tok_own, gout_own, kv, firsts, wqkv), refs = refs[:9], refs[9:]
    if fused:
        (po_all, pm_all), refs = refs[:2], refs[2:]
    (tok_all, kvb, fb, wq, cos, sine, gcol, acc, top, total, tsend, trecv, loc), refs = refs[:13], refs[13:]
    me = Place(nz)
    own = me.shard

    def here(src, dst, k):
        return pltpu.make_async_copy(src, dst, loc.at[k])

    def there(src, dst, device, k):
        return remote(src, dst, tsend.at[k], trecv.at[k], device)

    def rows_to(src, c, device, k, i):
        at = pl.ds(i * (rows // 2), rows // 2)
        src = tok_all.at[c] if src is None else src
        return there(src.at[at], tok_all.at[c, at], device, k + 5 * i)

    @pl.when(me.stays)
    def _():
        here(tok, tok_all.at[own], 0).start()
        here(gout, gout_own, 1).start()

    here(cos_in, cos, 2).start()
    groups, later = [], []
    every, rest = range(nz), (2, 1, 3)
    if fused:
        p0, p1, po, pm, g0_all, g1_all, *sems = refs
        row = lax.broadcasted_iota(jnp.int32, (128, 128), 0)

        def tile_of(part):
            line = jnp.concatenate([part[...].astype(F32), jnp.zeros((1, 128 - SLIVER), F32)], 1)
            return jnp.where(row == 0, line, 0.0).T[:SLIVER]

        p0[...] = pack_group(w_qkv[...].astype(F32), tile_of(gain_a), 0).astype(BF)
        g0_all[me.dp, me.z] = p0[...]
    me.greet(masks or (1,))
    if fused:
        shapes = ((p0, g0_all), (p1, g1_all), (po, po_all), (pm, pm_all))
        packs = [
            Gather(src, dst, CUTS[src.shape[-1]], nz, masks, sems[2 * i], sems[2 * i + 1]) for i, (src, dst) in enumerate(shapes)
        ]
        groups, later = packs[:2], packs[2:]
        for o in rest:
            groups[0].along(o)
        groups[0].first(0)

    @pl.when(me.stays)
    def _():
        for i in range(2):
            rows_to(tok, own, me.twin, 1, i).start()
            rows_to(tok, own, me.beside, 2, i).start()

    @pl.when(me.moves)
    def _():
        for i in range(2):
            rows_to(tok, me.z, me.opposite, 0, i).start()

    def swapped(i):
        @pl.when(me.moves)
        def _():
            rows_to(None, own, me.opposite, 0, i).wait_recv()
            rows_to(None, own, me.beside, 2, i).start()
            rows_to(None, own, me.twin, 1, i).start()

    if fused:
        w = w_qkv[...].astype(F32)
        p1[...] = pack_group(w, jnp.zeros((SLIVER, 128), F32), 1).astype(BF)
        g1_all[me.dp, me.z] = p1[...]
        po[...] = pack_out(w_out[...].astype(F32), tile_of(gain_m)).astype(BF)
        pm[...] = pack_mlp(w_in[:, 0, :].astype(F32), w_in[:, 1, :].astype(F32), w_down[...].astype(F32).T).astype(BF)
        here(po, po_all.at[me.dp, me.z], 4).start()
        here(pm, pm_all.at[me.dp, me.z], 5).start()
        for o in rest:
            groups[1].along(o)
        groups[1].first(0)
        groups[0].second(0)
        for o in rest:
            groups[0].first(o)
        swapped(0)
        for o in rest:
            groups[0].second(o)
        for o in rest:
            groups[1].first(o)
        for g in later:
            g.along(1)
            g.first(0)

    if not fused:
        swapped(0)
    swapped(1)

    @pl.when(me.stays)
    def _():
        here(tok, tok_all.at[own], 0).wait()

    here(tok_all.at[own], tok_own, 6).start()
    if fused:
        for g in later:
            g.along(2)
        for o in range(nz):
            groups[0].third(o)
        for o in range(nz):
            groups[0].finish(o)

    @pl.when(me.moves)
    def _():
        there(gout, gout_own, me.opposite, 4).start()

    here(cos_in, cos, 2).wait()
    spread_tables(cos, sine)

    def build(i, whole):
        def band_of(g, _):
            slabs = [unpack_group(whole[g, s].astype(F32)) for s in range(LINE)]
            band = pl.ds(pl.multiple_of(g * BAND, BAND), BAND)
            q, k, v0, v1, t = [jnp.concatenate([x[j] for x in slabs], 0) for j in range(5)]
            at = WIDTH * i
            wq[band, at : at + HALF] = k.astype(BF)
            wq[band, at + HALF : at + HALF + 256] = v0.astype(BF)
            wq[band, at + HALF + 256 : at + WIDTH] = v1.astype(BF)
            wq[band, 2 * WIDTH + HALF * i : 2 * WIDTH + HALF * i + HALF] = q.astype(BF)
            if i == 0:
                gcol[band, :] = t
            return 0

        lax.fori_loop(0, GROUPS, band_of, 0)

    def norm_chunk(c):
        def block(i, _):
            at = pl.ds(pl.multiple_of(i * 64, 64), 64)
            hat, _ = normed(tok_all[c, at, :].astype(F32))
            fb[c, at, :] = (hat * gain[0:1, :]).astype(BF)
            return 0

        lax.fori_loop(0, rows // 64, block, 0)
        here(fb.at[c], firsts.at[c], 8 + c).start()

    def queries(i):
        u = dot(fb[own], wq[:, 2 * WIDTH + HALF * i : 2 * WIDTH + HALF * i + HALF], NN)
        for j in range(3):
            tile = rope(u[:, 128 * j : 128 * j + 128], cos[own], sine[own])
            query[:, HALF * i + 128 * j : HALF * i + 128 * j + 128] = (tile * (SCALE * LOG2E)).astype(BF)

    def visits(steps):
        def visit(n, _):
            t, grp = lax.rem(n, nz), n // nz
            stay = jnp.where(t == 1, 1, jnp.where(t == 2, 3, 2))
            move = jnp.where(t == 1, 3, jnp.where(t == 2, 2, 1))
            turn = jnp.where(me.stays, stay, move)
            c = jnp.where(t == 0, own, own ^ turn)
            @pl.when((n > 0) & (n < nz))
            def _():
                for i in range(2):
                    rows_to(None, c, me.twin, jnp.where(turn == 1, 2, jnp.where(turn == 3, 1, 3)), i).wait_recv()

                    @pl.when(turn == 1)
                    def _(i=i):
                        rows_to(None, c, me.twin, 3, i).start()

                norm_chunk(c)

            for j in range(3):
                u = dot(fb[c], wq[:, tiles(WIDTH * grp + 256 * j, 256)], NN)
                for i in range(2):
                    tile = 2 * j + i
                    x = u[:, 128 * i : 128 * i + 128]
                    x = rope(x, cos[c], sine[c]) if tile < 3 else x
                    kvb[grp, c, :, 128 * tile : 128 * tile + 128] = x.astype(BF)
            here(kvb.at[grp, c], kv.at[grp, c], 8 + nz * (1 + grp) + c).start()
            jobs = [(i, h) for i in range(3) for h in range(2)]

            def score(i, h):
                q = query[:, tiles(HALF * grp + 128 * i, 128)]
                mask = (lane_iota() < 64) if h == 0 else (lane_iota() >= 64)
                return dot(kvb[grp, c, :, 128 * i : 128 * i + 128], jnp.where(mask, q, jnp.zeros_like(q)), NT)

            ready = [score(*j) for j in jobs[:2]]
            for m, (i, h) in enumerate(jobs):
                if h == 0:
                    vt = kvb[grp, c, :, HALF + 128 * i : HALF + 128 * i + 128].T
                s = ready[m]
                if m + 2 < len(jobs):
                    ready.append(score(*jobs[m + 2]))
                head = pl.ds(6 * grp + m, 1)
                band = tiles(64 * (6 * grp + m), 64)
                old = top[head, :]
                new = jnp.maximum(old, jnp.max(s, 0, keepdims=True))
                p = jnp.exp2(s - new)
                fade = jnp.exp2(old - new)
                top[head, :] = new
                lhs = jnp.concatenate([vt[h * 64 : h * 64 + 64], jnp.ones((16, rows), BF)], 0)
                oo = dot(lhs, p.astype(BF), NN)
                total[head, :] = total[head, :] * fade + oo[64:65]
                acc[band, :] = acc[band, :] * fade + oo[:64]
            for k, step in steps.items():

                @pl.when(n == k)
                def _(k=k, step=step):
                    for which, name, order in step:
                        for g in which:
                            for o in order:
                                getattr(g, name)(o)
                    if k == nz - 1:
                        build(1, g1_all)
                        here(wq, wqkv, 7).start()
                        queries(1)

            return 0

        lax.fori_loop(0, 2 * nz, visit, 0)

    build(0, g0_all)
    gain[...] = gcol[...].T[:8]
    norm_chunk(own)
    queries(0)
    acc[...] = jnp.zeros_like(acc)
    total[...] = jnp.zeros_like(total)
    top[...] = jnp.full_like(top, -1e30)
    one = groups[1:]
    visits({
        0: [(one, "second", every), (later, "first", (1,))],
        1: [(one, "third", every)],
        2: [(later, "relay", (2,)), (later, "first", (2,))],
        3: [(one, "finish", every), (later, "second", (0, 1))],
        4: [(later, "first", (3,))],
        5: [(later, "second", (2,))],
        6: [(later, "second", (3,))],
        7: [(later, "third", every)],
    })

    for hp in range(PAIRS):
        parts = [
            acc[128 * hp + 64 * h : 128 * hp + 64 * h + 64, :] / total[2 * hp + h : 2 * hp + h + 1, :] for h in range(2)
        ]
        mixed[:, 128 * hp : 128 * hp + 128] = jnp.concatenate(parts, 0).T.astype(BF)
    lse[...] = top[...] + jnp.log(jnp.maximum(total[...], 1e-30)) * LOG2E

    if fused:
        for g in later:
            for o in range(nz):
                g.finish(o)
        for g in packs:
            g.done()
        here(po, po_all.at[me.dp, me.z], 4).wait()
        here(pm, pm_all.at[me.dp, me.z], 5).wait()
    for i in range(2):
        for k in (1, 2, 3):
            rows_to(None, own, me.twin, k, i).wait_send()

    @pl.when(me.moves)
    def _():
        for i in range(2):
            rows_to(None, own, me.opposite, 0, i).wait_send()
        there(gout, gout_own, me.opposite, 4).wait()

    @pl.when(me.stays)
    def _():
        here(gout, gout_own, 1).wait()

    here(tok_all.at[own], tok_own, 6).wait()
    here(wq, wqkv, 7).wait()
    for c in range(nz):
        here(fb.at[c], firsts.at[c], 8 + c).wait()
        for grp in range(2):
            here(kvb.at[grp, c], kv.at[grp, c], 8 + nz * (1 + grp) + c).wait()


def front(tok, gout, weights, tables, nz, masks):
    rows = tok.shape[0]
    vmem, anyspace = pl.BlockSpec(memory_space=pltpu.VMEM), pl.BlockSpec(memory_space=pl.ANY)
    shape, vm = jax.ShapeDtypeStruct, pltpu.VMEM
    outs = [shape((rows, WIDTH), BF), shape((16, rows), F32), shape((rows, WIDTH), BF), shape((8, WIDTH), F32)]
    outs += [shape((rows, WIDTH), BF)] * 2
    outs += [shape((2, nz, rows, WIDTH), BF), shape((nz, rows, WIDTH), BF), shape((WIDTH, 3 * WIDTH), BF)]
    out_specs = [vmem] * 4 + [anyspace, vmem] + [anyspace] * 3
    scratch = [
        vm((nz, rows, WIDTH), BF),
        vm((2, nz, rows, WIDTH), BF),
        vm((nz, rows, WIDTH), BF),
        vm((WIDTH, 3 * WIDTH), BF),
        vm((nz, rows, 128), F32),
        vm((nz, rows, 128), F32),
        vm((WIDTH, 128), F32),
        vm((WIDTH, rows), F32),
        vm((16, rows), F32),
        vm((16, rows), F32),
        pltpu.SemaphoreType.DMA((9,)),
        pltpu.SemaphoreType.DMA((9,)),
        pltpu.SemaphoreType.DMA((8 + 3 * nz,)),
    ]
    if masks:
        grp, out, mlp = (2 * SLIVER, 640), (2 * SLIVER, 512), (BAND, 896)
        outs += [shape((GROUPS, nz) + out, BF), shape((GROUPS, nz) + mlp, BF)]
        out_specs += [anyspace] * 2
        scratch += [vm(x, BF) for x in (grp, grp, out, mlp)] + [vm((GROUPS, nz) + grp, BF)] * 2
        scratch += [pltpu.SemaphoreType.DMA((Gather.sems(nz),)) for _ in range(8)]
    return pl.pallas_call(
        functools.partial(front_kernel, nz, masks, rows),
        out_shape=outs,
        in_specs=[anyspace] * 2 + [vmem] * len(weights) + [anyspace],
        out_specs=out_specs,
        scratch_shapes=scratch,
        compiler_params=pltpu.CompilerParams(collective_id=0, has_side_effects=True, vmem_limit_bytes=60 << 20),
        cost_estimate=pl.CostEstimate(flops=14_000_000_000, bytes_accessed=40_000_000, transcendentals=13_000_000),
        name="front",
    )(tok, gout, *weights, tables)


def middle_kernel(rows, tok, mixed, gout, po_all, pm_all, out, gmid, gmixed, delta, po_g, pm_g,
                  wout, wg, wu, wd, gcol, gain, resid, hat, inv, second, hidden, ggate, gup, gsec, gattn, dwout):
    lane = lane_iota()

    def build(g, _):
        band = pl.ds(pl.multiple_of(g * BAND, BAND), BAND)
        slabs = [po_all[g, s].astype(F32) for s in range(LINE)]
        wout[band, :384] = jnp.concatenate([x[:SLIVER, :384] for x in slabs], 0).astype(BF)
        wout[band, 384:] = jnp.concatenate([x[SLIVER:, :384] for x in slabs], 0).astype(BF)
        gcol[band, :] = jnp.concatenate([x[:SLIVER, 384:] for x in slabs], 0)
        for i, w in enumerate((wg, wu, wd)):
            tail = jnp.zeros((BAND, 128), F32)
            for s in range(LINE):
                w[band, MAIN * s : MAIN * s + MAIN] = pm_all[g, s, :, MAIN * i : MAIN * i + MAIN]
                rest = pm_all[g, s, :, 3 * MAIN :].astype(F32)
                turn = (REST * (s - i)) % 128
                rest = pltpu.roll(rest, turn, 1) if turn else rest
                tail = jnp.where((lane >= REST * s) & (lane < REST * (s + 1)), rest, tail)
            w[band, MAIN * LINE :] = tail.astype(BF)
        return 0

    lax.fori_loop(0, GROUPS, build, 0)
    gain[...] = gcol[...].T[:8]

    for j in range(3):
        at = slice(256 * j, 256 * j + 256)
        resid[:, at] = tok[:, at].astype(F32) + dot(mixed[...], wout[:, at], NN)

    def norm_block(i, _):
        at = pl.ds(pl.multiple_of(i * 64, 64), 64)
        h, r = normed(resid[at, :])
        hat[at, :] = h
        inv[at, :] = jnp.broadcast_to(r, (64, 128))
        second[at, :] = (h * gain[0:1, :]).astype(BF)
        return 0

    lax.fori_loop(0, rows // 64, norm_block, 0)

    def units(start, width):
        at = pl.ds(start, width)
        gate, up, gh = dot(second[...], wg[:, at], NN), dot(second[...], wu[:, at], NN), dot(gout[...], wd[:, at], NN)
        cdf = 0.5 + 0.5 * lax.erf(gate * math.sqrt(0.5))
        pdf = jnp.exp2(gate * gate * (-0.5 * LOG2E)) * (1.0 / math.sqrt(2.0 * math.pi))
        act = gate * cdf
        hidden[:, at] = (act * up).astype(BF)
        gup[:, at] = (gh * act).astype(BF)
        ggate[:, at] = (gh * up * (cdf + gate * pdf)).astype(BF)

    for start in range(0, UNITS, 256):
        units(start, min(256, UNITS - start))

    for j in range(3):
        at = slice(256 * j, 256 * j + 256)
        out[:, at] = (resid[:, at] + dot(hidden[...], wd[at, :], NT)).astype(BF)
        gsec[:, at] = dot(ggate[...], wg[at, :], NT) + dot(gup[...], wu[at, :], NT)

    def back_block(i, dgain):
        at = pl.ds(pl.multiple_of(i * 64, 64), 64)
        dy, h = gsec[at, :], hat[at, :]
        gm = gout[at, :].astype(F32) + norm_back(dy, gain[0:1, :], h, inv[at, 0:1])
        gmid[at, :] = gm
        gattn[at, :] = gm.astype(BF)
        return dgain + jnp.sum(dy * h, 0, keepdims=True)

    dgain = lax.fori_loop(0, rows // 64, back_block, jnp.zeros((1, WIDTH), F32))

    heads = lax.broadcasted_iota(jnp.int32, (16, 256), 0)
    for j in range(3):
        at = slice(256 * j, 256 * j + 256)
        gmx = dot(gattn[...], wout[at, :], NT).astype(BF)
        gmixed[:, at] = gmx
        prod = gmx.astype(F32) * mixed[:, at].astype(F32)
        high = prod.astype(BF)
        low = (prod - high.astype(F32)).astype(BF)
        pick = ((lax.broadcasted_iota(jnp.int32, (16, 256), 1) + 256 * j) // HEAD_DIM == heads).astype(BF)
        part = dot(pick, high, NT) + dot(pick, low, NT)
        delta[...] = part if j == 0 else delta[...] + part

    for j in range(2):
        at = slice(384 * j, 384 * j + 384)
        dwout[at, :] = dot(mixed[:, at], gattn[...], TN)
    row = lax.broadcasted_iota(jnp.int32, (128, WIDTH), 0)
    gcol[...] = jnp.where(row == 0, dgain, 0.0).T

    def pack_out(g, _):
        for s in range(LINE):
            at = pl.ds(pl.multiple_of(g * BAND + s * SLIVER, 8), SLIVER)
            x, c = dwout[at, :], gcol[at, :]
            po_g[g, s, :, :384] = jnp.concatenate([x[:, :384], x[:, 384:]], 0).astype(BF)
            po_g[g, s, :, 384:] = jnp.concatenate([c, jnp.zeros_like(c)], 0).astype(BF)
        return 0

    lax.fori_loop(0, GROUPS, pack_out, 0)

    for j in range(2):
        at = slice(384 * j, 384 * j + 384)
        tails = []
        for i, (a, b) in enumerate(((second, ggate), (second, gup), (gout, hidden))):
            for s in range(LINE):
                x = dot(a[:, at], b[:, MAIN * s : MAIN * s + MAIN], TN).astype(BF)
                for g in range(4):
                    pm_g[4 * j + g, s, :, MAIN * i : MAIN * i + MAIN] = x[BAND * g : BAND * g + BAND]
            tails.append(dot(a[:, at], b[:, MAIN * LINE :], TN))
        for s in range(LINE):
            y = jnp.zeros((384, 128), F32)
            for i, tail in enumerate(tails):
                turn = (REST * (i - s)) % 128
                tail = pltpu.roll(tail, turn, 1) if turn else tail
                y = jnp.where((lane >= REST * i) & (lane < REST * (i + 1)), tail, y)
            y = y.astype(BF)
            for g in range(4):
                pm_g[4 * j + g, s, :, 3 * MAIN :] = y[BAND * g : BAND * g + BAND]


def middle(tok, mixed, gout, po_all, pm_all):
    rows = tok.shape[0]
    shape, vm = jax.ShapeDtypeStruct, pltpu.VMEM
    vmem = pl.BlockSpec(memory_space=pltpu.VMEM)
    return pl.pallas_call(
        functools.partial(middle_kernel, rows),
        out_shape=[
            shape((rows, WIDTH), BF),
            shape((rows, WIDTH), F32),
            shape((rows, WIDTH), BF),
            shape((16, rows), F32),
            shape(po_all.shape, BF),
            shape(pm_all.shape, BF),
        ],
        in_specs=[vmem] * 5,
        out_specs=[vmem] * 6,
        scratch_shapes=[
            vm((WIDTH, WIDTH), BF),
            vm((WIDTH, UNITS), BF),
            vm((WIDTH, UNITS), BF),
            vm((WIDTH, UNITS), BF),
            vm((WIDTH, 128), F32),
            vm((8, WIDTH), F32),
            vm((rows, WIDTH), F32),
            vm((rows, WIDTH), F32),
            vm((rows, 128), F32),
            vm((rows, WIDTH), BF),
            vm((rows, UNITS), BF),
            vm((rows, UNITS), BF),
            vm((rows, UNITS), BF),
            vm((rows, WIDTH), F32),
            vm((rows, WIDTH), BF),
            vm((WIDTH, WIDTH), F32),
        ],
        compiler_params=pltpu.CompilerParams(vmem_limit_bytes=58 << 20),
        cost_estimate=pl.CostEstimate(flops=11_000_000_000, bytes_accessed=25_000_000, transcendentals=1_200_000),
        name="middle",
    )(tok, mixed, gout, po_all, pm_all)


class Reduce:
    COPIES = 10

    def __init__(self, src, total, cut, nz, masks, bufs, send, recv, loc=None):
        self.src, self.total, self.cut, self.nz, self.masks = src, total, cut, nz, masks
        self.near, self.side0, self.side1, self.far, *mine = bufs
        self.mine = mine[0] if mine else None
        self.send, self.recv, self.loc = send, recv, loc
        self.dp, self.z = lax.axis_index("dp"), lax.axis_index("seq")
        my, mx, mc = masks
        self.turns = (0, my, mx, my ^ mx)
        self.started = []

    @staticmethod
    def scratch(shape, nz, held):
        r, c = shape
        cut = CUTS[c]
        bufs = [
            pltpu.VMEM((4, nz, r, c), BF),
            pltpu.VMEM((3, nz, r, cut), BF),
            pltpu.VMEM((3, nz, r, c - cut), BF),
            pltpu.VMEM((nz - 1, r, c), BF),
        ]
        sems = [pltpu.SemaphoreType.DMA((Reduce.COPIES * nz + nz,))] * 2
        if not held:
            bufs += [pltpu.VMEM((4, nz, r, c), BF)]
            sems += [pltpu.SemaphoreType.DMA((4 * nz,))]
        return bufs, sems

    def begin(self, src, dst, device, k):
        remote(src, dst, self.send.at[k], self.recv.at[k], device).start()
        self.started.append((k, src.shape[-1]))

    def arrived(self, ref, k):
        remote(ref, ref, self.send.at[k], self.recv.at[k], {"dp": self.dp ^ self.masks[2]}).wait_recv()

    def seat(self, o):
        return self.z ^ LINKED[o]

    def held(self, i, s):
        return self.mine.at[i, s] if self.mine is not None else self.src.at[self.dp ^ self.turns[i], s]

    def local(self, i, o):
        s = self.seat(o)
        return pltpu.make_async_copy(self.src.at[self.dp ^ self.turns[i], s], self.mine.at[i, s], self.loc.at[4 * o + i])

    def zero(self, o):
        s, mc = self.seat(o), self.masks[2]
        for i in (3, 1, 2, 0):
            if self.mine is not None:
                self.local(i, o).start()
            self.begin(self.src.at[self.dp ^ mc ^ self.turns[i], s], self.near.at[i, s], {"dp": self.dp ^ mc}, self.COPIES * o + i)

    def add(self, ref, other):
        ref[...] = (ref[...].astype(F32) + other[...].astype(F32)).astype(BF)

    def p0(self, i, s):
        return self.held(i, s).at[:, pl.ds(0, self.cut)]

    def p1(self, i, s):
        return self.held(i, s).at[:, pl.ds(self.cut, self.src.shape[-1] - self.cut)]

    def one(self, o):
        my, mx, _ = self.masks
        s, k = self.seat(o), self.COPIES * o
        for i in (3, 1, 2, 0):
            if self.mine is not None:
                self.local(i, o).wait()
            self.arrived(self.near.at[i, s], k + i)
            self.add(self.held(i, s), self.near.at[i, s])
            if i == 3:
                self.begin(self.p0(3, s), self.side0.at[1, s], {"dp": self.dp ^ my}, k + 4)
                self.begin(self.p1(3, s), self.side1.at[1, s], {"dp": self.dp ^ mx}, k + 5)
            if i == 1:
                self.begin(self.p0(1, s), self.side0.at[0, s], {"dp": self.dp ^ my}, k + 6)
            if i == 2:
                self.begin(self.p1(2, s), self.side1.at[0, s], {"dp": self.dp ^ mx}, k + 7)

    def two(self, o):
        my, mx, _ = self.masks
        s, k = self.seat(o), self.COPIES * o
        self.arrived(self.side0.at[1, s], k + 4)
        self.add(self.p0(2, s), self.side0.at[1, s])
        self.begin(self.p0(2, s), self.side0.at[2, s], {"dp": self.dp ^ mx}, k + 8)
        self.arrived(self.side1.at[1, s], k + 5)
        self.add(self.p1(1, s), self.side1.at[1, s])
        self.begin(self.p1(1, s), self.side1.at[2, s], {"dp": self.dp ^ my}, k + 9)

    def three(self, o):
        s, k = self.seat(o), self.COPIES * o
        for ref, side, k1, k2 in ((self.p0(0, s), self.side0, k + 6, k + 8), (self.p1(0, s), self.side1, k + 7, k + 9)):
            self.arrived(side.at[0, s], k1)
            self.arrived(side.at[2, s], k2)
            ref[...] = (ref[...].astype(F32) + side[0, s].astype(F32) + side[2, s].astype(F32)).astype(BF)
        if o:
            self.begin(self.held(0, s), self.far.at[o - 1], {"seq": s}, self.COPIES * self.nz + o)

    def four(self):
        out = self.held(0, self.z)[...].astype(F32)
        for o in range(1, self.nz):
            self.arrived(self.far.at[o - 1], self.COPIES * self.nz + o)
            out = out + self.far[o - 1].astype(F32)
        self.total[...] = out

    def done(self):
        for k, width in self.started:
            whole = width == self.src.shape[-1]
            ref = self.near.at[0, 0] if whole else (self.side0 if k % self.COPIES in (4, 6, 8) else self.side1).at[0, 0]
            remote(ref, ref, self.send.at[k], self.recv.at[k], {"dp": self.dp ^ self.masks[2]}).wait_send()


def back_kernel(nz, masks, rows, *refs):
    fused = masks is not None
    (tok, gmid, out_own, query, kv, firsts, wqkv, gain, gmixed, lse, delta, cos_in), refs = refs[:12], refs[12:]
    if fused:
        (po_g, pm_g, gtok, out, s0, s1, so, sm), refs = refs[:8], refs[8:]
    else:
        (gtok, out, p0_g, p1_g), refs = refs[:4], refs[4:]
    (kvb, fb, ft, wq, cos, sine, dq, dqb, dkv, dx, dw, sent, landed, gown, gcol, send, recv, loc), refs = refs[:18], refs[18:]
    me = Place(nz)
    own = me.shard

    def here(src, dst, k):
        return pltpu.make_async_copy(src, dst, loc.at[k])

    def there(src, dst, device, k):
        return remote(src, dst, send.at[k], recv.at[k], device)

    def chunk(t):
        return jnp.where(t == 0, own ^ 2, jnp.where(t == 1, own ^ 1, jnp.where(t == 2, own ^ 3, own)))

    def fetch(n):
        return here(kv.at[n // nz, chunk(lax.rem(n, nz))], kvb.at[lax.rem(n, 2)], lax.rem(n, 2))

    def fetch_first(t):
        return here(firsts.at[chunk(t)], fb.at[lax.rem(t, 2)], 2 + lax.rem(t, 2))

    fetch(0).start()
    fetch_first(0).start()
    whole = [here(wqkv, wq, 4), here(cos_in, cos, 5)]
    for c in whole:
        c.start()
    me.greet(masks or (1,))
    jobs, sums = [], []
    if fused:
        (p0_g, p1_g), refs = refs[:2], refs[2:]
        for src, total in ((p0_g, s0), (p1_g, s1)):
            sums.append(Reduce(src, total, CUTS[src.shape[-1]], nz, masks, refs[:4], *refs[4:6]))
            refs = refs[6:]
        for src, total in ((po_g, so), (pm_g, sm)):
            jobs.append(Reduce(src, total, CUTS[src.shape[-1]], nz, masks, refs[:5], *refs[5:8]))
            refs = refs[8:]
    order = (3, 2, 1, 0)

    def advance(which, step):
        for j in which:
            for o in order:
                getattr(j, step)(o)

    def wave(which):
        for i in range(nz + 2):
            for k, step in enumerate(("one", "two", "three")):
                if 0 <= i - k < nz:
                    for j in which:
                        getattr(j, step)(order[i - k])

    advance(jobs, "zero")

    @pl.when(me.moves)
    def _():
        there(out_own, out, me.opposite, 3).start()

    @pl.when(me.stays)
    def _():
        here(out_own, out, 7).start()

    dq[...] = jnp.zeros_like(dq)
    for c in whole:
        c.wait()
    spread_tables(cos, sine)

    def visits(steps):
        def visit(n, _):
            t, grp = lax.rem(n, nz), n // nz
            c, slot = chunk(t), lax.rem(t, 2)
            fetch(n).wait()

            @pl.when(n < nz)
            def _():
                fetch_first(t).wait()

            @pl.when(n + 1 < 2 * nz)
            def _():
                fetch(n + 1).start()

            @pl.when(n + 1 < nz)
            def _():
                fetch_first(n + 1).start()

            band = pl.ds(pl.multiple_of(t * rows, rows), rows)
            todo = [(i, h) for i in range(3) for h in range(2)]

            def pick(ref, i, h):
                x = ref[:, tiles(HALF * grp + 128 * i, 128)]
                mask = (lane_iota() < 64) if h == 0 else (lane_iota() >= 64)
                return jnp.where(mask, x, jnp.zeros_like(x))

            def score(i, h):
                qh, gh = pick(query, i, h), pick(gmixed, i, h)
                k, v = kvb[slot, :, 128 * i : 128 * i + 128], kvb[slot, :, HALF + 128 * i : HALF + 128 * i + 128]
                return dot(k, qh, NT), dot(v, gh, NT), qh, gh

            ready = [score(*todo[0])]
            dk = dv = None
            for m, (i, h) in enumerate(todo):
                s, dp, qh, gh = ready[m]
                if m + 1 < len(todo):
                    ready.append(score(*todo[m + 1]))
                if h == 0:
                    kt = kvb[slot, :, 128 * i : 128 * i + 128].T
                head = pl.ds(6 * grp + m, 1)
                rows_of = tiles(64 * (6 * grp + m), 64)
                p = jnp.exp2(s - lse[head, :])
                ds = (p * (dp - delta[head, :])).astype(BF)
                a = dot(p.astype(BF), gh, NN)
                dv = a if h == 0 else dv + a
                a = dot(ds, qh, NN)
                dk = a if h == 0 else dk + a
                dq[rows_of, :] += dot(kt[h * 64 : h * 64 + 64], ds, NN)
                if h == 1:
                    at = WIDTH * grp + 128 * i
                    dkv[band, tiles(at, 128)] = rope_back(dk * (1.0 / LOG2E), cos[c], sine[c]).astype(BF)
                    dkv[band, tiles(at + HALF, 128)] = dv.astype(BF)

            @pl.when(n < nz)
            def _():
                for j in range(6):
                    ft[128 * j : 128 * j + 128, band] = fb[slot, :, 128 * j : 128 * j + 128].T
            @pl.when(n >= nz)
            def _():
                for j in range(3):
                    at = slice(256 * j, 256 * j + 256)
                    dx[:, at] = dot(dkv[band, :], wq[at, : 2 * WIDTH], NT)

                @pl.when(lax.rem(t, 2) == 0)
                def _():
                    sent[t] = dx[...].astype(BF)
                    there(sent.at[t], landed.at[t], me.twin, t).start()

                @pl.when(t == 1)
                def _():
                    there(sent.at[0], landed.at[0], me.twin, 0).wait_recv()
                    sent[1] = (dx[...] + landed[0].astype(F32)).astype(BF)
                    there(sent.at[1], landed.at[1], me.beside, 1).start()

            for k, step in steps.items():

                @pl.when(n == k)
                def _(k=k, step=step):
                    if k == nz - 1:
                        close(0)
                        weigh(0)
                        pack(0, p0_g)
                    for which, name in step:
                        advance(which, name)

            return 0

        lax.fori_loop(0, 2 * nz, visit, 0)

    def close(grp):
        for i in range(3 * grp, 3 * grp + 3):
            at = slice(128 * i, 128 * i + 128)
            dqb[:, at] = rope_back(dq[at, :].T * SCALE, cos[own], sine[own]).astype(BF)

    def weigh(grp):
        for r in (slice(0, HALF), slice(HALF, WIDTH)):
            for j in range(3):
                at = WIDTH * grp + 256 * j
                dw[r, HALF + 256 * j : HALF + 256 * j + 256] = dot(ft[r, :], dkv[:, at : at + 256], NN)
            dw[r, :HALF] = dot(ft[r, (nz - 1) * rows :], dqb[:, HALF * grp : HALF * grp + HALF], NN)

    def pack(grp, dst):
        def band_of(g, _):
            for s in range(LINE):
                at = pl.ds(pl.multiple_of(g * BAND + s * SLIVER, 8), SLIVER)
                q, k, v0, v1 = dw[at, :HALF], dw[at, HALF:WIDTH], dw[at, WIDTH : WIDTH + 256], dw[at, WIDTH + 256 :]
                tile = gcol[at, :] if grp else jnp.zeros((SLIVER, 128), F32)
                dst[g, s] = jnp.concatenate(
                    [jnp.concatenate([q, v0], 1), jnp.concatenate([k, v1, tile], 1)], 0
                ).astype(BF)
            return 0

        lax.fori_loop(0, GROUPS, band_of, 0)

    early = sums[:1]
    visits({
        0: [(jobs, "one")],
        3: [(early, "zero")],
        4: [(jobs, "two"), (early, "one")],
        6: [(jobs, "three")],
        7: [(early, "two"), (early, "three")],
    })
    close(1)
    for j in range(3):
        at = slice(256 * j, 256 * j + 256)
        dx[:, at] += dot(dqb[...], wq[at, 2 * WIDTH :], NT)
    there(sent.at[1], landed.at[1], me.beside, 1).wait_recv()
    there(sent.at[2], landed.at[2], me.twin, 2).wait_recv()

    def norm_block(i, dgain):
        at = pl.ds(pl.multiple_of(i * 64, 64), 64)
        dy = dx[at, :] + landed[1, at, :].astype(F32) + landed[2, at, :].astype(F32)
        h, r = normed(tok[at, :].astype(F32))
        gown[at, :] = (gmid[at, :] + norm_back(dy, gain[0:1, :], h, r)).astype(BF)
        return dgain + jnp.sum(dy * h, 0, keepdims=True)

    dgain = lax.fori_loop(0, rows // 64, norm_block, jnp.zeros((1, WIDTH), F32))

    @pl.when(me.moves)
    def _():
        there(gown, gtok, me.opposite, 4).start()

    @pl.when(me.stays)
    def _():
        here(gown, gtok, 8).start()

    row = lax.broadcasted_iota(jnp.int32, (128, WIDTH), 0)
    gcol[...] = jnp.where(row == 0, dgain, 0.0).T
    weigh(1)
    pack(1, p1_g)
    if fused:
        advance(sums[1:], "zero")
        wave(sums[1:])
        for j in jobs + sums:
            j.four()
        for j in jobs + sums:
            j.done()
    for k, device in ((0, me.twin), (1, me.beside), (2, me.twin)):
        there(sent.at[k], landed.at[k], device, k).wait_send()

    @pl.when(me.moves)
    def _():
        there(out_own, out, me.opposite, 3).wait()
        there(gown, gtok, me.opposite, 4).wait()

    @pl.when(me.stays)
    def _():
        here(out_own, out, 7).wait()
        here(gown, gtok, 8).wait()


def back(tok, gmid, out_own, query, kv, firsts, wqkv, gain, gmixed, lse, delta, tables, packs, nz, masks):
    rows = tok.shape[0]
    shape, vm = jax.ShapeDtypeStruct, pltpu.VMEM
    vmem, anyspace = pl.BlockSpec(memory_space=pltpu.VMEM), pl.BlockSpec(memory_space=pl.ANY)
    in_specs = [vmem] * 4 + [anyspace] * 3 + [vmem] * 4 + [anyspace]
    slab = (2 * SLIVER, 640)
    outs, out_specs = [shape((rows, WIDTH), BF)] * 2, [vmem] * 2
    scratch = [
        vm((2, rows, WIDTH), BF),
        vm((2, rows, WIDTH), BF),
        vm((WIDTH, nz * rows), BF),
        vm((WIDTH, 3 * WIDTH), BF),
        vm((nz, rows, 128), F32),
        vm((nz, rows, 128), F32),
        vm((WIDTH, rows), F32),
        vm((rows, WIDTH), BF),
        vm((nz * rows, 2 * WIDTH), BF),
        vm((rows, WIDTH), F32),
        vm((WIDTH, 3 * HALF), F32),
        vm((3, rows, WIDTH), BF),
        vm((3, rows, WIDTH), BF),
        vm((rows, WIDTH), BF),
        vm((WIDTH, 128), F32),
        pltpu.SemaphoreType.DMA((5,)),
        pltpu.SemaphoreType.DMA((5,)),
        pltpu.SemaphoreType.DMA((9,)),
    ]
    if masks:
        in_specs += [anyspace] * 2
        outs += [shape(s, F32) for s in (slab, slab, packs[0].shape[-2:], packs[1].shape[-2:])]
        out_specs += [vmem] * 4
        scratch += [vm((GROUPS, LINE) + slab, BF)] * 2
        for s, held in ((slab, True), (slab, True), (packs[0].shape[-2:], False), (packs[1].shape[-2:], False)):
            bufs, sems = Reduce.scratch(s, nz, held)
            scratch += bufs + sems
    else:
        outs += [shape((GROUPS, LINE) + slab, BF)] * 2
        out_specs += [vmem] * 2
        packs = []
    return pl.pallas_call(
        functools.partial(back_kernel, nz, masks, rows),
        out_shape=outs,
        in_specs=in_specs,
        out_specs=out_specs,
        scratch_shapes=scratch,
        compiler_params=pltpu.CompilerParams(collective_id=1, has_side_effects=True, vmem_limit_bytes=62 << 20),
        cost_estimate=pl.CostEstimate(flops=24_000_000_000, bytes_accessed=40_000_000, transcendentals=13_000_000),
        name="back",
    )(tok, gmid, out_own, query, kv, firsts, wqkv, gain, gmixed, lse, delta, tables, *packs)


def finish_kernel(out, gtok, s0, s1, so, sm, out_o, gtok_o, qkv_o, w_out_o, gain_a_o, gain_m_o, w_in_o, down_o):
    out_o[...] = out[...]
    gtok_o[...] = gtok[...]
    for i, total in enumerate((s0, s1)):
        q, k, v0, v1, tile = unpack_group(total[...])
        for j, x in enumerate((q, k)):
            qkv_o[:, WIDTH * j + HALF * i : WIDTH * j + HALF * i + HALF] = x
        at = 2 * WIDTH + HALF * i
        qkv_o[:, at : at + 256] = v0
        qkv_o[:, at + 256 : at + HALF] = v1
    w_out_o[:, :HALF] = so[:SLIVER, :HALF]
    w_out_o[:, HALF:] = so[SLIVER:, :HALF]
    zeros = jnp.zeros((128 - SLIVER, 128), F32)
    for dst, col in ((gain_a_o, tile), (gain_m_o, so[:SLIVER, HALF:])):
        dst[...] = jnp.concatenate([col, zeros], 0).T[:1, :SLIVER]
    gate, up, down = unpack_mlp(sm[...])
    w_in_o[:, 0, :] = gate
    w_in_o[:, 1, :] = up
    down_o[...] = down.T


def finish(out, gtok, s0, s1, so, sm):
    shape = jax.ShapeDtypeStruct
    vmem = pl.BlockSpec(memory_space=pltpu.VMEM)
    return pl.pallas_call(
        finish_kernel,
        out_shape=[
            shape(out.shape, BF),
            shape(gtok.shape, BF),
            shape((SLIVER, 3 * WIDTH), F32),
            shape((SLIVER, WIDTH), F32),
            shape((1, SLIVER), F32),
            shape((1, SLIVER), F32),
            shape((BAND, 2, SHARE), F32),
            shape((SHARE, BAND), F32),
        ],
        in_specs=[vmem] * 6,
        out_specs=[vmem] * 8,
        compiler_params=pltpu.CompilerParams(vmem_limit_bytes=60 << 20),
        name="finish",
    )(out, gtok, s0, s1, so, sm)


def whole_packs(w_qkv, w_out, attn_gain, mlp_gain, w_in, w_down):
    both = ("dp", "seq")

    def shards_of(w):
        w = lax.all_gather(w, both, axis=0, tiled=True)
        return w.reshape(GROUPS * LINE, SLIVER, -1)

    def slabs(pack, w, gain):
        found = jax.vmap(pack)(w, jnp.pad(gain, ((0, 0), (0, 0), (0, 127))))
        return found.reshape((GROUPS, LINE) + found.shape[1:])

    qkv, gain_a, gain_m = shards_of(w_qkv), shards_of(attn_gain), shards_of(mlp_gain)
    groups = [slabs(lambda w, t, i=i: pack_group(w, t, i), qkv, gain_a) for i in range(2)]
    w_in, w_down = lax.all_gather(w_in, "dp", axis=0, tiled=True), lax.all_gather(w_down, "dp", axis=1, tiled=True)
    mlp = lax.all_gather(pack_mlp(w_in[:, 0], w_in[:, 1], w_down.T), "seq", axis=0, tiled=False)
    mlp = mlp.reshape(LINE, GROUPS, BAND, -1).transpose(1, 0, 2, 3)
    return groups, slabs(pack_out, shards_of(w_out), gain_m), mlp


def whole_sums(p0_g, p1_g, po_g, pm_g):
    both = ("dp", "seq")

    def scattered(x):
        return lax.psum_scatter(x.reshape(WIDTH, -1), both, scatter_dimension=0, tiled=True)

    parts = [jax.vmap(unpack_group)(p.reshape((GROUPS * LINE,) + p.shape[2:]).astype(F32)) for p in (p0_g, p1_g)]
    columns = [parts[0][0], parts[1][0], parts[0][1], parts[1][1], parts[0][2], parts[0][3], parts[1][2], parts[1][3]]
    g_qkv, gain_a = scattered(jnp.concatenate(columns, -1)), scattered(parts[1][4][..., :1])[:, 0]
    po = po_g.reshape(GROUPS * LINE, 2 * SLIVER, -1).astype(F32)
    g_out = scattered(jnp.concatenate([po[:, :SLIVER, :HALF], po[:, SLIVER:, :HALF]], -1))
    gain_m = scattered(po[:, :SLIVER, HALF : HALF + 1])[:, 0]
    mlp = pm_g.astype(F32).transpose(1, 0, 2, 3).reshape(LINE, WIDTH, -1)
    mlp = lax.psum_scatter(mlp, "seq", scatter_dimension=0, tiled=False)
    gate, up, down = unpack_mlp(lax.psum_scatter(mlp, "dp", scatter_dimension=0, tiled=True))
    return g_qkv, g_out, gain_a, gain_m, jnp.stack([gate, up], 1), down.T


def on_device(tokens, w_qkv, w_out, attn_gain, mlp_gain, w_in, w_down, grad_out, *, dp, nz):
    rows = tokens.shape[0]
    masks = (dp // 2, dp // 4, 1) if dp == GROUPS else None
    tables = jnp.asarray(rope_tables(nz * rows)).reshape(nz, rows, 128)
    if masks:
        weights = [w_qkv, w_out, attn_gain[None], mlp_gain[None], w_in, w_down]
        got = front(tokens, grad_out, weights, tables, nz, masks)
        po_all, pm_all = got[-2:]
    else:
        groups, po_all, pm_all = whole_packs(w_qkv, w_out, attn_gain, mlp_gain, w_in, w_down)
        got = front(tokens, grad_out, groups, tables, nz, None)
    mixed, lse, query, gain, tok_own, gout_own, kv, firsts, wqkv = got[:9]
    out_own, gmid, gmixed, delta, po_g, pm_g = middle(tok_own, mixed, gout_own, po_all, pm_all)
    found = back(tok_own, gmid, out_own, query, kv, firsts, wqkv, gain, gmixed, lse, delta, tables, [po_g, pm_g], nz, masks)
    gtok, out, *sums = found
    if not masks:
        return (out, gtok, *whole_sums(*sums, po_g, pm_g))
    out, gtok, g_qkv, g_out, gain_a, gain_m, g_in, g_down = finish(out, gtok, *sums)
    return out, gtok, g_qkv, g_out, gain_a[0], gain_m[0], g_in, g_down


def solution(mesh):
    both = P(("dp", "seq"), None)
    vector = P(("dp", "seq"))
    w_in, w_down = P("dp", None, "seq"), P("seq", "dp")
    step = functools.partial(on_device, dp=mesh.shape["dp"], nz=mesh.shape["seq"])
    return jax.shard_map(
        step,
        mesh=mesh,
        in_specs=(both, both, both, vector, vector, w_in, w_down, both),
        out_specs=(both, both, both, both, vector, vector, w_in, w_down),
        check_vma=False,
    )
```

```python
import functools
import math

import jax
import jax.numpy as jnp
import numpy as np
from jax import lax
from jax.experimental import pallas as pl
from jax.experimental.pallas import tpu as pltpu
from jax.sharding import PartitionSpec as P

HEADS = 12
HEAD_DIM = 64
NORM_EPS = 1e-05
ROPE_THETA = 160000.0

F32 = jnp.float32
BF = jnp.bfloat16
MESH = pl.DeviceIdType.MESH
NT = (((1,), (1,)), ((), ()))
NN = (((1,), (0,)), ((), ()))
TN = (((0,), (0,)), ((), ()))

WIDTH = 768
PAIRS = HEADS // 2
UNITS = 1152
GROUPS = 8
LINE = 4
BAND = WIDTH // GROUPS
SLIVER = BAND // LINE
SHARE = UNITS // LINE
MAIN = 256
REST = SHARE - MAIN
LINKED = (0, 1, 3, 2)
HALF = WIDTH // 2
CUTS = {640: 256, 512: 256, 896: 384}
LOG2E = math.log2(math.e)
SCALE = HEAD_DIM**-0.5


def dot(a, b, dims):
    return lax.dot_general(a, b, dims, preferred_element_type=F32)


def lanes_of(tile, width=128):
    return pl.ds(pl.multiple_of(tile * width, width), width)


def tiles(start, width):
    return pl.ds(pl.multiple_of(start, width if width < 128 else 128), width)


def lane_iota():
    return lax.broadcasted_iota(jnp.int32, (1, 128), 1)


def swap_halves(u):
    low = lax.rem(lane_iota(), 64) < 32
    return jnp.where(low, pltpu.roll(u, 96, 1), pltpu.roll(u, 32, 1))


def rope(u, cos, sine):
    return u * cos + swap_halves(u) * sine


def rope_back(u, cos, sine):
    return u * cos - swap_halves(u) * sine


def rope_tables(rows):
    position = np.arange(rows, dtype=np.float32)
    half = HEAD_DIM // 2
    freq = (ROPE_THETA ** (-np.arange(half) * 2.0 / HEAD_DIM)).astype(np.float32)
    angle = (position[:, None] * freq[None, :]).astype(np.float64)
    cos, sine = np.cos(angle), np.sin(angle)
    return np.concatenate([cos, cos, -sine, sine], 1).astype(np.float32)


def spread_tables(cos, sine):
    low = lane_iota() < 64

    def chunk(c, _):
        both = cos[c]
        other = pltpu.roll(both, 64, 1)
        cos[c] = jnp.where(low, both, other)
        sine[c] = jnp.where(low, other, both)
        return 0

    lax.fori_loop(0, cos.shape[0], chunk, 0)


def normed(x):
    centred = x - jnp.mean(x, -1, keepdims=True)
    inv = lax.rsqrt(jnp.mean(centred * centred, -1, keepdims=True) + NORM_EPS)
    return centred * inv, inv


def norm_back(dy, gain, hat, inv):
    d = dy * gain
    return inv * (d - jnp.mean(d, -1, keepdims=True) - hat * jnp.mean(d * hat, -1, keepdims=True))


def remote(src, dst, send, recv, device):
    return pltpu.make_async_remote_copy(src, dst, send, recv, device_id=device, device_id_type=MESH)


class Place:
    def __init__(self, nz):
        self.dp, self.z = lax.axis_index("dp"), lax.axis_index("seq")
        self.nz = nz
        upper = self.z // (nz // 2)
        self.moves = lax.rem(self.dp, 2) != upper
        self.stays = lax.rem(self.dp, 2) == upper
        self.shard = jnp.where(self.moves, nz - 1 - self.z, self.z)
        self.opposite = {"dp": self.dp ^ 1, "seq": nz - 1 - self.z}
        self.twin = {"dp": self.dp ^ 1}
        self.beside = {"seq": self.z ^ 1}

    def greet(self, masks):
        bar = pltpu.get_barrier_semaphore()

        def hello(device):
            pl.semaphore_signal(bar, inc=1, device_id=device, device_id_type=MESH)

        for o in range(1, self.nz):
            hello({"seq": lax.rem(self.z + o, self.nz)})
        for m in masks:
            hello({"dp": self.dp ^ m})
        hello(self.opposite)
        pl.semaphore_wait(bar, self.nz + len(masks))


class Gather:
    COPIES = 9

    def __init__(self, src, out, cut, nz, masks, send, recv):
        self.src, self.out, self.cut, self.nz, self.masks = src, out, cut, nz, masks
        self.send, self.recv = send, recv
        self.dp, self.z = lax.axis_index("dp"), lax.axis_index("seq")
        self.started = []
        self.relayed = None

    @staticmethod
    def sems(nz):
        return Gather.COPIES * nz + nz

    def key(self, o, k):
        return o * self.COPIES + k

    def copy(self, src, dst, device, k):
        return remote(src, dst, self.send.at[k], self.recv.at[k], device)

    def begin(self, src, dst, device, k, p=None):
        self.copy(src, dst, device, k).start()
        self.started.append((k, p))

    def arrived(self, ref, k):
        self.copy(ref, ref, {"dp": self.dp ^ self.masks[0]}, k).wait_recv()

    def slot(self, o):
        return self.z ^ LINKED[o]

    def part(self, ref, p):
        if p is None:
            return ref
        width = self.out.shape[-1]
        return ref.at[:, pl.ds(0, self.cut)] if p == 0 else ref.at[:, pl.ds(self.cut, width - self.cut)]

    def along(self, o):
        self.begin(self.src, self.out.at[self.dp, self.z], {"seq": self.z ^ LINKED[o]}, self.COPIES * self.nz + o)

    def relay(self, o):
        ref = self.out.at[self.dp, self.slot(o)]
        self.arrived(ref, self.COPIES * self.nz + o)
        self.relayed = o
        self.begin(ref, ref, {"seq": self.z ^ 1}, self.COPIES * self.nz + 3)

    def forward(self, src, d, s, mask, k, p=None):
        dst = self.out.at[d, s]
        self.begin(self.part(src, p), self.part(dst, p), {"dp": self.dp ^ mask}, k, p)

    def first(self, o):
        my, mx, mc = self.masks
        s = self.slot(o)
        src = self.src
        if o:
            src = self.out.at[self.dp, s]
            if o != self.relayed:
                self.arrived(src, self.COPIES * self.nz + o)
        self.forward(src, self.dp, s, my, self.key(o, 0))
        self.forward(src, self.dp, s, mx, self.key(o, 1))
        self.forward(src, self.dp, s, mc, self.key(o, 2))

    def second(self, o):
        my, mx, mc = self.masks
        s = self.slot(o)
        for m, k, k2, kc, p, m2 in ((my, 0, 3, 4, 0, mx), (mx, 1, 5, 6, 1, my)):
            ref = self.out.at[self.dp ^ m, s]
            self.arrived(ref, self.key(o, k))
            self.forward(ref, self.dp ^ m, s, m2, self.key(o, k2), p)
            self.forward(ref, self.dp ^ m, s, mc, self.key(o, kc))

    def third(self, o):
        my, mx, mc = self.masks
        s = self.slot(o)
        d = self.dp ^ my ^ mx
        for p, k, kc in ((0, 3, 7), (1, 5, 8)):
            ref = self.out.at[d, s]
            self.arrived(self.part(ref, p), self.key(o, k))
            self.forward(ref, d, s, mc, self.key(o, kc), p)

    def finish(self, o):
        my, mx, mc = self.masks
        s = self.slot(o)
        for k, d in ((2, mc), (4, mc ^ my), (6, mc ^ mx)):
            self.arrived(self.out.at[self.dp ^ d, s], self.key(o, k))
        for k, p in ((7, 0), (8, 1)):
            self.arrived(self.part(self.out.at[self.dp ^ mc ^ my ^ mx, s], p), self.key(o, k))

    def done(self):
        for k, p in self.started:
            ref = self.part(self.out.at[self.dp, self.z], p)
            self.copy(ref, ref, {"dp": self.dp ^ self.masks[0]}, k).wait_send()


def pack_group(w, tile, i):
    q, k, v = [w[:, WIDTH * j + HALF * i : WIDTH * j + HALF * i + HALF] for j in range(3)]
    return jnp.concatenate([jnp.concatenate([q, v[:, :256]], 1), jnp.concatenate([k, v[:, 256:], tile], 1)], 0)


def unpack_group(total):
    r = total.shape[0] // 2
    upper, lower = total[:r], total[r:]
    return upper[:, :HALF], lower[:, :HALF], upper[:, HALF:], lower[:, HALF : HALF + 128], lower[:, HALF + 128 :]


def pack_out(w, tile):
    return jnp.concatenate([jnp.concatenate([w[:, :HALF], w[:, HALF:]], 0), jnp.concatenate([tile, jnp.zeros_like(tile)], 0)], 1)


def pack_mlp(gate, up, down):
    parts = (gate, up, down)
    pads = jnp.zeros((gate.shape[0], 128 - 3 * REST), gate.dtype)
    return jnp.concatenate([x[:, :MAIN] for x in parts] + [x[:, MAIN:] for x in parts] + [pads], 1)


def unpack_mlp(total):
    return [
        jnp.concatenate([total[:, MAIN * i : MAIN * i + MAIN], total[:, 3 * MAIN + REST * i : 3 * MAIN + REST * i + REST]], 1)
        for i in range(3)
    ]


def front_kernel(nz, masks, rows, *refs):
    fused = masks is not None
    if fused:
        (tok, gout, w_qkv, w_out, gain_a, gain_m, w_in, w_down, cos_in), refs = refs[:9], refs[9:]
    else:
        (tok, gout, g0_all, g1_all, cos_in), refs = refs[:5], refs[5:]
    (mixed, lse, query, gain, tok_own, gout_own, kv, firsts, wqkv), refs = refs[:9], refs[9:]
    if fused:
        (po_all, pm_all), refs = refs[:2], refs[2:]
    (tok_all, kvb, fb, wq, cos, sine, gcol, acc, top, total, tsend, trecv, loc), refs = refs[:13], refs[13:]
    me = Place(nz)
    own = me.shard

    def here(src, dst, k):
        return pltpu.make_async_copy(src, dst, loc.at[k])

    def there(src, dst, device, k):
        return remote(src, dst, tsend.at[k], trecv.at[k], device)

    def rows_to(src, c, device, k, i):
        at = pl.ds(i * (rows // 2), rows // 2)
        src = tok_all.at[c] if src is None else src
        return there(src.at[at], tok_all.at[c, at], device, k + 5 * i)

    @pl.when(me.stays)
    def _():
        here(tok, tok_all.at[own], 0).start()
        here(gout, gout_own, 1).start()

    here(cos_in, cos, 2).start()
    groups, later = [], []
    every, rest = range(nz), (2, 1, 3)
    if fused:
        p0, p1, po, pm, g0_all, g1_all, *sems = refs
        row = lax.broadcasted_iota(jnp.int32, (128, 128), 0)

        def tile_of(part):
            line = jnp.concatenate([part[...].astype(F32), jnp.zeros((1, 128 - SLIVER), F32)], 1)
            return jnp.where(row == 0, line, 0.0).T[:SLIVER]

        p0[...] = pack_group(w_qkv[...].astype(F32), tile_of(gain_a), 0).astype(BF)
        g0_all[me.dp, me.z] = p0[...]
    me.greet(masks or (1,))
    if fused:
        shapes = ((p0, g0_all), (p1, g1_all), (po, po_all), (pm, pm_all))
        packs = [
            Gather(src, dst, CUTS[src.shape[-1]], nz, masks, sems[2 * i], sems[2 * i + 1]) for i, (src, dst) in enumerate(shapes)
        ]
        groups, later = packs[:2], packs[2:]
        for o in rest:
            groups[0].along(o)
        groups[0].first(0)

    @pl.when(me.stays)
    def _():
        for i in range(2):
            rows_to(tok, own, me.twin, 1, i).start()
            rows_to(tok, own, me.beside, 2, i).start()

    @pl.when(me.moves)
    def _():
        for i in range(2):
            rows_to(tok, me.z, me.opposite, 0, i).start()

    def swapped(i):
        @pl.when(me.moves)
        def _():
            rows_to(None, own, me.opposite, 0, i).wait_recv()
            rows_to(None, own, me.beside, 2, i).start()
            rows_to(None, own, me.twin, 1, i).start()

    if fused:
        w = w_qkv[...].astype(F32)
        p1[...] = pack_group(w, jnp.zeros((SLIVER, 128), F32), 1).astype(BF)
        g1_all[me.dp, me.z] = p1[...]
        po[...] = pack_out(w_out[...].astype(F32), tile_of(gain_m)).astype(BF)
        pm[...] = pack_mlp(w_in[:, 0, :].astype(F32), w_in[:, 1, :].astype(F32), w_down[...].astype(F32).T).astype(BF)
        here(po, po_all.at[me.dp, me.z], 4).start()
        here(pm, pm_all.at[me.dp, me.z], 5).start()
        for o in rest:
            groups[1].along(o)
        groups[1].first(0)
        groups[0].second(0)
        for o in rest:
            groups[0].first(o)
        swapped(0)
        for o in rest:
            groups[0].second(o)
        for o in rest:
            groups[1].first(o)
        for g in later:
            g.along(1)
            g.first(0)

    if not fused:
        swapped(0)
    swapped(1)

    @pl.when(me.stays)
    def _():
        here(tok, tok_all.at[own], 0).wait()

    here(tok_all.at[own], tok_own, 6).start()
    if fused:
        for g in later:
            g.along(2)
        for o in range(nz):
            groups[0].third(o)
        for o in range(nz):
            groups[0].finish(o)

    @pl.when(me.moves)
    def _():
        there(gout, gout_own, me.opposite, 4).start()

    here(cos_in, cos, 2).wait()
    spread_tables(cos, sine)

    def build(i, whole):
        def band_of(g, _):
            slabs = [unpack_group(whole[g, s].astype(F32)) for s in range(LINE)]
            band = pl.ds(pl.multiple_of(g * BAND, BAND), BAND)
            q, k, v0, v1, t = [jnp.concatenate([x[j] for x in slabs], 0) for j in range(5)]
            at = WIDTH * i
            wq[band, at : at + HALF] = k.astype(BF)
            wq[band, at + HALF : at + HALF + 256] = v0.astype(BF)
            wq[band, at + HALF + 256 : at + WIDTH] = v1.astype(BF)
            wq[band, 2 * WIDTH + HALF * i : 2 * WIDTH + HALF * i + HALF] = q.astype(BF)
            if i == 0:
                gcol[band, :] = t
            return 0

        lax.fori_loop(0, GROUPS, band_of, 0)

    def norm_chunk(c):
        def block(i, _):
            at = pl.ds(pl.multiple_of(i * 64, 64), 64)
            hat, _ = normed(tok_all[c, at, :].astype(F32))
            fb[c, at, :] = (hat * gain[0:1, :]).astype(BF)
            return 0

        lax.fori_loop(0, rows // 64, block, 0)
        here(fb.at[c], firsts.at[c], 8 + c).start()

    def queries(i):
        u = dot(fb[own], wq[:, 2 * WIDTH + HALF * i : 2 * WIDTH + HALF * i + HALF], NN)
        for j in range(3):
            tile = rope(u[:, 128 * j : 128 * j + 128], cos[own], sine[own])
            query[:, HALF * i + 128 * j : HALF * i + 128 * j + 128] = (tile * (SCALE * LOG2E)).astype(BF)

    def visits(steps):
        def visit(n, _):
            t, grp = lax.rem(n, nz), n // nz
            stay = jnp.where(t == 1, 1, jnp.where(t == 2, 3, 2))
            move = jnp.where(t == 1, 3, jnp.where(t == 2, 2, 1))
            turn = jnp.where(me.stays, stay, move)
            c = jnp.where(t == 0, own, own ^ turn)
            @pl.when((n > 0) & (n < nz))
            def _():
                for i in range(2):
                    rows_to(None, c, me.twin, jnp.where(turn == 1, 2, jnp.where(turn == 3, 1, 3)), i).wait_recv()

                    @pl.when(turn == 1)
                    def _(i=i):
                        rows_to(None, c, me.twin, 3, i).start()

                norm_chunk(c)

            for j in range(3):
                u = dot(fb[c], wq[:, tiles(WIDTH * grp + 256 * j, 256)], NN)
                for i in range(2):
                    tile = 2 * j + i
                    x = u[:, 128 * i : 128 * i + 128]
                    x = rope(x, cos[c], sine[c]) if tile < 3 else x
                    kvb[grp, c, :, 128 * tile : 128 * tile + 128] = x.astype(BF)
            here(kvb.at[grp, c], kv.at[grp, c], 8 + nz * (1 + grp) + c).start()
            jobs = [(i, h) for i in range(3) for h in range(2)]

            def score(i, h):
                q = query[:, tiles(HALF * grp + 128 * i, 128)]
                mask = (lane_iota() < 64) if h == 0 else (lane_iota() >= 64)
                return dot(kvb[grp, c, :, 128 * i : 128 * i + 128], jnp.where(mask, q, jnp.zeros_like(q)), NT)

            ready = [score(*j) for j in jobs[:2]]
            for m, (i, h) in enumerate(jobs):
                if h == 0:
                    vt = kvb[grp, c, :, HALF + 128 * i : HALF + 128 * i + 128].T
                s = ready[m]
                if m + 2 < len(jobs):
                    ready.append(score(*jobs[m + 2]))
                head = pl.ds(6 * grp + m, 1)
                band = tiles(64 * (6 * grp + m), 64)
                old = top[head, :]
                new = jnp.maximum(old, jnp.max(s, 0, keepdims=True))
                p = jnp.exp2(s - new)
                fade = jnp.exp2(old - new)
                top[head, :] = new
                lhs = jnp.concatenate([vt[h * 64 : h * 64 + 64], jnp.ones((16, rows), BF)], 0)
                oo = dot(lhs, p.astype(BF), NN)
                total[head, :] = total[head, :] * fade + oo[64:65]
                acc[band, :] = acc[band, :] * fade + oo[:64]
            for k, step in steps.items():

                @pl.when(n == k)
                def _(k=k, step=step):
                    for which, name, order in step:
                        for g in which:
                            for o in order:
                                getattr(g, name)(o)
                    if k == nz - 1:
                        build(1, g1_all)
                        here(wq, wqkv, 7).start()
                        queries(1)

            return 0

        lax.fori_loop(0, 2 * nz, visit, 0)

    build(0, g0_all)
    gain[...] = gcol[...].T[:8]
    norm_chunk(own)
    queries(0)
    acc[...] = jnp.zeros_like(acc)
    total[...] = jnp.zeros_like(total)
    top[...] = jnp.full_like(top, -1e30)
    one = groups[1:]
    visits({
        0: [(one, "second", every), (later, "first", (1,))],
        1: [(one, "third", every)],
        2: [(later, "relay", (2,)), (later, "first", (2,))],
        3: [(one, "finish", every), (later, "second", (0, 1))],
        4: [(later, "first", (3,))],
        5: [(later, "second", (2,))],
        6: [(later, "second", (3,))],
        7: [(later, "third", every)],
    })

    for hp in range(PAIRS):
        parts = [
            acc[128 * hp + 64 * h : 128 * hp + 64 * h + 64, :] / total[2 * hp + h : 2 * hp + h + 1, :] for h in range(2)
        ]
        mixed[:, 128 * hp : 128 * hp + 128] = jnp.concatenate(parts, 0).T.astype(BF)
    lse[...] = top[...] + jnp.log(jnp.maximum(total[...], 1e-30)) * LOG2E

    if fused:
        for g in later:
            for o in range(nz):
                g.finish(o)
        for g in packs:
            g.done()
        here(po, po_all.at[me.dp, me.z], 4).wait()
        here(pm, pm_all.at[me.dp, me.z], 5).wait()
    for i in range(2):
        for k in (1, 2, 3):
            rows_to(None, own, me.twin, k, i).wait_send()

    @pl.when(me.moves)
    def _():
        for i in range(2):
            rows_to(None, own, me.opposite, 0, i).wait_send()
        there(gout, gout_own, me.opposite, 4).wait()

    @pl.when(me.stays)
    def _():
        here(gout, gout_own, 1).wait()

    here(tok_all.at[own], tok_own, 6).wait()
    here(wq, wqkv, 7).wait()
    for c in range(nz):
        here(fb.at[c], firsts.at[c], 8 + c).wait()
        for grp in range(2):
            here(kvb.at[grp, c], kv.at[grp, c], 8 + nz * (1 + grp) + c).wait()


def front(tok, gout, weights, tables, nz, masks):
    rows = tok.shape[0]
    vmem, anyspace = pl.BlockSpec(memory_space=pltpu.VMEM), pl.BlockSpec(memory_space=pl.ANY)
    shape, vm = jax.ShapeDtypeStruct, pltpu.VMEM
    outs = [shape((rows, WIDTH), BF), shape((16, rows), F32), shape((rows, WIDTH), BF), shape((8, WIDTH), F32)]
    outs += [shape((rows, WIDTH), BF)] * 2
    outs += [shape((2, nz, rows, WIDTH), BF), shape((nz, rows, WIDTH), BF), shape((WIDTH, 3 * WIDTH), BF)]
    out_specs = [vmem] * 4 + [anyspace, vmem] + [anyspace] * 3
    scratch = [
        vm((nz, rows, WIDTH), BF),
        vm((2, nz, rows, WIDTH), BF),
        vm((nz, rows, WIDTH), BF),
        vm((WIDTH, 3 * WIDTH), BF),
        vm((nz, rows, 128), F32),
        vm((nz, rows, 128), F32),
        vm((WIDTH, 128), F32),
        vm((WIDTH, rows), F32),
        vm((16, rows), F32),
        vm((16, rows), F32),
        pltpu.SemaphoreType.DMA((9,)),
        pltpu.SemaphoreType.DMA((9,)),
        pltpu.SemaphoreType.DMA((8 + 3 * nz,)),
    ]
    if masks:
        grp, out, mlp = (2 * SLIVER, 640), (2 * SLIVER, 512), (BAND, 896)
        outs += [shape((GROUPS, nz) + out, BF), shape((GROUPS, nz) + mlp, BF)]
        out_specs += [anyspace] * 2
        scratch += [vm(x, BF) for x in (grp, grp, out, mlp)] + [vm((GROUPS, nz) + grp, BF)] * 2
        scratch += [pltpu.SemaphoreType.DMA((Gather.sems(nz),)) for _ in range(8)]
    return pl.pallas_call(
        functools.partial(front_kernel, nz, masks, rows),
        out_shape=outs,
        in_specs=[anyspace] * 2 + [vmem] * len(weights) + [anyspace],
        out_specs=out_specs,
        scratch_shapes=scratch,
        compiler_params=pltpu.CompilerParams(collective_id=0, has_side_effects=True, vmem_limit_bytes=60 << 20),
        cost_estimate=pl.CostEstimate(flops=14_000_000_000, bytes_accessed=40_000_000, transcendentals=13_000_000),
        name="front",
    )(tok, gout, *weights, tables)


def middle_kernel(rows, tok, mixed, gout, po_all, pm_in, out_own, gmid_own, gmixed, delta, po_g, pm_sums,
                  pm_all, pm_g, out, gmid, loc, wout, wg, wu, wd, gcol, gain, resid, hat, inv, second, hidden, ggate, gup, gsec, gattn, dwout):
    lane = lane_iota()

    def here(src, dst, k):
        return pltpu.make_async_copy(src, dst, loc.at[k])

    here(pm_in, pm_all, 0).start()

    def build(g, _):
        band = pl.ds(pl.multiple_of(g * BAND, BAND), BAND)
        slabs = [po_all[g, s].astype(F32) for s in range(LINE)]
        wout[band, :384] = jnp.concatenate([x[:SLIVER, :384] for x in slabs], 0).astype(BF)
        wout[band, 384:] = jnp.concatenate([x[SLIVER:, :384] for x in slabs], 0).astype(BF)
        gcol[band, :] = jnp.concatenate([x[:SLIVER, 384:] for x in slabs], 0)
        return 0

    def build_units(g, _):
        band = pl.ds(pl.multiple_of(g * BAND, BAND), BAND)
        for i, w in enumerate((wg, wu, wd)):
            tail = jnp.zeros((BAND, 128), F32)
            for s in range(LINE):
                w[band, MAIN * s : MAIN * s + MAIN] = pm_all[g, s, :, MAIN * i : MAIN * i + MAIN]
                rest = pm_all[g, s, :, 3 * MAIN :].astype(F32)
                turn = (REST * (s - i)) % 128
                rest = pltpu.roll(rest, turn, 1) if turn else rest
                tail = jnp.where((lane >= REST * s) & (lane < REST * (s + 1)), rest, tail)
            w[band, MAIN * LINE :] = tail.astype(BF)
        return 0

    lax.fori_loop(0, GROUPS, build, 0)
    gain[...] = gcol[...].T[:8]

    for j in range(3):
        at = slice(256 * j, 256 * j + 256)
        resid[:, at] = tok[:, at].astype(F32) + dot(mixed[...], wout[:, at], NN)

    def norm_block(i, _):
        at = pl.ds(pl.multiple_of(i * 64, 64), 64)
        h, r = normed(resid[at, :])
        hat[at, :] = h
        inv[at, :] = jnp.broadcast_to(r, (64, 128))
        second[at, :] = (h * gain[0:1, :]).astype(BF)
        return 0

    lax.fori_loop(0, rows // 64, norm_block, 0)
    here(pm_in, pm_all, 0).wait()
    lax.fori_loop(0, GROUPS, build_units, 0)

    def units(start, width):
        at = pl.ds(start, width)
        gate, up, gh = dot(second[...], wg[:, at], NN), dot(second[...], wu[:, at], NN), dot(gout[...], wd[:, at], NN)
        cdf = 0.5 + 0.5 * lax.erf(gate * math.sqrt(0.5))
        pdf = jnp.exp2(gate * gate * (-0.5 * LOG2E)) * (1.0 / math.sqrt(2.0 * math.pi))
        act = gate * cdf
        hidden[:, at] = (act * up).astype(BF)
        gup[:, at] = (gh * act).astype(BF)
        ggate[:, at] = (gh * up * (cdf + gate * pdf)).astype(BF)

    for start in range(0, UNITS, 256):
        units(start, min(256, UNITS - start))

    for j in range(3):
        at = slice(256 * j, 256 * j + 256)
        out[:, at] = (resid[:, at] + dot(hidden[...], wd[at, :], NT)).astype(BF)
        gsec[:, at] = dot(ggate[...], wg[at, :], NT) + dot(gup[...], wu[at, :], NT)

    here(out, out_own, 1).start()

    for j in range(2):
        at = slice(384 * j, 384 * j + 384)
        tails = []
        for i, (a, b) in enumerate(((second, ggate), (second, gup), (gout, hidden))):
            for s in range(LINE):
                x = dot(a[:, at], b[:, MAIN * s : MAIN * s + MAIN], TN).astype(BF)
                for g in range(4):
                    pm_g[4 * j + g, s, :, MAIN * i : MAIN * i + MAIN] = x[BAND * g : BAND * g + BAND]
            tails.append(dot(a[:, at], b[:, MAIN * LINE :], TN))
        for s in range(LINE):
            y = jnp.zeros((384, 128), F32)
            for i, tail in enumerate(tails):
                turn = (REST * (i - s)) % 128
                tail = pltpu.roll(tail, turn, 1) if turn else tail
                y = jnp.where((lane >= REST * i) & (lane < REST * (i + 1)), tail, y)
            y = y.astype(BF)
            for g in range(4):
                pm_g[4 * j + g, s, :, 3 * MAIN :] = y[BAND * g : BAND * g + BAND]
        here(pm_g.at[pl.ds(4 * j, 4)], pm_sums.at[pl.ds(4 * j, 4)], 3 + j).start()

    def back_block(i, dgain):
        at = pl.ds(pl.multiple_of(i * 64, 64), 64)
        dy, h = gsec[at, :], hat[at, :]
        gm = gout[at, :].astype(F32) + norm_back(dy, gain[0:1, :], h, inv[at, 0:1])
        gmid[at, :] = gm
        gattn[at, :] = gm.astype(BF)
        return dgain + jnp.sum(dy * h, 0, keepdims=True)

    dgain = lax.fori_loop(0, rows // 64, back_block, jnp.zeros((1, WIDTH), F32))

    here(gmid, gmid_own, 2).start()
    heads = lax.broadcasted_iota(jnp.int32, (16, 256), 0)
    for j in range(3):
        at = slice(256 * j, 256 * j + 256)
        gmx = dot(gattn[...], wout[at, :], NT).astype(BF)
        gmixed[:, at] = gmx
        prod = gmx.astype(F32) * mixed[:, at].astype(F32)
        high = prod.astype(BF)
        low = (prod - high.astype(F32)).astype(BF)
        pick = ((lax.broadcasted_iota(jnp.int32, (16, 256), 1) + 256 * j) // HEAD_DIM == heads).astype(BF)
        part = dot(pick, high, NT) + dot(pick, low, NT)
        delta[...] = part if j == 0 else delta[...] + part

    for j in range(2):
        at = slice(384 * j, 384 * j + 384)
        dwout[at, :] = dot(mixed[:, at], gattn[...], TN)
    row = lax.broadcasted_iota(jnp.int32, (128, WIDTH), 0)
    gcol[...] = jnp.where(row == 0, dgain, 0.0).T

    def pack_out(g, _):
        for s in range(LINE):
            at = pl.ds(pl.multiple_of(g * BAND + s * SLIVER, 8), SLIVER)
            x, c = dwout[at, :], gcol[at, :]
            po_g[g, s, :, :384] = jnp.concatenate([x[:, :384], x[:, 384:]], 0).astype(BF)
            po_g[g, s, :, 384:] = jnp.concatenate([c, jnp.zeros_like(c)], 0).astype(BF)
        return 0

    lax.fori_loop(0, GROUPS, pack_out, 0)

    here(out, out_own, 1).wait()
    here(gmid, gmid_own, 2).wait()
    for j in range(2):
        here(pm_g.at[pl.ds(4 * j, 4)], pm_sums.at[pl.ds(4 * j, 4)], 3 + j).wait()


def middle(tok, mixed, gout, po_all, pm_all):
    rows = tok.shape[0]
    shape, vm = jax.ShapeDtypeStruct, pltpu.VMEM
    vmem, anyspace = pl.BlockSpec(memory_space=pltpu.VMEM), pl.BlockSpec(memory_space=pl.ANY)
    return pl.pallas_call(
        functools.partial(middle_kernel, rows),
        out_shape=[
            shape((rows, WIDTH), BF),
            shape((rows, WIDTH), F32),
            shape((rows, WIDTH), BF),
            shape((16, rows), F32),
            shape(po_all.shape, BF),
            shape(pm_all.shape, BF),
        ],
        in_specs=[vmem] * 4 + [anyspace],
        out_specs=[anyspace, anyspace, vmem, vmem, vmem, anyspace],
        scratch_shapes=[
            vm(pm_all.shape, BF),
            vm(pm_all.shape, BF),
            vm((rows, WIDTH), BF),
            vm((rows, WIDTH), F32),
            pltpu.SemaphoreType.DMA((5,)),
            vm((WIDTH, WIDTH), BF),
            vm((WIDTH, UNITS), BF),
            vm((WIDTH, UNITS), BF),
            vm((WIDTH, UNITS), BF),
            vm((WIDTH, 128), F32),
            vm((8, WIDTH), F32),
            vm((rows, WIDTH), F32),
            vm((rows, WIDTH), F32),
            vm((rows, 128), F32),
            vm((rows, WIDTH), BF),
            vm((rows, UNITS), BF),
            vm((rows, UNITS), BF),
            vm((rows, UNITS), BF),
            vm((rows, WIDTH), F32),
            vm((rows, WIDTH), BF),
            vm((WIDTH, WIDTH), F32),
        ],
        compiler_params=pltpu.CompilerParams(vmem_limit_bytes=58 << 20),
        cost_estimate=pl.CostEstimate(flops=11_000_000_000, bytes_accessed=25_000_000, transcendentals=1_200_000),
        name="middle",
    )(tok, mixed, gout, po_all, pm_all)


class Reduce:
    COPIES = 10

    def __init__(self, src, total, cut, nz, masks, bufs, send, recv, loc=None):
        self.src, self.total, self.cut, self.nz, self.masks = src, total, cut, nz, masks
        self.near, self.side0, self.side1, self.far, *mine = bufs
        self.mine = mine[0] if mine else None
        self.send, self.recv, self.loc = send, recv, loc
        self.dp, self.z = lax.axis_index("dp"), lax.axis_index("seq")
        my, mx, mc = masks
        self.turns = (0, my, mx, my ^ mx)
        self.started = []

    @staticmethod
    def scratch(shape, nz, held):
        r, c = shape
        cut = CUTS[c]
        bufs = [
            pltpu.VMEM((4, nz, r, c), BF),
            pltpu.VMEM((3, nz, r, cut), BF),
            pltpu.VMEM((3, nz, r, c - cut), BF),
            pltpu.VMEM((nz - 1, r, c), BF),
        ]
        sems = [pltpu.SemaphoreType.DMA((Reduce.COPIES * nz + nz,))] * 2
        if not held:
            bufs += [pltpu.VMEM((4, nz, r, c), BF)]
            sems += [pltpu.SemaphoreType.DMA((4 * nz,))]
        return bufs, sems

    def begin(self, src, dst, device, k):
        remote(src, dst, self.send.at[k], self.recv.at[k], device).start()
        self.started.append((k, src.shape[-1]))

    def arrived(self, ref, k):
        remote(ref, ref, self.send.at[k], self.recv.at[k], {"dp": self.dp ^ self.masks[2]}).wait_recv()

    def seat(self, o):
        return self.z ^ LINKED[o]

    def held(self, i, s):
        return self.mine.at[i, s] if self.mine is not None else self.src.at[self.dp ^ self.turns[i], s]

    def local(self, i, o):
        s = self.seat(o)
        return pltpu.make_async_copy(self.src.at[self.dp ^ self.turns[i], s], self.mine.at[i, s], self.loc.at[4 * o + i])

    def zero(self, o):
        s, mc = self.seat(o), self.masks[2]
        for i in (3, 1, 2, 0):
            if self.mine is not None:
                self.local(i, o).start()
            self.begin(self.src.at[self.dp ^ mc ^ self.turns[i], s], self.near.at[i, s], {"dp": self.dp ^ mc}, self.COPIES * o + i)

    def add(self, ref, other):
        ref[...] = (ref[...].astype(F32) + other[...].astype(F32)).astype(BF)

    def p0(self, i, s):
        return self.held(i, s).at[:, pl.ds(0, self.cut)]

    def p1(self, i, s):
        return self.held(i, s).at[:, pl.ds(self.cut, self.src.shape[-1] - self.cut)]

    def one(self, o):
        my, mx, _ = self.masks
        s, k = self.seat(o), self.COPIES * o
        for i in (3, 1, 2, 0):
            if self.mine is not None:
                self.local(i, o).wait()
            self.arrived(self.near.at[i, s], k + i)
            self.add(self.held(i, s), self.near.at[i, s])
            if i == 3:
                self.begin(self.p0(3, s), self.side0.at[1, s], {"dp": self.dp ^ my}, k + 4)
                self.begin(self.p1(3, s), self.side1.at[1, s], {"dp": self.dp ^ mx}, k + 5)
            if i == 1:
                self.begin(self.p0(1, s), self.side0.at[0, s], {"dp": self.dp ^ my}, k + 6)
            if i == 2:
                self.begin(self.p1(2, s), self.side1.at[0, s], {"dp": self.dp ^ mx}, k + 7)

    def two(self, o):
        my, mx, _ = self.masks
        s, k = self.seat(o), self.COPIES * o
        self.arrived(self.side0.at[1, s], k + 4)
        self.add(self.p0(2, s), self.side0.at[1, s])
        self.begin(self.p0(2, s), self.side0.at[2, s], {"dp": self.dp ^ mx}, k + 8)
        self.arrived(self.side1.at[1, s], k + 5)
        self.add(self.p1(1, s), self.side1.at[1, s])
        self.begin(self.p1(1, s), self.side1.at[2, s], {"dp": self.dp ^ my}, k + 9)

    def three(self, o):
        s, k = self.seat(o), self.COPIES * o
        for ref, side, k1, k2 in ((self.p0(0, s), self.side0, k + 6, k + 8), (self.p1(0, s), self.side1, k + 7, k + 9)):
            self.arrived(side.at[0, s], k1)
            self.arrived(side.at[2, s], k2)
            ref[...] = (ref[...].astype(F32) + side[0, s].astype(F32) + side[2, s].astype(F32)).astype(BF)
        if o:
            self.begin(self.held(0, s), self.far.at[o - 1], {"seq": s}, self.COPIES * self.nz + o)

    def four(self):
        out = self.held(0, self.z)[...].astype(F32)
        for o in range(1, self.nz):
            self.arrived(self.far.at[o - 1], self.COPIES * self.nz + o)
            out = out + self.far[o - 1].astype(F32)
        self.total[...] = out

    def done(self):
        for k, width in self.started:
            whole = width == self.src.shape[-1]
            ref = self.near.at[0, 0] if whole else (self.side0 if k % self.COPIES in (4, 6, 8) else self.side1).at[0, 0]
            remote(ref, ref, self.send.at[k], self.recv.at[k], {"dp": self.dp ^ self.masks[2]}).wait_send()


def back_kernel(nz, masks, rows, *refs):
    fused = masks is not None
    (tok, gmid, out_own, query, kv, firsts, wqkv, gain, gmixed, lse, delta, cos_in), refs = refs[:12], refs[12:]
    if fused:
        (po_g, pm_g, gtok, out, s0, s1, so, sm), refs = refs[:8], refs[8:]
    else:
        (gtok, out, p0_g, p1_g), refs = refs[:4], refs[4:]
    (kvb, fb, ft, wq, cos, sine, dq, dqb, dkv, dx, dw, sent, landed, gown, gcol, send, recv, loc), refs = refs[:18], refs[18:]
    me = Place(nz)
    own = me.shard

    def here(src, dst, k):
        return pltpu.make_async_copy(src, dst, loc.at[k])

    def there(src, dst, device, k):
        return remote(src, dst, send.at[k], recv.at[k], device)

    def chunk(t):
        return jnp.where(t == 0, own ^ 2, jnp.where(t == 1, own ^ 1, jnp.where(t == 2, own ^ 3, own)))

    def fetch(n):
        return here(kv.at[n // nz, chunk(lax.rem(n, nz))], kvb.at[lax.rem(n, 2)], lax.rem(n, 2))

    def fetch_first(t):
        return here(firsts.at[chunk(t)], fb.at[lax.rem(t, 2)], 2 + lax.rem(t, 2))

    fetch(0).start()
    fetch_first(0).start()
    whole = [here(wqkv, wq, 4), here(cos_in, cos, 5)]
    for c in whole:
        c.start()
    me.greet(masks or (1,))
    jobs, sums = [], []
    if fused:
        (p0_g, p1_g), refs = refs[:2], refs[2:]
        for src, total in ((p0_g, s0), (p1_g, s1)):
            sums.append(Reduce(src, total, CUTS[src.shape[-1]], nz, masks, refs[:4], *refs[4:6]))
            refs = refs[6:]
        for src, total in ((po_g, so), (pm_g, sm)):
            jobs.append(Reduce(src, total, CUTS[src.shape[-1]], nz, masks, refs[:5], *refs[5:8]))
            refs = refs[8:]
    order = (3, 2, 1, 0)

    def advance(which, step):
        for j in which:
            for o in order:
                getattr(j, step)(o)

    def wave(which):
        for i in range(nz + 2):
            for k, step in enumerate(("one", "two", "three")):
                if 0 <= i - k < nz:
                    for j in which:
                        getattr(j, step)(order[i - k])

    advance(jobs, "zero")

    @pl.when(me.moves)
    def _():
        there(out_own, out, me.opposite, 3).start()

    @pl.when(me.stays)
    def _():
        here(out_own, out, 7).start()

    dq[...] = jnp.zeros_like(dq)
    for c in whole:
        c.wait()
    spread_tables(cos, sine)

    def visits(steps):
        def visit(n, _):
            t, grp = lax.rem(n, nz), n // nz
            c, slot = chunk(t), lax.rem(t, 2)
            fetch(n).wait()

            @pl.when(n < nz)
            def _():
                fetch_first(t).wait()

            @pl.when(n + 1 < 2 * nz)
            def _():
                fetch(n + 1).start()

            @pl.when(n + 1 < nz)
            def _():
                fetch_first(n + 1).start()

            band = pl.ds(pl.multiple_of(t * rows, rows), rows)
            todo = [(i, h) for i in range(3) for h in range(2)]

            def pick(ref, i, h):
                x = ref[:, tiles(HALF * grp + 128 * i, 128)]
                mask = (lane_iota() < 64) if h == 0 else (lane_iota() >= 64)
                return jnp.where(mask, x, jnp.zeros_like(x))

            def score(i, h):
                qh, gh = pick(query, i, h), pick(gmixed, i, h)
                k, v = kvb[slot, :, 128 * i : 128 * i + 128], kvb[slot, :, HALF + 128 * i : HALF + 128 * i + 128]
                return dot(k, qh, NT), dot(v, gh, NT), qh, gh

            ready = [score(*todo[0])]
            dk = dv = None
            for m, (i, h) in enumerate(todo):
                s, dp, qh, gh = ready[m]
                if m + 1 < len(todo):
                    ready.append(score(*todo[m + 1]))
                if h == 0:
                    kt = kvb[slot, :, 128 * i : 128 * i + 128].T
                head = pl.ds(6 * grp + m, 1)
                rows_of = tiles(64 * (6 * grp + m), 64)
                p = jnp.exp2(s - lse[head, :])
                ds = (p * (dp - delta[head, :])).astype(BF)
                a = dot(p.astype(BF), gh, NN)
                dv = a if h == 0 else dv + a
                a = dot(ds, qh, NN)
                dk = a if h == 0 else dk + a
                dq[rows_of, :] += dot(kt[h * 64 : h * 64 + 64], ds, NN)
                if h == 1:
                    at = WIDTH * grp + 128 * i
                    dkv[band, tiles(at, 128)] = rope_back(dk * (1.0 / LOG2E), cos[c], sine[c]).astype(BF)
                    dkv[band, tiles(at + HALF, 128)] = dv.astype(BF)

            @pl.when(n < nz)
            def _():
                for j in range(6):
                    ft[128 * j : 128 * j + 128, band] = fb[slot, :, 128 * j : 128 * j + 128].T
            @pl.when(n >= nz)
            def _():
                for j in range(3):
                    at = slice(256 * j, 256 * j + 256)
                    dx[:, at] = dot(dkv[band, :], wq[at, : 2 * WIDTH], NT)

                @pl.when(lax.rem(t, 2) == 0)
                def _():
                    sent[t] = dx[...].astype(BF)
                    there(sent.at[t], landed.at[t], me.twin, t).start()

                @pl.when(t == 1)
                def _():
                    there(sent.at[0], landed.at[0], me.twin, 0).wait_recv()
                    sent[1] = (dx[...] + landed[0].astype(F32)).astype(BF)
                    there(sent.at[1], landed.at[1], me.beside, 1).start()

            for k, step in steps.items():

                @pl.when(n == k)
                def _(k=k, step=step):
                    if k == nz - 1:
                        close(0)
                        weigh(0)
                        pack(0, p0_g)
                    for which, name in step:
                        advance(which, name)

            return 0

        lax.fori_loop(0, 2 * nz, visit, 0)

    def close(grp):
        for i in range(3 * grp, 3 * grp + 3):
            at = slice(128 * i, 128 * i + 128)
            dqb[:, at] = rope_back(dq[at, :].T * SCALE, cos[own], sine[own]).astype(BF)

    def weigh(grp):
        for r in (slice(0, HALF), slice(HALF, WIDTH)):
            for j in range(3):
                at = WIDTH * grp + 256 * j
                dw[r, HALF + 256 * j : HALF + 256 * j + 256] = dot(ft[r, :], dkv[:, at : at + 256], NN)
            dw[r, :HALF] = dot(ft[r, (nz - 1) * rows :], dqb[:, HALF * grp : HALF * grp + HALF], NN)

    def pack(grp, dst):
        def band_of(g, _):
            for s in range(LINE):
                at = pl.ds(pl.multiple_of(g * BAND + s * SLIVER, 8), SLIVER)
                q, k, v0, v1 = dw[at, :HALF], dw[at, HALF:WIDTH], dw[at, WIDTH : WIDTH + 256], dw[at, WIDTH + 256 :]
                tile = gcol[at, :] if grp else jnp.zeros((SLIVER, 128), F32)
                dst[g, s] = jnp.concatenate(
                    [jnp.concatenate([q, v0], 1), jnp.concatenate([k, v1, tile], 1)], 0
                ).astype(BF)
            return 0

        lax.fori_loop(0, GROUPS, band_of, 0)

    early = sums[:1]
    visits({
        0: [(jobs, "one")],
        3: [(early, "zero")],
        4: [(jobs, "two"), (early, "one")],
        6: [(jobs, "three")],
        7: [(early, "two"), (early, "three")],
    })
    close(1)
    for j in range(3):
        at = slice(256 * j, 256 * j + 256)
        dx[:, at] += dot(dqb[...], wq[at, 2 * WIDTH :], NT)
    there(sent.at[1], landed.at[1], me.beside, 1).wait_recv()
    there(sent.at[2], landed.at[2], me.twin, 2).wait_recv()

    def norm_block(i, dgain):
        at = pl.ds(pl.multiple_of(i * 64, 64), 64)
        dy = dx[at, :] + landed[1, at, :].astype(F32) + landed[2, at, :].astype(F32)
        h, r = normed(tok[at, :].astype(F32))
        gown[at, :] = (gmid[at, :] + norm_back(dy, gain[0:1, :], h, r)).astype(BF)
        return dgain + jnp.sum(dy * h, 0, keepdims=True)

    dgain = lax.fori_loop(0, rows // 64, norm_block, jnp.zeros((1, WIDTH), F32))

    @pl.when(me.moves)
    def _():
        there(gown, gtok, me.opposite, 4).start()

    @pl.when(me.stays)
    def _():
        here(gown, gtok, 8).start()

    row = lax.broadcasted_iota(jnp.int32, (128, WIDTH), 0)
    gcol[...] = jnp.where(row == 0, dgain, 0.0).T
    weigh(1)
    pack(1, p1_g)
    if fused:
        advance(sums[1:], "zero")
        wave(sums[1:])
        for j in jobs + sums:
            j.four()
        for j in jobs + sums:
            j.done()
    for k, device in ((0, me.twin), (1, me.beside), (2, me.twin)):
        there(sent.at[k], landed.at[k], device, k).wait_send()

    @pl.when(me.moves)
    def _():
        there(out_own, out, me.opposite, 3).wait()
        there(gown, gtok, me.opposite, 4).wait()

    @pl.when(me.stays)
    def _():
        here(out_own, out, 7).wait()
        here(gown, gtok, 8).wait()


def back(tok, gmid, out_own, query, kv, firsts, wqkv, gain, gmixed, lse, delta, tables, packs, nz, masks):
    rows = tok.shape[0]
    shape, vm = jax.ShapeDtypeStruct, pltpu.VMEM
    vmem, anyspace = pl.BlockSpec(memory_space=pltpu.VMEM), pl.BlockSpec(memory_space=pl.ANY)
    in_specs = [vmem] * 4 + [anyspace] * 3 + [vmem] * 4 + [anyspace]
    slab = (2 * SLIVER, 640)
    outs, out_specs = [shape((rows, WIDTH), BF)] * 2, [vmem] * 2
    scratch = [
        vm((2, rows, WIDTH), BF),
        vm((2, rows, WIDTH), BF),
        vm((WIDTH, nz * rows), BF),
        vm((WIDTH, 3 * WIDTH), BF),
        vm((nz, rows, 128), F32),
        vm((nz, rows, 128), F32),
        vm((WIDTH, rows), F32),
        vm((rows, WIDTH), BF),
        vm((nz * rows, 2 * WIDTH), BF),
        vm((rows, WIDTH), F32),
        vm((WIDTH, 3 * HALF), F32),
        vm((3, rows, WIDTH), BF),
        vm((3, rows, WIDTH), BF),
        vm((rows, WIDTH), BF),
        vm((WIDTH, 128), F32),
        pltpu.SemaphoreType.DMA((5,)),
        pltpu.SemaphoreType.DMA((5,)),
        pltpu.SemaphoreType.DMA((9,)),
    ]
    if masks:
        in_specs += [anyspace] * 2
        outs += [shape(s, F32) for s in (slab, slab, packs[0].shape[-2:], packs[1].shape[-2:])]
        out_specs += [vmem] * 4
        scratch += [vm((GROUPS, LINE) + slab, BF)] * 2
        for s, held in ((slab, True), (slab, True), (packs[0].shape[-2:], False), (packs[1].shape[-2:], False)):
            bufs, sems = Reduce.scratch(s, nz, held)
            scratch += bufs + sems
    else:
        outs += [shape((GROUPS, LINE) + slab, BF)] * 2
        out_specs += [vmem] * 2
        packs = []
    return pl.pallas_call(
        functools.partial(back_kernel, nz, masks, rows),
        out_shape=outs,
        in_specs=in_specs,
        out_specs=out_specs,
        scratch_shapes=scratch,
        compiler_params=pltpu.CompilerParams(collective_id=1, has_side_effects=True, vmem_limit_bytes=62 << 20),
        cost_estimate=pl.CostEstimate(flops=24_000_000_000, bytes_accessed=40_000_000, transcendentals=13_000_000),
        name="back",
    )(tok, gmid, out_own, query, kv, firsts, wqkv, gain, gmixed, lse, delta, tables, *packs)


def finish_kernel(out, gtok, s0, s1, so, sm, out_o, gtok_o, qkv_o, w_out_o, gain_a_o, gain_m_o, w_in_o, down_o):
    out_o[...] = out[...]
    gtok_o[...] = gtok[...]
    for i, total in enumerate((s0, s1)):
        q, k, v0, v1, tile = unpack_group(total[...])
        for j, x in enumerate((q, k)):
            qkv_o[:, WIDTH * j + HALF * i : WIDTH * j + HALF * i + HALF] = x
        at = 2 * WIDTH + HALF * i
        qkv_o[:, at : at + 256] = v0
        qkv_o[:, at + 256 : at + HALF] = v1
    w_out_o[:, :HALF] = so[:SLIVER, :HALF]
    w_out_o[:, HALF:] = so[SLIVER:, :HALF]
    zeros = jnp.zeros((128 - SLIVER, 128), F32)
    for dst, col in ((gain_a_o, tile), (gain_m_o, so[:SLIVER, HALF:])):
        dst[...] = jnp.concatenate([col, zeros], 0).T[:1, :SLIVER]
    gate, up, down = unpack_mlp(sm[...])
    w_in_o[:, 0, :] = gate
    w_in_o[:, 1, :] = up
    down_o[...] = down.T


def finish(out, gtok, s0, s1, so, sm):
    shape = jax.ShapeDtypeStruct
    vmem = pl.BlockSpec(memory_space=pltpu.VMEM)
    return pl.pallas_call(
        finish_kernel,
        out_shape=[
            shape(out.shape, BF),
            shape(gtok.shape, BF),
            shape((SLIVER, 3 * WIDTH), F32),
            shape((SLIVER, WIDTH), F32),
            shape((1, SLIVER), F32),
            shape((1, SLIVER), F32),
            shape((BAND, 2, SHARE), F32),
            shape((SHARE, BAND), F32),
        ],
        in_specs=[vmem] * 6,
        out_specs=[vmem] * 8,
        compiler_params=pltpu.CompilerParams(vmem_limit_bytes=60 << 20),
        name="finish",
    )(out, gtok, s0, s1, so, sm)


def whole_packs(w_qkv, w_out, attn_gain, mlp_gain, w_in, w_down):
    both = ("dp", "seq")

    def shards_of(w):
        w = lax.all_gather(w, both, axis=0, tiled=True)
        return w.reshape(GROUPS * LINE, SLIVER, -1)

    def slabs(pack, w, gain):
        found = jax.vmap(pack)(w, jnp.pad(gain, ((0, 0), (0, 0), (0, 127))))
        return found.reshape((GROUPS, LINE) + found.shape[1:])

    qkv, gain_a, gain_m = shards_of(w_qkv), shards_of(attn_gain), shards_of(mlp_gain)
    groups = [slabs(lambda w, t, i=i: pack_group(w, t, i), qkv, gain_a) for i in range(2)]
    w_in, w_down = lax.all_gather(w_in, "dp", axis=0, tiled=True), lax.all_gather(w_down, "dp", axis=1, tiled=True)
    mlp = lax.all_gather(pack_mlp(w_in[:, 0], w_in[:, 1], w_down.T), "seq", axis=0, tiled=False)
    mlp = mlp.reshape(LINE, GROUPS, BAND, -1).transpose(1, 0, 2, 3)
    return groups, slabs(pack_out, shards_of(w_out), gain_m), mlp


def whole_sums(p0_g, p1_g, po_g, pm_g):
    both = ("dp", "seq")

    def scattered(x):
        return lax.psum_scatter(x.reshape(WIDTH, -1), both, scatter_dimension=0, tiled=True)

    parts = [jax.vmap(unpack_group)(p.reshape((GROUPS * LINE,) + p.shape[2:]).astype(F32)) for p in (p0_g, p1_g)]
    columns = [parts[0][0], parts[1][0], parts[0][1], parts[1][1], parts[0][2], parts[0][3], parts[1][2], parts[1][3]]
    g_qkv, gain_a = scattered(jnp.concatenate(columns, -1)), scattered(parts[1][4][..., :1])[:, 0]
    po = po_g.reshape(GROUPS * LINE, 2 * SLIVER, -1).astype(F32)
    g_out = scattered(jnp.concatenate([po[:, :SLIVER, :HALF], po[:, SLIVER:, :HALF]], -1))
    gain_m = scattered(po[:, :SLIVER, HALF : HALF + 1])[:, 0]
    mlp = pm_g.astype(F32).transpose(1, 0, 2, 3).reshape(LINE, WIDTH, -1)
    mlp = lax.psum_scatter(mlp, "seq", scatter_dimension=0, tiled=False)
    gate, up, down = unpack_mlp(lax.psum_scatter(mlp, "dp", scatter_dimension=0, tiled=True))
    return g_qkv, g_out, gain_a, gain_m, jnp.stack([gate, up], 1), down.T


def on_device(tokens, w_qkv, w_out, attn_gain, mlp_gain, w_in, w_down, grad_out, *, dp, nz):
    rows = tokens.shape[0]
    masks = (dp // 2, dp // 4, 1) if dp == GROUPS else None
    tables = jnp.asarray(rope_tables(nz * rows)).reshape(nz, rows, 128)
    if masks:
        weights = [w_qkv, w_out, attn_gain[None], mlp_gain[None], w_in, w_down]
        got = front(tokens, grad_out, weights, tables, nz, masks)
        po_all, pm_all = got[-2:]
    else:
        groups, po_all, pm_all = whole_packs(w_qkv, w_out, attn_gain, mlp_gain, w_in, w_down)
        got = front(tokens, grad_out, groups, tables, nz, None)
    mixed, lse, query, gain, tok_own, gout_own, kv, firsts, wqkv = got[:9]
    out_own, gmid, gmixed, delta, po_g, pm_g = middle(tok_own, mixed, gout_own, po_all, pm_all)
    found = back(tok_own, gmid, out_own, query, kv, firsts, wqkv, gain, gmixed, lse, delta, tables, [po_g, pm_g], nz, masks)
    gtok, out, *sums = found
    if not masks:
        return (out, gtok, *whole_sums(*sums, po_g, pm_g))
    out, gtok, g_qkv, g_out, gain_a, gain_m, g_in, g_down = finish(out, gtok, *sums)
    return out, gtok, g_qkv, g_out, gain_a[0], gain_m[0], g_in, g_down


def solution(mesh):
    both = P(("dp", "seq"), None)
    vector = P(("dp", "seq"))
    w_in, w_down = P("dp", None, "seq"), P("seq", "dp")
    step = functools.partial(on_device, dp=mesh.shape["dp"], nz=mesh.shape["seq"])
    return jax.shard_map(
        step,
        mesh=mesh,
        in_specs=(both, both, both, vector, vector, w_in, w_down, both),
        out_specs=(both, both, both, both, vector, vector, w_in, w_down),
        check_vma=False,
    )
```

```python
import functools
import math

import jax
import jax.numpy as jnp
import numpy as np
from jax import lax
from jax.experimental import pallas as pl
from jax.experimental.pallas import tpu as pltpu
from jax.sharding import PartitionSpec as P

HEADS = 12
HEAD_DIM = 64
NORM_EPS = 1e-05
ROPE_THETA = 160000.0

F32 = jnp.float32
BF = jnp.bfloat16
MESH = pl.DeviceIdType.MESH
NT = (((1,), (1,)), ((), ()))
NN = (((1,), (0,)), ((), ()))
TN = (((0,), (0,)), ((), ()))

WIDTH = 768
PAIRS = HEADS // 2
UNITS = 1152
GROUPS = 8
LINE = 4
BAND = WIDTH // GROUPS
SLIVER = BAND // LINE
SHARE = UNITS // LINE
MAIN = 256
REST = SHARE - MAIN
LINKED = (0, 1, 3, 2)
HALF = WIDTH // 2
CUTS = {640: 256, 512: 256, 896: 384}
LOG2E = math.log2(math.e)
SCALE = HEAD_DIM**-0.5


def dot(a, b, dims):
    return lax.dot_general(a, b, dims, preferred_element_type=F32)


def lanes_of(tile, width=128):
    return pl.ds(pl.multiple_of(tile * width, width), width)


def tiles(start, width):
    return pl.ds(pl.multiple_of(start, width if width < 128 else 128), width)


def lane_iota():
    return lax.broadcasted_iota(jnp.int32, (1, 128), 1)


def swap_halves(u):
    low = lax.rem(lane_iota(), 64) < 32
    return jnp.where(low, pltpu.roll(u, 96, 1), pltpu.roll(u, 32, 1))


def rope(u, cos, sine):
    return u * cos + swap_halves(u) * sine


def rope_back(u, cos, sine):
    return u * cos - swap_halves(u) * sine


def rope_tables(rows):
    position = np.arange(rows, dtype=np.float32)
    half = HEAD_DIM // 2
    freq = (ROPE_THETA ** (-np.arange(half) * 2.0 / HEAD_DIM)).astype(np.float32)
    angle = (position[:, None] * freq[None, :]).astype(np.float64)
    cos, sine = np.cos(angle), np.sin(angle)
    return np.concatenate([cos, cos, -sine, sine], 1).astype(np.float32)


def spread_tables(cos, sine):
    low = lane_iota() < 64

    def chunk(c, _):
        both = cos[c]
        other = pltpu.roll(both, 64, 1)
        cos[c] = jnp.where(low, both, other)
        sine[c] = jnp.where(low, other, both)
        return 0

    lax.fori_loop(0, cos.shape[0], chunk, 0)


def normed(x):
    centred = x - jnp.mean(x, -1, keepdims=True)
    inv = lax.rsqrt(jnp.mean(centred * centred, -1, keepdims=True) + NORM_EPS)
    return centred * inv, inv


def norm_back(dy, gain, hat, inv):
    d = dy * gain
    return inv * (d - jnp.mean(d, -1, keepdims=True) - hat * jnp.mean(d * hat, -1, keepdims=True))


def remote(src, dst, send, recv, device):
    return pltpu.make_async_remote_copy(src, dst, send, recv, device_id=device, device_id_type=MESH)


class Place:
    def __init__(self, nz):
        self.dp, self.z = lax.axis_index("dp"), lax.axis_index("seq")
        self.nz = nz
        upper = self.z // (nz // 2)
        self.moves = lax.rem(self.dp, 2) != upper
        self.stays = lax.rem(self.dp, 2) == upper
        self.shard = jnp.where(self.moves, nz - 1 - self.z, self.z)
        self.opposite = {"dp": self.dp ^ 1, "seq": nz - 1 - self.z}
        self.twin = {"dp": self.dp ^ 1}
        self.beside = {"seq": self.z ^ 1}

    def greet(self, masks):
        bar = pltpu.get_barrier_semaphore()

        def hello(device):
            pl.semaphore_signal(bar, inc=1, device_id=device, device_id_type=MESH)

        for o in range(1, self.nz):
            hello({"seq": lax.rem(self.z + o, self.nz)})
        for m in masks:
            hello({"dp": self.dp ^ m})
        hello(self.opposite)
        pl.semaphore_wait(bar, self.nz + len(masks))


class Gather:
    COPIES = 9

    def __init__(self, src, out, cut, nz, masks, send, recv):
        self.src, self.out, self.cut, self.nz, self.masks = src, out, cut, nz, masks
        self.send, self.recv = send, recv
        self.dp, self.z = lax.axis_index("dp"), lax.axis_index("seq")
        self.started = []
        self.relayed = None

    @staticmethod
    def sems(nz):
        return Gather.COPIES * nz + nz

    def key(self, o, k):
        return o * self.COPIES + k

    def copy(self, src, dst, device, k):
        return remote(src, dst, self.send.at[k], self.recv.at[k], device)

    def begin(self, src, dst, device, k, p=None):
        self.copy(src, dst, device, k).start()
        self.started.append((k, p))

    def arrived(self, ref, k):
        self.copy(ref, ref, {"dp": self.dp ^ self.masks[0]}, k).wait_recv()

    def slot(self, o):
        return self.z ^ LINKED[o]

    def part(self, ref, p):
        if p is None:
            return ref
        width = self.out.shape[-1]
        return ref.at[:, pl.ds(0, self.cut)] if p == 0 else ref.at[:, pl.ds(self.cut, width - self.cut)]

    def along(self, o):
        self.begin(self.src, self.out.at[self.dp, self.z], {"seq": self.z ^ LINKED[o]}, self.COPIES * self.nz + o)

    def relay(self, o):
        ref = self.out.at[self.dp, self.slot(o)]
        self.arrived(ref, self.COPIES * self.nz + o)
        self.relayed = o
        self.begin(ref, ref, {"seq": self.z ^ 1}, self.COPIES * self.nz + 3)

    def forward(self, src, d, s, mask, k, p=None):
        dst = self.out.at[d, s]
        self.begin(self.part(src, p), self.part(dst, p), {"dp": self.dp ^ mask}, k, p)

    def first(self, o):
        my, mx, mc = self.masks
        s = self.slot(o)
        src = self.src
        if o:
            src = self.out.at[self.dp, s]
            if o != self.relayed:
                self.arrived(src, self.COPIES * self.nz + o)
        self.forward(src, self.dp, s, my, self.key(o, 0))
        self.forward(src, self.dp, s, mx, self.key(o, 1))
        self.forward(src, self.dp, s, mc, self.key(o, 2))

    def second(self, o):
        my, mx, mc = self.masks
        s = self.slot(o)
        for m, k, k2, kc, p, m2 in ((my, 0, 3, 4, 0, mx), (mx, 1, 5, 6, 1, my)):
            ref = self.out.at[self.dp ^ m, s]
            self.arrived(ref, self.key(o, k))
            self.forward(ref, self.dp ^ m, s, m2, self.key(o, k2), p)
            self.forward(ref, self.dp ^ m, s, mc, self.key(o, kc))

    def third(self, o):
        my, mx, mc = self.masks
        s = self.slot(o)
        d = self.dp ^ my ^ mx
        for p, k, kc in ((0, 3, 7), (1, 5, 8)):
            ref = self.out.at[d, s]
            self.arrived(self.part(ref, p), self.key(o, k))
            self.forward(ref, d, s, mc, self.key(o, kc), p)

    def finish(self, o):
        my, mx, mc = self.masks
        s = self.slot(o)
        for k, d in ((2, mc), (4, mc ^ my), (6, mc ^ mx)):
            self.arrived(self.out.at[self.dp ^ d, s], self.key(o, k))
        for k, p in ((7, 0), (8, 1)):
            self.arrived(self.part(self.out.at[self.dp ^ mc ^ my ^ mx, s], p), self.key(o, k))

    def done(self):
        for k, p in self.started:
            ref = self.part(self.out.at[self.dp, self.z], p)
            self.copy(ref, ref, {"dp": self.dp ^ self.masks[0]}, k).wait_send()


def pack_group(w, tile, i):
    q, k, v = [w[:, WIDTH * j + HALF * i : WIDTH * j + HALF * i + HALF] for j in range(3)]
    return jnp.concatenate([jnp.concatenate([q, v[:, :256]], 1), jnp.concatenate([k, v[:, 256:], tile], 1)], 0)


def unpack_group(total):
    r = total.shape[0] // 2
    upper, lower = total[:r], total[r:]
    return upper[:, :HALF], lower[:, :HALF], upper[:, HALF:], lower[:, HALF : HALF + 128], lower[:, HALF + 128 :]


def pack_out(w, tile):
    return jnp.concatenate([jnp.concatenate([w[:, :HALF], w[:, HALF:]], 0), jnp.concatenate([tile, jnp.zeros_like(tile)], 0)], 1)


def pack_mlp(gate, up, down):
    parts = (gate, up, down)
    pads = jnp.zeros((gate.shape[0], 128 - 3 * REST), gate.dtype)
    return jnp.concatenate([x[:, :MAIN] for x in parts] + [x[:, MAIN:] for x in parts] + [pads], 1)


def unpack_mlp(total):
    return [
        jnp.concatenate([total[:, MAIN * i : MAIN * i + MAIN], total[:, 3 * MAIN + REST * i : 3 * MAIN + REST * i + REST]], 1)
        for i in range(3)
    ]


def front_kernel(nz, masks, rows, *refs):
    fused = masks is not None
    if fused:
        (tok, gout, w_qkv, w_out, gain_a, gain_m, w_in, w_down, cos_in), refs = refs[:9], refs[9:]
    else:
        (tok, gout, g0_all, g1_all, cos_in), refs = refs[:5], refs[5:]
    (mixed, lse, query, gain, tok_own, gout_own, kv, firsts, wqkv), refs = refs[:9], refs[9:]
    if fused:
        (po_all, pm_all), refs = refs[:2], refs[2:]
    (tok_all, kvb, fb, wq, cos, sine, gcol, acc, top, total, tsend, trecv, loc), refs = refs[:13], refs[13:]
    me = Place(nz)
    own = me.shard

    def here(src, dst, k):
        return pltpu.make_async_copy(src, dst, loc.at[k])

    def there(src, dst, device, k):
        return remote(src, dst, tsend.at[k], trecv.at[k], device)

    def rows_to(src, c, device, k, i):
        at = pl.ds(i * (rows // 2), rows // 2)
        src = tok_all.at[c] if src is None else src
        return there(src.at[at], tok_all.at[c, at], device, k + 5 * i)

    @pl.when(me.stays)
    def _():
        here(tok, tok_all.at[own], 0).start()
        here(gout, gout_own, 1).start()

    here(cos_in, cos, 2).start()
    groups, later = [], []
    every, rest = range(nz), (2, 1, 3)
    if fused:
        p0, p1, po, pm, g0_all, g1_all, *sems = refs
        row = lax.broadcasted_iota(jnp.int32, (128, 128), 0)

        def tile_of(part):
            line = jnp.concatenate([part[...].astype(F32), jnp.zeros((1, 128 - SLIVER), F32)], 1)
            return jnp.where(row == 0, line, 0.0).T[:SLIVER]

        p0[...] = pack_group(w_qkv[...].astype(F32), tile_of(gain_a), 0).astype(BF)
        g0_all[me.dp, me.z] = p0[...]
    me.greet(masks or (1,))
    if fused:
        shapes = ((p0, g0_all), (p1, g1_all), (po, po_all), (pm, pm_all))
        packs = [
            Gather(src, dst, CUTS[src.shape[-1]], nz, masks, sems[2 * i], sems[2 * i + 1]) for i, (src, dst) in enumerate(shapes)
        ]
        groups, later = packs[:2], packs[2:]
        for o in rest:
            groups[0].along(o)
        groups[0].first(0)

    @pl.when(me.stays)
    def _():
        for i in range(2):
            rows_to(tok, own, me.twin, 1, i).start()
            rows_to(tok, own, me.beside, 2, i).start()

    @pl.when(me.moves)
    def _():
        for i in range(2):
            rows_to(tok, me.z, me.opposite, 0, i).start()

    def swapped(i):
        @pl.when(me.moves)
        def _():
            rows_to(None, own, me.opposite, 0, i).wait_recv()
            rows_to(None, own, me.beside, 2, i).start()
            rows_to(None, own, me.twin, 1, i).start()

    if fused:
        w = w_qkv[...].astype(F32)
        p1[...] = pack_group(w, jnp.zeros((SLIVER, 128), F32), 1).astype(BF)
        g1_all[me.dp, me.z] = p1[...]
        po[...] = pack_out(w_out[...].astype(F32), tile_of(gain_m)).astype(BF)
        pm[...] = pack_mlp(w_in[:, 0, :].astype(F32), w_in[:, 1, :].astype(F32), w_down[...].astype(F32).T).astype(BF)
        here(po, po_all.at[me.dp, me.z], 4).start()
        here(pm, pm_all.at[me.dp, me.z], 5).start()
        for o in rest:
            groups[1].along(o)
        groups[1].first(0)
        groups[0].second(0)
        for o in rest:
            groups[0].first(o)
        swapped(0)
        for o in rest:
            groups[0].second(o)
        for o in rest:
            groups[1].first(o)
        for g in later:
            g.along(1)
            g.first(0)

    if not fused:
        swapped(0)
    swapped(1)

    @pl.when(me.stays)
    def _():
        here(tok, tok_all.at[own], 0).wait()

    here(tok_all.at[own], tok_own, 6).start()
    if fused:
        for g in later:
            g.along(2)
        for o in range(nz):
            groups[0].third(o)
        for o in range(nz):
            groups[0].finish(o)

    @pl.when(me.moves)
    def _():
        there(gout, gout_own, me.opposite, 4).start()

    here(cos_in, cos, 2).wait()
    spread_tables(cos, sine)

    def build(i, whole):
        def band_of(g, _):
            slabs = [unpack_group(whole[g, s].astype(F32)) for s in range(LINE)]
            band = pl.ds(pl.multiple_of(g * BAND, BAND), BAND)
            q, k, v0, v1, t = [jnp.concatenate([x[j] for x in slabs], 0) for j in range(5)]
            at = WIDTH * i
            wq[band, at : at + HALF] = k.astype(BF)
            wq[band, at + HALF : at + HALF + 256] = v0.astype(BF)
            wq[band, at + HALF + 256 : at + WIDTH] = v1.astype(BF)
            wq[band, 2 * WIDTH + HALF * i : 2 * WIDTH + HALF * i + HALF] = q.astype(BF)
            if i == 0:
                gcol[band, :] = t
            return 0

        lax.fori_loop(0, GROUPS, band_of, 0)

    def norm_chunk(c):
        def block(i, _):
            at = pl.ds(pl.multiple_of(i * 64, 64), 64)
            hat, _ = normed(tok_all[c, at, :].astype(F32))
            fb[c, at, :] = (hat * gain[0:1, :]).astype(BF)
            return 0

        lax.fori_loop(0, rows // 64, block, 0)
        here(fb.at[c], firsts.at[c], 8 + c).start()

    def queries(i):
        u = dot(fb[own], wq[:, 2 * WIDTH + HALF * i : 2 * WIDTH + HALF * i + HALF], NN)
        for j in range(3):
            tile = rope(u[:, 128 * j : 128 * j + 128], cos[own], sine[own])
            query[:, HALF * i + 128 * j : HALF * i + 128 * j + 128] = (tile * (SCALE * LOG2E)).astype(BF)

    def visits(steps):
        def visit(n, _):
            t, grp = lax.rem(n, nz), n // nz
            stay = jnp.where(t == 1, 1, jnp.where(t == 2, 3, 2))
            move = jnp.where(t == 1, 3, jnp.where(t == 2, 2, 1))
            turn = jnp.where(me.stays, stay, move)
            c = jnp.where(t == 0, own, own ^ turn)
            @pl.when((n > 0) & (n < nz))
            def _():
                for i in range(2):
                    rows_to(None, c, me.twin, jnp.where(turn == 1, 2, jnp.where(turn == 3, 1, 3)), i).wait_recv()

                    @pl.when(turn == 1)
                    def _(i=i):
                        rows_to(None, c, me.twin, 3, i).start()

                norm_chunk(c)

            for j in range(3):
                u = dot(fb[c], wq[:, tiles(WIDTH * grp + 256 * j, 256)], NN)
                for i in range(2):
                    tile = 2 * j + i
                    x = u[:, 128 * i : 128 * i + 128]
                    x = rope(x, cos[c], sine[c]) if tile < 3 else x
                    kvb[grp, c, :, 128 * tile : 128 * tile + 128] = x.astype(BF)
            here(kvb.at[grp, c], kv.at[grp, c], 8 + nz * (1 + grp) + c).start()
            jobs = [(i, h) for i in range(3) for h in range(2)]

            def score(i, h):
                q = query[:, tiles(HALF * grp + 128 * i, 128)]
                mask = (lane_iota() < 64) if h == 0 else (lane_iota() >= 64)
                return dot(kvb[grp, c, :, 128 * i : 128 * i + 128], jnp.where(mask, q, jnp.zeros_like(q)), NT)

            ready = [score(*j) for j in jobs[:2]]
            for m, (i, h) in enumerate(jobs):
                if h == 0:
                    vt = kvb[grp, c, :, HALF + 128 * i : HALF + 128 * i + 128].T
                s = ready[m]
                if m + 2 < len(jobs):
                    ready.append(score(*jobs[m + 2]))
                head = pl.ds(6 * grp + m, 1)
                band = tiles(64 * (6 * grp + m), 64)
                old = top[head, :]
                new = jnp.maximum(old, jnp.max(s, 0, keepdims=True))
                p = jnp.exp2(s - new)
                fade = jnp.exp2(old - new)
                top[head, :] = new
                lhs = jnp.concatenate([vt[h * 64 : h * 64 + 64], jnp.ones((16, rows), BF)], 0)
                oo = dot(lhs, p.astype(BF), NN)
                total[head, :] = total[head, :] * fade + oo[64:65]
                acc[band, :] = acc[band, :] * fade + oo[:64]
            for k, step in steps.items():

                @pl.when(n == k)
                def _(k=k, step=step):
                    for which, name, order in step:
                        for g in which:
                            for o in order:
                                getattr(g, name)(o)
                    if k == nz - 1:
                        build(1, g1_all)
                        here(wq, wqkv, 7).start()
                        queries(1)

            return 0

        lax.fori_loop(0, 2 * nz, visit, 0)

    build(0, g0_all)
    gain[...] = gcol[...].T[:8]
    norm_chunk(own)
    queries(0)
    acc[...] = jnp.zeros_like(acc)
    total[...] = jnp.zeros_like(total)
    top[...] = jnp.full_like(top, -1e30)
    one = groups[1:]
    visits({
        0: [(one, "second", every), (later, "first", (1,))],
        1: [(one, "third", every)],
        2: [(later, "relay", (2,)), (later, "first", (2,))],
        3: [(one, "finish", every), (later, "second", (0, 1))],
        4: [(later, "first", (3,))],
        5: [(later, "second", (2,))],
        6: [(later, "second", (3,))],
        7: [(later, "third", every)],
    })

    for hp in range(PAIRS):
        parts = [
            acc[128 * hp + 64 * h : 128 * hp + 64 * h + 64, :] / total[2 * hp + h : 2 * hp + h + 1, :] for h in range(2)
        ]
        mixed[:, 128 * hp : 128 * hp + 128] = jnp.concatenate(parts, 0).T.astype(BF)
    lse[...] = top[...] + jnp.log(jnp.maximum(total[...], 1e-30)) * LOG2E

    if fused:
        for g in later:
            for o in range(nz):
                g.finish(o)
        for g in packs:
            g.done()
        here(po, po_all.at[me.dp, me.z], 4).wait()
        here(pm, pm_all.at[me.dp, me.z], 5).wait()
    for i in range(2):
        for k in (1, 2, 3):
            rows_to(None, own, me.twin, k, i).wait_send()

    @pl.when(me.moves)
    def _():
        for i in range(2):
            rows_to(None, own, me.opposite, 0, i).wait_send()
        there(gout, gout_own, me.opposite, 4).wait()

    @pl.when(me.stays)
    def _():
        here(gout, gout_own, 1).wait()

    here(tok_all.at[own], tok_own, 6).wait()
    here(wq, wqkv, 7).wait()
    for c in range(nz):
        here(fb.at[c], firsts.at[c], 8 + c).wait()
        for grp in range(2):
            here(kvb.at[grp, c], kv.at[grp, c], 8 + nz * (1 + grp) + c).wait()


def front(tok, gout, weights, tables, nz, masks):
    rows = tok.shape[0]
    vmem, anyspace = pl.BlockSpec(memory_space=pltpu.VMEM), pl.BlockSpec(memory_space=pl.ANY)
    shape, vm = jax.ShapeDtypeStruct, pltpu.VMEM
    outs = [shape((rows, WIDTH), BF), shape((16, rows), F32), shape((rows, WIDTH), BF), shape((8, WIDTH), F32)]
    outs += [shape((rows, WIDTH), BF)] * 2
    outs += [shape((2, nz, rows, WIDTH), BF), shape((nz, rows, WIDTH), BF), shape((WIDTH, 3 * WIDTH), BF)]
    out_specs = [vmem] * 4 + [anyspace, vmem] + [anyspace] * 3
    scratch = [
        vm((nz, rows, WIDTH), BF),
        vm((2, nz, rows, WIDTH), BF),
        vm((nz, rows, WIDTH), BF),
        vm((WIDTH, 3 * WIDTH), BF),
        vm((nz, rows, 128), F32),
        vm((nz, rows, 128), F32),
        vm((WIDTH, 128), F32),
        vm((WIDTH, rows), F32),
        vm((16, rows), F32),
        vm((16, rows), F32),
        pltpu.SemaphoreType.DMA((9,)),
        pltpu.SemaphoreType.DMA((9,)),
        pltpu.SemaphoreType.DMA((8 + 3 * nz,)),
    ]
    if masks:
        grp, out, mlp = (2 * SLIVER, 640), (2 * SLIVER, 512), (BAND, 896)
        outs += [shape((GROUPS, nz) + out, BF), shape((GROUPS, nz) + mlp, BF)]
        out_specs += [anyspace] * 2
        scratch += [vm(x, BF) for x in (grp, grp, out, mlp)] + [vm((GROUPS, nz) + grp, BF)] * 2
        scratch += [pltpu.SemaphoreType.DMA((Gather.sems(nz),)) for _ in range(8)]
    return pl.pallas_call(
        functools.partial(front_kernel, nz, masks, rows),
        out_shape=outs,
        in_specs=[anyspace] * 2 + [vmem] * len(weights) + [anyspace],
        out_specs=out_specs,
        scratch_shapes=scratch,
        compiler_params=pltpu.CompilerParams(collective_id=0, has_side_effects=True, vmem_limit_bytes=60 << 20),
        cost_estimate=pl.CostEstimate(flops=14_000_000_000, bytes_accessed=40_000_000, transcendentals=13_000_000),
        name="front",
    )(tok, gout, *weights, tables)


def middle_kernel(rows, tok, mixed, gout, po_all, pm_in, out_own, gmid_own, gmixed, delta, po_g, pm_sums,
                  pm_all, pm_g, out, gmid, loc, wout, wg, wu, wd, gcol, gain, resid, hat, inv, second, hidden, ggate, gup, gsec, gattn, dwout):
    lane = lane_iota()

    def here(src, dst, k):
        return pltpu.make_async_copy(src, dst, loc.at[k])

    here(pm_in, pm_all, 0).start()

    def build(g, _):
        band = pl.ds(pl.multiple_of(g * BAND, BAND), BAND)
        slabs = [po_all[g, s].astype(F32) for s in range(LINE)]
        wout[band, :384] = jnp.concatenate([x[:SLIVER, :384] for x in slabs], 0).astype(BF)
        wout[band, 384:] = jnp.concatenate([x[SLIVER:, :384] for x in slabs], 0).astype(BF)
        gcol[band, :] = jnp.concatenate([x[:SLIVER, 384:] for x in slabs], 0)
        return 0

    def build_units(g, _):
        band = pl.ds(pl.multiple_of(g * BAND, BAND), BAND)
        for i, w in enumerate((wg, wu, wd)):
            tail = jnp.zeros((BAND, 128), F32)
            for s in range(LINE):
                w[band, MAIN * s : MAIN * s + MAIN] = pm_all[g, s, :, MAIN * i : MAIN * i + MAIN]
                rest = pm_all[g, s, :, 3 * MAIN :].astype(F32)
                turn = (REST * (s - i)) % 128
                rest = pltpu.roll(rest, turn, 1) if turn else rest
                tail = jnp.where((lane >= REST * s) & (lane < REST * (s + 1)), rest, tail)
            w[band, MAIN * LINE :] = tail.astype(BF)
        return 0

    lax.fori_loop(0, GROUPS, build, 0)
    gain[...] = gcol[...].T[:8]

    for j in range(3):
        at = slice(256 * j, 256 * j + 256)
        resid[:, at] = tok[:, at].astype(F32) + dot(mixed[...], wout[:, at], NN)

    def norm_block(i, _):
        at = pl.ds(pl.multiple_of(i * 64, 64), 64)
        h, r = normed(resid[at, :])
        hat[at, :] = h
        inv[at, :] = jnp.broadcast_to(r, (64, 128))
        second[at, :] = (h * gain[0:1, :]).astype(BF)
        return 0

    lax.fori_loop(0, rows // 64, norm_block, 0)
    here(pm_in, pm_all, 0).wait()
    lax.fori_loop(0, GROUPS, build_units, 0)

    def units(start, width):
        at = pl.ds(start, width)
        gate, up, gh = dot(second[...], wg[:, at], NN), dot(second[...], wu[:, at], NN), dot(gout[...], wd[:, at], NN)
        cdf = 0.5 + 0.5 * lax.erf(gate * math.sqrt(0.5))
        pdf = jnp.exp2(gate * gate * (-0.5 * LOG2E)) * (1.0 / math.sqrt(2.0 * math.pi))
        act = gate * cdf
        hidden[:, at] = (act * up).astype(BF)
        gup[:, at] = (gh * act).astype(BF)
        ggate[:, at] = (gh * up * (cdf + gate * pdf)).astype(BF)

    for start in range(0, UNITS, 256):
        units(start, min(256, UNITS - start))

    for j in range(3):
        at = slice(256 * j, 256 * j + 256)
        out[:, at] = (resid[:, at] + dot(hidden[...], wd[at, :], NT)).astype(BF)
        gsec[:, at] = dot(ggate[...], wg[at, :], NT) + dot(gup[...], wu[at, :], NT)

    here(out, out_own, 1).start()

    for j in range(2):
        at = slice(384 * j, 384 * j + 384)
        tails = []
        for i, (a, b) in enumerate(((second, ggate), (second, gup), (gout, hidden))):
            for s in range(LINE):
                x = dot(a[:, at], b[:, MAIN * s : MAIN * s + MAIN], TN).astype(BF)
                for g in range(4):
                    pm_g[4 * j + g, s, :, MAIN * i : MAIN * i + MAIN] = x[BAND * g : BAND * g + BAND]
            tails.append(dot(a[:, at], b[:, MAIN * LINE :], TN))
        for s in range(LINE):
            y = jnp.zeros((384, 128), F32)
            for i, tail in enumerate(tails):
                turn = (REST * (i - s)) % 128
                tail = pltpu.roll(tail, turn, 1) if turn else tail
                y = jnp.where((lane >= REST * i) & (lane < REST * (i + 1)), tail, y)
            y = y.astype(BF)
            for g in range(4):
                pm_g[4 * j + g, s, :, 3 * MAIN :] = y[BAND * g : BAND * g + BAND]
        here(pm_g.at[pl.ds(4 * j, 4)], pm_sums.at[pl.ds(4 * j, 4)], 3 + j).start()

    def back_block(i, dgain):
        at = pl.ds(pl.multiple_of(i * 64, 64), 64)
        dy, h = gsec[at, :], hat[at, :]
        gm = gout[at, :].astype(F32) + norm_back(dy, gain[0:1, :], h, inv[at, 0:1])
        gmid[at, :] = gm
        gattn[at, :] = gm.astype(BF)
        return dgain + jnp.sum(dy * h, 0, keepdims=True)

    dgain = lax.fori_loop(0, rows // 64, back_block, jnp.zeros((1, WIDTH), F32))

    here(gmid, gmid_own, 2).start()
    heads = lax.broadcasted_iota(jnp.int32, (16, 256), 0)
    for j in range(3):
        at = slice(256 * j, 256 * j + 256)
        gmx = dot(gattn[...], wout[at, :], NT).astype(BF)
        gmixed[:, at] = gmx
        prod = gmx.astype(F32) * mixed[:, at].astype(F32)
        high = prod.astype(BF)
        low = (prod - high.astype(F32)).astype(BF)
        pick = ((lax.broadcasted_iota(jnp.int32, (16, 256), 1) + 256 * j) // HEAD_DIM == heads).astype(BF)
        part = dot(pick, high, NT) + dot(pick, low, NT)
        delta[...] = part if j == 0 else delta[...] + part

    for j in range(2):
        at = slice(384 * j, 384 * j + 384)
        dwout[at, :] = dot(mixed[:, at], gattn[...], TN)
    row = lax.broadcasted_iota(jnp.int32, (128, WIDTH), 0)
    gcol[...] = jnp.where(row == 0, dgain, 0.0).T

    def pack_out(g, _):
        for s in range(LINE):
            at = pl.ds(pl.multiple_of(g * BAND + s * SLIVER, 8), SLIVER)
            x, c = dwout[at, :], gcol[at, :]
            po_g[g, s, :, :384] = jnp.concatenate([x[:, :384], x[:, 384:]], 0).astype(BF)
            po_g[g, s, :, 384:] = jnp.concatenate([c, jnp.zeros_like(c)], 0).astype(BF)
        return 0

    lax.fori_loop(0, GROUPS, pack_out, 0)

    here(out, out_own, 1).wait()
    here(gmid, gmid_own, 2).wait()
    for j in range(2):
        here(pm_g.at[pl.ds(4 * j, 4)], pm_sums.at[pl.ds(4 * j, 4)], 3 + j).wait()


def middle(tok, mixed, gout, po_all, pm_all):
    rows = tok.shape[0]
    shape, vm = jax.ShapeDtypeStruct, pltpu.VMEM
    vmem, anyspace = pl.BlockSpec(memory_space=pltpu.VMEM), pl.BlockSpec(memory_space=pl.ANY)
    return pl.pallas_call(
        functools.partial(middle_kernel, rows),
        out_shape=[
            shape((rows, WIDTH), BF),
            shape((rows, WIDTH), F32),
            shape((rows, WIDTH), BF),
            shape((16, rows), F32),
            shape(po_all.shape, BF),
            shape(pm_all.shape, BF),
        ],
        in_specs=[vmem] * 4 + [anyspace],
        out_specs=[anyspace, anyspace, vmem, vmem, vmem, anyspace],
        scratch_shapes=[
            vm(pm_all.shape, BF),
            vm(pm_all.shape, BF),
            vm((rows, WIDTH), BF),
            vm((rows, WIDTH), F32),
            pltpu.SemaphoreType.DMA((5,)),
            vm((WIDTH, WIDTH), BF),
            vm((WIDTH, UNITS), BF),
            vm((WIDTH, UNITS), BF),
            vm((WIDTH, UNITS), BF),
            vm((WIDTH, 128), F32),
            vm((8, WIDTH), F32),
            vm((rows, WIDTH), F32),
            vm((rows, WIDTH), F32),
            vm((rows, 128), F32),
            vm((rows, WIDTH), BF),
            vm((rows, UNITS), BF),
            vm((rows, UNITS), BF),
            vm((rows, UNITS), BF),
            vm((rows, WIDTH), F32),
            vm((rows, WIDTH), BF),
            vm((WIDTH, WIDTH), F32),
        ],
        compiler_params=pltpu.CompilerParams(vmem_limit_bytes=58 << 20),
        cost_estimate=pl.CostEstimate(flops=11_000_000_000, bytes_accessed=25_000_000, transcendentals=1_200_000),
        name="middle",
    )(tok, mixed, gout, po_all, pm_all)


class Reduce:
    COPIES = 10

    def __init__(self, src, total, cut, nz, masks, bufs, send, recv, loc=None):
        self.src, self.total, self.cut, self.nz, self.masks = src, total, cut, nz, masks
        self.near, self.side0, self.side1, self.far, *mine = bufs
        self.mine = mine[0] if mine else None
        self.send, self.recv, self.loc = send, recv, loc
        self.dp, self.z = lax.axis_index("dp"), lax.axis_index("seq")
        my, mx, mc = masks
        self.turns = (0, my, mx, my ^ mx)
        self.started = []

    @staticmethod
    def scratch(shape, nz, held):
        r, c = shape
        cut = CUTS[c]
        bufs = [
            pltpu.VMEM((4, nz, r, c), BF),
            pltpu.VMEM((3, nz, r, cut), BF),
            pltpu.VMEM((3, nz, r, c - cut), BF),
            pltpu.VMEM((nz - 1, r, c), BF),
        ]
        sems = [pltpu.SemaphoreType.DMA((Reduce.COPIES * nz + nz,))] * 2
        if not held:
            bufs += [pltpu.VMEM((4, nz, r, c), BF)]
            sems += [pltpu.SemaphoreType.DMA((4 * nz,))]
        return bufs, sems

    def begin(self, src, dst, device, k):
        remote(src, dst, self.send.at[k], self.recv.at[k], device).start()
        self.started.append((k, src.shape[-1]))

    def arrived(self, ref, k):
        remote(ref, ref, self.send.at[k], self.recv.at[k], {"dp": self.dp ^ self.masks[2]}).wait_recv()

    def seat(self, o):
        return self.z ^ LINKED[o]

    def held(self, i, s):
        return self.mine.at[i, s] if self.mine is not None else self.src.at[self.dp ^ self.turns[i], s]

    def local(self, i, o):
        s = self.seat(o)
        return pltpu.make_async_copy(self.src.at[self.dp ^ self.turns[i], s], self.mine.at[i, s], self.loc.at[4 * o + i])

    def zero(self, o):
        s, mc = self.seat(o), self.masks[2]
        for i in (3, 1, 2, 0):
            if self.mine is not None:
                self.local(i, o).start()
            self.begin(self.src.at[self.dp ^ mc ^ self.turns[i], s], self.near.at[i, s], {"dp": self.dp ^ mc}, self.COPIES * o + i)

    def add(self, ref, other):
        ref[...] = (ref[...].astype(F32) + other[...].astype(F32)).astype(BF)

    def p0(self, i, s):
        return self.held(i, s).at[:, pl.ds(0, self.cut)]

    def p1(self, i, s):
        return self.held(i, s).at[:, pl.ds(self.cut, self.src.shape[-1] - self.cut)]

    def one(self, o):
        my, mx, _ = self.masks
        s, k = self.seat(o), self.COPIES * o
        for i in (3, 1, 2, 0):
            if self.mine is not None:
                self.local(i, o).wait()
            self.arrived(self.near.at[i, s], k + i)
            self.add(self.held(i, s), self.near.at[i, s])
            if i == 3:
                self.begin(self.p0(3, s), self.side0.at[1, s], {"dp": self.dp ^ my}, k + 4)
                self.begin(self.p1(3, s), self.side1.at[1, s], {"dp": self.dp ^ mx}, k + 5)
            if i == 1:
                self.begin(self.p0(1, s), self.side0.at[0, s], {"dp": self.dp ^ my}, k + 6)
            if i == 2:
                self.begin(self.p1(2, s), self.side1.at[0, s], {"dp": self.dp ^ mx}, k + 7)

    def two(self, o):
        my, mx, _ = self.masks
        s, k = self.seat(o), self.COPIES * o
        self.arrived(self.side0.at[1, s], k + 4)
        self.add(self.p0(2, s), self.side0.at[1, s])
        self.begin(self.p0(2, s), self.side0.at[2, s], {"dp": self.dp ^ mx}, k + 8)
        self.arrived(self.side1.at[1, s], k + 5)
        self.add(self.p1(1, s), self.side1.at[1, s])
        self.begin(self.p1(1, s), self.side1.at[2, s], {"dp": self.dp ^ my}, k + 9)

    def three(self, o):
        s, k = self.seat(o), self.COPIES * o
        for ref, side, k1, k2 in ((self.p0(0, s), self.side0, k + 6, k + 8), (self.p1(0, s), self.side1, k + 7, k + 9)):
            self.arrived(side.at[0, s], k1)
            self.arrived(side.at[2, s], k2)
            ref[...] = (ref[...].astype(F32) + side[0, s].astype(F32) + side[2, s].astype(F32)).astype(BF)
        if o:
            self.begin(self.held(0, s), self.far.at[o - 1], {"seq": s}, self.COPIES * self.nz + o)

    def four(self):
        out = self.held(0, self.z)[...].astype(F32)
        for o in range(1, self.nz):
            self.arrived(self.far.at[o - 1], self.COPIES * self.nz + o)
            out = out + self.far[o - 1].astype(F32)
        self.total[...] = out

    def done(self):
        for k, width in self.started:
            whole = width == self.src.shape[-1]
            ref = self.near.at[0, 0] if whole else (self.side0 if k % self.COPIES in (4, 6, 8) else self.side1).at[0, 0]
            remote(ref, ref, self.send.at[k], self.recv.at[k], {"dp": self.dp ^ self.masks[2]}).wait_send()


def back_kernel(nz, masks, rows, *refs):
    fused = masks is not None
    (tok, gmid, out_own, query, kv, firsts, wqkv, gain, gmixed, lse, delta, cos_in), refs = refs[:12], refs[12:]
    if fused:
        (po_g, pm_g, gtok, out, s0, s1, so, sm), refs = refs[:8], refs[8:]
    else:
        (gtok, out, p0_g, p1_g), refs = refs[:4], refs[4:]
    (kvb, fb, ft, wq, cos, sine, dq, dqb, dkv, dx, dw, sent, landed, gown, gcol, send, recv, loc), refs = refs[:18], refs[18:]
    me = Place(nz)
    own = me.shard

    def here(src, dst, k):
        return pltpu.make_async_copy(src, dst, loc.at[k])

    def there(src, dst, device, k):
        return remote(src, dst, send.at[k], recv.at[k], device)

    def chunk(t):
        return jnp.where(t == 0, own ^ 2, jnp.where(t == 1, own ^ 1, jnp.where(t == 2, own ^ 3, own)))

    def fetch(grp, t):
        c, slot = chunk(t), lax.rem(t, 2)
        found = [here(kv.at[grp, c], kvb.at[slot], slot)]
        if grp == 0:
            found.append(here(firsts.at[c], fb.at[slot], 2 + slot))
        return found

    for c in fetch(0, 0):
        c.start()
    whole = [here(wqkv, wq, 4), here(cos_in, cos, 5)]
    for c in whole:
        c.start()
    me.greet(masks or (1,))
    jobs, sums = [], []
    if fused:
        (p0_g, p1_g), refs = refs[:2], refs[2:]
        for src, total in ((p0_g, s0), (p1_g, s1)):
            sums.append(Reduce(src, total, CUTS[src.shape[-1]], nz, masks, refs[:4], *refs[4:6]))
            refs = refs[6:]
        for src, total in ((po_g, so), (pm_g, sm)):
            jobs.append(Reduce(src, total, CUTS[src.shape[-1]], nz, masks, refs[:5], *refs[5:8]))
            refs = refs[8:]
    order = (3, 2, 1, 0)

    def advance(which, step):
        for j in which:
            for o in order:
                getattr(j, step)(o)

    def wave(which):
        for i in range(nz + 2):
            for k, step in enumerate(("one", "two", "three")):
                if 0 <= i - k < nz:
                    for j in which:
                        getattr(j, step)(order[i - k])

    advance(jobs, "zero")

    @pl.when(me.moves)
    def _():
        there(out_own, out, me.opposite, 3).start()

    @pl.when(me.stays)
    def _():
        here(out_own, out, 7).start()

    dq[...] = jnp.zeros_like(dq)
    for c in whole:
        c.wait()
    spread_tables(cos, sine)

    def visits(grp, steps):
        def visit(t, _):
            c, slot = chunk(t), lax.rem(t, 2)
            for f in fetch(grp, t):
                f.wait()

            @pl.when(t + 1 < nz)
            def _():
                for f in fetch(grp, t + 1):
                    f.start()

            if grp == 0:

                @pl.when(t + 1 == nz)
                def _():
                    for f in fetch(1, 0):
                        f.start()

            band = pl.ds(pl.multiple_of(t * rows, rows), rows)
            todo = [(i, h) for i in range(3) for h in range(2)]

            def pick(ref, i, h):
                x = ref[:, HALF * grp + 128 * i : HALF * grp + 128 * i + 128]
                mask = (lane_iota() < 64) if h == 0 else (lane_iota() >= 64)
                return jnp.where(mask, x, jnp.zeros_like(x))

            def score(i, h):
                qh, gh = pick(query, i, h), pick(gmixed, i, h)
                k, v = kvb[slot, :, 128 * i : 128 * i + 128], kvb[slot, :, HALF + 128 * i : HALF + 128 * i + 128]
                return dot(k, qh, NT), dot(v, gh, NT), qh, gh

            ready = [score(*todo[0])]
            dk = dv = None
            for n, (i, h) in enumerate(todo):
                s, dp, qh, gh = ready[n]
                if n + 1 < len(todo):
                    ready.append(score(*todo[n + 1]))
                if h == 0:
                    kt = kvb[slot, :, 128 * i : 128 * i + 128].T
                head = 6 * grp + n
                p = jnp.exp2(s - lse[head : head + 1, :])
                ds = (p * (dp - delta[head : head + 1, :])).astype(BF)
                a = dot(p.astype(BF), gh, NN)
                dv = a if h == 0 else dv + a
                a = dot(ds, qh, NN)
                dk = a if h == 0 else dk + a
                dq[64 * head : 64 * head + 64, :] += dot(kt[h * 64 : h * 64 + 64], ds, NN)
                if h == 1:
                    at = WIDTH * grp + 128 * i
                    dkv[band, at : at + 128] = rope_back(dk * (1.0 / LOG2E), cos[c], sine[c]).astype(BF)
                    dkv[band, at + HALF : at + HALF + 128] = dv.astype(BF)

            if grp == 0:
                for j in range(6):
                    ft[128 * j : 128 * j + 128, band] = fb[slot, :, 128 * j : 128 * j + 128].T
            else:
                for j in range(3):
                    at = slice(256 * j, 256 * j + 256)
                    dx[:, at] = dot(dkv[band, :], wq[at, : 2 * WIDTH], NT)

                @pl.when(lax.rem(t, 2) == 0)
                def _():
                    sent[t] = dx[...].astype(BF)
                    there(sent.at[t], landed.at[t], me.twin, t).start()

                @pl.when(t == 1)
                def _():
                    there(sent.at[0], landed.at[0], me.twin, 0).wait_recv()
                    sent[1] = (dx[...] + landed[0].astype(F32)).astype(BF)
                    there(sent.at[1], landed.at[1], me.beside, 1).start()

            if fused:
                for k, step in steps.items():

                    @pl.when(t == k)
                    def _(step=step):
                        for which, name in step:
                            if name == "four":
                                for j in which:
                                    j.four()
                            else:
                                advance(which, name)

            return 0

        lax.fori_loop(0, nz, visit, 0)
        for i in range(3 * grp, 3 * grp + 3):
            at = slice(128 * i, 128 * i + 128)
            dqb[:, at] = rope_back(dq[at, :].T * SCALE, cos[own], sine[own]).astype(BF)

    def weigh(grp):
        for r in (slice(0, HALF), slice(HALF, WIDTH)):
            for j in range(3):
                at = WIDTH * grp + 256 * j
                dw[r, HALF + 256 * j : HALF + 256 * j + 256] = dot(ft[r, :], dkv[:, at : at + 256], NN)
            dw[r, :HALF] = dot(ft[r, (nz - 1) * rows :], dqb[:, HALF * grp : HALF * grp + HALF], NN)

    def pack(grp, dst):
        def band_of(g, _):
            for s in range(LINE):
                at = pl.ds(pl.multiple_of(g * BAND + s * SLIVER, 8), SLIVER)
                q, k, v0, v1 = dw[at, :HALF], dw[at, HALF:WIDTH], dw[at, WIDTH : WIDTH + 256], dw[at, WIDTH + 256 :]
                tile = gcol[at, :] if grp else jnp.zeros((SLIVER, 128), F32)
                dst[g, s] = jnp.concatenate(
                    [jnp.concatenate([q, v0], 1), jnp.concatenate([k, v1, tile], 1)], 0
                ).astype(BF)
            return 0

        lax.fori_loop(0, GROUPS, band_of, 0)

    visits(0, {0: [(jobs, "one")]})
    weigh(0)
    pack(0, p0_g)
    early = sums[:1]
    advance(early, "zero")
    visits(1, {0: [(jobs, "two"), (early, "one")], 2: [(jobs, "three")], 3: [(early, "two"), (early, "three")]})
    for j in range(3):
        at = slice(256 * j, 256 * j + 256)
        dx[:, at] += dot(dqb[...], wq[at, 2 * WIDTH :], NT)
    there(sent.at[1], landed.at[1], me.beside, 1).wait_recv()
    there(sent.at[2], landed.at[2], me.twin, 2).wait_recv()

    def norm_block(i, dgain):
        at = pl.ds(pl.multiple_of(i * 64, 64), 64)
        dy = dx[at, :] + landed[1, at, :].astype(F32) + landed[2, at, :].astype(F32)
        h, r = normed(tok[at, :].astype(F32))
        gown[at, :] = (gmid[at, :] + norm_back(dy, gain[0:1, :], h, r)).astype(BF)
        return dgain + jnp.sum(dy * h, 0, keepdims=True)

    dgain = lax.fori_loop(0, rows // 64, norm_block, jnp.zeros((1, WIDTH), F32))

    @pl.when(me.moves)
    def _():
        there(gown, gtok, me.opposite, 4).start()

    @pl.when(me.stays)
    def _():
        here(gown, gtok, 8).start()

    row = lax.broadcasted_iota(jnp.int32, (128, WIDTH), 0)
    gcol[...] = jnp.where(row == 0, dgain, 0.0).T
    weigh(1)
    pack(1, p1_g)
    if fused:
        advance(sums[1:], "zero")
        wave(sums[1:])
        for j in jobs + sums:
            j.four()
        for j in jobs + sums:
            j.done()
    for k, device in ((0, me.twin), (1, me.beside), (2, me.twin)):
        there(sent.at[k], landed.at[k], device, k).wait_send()

    @pl.when(me.moves)
    def _():
        there(out_own, out, me.opposite, 3).wait()
        there(gown, gtok, me.opposite, 4).wait()

    @pl.when(me.stays)
    def _():
        here(out_own, out, 7).wait()
        here(gown, gtok, 8).wait()


def back(tok, gmid, out_own, query, kv, firsts, wqkv, gain, gmixed, lse, delta, tables, packs, nz, masks):
    rows = tok.shape[0]
    shape, vm = jax.ShapeDtypeStruct, pltpu.VMEM
    vmem, anyspace = pl.BlockSpec(memory_space=pltpu.VMEM), pl.BlockSpec(memory_space=pl.ANY)
    in_specs = [vmem, vmem, anyspace, vmem] + [anyspace] * 3 + [vmem] * 4 + [anyspace]
    slab = (2 * SLIVER, 640)
    outs, out_specs = [shape((rows, WIDTH), BF)] * 2, [vmem] * 2
    scratch = [
        vm((2, rows, WIDTH), BF),
        vm((2, rows, WIDTH), BF),
        vm((WIDTH, nz * rows), BF),
        vm((WIDTH, 3 * WIDTH), BF),
        vm((nz, rows, 128), F32),
        vm((nz, rows, 128), F32),
        vm((WIDTH, rows), F32),
        vm((rows, WIDTH), BF),
        vm((nz * rows, 2 * WIDTH), BF),
        vm((rows, WIDTH), F32),
        vm((WIDTH, 3 * HALF), F32),
        vm((3, rows, WIDTH), BF),
        vm((3, rows, WIDTH), BF),
        vm((rows, WIDTH), BF),
        vm((WIDTH, 128), F32),
        pltpu.SemaphoreType.DMA((5,)),
        pltpu.SemaphoreType.DMA((5,)),
        pltpu.SemaphoreType.DMA((9,)),
    ]
    if masks:
        in_specs += [anyspace] * 2
        outs += [shape(s, F32) for s in (slab, slab, packs[0].shape[-2:], packs[1].shape[-2:])]
        out_specs += [vmem] * 4
        scratch += [vm((GROUPS, LINE) + slab, BF)] * 2
        for s, held in ((slab, True), (slab, True), (packs[0].shape[-2:], False), (packs[1].shape[-2:], False)):
            bufs, sems = Reduce.scratch(s, nz, held)
            scratch += bufs + sems
    else:
        outs += [shape((GROUPS, LINE) + slab, BF)] * 2
        out_specs += [vmem] * 2
        packs = []
    return pl.pallas_call(
        functools.partial(back_kernel, nz, masks, rows),
        out_shape=outs,
        in_specs=in_specs,
        out_specs=out_specs,
        scratch_shapes=scratch,
        compiler_params=pltpu.CompilerParams(collective_id=1, has_side_effects=True, vmem_limit_bytes=62 << 20),
        cost_estimate=pl.CostEstimate(flops=24_000_000_000, bytes_accessed=40_000_000, transcendentals=13_000_000),
        name="back",
    )(tok, gmid, out_own, query, kv, firsts, wqkv, gain, gmixed, lse, delta, tables, *packs)


def finish_kernel(out, gtok, s0, s1, so, sm, out_o, gtok_o, qkv_o, w_out_o, gain_a_o, gain_m_o, w_in_o, down_o):
    out_o[...] = out[...]
    gtok_o[...] = gtok[...]
    for i, total in enumerate((s0, s1)):
        q, k, v0, v1, tile = unpack_group(total[...])
        for j, x in enumerate((q, k)):
            qkv_o[:, WIDTH * j + HALF * i : WIDTH * j + HALF * i + HALF] = x
        at = 2 * WIDTH + HALF * i
        qkv_o[:, at : at + 256] = v0
        qkv_o[:, at + 256 : at + HALF] = v1
    w_out_o[:, :HALF] = so[:SLIVER, :HALF]
    w_out_o[:, HALF:] = so[SLIVER:, :HALF]
    zeros = jnp.zeros((128 - SLIVER, 128), F32)
    for dst, col in ((gain_a_o, tile), (gain_m_o, so[:SLIVER, HALF:])):
        dst[...] = jnp.concatenate([col, zeros], 0).T[:1, :SLIVER]
    gate, up, down = unpack_mlp(sm[...])
    w_in_o[:, 0, :] = gate
    w_in_o[:, 1, :] = up
    down_o[...] = down.T


def finish(out, gtok, s0, s1, so, sm):
    shape = jax.ShapeDtypeStruct
    vmem = pl.BlockSpec(memory_space=pltpu.VMEM)
    return pl.pallas_call(
        finish_kernel,
        out_shape=[
            shape(out.shape, BF),
            shape(gtok.shape, BF),
            shape((SLIVER, 3 * WIDTH), F32),
            shape((SLIVER, WIDTH), F32),
            shape((1, SLIVER), F32),
            shape((1, SLIVER), F32),
            shape((BAND, 2, SHARE), F32),
            shape((SHARE, BAND), F32),
        ],
        in_specs=[vmem] * 6,
        out_specs=[vmem] * 8,
        compiler_params=pltpu.CompilerParams(vmem_limit_bytes=60 << 20),
        name="finish",
    )(out, gtok, s0, s1, so, sm)


def whole_packs(w_qkv, w_out, attn_gain, mlp_gain, w_in, w_down):
    both = ("dp", "seq")

    def shards_of(w):
        w = lax.all_gather(w, both, axis=0, tiled=True)
        return w.reshape(GROUPS * LINE, SLIVER, -1)

    def slabs(pack, w, gain):
        found = jax.vmap(pack)(w, jnp.pad(gain, ((0, 0), (0, 0), (0, 127))))
        return found.reshape((GROUPS, LINE) + found.shape[1:])

    qkv, gain_a, gain_m = shards_of(w_qkv), shards_of(attn_gain), shards_of(mlp_gain)
    groups = [slabs(lambda w, t, i=i: pack_group(w, t, i), qkv, gain_a) for i in range(2)]
    w_in, w_down = lax.all_gather(w_in, "dp", axis=0, tiled=True), lax.all_gather(w_down, "dp", axis=1, tiled=True)
    mlp = lax.all_gather(pack_mlp(w_in[:, 0], w_in[:, 1], w_down.T), "seq", axis=0, tiled=False)
    mlp = mlp.reshape(LINE, GROUPS, BAND, -1).transpose(1, 0, 2, 3)
    return groups, slabs(pack_out, shards_of(w_out), gain_m), mlp


def whole_sums(p0_g, p1_g, po_g, pm_g):
    both = ("dp", "seq")

    def scattered(x):
        return lax.psum_scatter(x.reshape(WIDTH, -1), both, scatter_dimension=0, tiled=True)

    parts = [jax.vmap(unpack_group)(p.reshape((GROUPS * LINE,) + p.shape[2:]).astype(F32)) for p in (p0_g, p1_g)]
    columns = [parts[0][0], parts[1][0], parts[0][1], parts[1][1], parts[0][2], parts[0][3], parts[1][2], parts[1][3]]
    g_qkv, gain_a = scattered(jnp.concatenate(columns, -1)), scattered(parts[1][4][..., :1])[:, 0]
    po = po_g.reshape(GROUPS * LINE, 2 * SLIVER, -1).astype(F32)
    g_out = scattered(jnp.concatenate([po[:, :SLIVER, :HALF], po[:, SLIVER:, :HALF]], -1))
    gain_m = scattered(po[:, :SLIVER, HALF : HALF + 1])[:, 0]
    mlp = pm_g.astype(F32).transpose(1, 0, 2, 3).reshape(LINE, WIDTH, -1)
    mlp = lax.psum_scatter(mlp, "seq", scatter_dimension=0, tiled=False)
    gate, up, down = unpack_mlp(lax.psum_scatter(mlp, "dp", scatter_dimension=0, tiled=True))
    return g_qkv, g_out, gain_a, gain_m, jnp.stack([gate, up], 1), down.T


def on_device(tokens, w_qkv, w_out, attn_gain, mlp_gain, w_in, w_down, grad_out, *, dp, nz):
    rows = tokens.shape[0]
    masks = (dp // 2, dp // 4, 1) if dp == GROUPS else None
    tables = jnp.asarray(rope_tables(nz * rows)).reshape(nz, rows, 128)
    if masks:
        weights = [w_qkv, w_out, attn_gain[None], mlp_gain[None], w_in, w_down]
        got = front(tokens, grad_out, weights, tables, nz, masks)
        po_all, pm_all = got[-2:]
    else:
        groups, po_all, pm_all = whole_packs(w_qkv, w_out, attn_gain, mlp_gain, w_in, w_down)
        got = front(tokens, grad_out, groups, tables, nz, None)
    mixed, lse, query, gain, tok_own, gout_own, kv, firsts, wqkv = got[:9]
    out_own, gmid, gmixed, delta, po_g, pm_g = middle(tok_own, mixed, gout_own, po_all, pm_all)
    found = back(tok_own, gmid, out_own, query, kv, firsts, wqkv, gain, gmixed, lse, delta, tables, [po_g, pm_g], nz, masks)
    gtok, out, *sums = found
    if not masks:
        return (out, gtok, *whole_sums(*sums, po_g, pm_g))
    out, gtok, g_qkv, g_out, gain_a, gain_m, g_in, g_down = finish(out, gtok, *sums)
    return out, gtok, g_qkv, g_out, gain_a[0], gain_m[0], g_in, g_down


def solution(mesh):
    both = P(("dp", "seq"), None)
    vector = P(("dp", "seq"))
    w_in, w_down = P("dp", None, "seq"), P("seq", "dp")
    step = functools.partial(on_device, dp=mesh.shape["dp"], nz=mesh.shape["seq"])
    return jax.shard_map(
        step,
        mesh=mesh,
        in_specs=(both, both, both, vector, vector, w_in, w_down, both),
        out_specs=(both, both, both, both, vector, vector, w_in, w_down),
        check_vma=False,
    )
```

```python
import functools
import math

import jax
import jax.numpy as jnp
import numpy as np
from jax import lax
from jax.experimental import pallas as pl
from jax.experimental.pallas import tpu as pltpu
from jax.sharding import PartitionSpec as P

HEADS = 12
HEAD_DIM = 64
NORM_EPS = 1e-05
ROPE_THETA = 160000.0

F32 = jnp.float32
BF = jnp.bfloat16
MESH = pl.DeviceIdType.MESH
NT = (((1,), (1,)), ((), ()))
NN = (((1,), (0,)), ((), ()))
TN = (((0,), (0,)), ((), ()))

WIDTH = 768
PAIRS = HEADS // 2
UNITS = 1152
GROUPS = 8
LINE = 4
BAND = WIDTH // GROUPS
SLIVER = BAND // LINE
SHARE = UNITS // LINE
MAIN = 256
REST = SHARE - MAIN
LINKED = (0, 1, 3, 2)
HALF = WIDTH // 2
CUTS = {640: 256, 512: 256, 896: 384}
LOG2E = math.log2(math.e)
SCALE = HEAD_DIM**-0.5


def dot(a, b, dims):
    return lax.dot_general(a, b, dims, preferred_element_type=F32)


def lanes_of(tile, width=128):
    return pl.ds(pl.multiple_of(tile * width, width), width)


def tiles(start, width):
    return pl.ds(pl.multiple_of(start, width if width < 128 else 128), width)


def lane_iota():
    return lax.broadcasted_iota(jnp.int32, (1, 128), 1)


def swap_halves(u):
    low = lax.rem(lane_iota(), 64) < 32
    return jnp.where(low, pltpu.roll(u, 96, 1), pltpu.roll(u, 32, 1))


def rope(u, cos, sine):
    return u * cos + swap_halves(u) * sine


def rope_back(u, cos, sine):
    return u * cos - swap_halves(u) * sine


def rope_tables(rows):
    position = np.arange(rows, dtype=np.float32)
    half = HEAD_DIM // 2
    freq = (ROPE_THETA ** (-np.arange(half) * 2.0 / HEAD_DIM)).astype(np.float32)
    angle = (position[:, None] * freq[None, :]).astype(np.float64)
    cos, sine = np.cos(angle), np.sin(angle)
    return np.concatenate([cos, cos, -sine, sine], 1).astype(np.float32)


def spread_tables(cos, sine):
    low = lane_iota() < 64

    def chunk(c, _):
        both = cos[c]
        other = pltpu.roll(both, 64, 1)
        cos[c] = jnp.where(low, both, other)
        sine[c] = jnp.where(low, other, both)
        return 0

    lax.fori_loop(0, cos.shape[0], chunk, 0)


def normed(x):
    centred = x - jnp.mean(x, -1, keepdims=True)
    inv = lax.rsqrt(jnp.mean(centred * centred, -1, keepdims=True) + NORM_EPS)
    return centred * inv, inv


def norm_back(dy, gain, hat, inv):
    d = dy * gain
    return inv * (d - jnp.mean(d, -1, keepdims=True) - hat * jnp.mean(d * hat, -1, keepdims=True))


def remote(src, dst, send, recv, device):
    return pltpu.make_async_remote_copy(src, dst, send, recv, device_id=device, device_id_type=MESH)


class Place:
    def __init__(self, nz):
        self.dp, self.z = lax.axis_index("dp"), lax.axis_index("seq")
        self.nz = nz
        upper = self.z // (nz // 2)
        self.moves = lax.rem(self.dp, 2) != upper
        self.stays = lax.rem(self.dp, 2) == upper
        self.shard = jnp.where(self.moves, nz - 1 - self.z, self.z)
        self.opposite = {"dp": self.dp ^ 1, "seq": nz - 1 - self.z}
        self.twin = {"dp": self.dp ^ 1}
        self.beside = {"seq": self.z ^ 1}

    def greet(self, masks):
        bar = pltpu.get_barrier_semaphore()

        def hello(device):
            pl.semaphore_signal(bar, inc=1, device_id=device, device_id_type=MESH)

        for o in range(1, self.nz):
            hello({"seq": lax.rem(self.z + o, self.nz)})
        for m in masks:
            hello({"dp": self.dp ^ m})
        hello(self.opposite)
        pl.semaphore_wait(bar, self.nz + len(masks))


class Gather:
    COPIES = 9

    def __init__(self, src, out, cut, nz, masks, send, recv):
        self.src, self.out, self.cut, self.nz, self.masks = src, out, cut, nz, masks
        self.send, self.recv = send, recv
        self.dp, self.z = lax.axis_index("dp"), lax.axis_index("seq")
        self.started = []
        self.relayed = None

    @staticmethod
    def sems(nz):
        return Gather.COPIES * nz + nz

    def key(self, o, k):
        return o * self.COPIES + k

    def copy(self, src, dst, device, k):
        return remote(src, dst, self.send.at[k], self.recv.at[k], device)

    def begin(self, src, dst, device, k, p=None):
        self.copy(src, dst, device, k).start()
        self.started.append((k, p))

    def arrived(self, ref, k):
        self.copy(ref, ref, {"dp": self.dp ^ self.masks[0]}, k).wait_recv()

    def slot(self, o):
        return self.z ^ LINKED[o]

    def part(self, ref, p):
        if p is None:
            return ref
        width = self.out.shape[-1]
        return ref.at[:, pl.ds(0, self.cut)] if p == 0 else ref.at[:, pl.ds(self.cut, width - self.cut)]

    def along(self, o):
        self.begin(self.src, self.out.at[self.dp, self.z], {"seq": self.z ^ LINKED[o]}, self.COPIES * self.nz + o)

    def relay(self, o):
        ref = self.out.at[self.dp, self.slot(o)]
        self.arrived(ref, self.COPIES * self.nz + o)
        self.relayed = o
        self.begin(ref, ref, {"seq": self.z ^ 1}, self.COPIES * self.nz + 3)

    def forward(self, src, d, s, mask, k, p=None):
        dst = self.out.at[d, s]
        self.begin(self.part(src, p), self.part(dst, p), {"dp": self.dp ^ mask}, k, p)

    def first(self, o):
        my, mx, mc = self.masks
        s = self.slot(o)
        src = self.src
        if o:
            src = self.out.at[self.dp, s]
            if o != self.relayed:
                self.arrived(src, self.COPIES * self.nz + o)
        self.forward(src, self.dp, s, my, self.key(o, 0))
        self.forward(src, self.dp, s, mx, self.key(o, 1))
        self.forward(src, self.dp, s, mc, self.key(o, 2))

    def second(self, o):
        my, mx, mc = self.masks
        s = self.slot(o)
        for m, k, k2, kc, p, m2 in ((my, 0, 3, 4, 0, mx), (mx, 1, 5, 6, 1, my)):
            ref = self.out.at[self.dp ^ m, s]
            self.arrived(ref, self.key(o, k))
            self.forward(ref, self.dp ^ m, s, m2, self.key(o, k2), p)
            self.forward(ref, self.dp ^ m, s, mc, self.key(o, kc))

    def third(self, o):
        my, mx, mc = self.masks
        s = self.slot(o)
        d = self.dp ^ my ^ mx
        for p, k, kc in ((0, 3, 7), (1, 5, 8)):
            ref = self.out.at[d, s]
            self.arrived(self.part(ref, p), self.key(o, k))
            self.forward(ref, d, s, mc, self.key(o, kc), p)

    def finish(self, o):
        my, mx, mc = self.masks
        s = self.slot(o)
        for k, d in ((2, mc), (4, mc ^ my), (6, mc ^ mx)):
            self.arrived(self.out.at[self.dp ^ d, s], self.key(o, k))
        for k, p in ((7, 0), (8, 1)):
            self.arrived(self.part(self.out.at[self.dp ^ mc ^ my ^ mx, s], p), self.key(o, k))

    def done(self):
        for k, p in self.started:
            ref = self.part(self.out.at[self.dp, self.z], p)
            self.copy(ref, ref, {"dp": self.dp ^ self.masks[0]}, k).wait_send()


def pack_group(w, tile, i):
    q, k, v = [w[:, WIDTH * j + HALF * i : WIDTH * j + HALF * i + HALF] for j in range(3)]
    return jnp.concatenate([jnp.concatenate([q, v[:, :256]], 1), jnp.concatenate([k, v[:, 256:], tile], 1)], 0)


def unpack_group(total):
    r = total.shape[0] // 2
    upper, lower = total[:r], total[r:]
    return upper[:, :HALF], lower[:, :HALF], upper[:, HALF:], lower[:, HALF : HALF + 128], lower[:, HALF + 128 :]


def pack_out(w, tile):
    return jnp.concatenate([jnp.concatenate([w[:, :HALF], w[:, HALF:]], 0), jnp.concatenate([tile, jnp.zeros_like(tile)], 0)], 1)


def pack_mlp(gate, up, down):
    parts = (gate, up, down)
    pads = jnp.zeros((gate.shape[0], 128 - 3 * REST), gate.dtype)
    return jnp.concatenate([x[:, :MAIN] for x in parts] + [x[:, MAIN:] for x in parts] + [pads], 1)


def unpack_mlp(total):
    return [
        jnp.concatenate([total[:, MAIN * i : MAIN * i + MAIN], total[:, 3 * MAIN + REST * i : 3 * MAIN + REST * i + REST]], 1)
        for i in range(3)
    ]


def front_kernel(nz, masks, rows, *refs):
    fused = masks is not None
    if fused:
        (tok, gout, w_qkv, w_out, gain_a, gain_m, w_in, w_down, cos_in), refs = refs[:9], refs[9:]
    else:
        (tok, gout, g0_all, g1_all, cos_in), refs = refs[:5], refs[5:]
    (mixed, lse, query, gain, tok_own, gout_own, kv, firsts, wqkv), refs = refs[:9], refs[9:]
    if fused:
        (po_all, pm_all), refs = refs[:2], refs[2:]
    (tok_all, kvb, fb, wq, cos, sine, gcol, acc, top, total, tsend, trecv, loc), refs = refs[:13], refs[13:]
    me = Place(nz)
    own = me.shard

    def here(src, dst, k):
        return pltpu.make_async_copy(src, dst, loc.at[k])

    def there(src, dst, device, k):
        return remote(src, dst, tsend.at[k], trecv.at[k], device)

    def rows_to(src, c, device, k, i):
        at = pl.ds(i * (rows // 2), rows // 2)
        src = tok_all.at[c] if src is None else src
        return there(src.at[at], tok_all.at[c, at], device, k + 5 * i)

    @pl.when(me.stays)
    def _():
        here(tok, tok_all.at[own], 0).start()
        here(gout, gout_own, 1).start()

    here(cos_in, cos, 2).start()
    groups, later = [], []
    every, rest = range(nz), (2, 1, 3)
    if fused:
        p0, p1, po, pm, g0_all, g1_all, *sems = refs
        row = lax.broadcasted_iota(jnp.int32, (128, 128), 0)

        def tile_of(part):
            line = jnp.concatenate([part[...].astype(F32), jnp.zeros((1, 128 - SLIVER), F32)], 1)
            return jnp.where(row == 0, line, 0.0).T[:SLIVER]

        p0[...] = pack_group(w_qkv[...].astype(F32), tile_of(gain_a), 0).astype(BF)
        g0_all[me.dp, me.z] = p0[...]
    me.greet(masks or (1,))
    if fused:
        shapes = ((p0, g0_all), (p1, g1_all), (po, po_all), (pm, pm_all))
        packs = [
            Gather(src, dst, CUTS[src.shape[-1]], nz, masks, sems[2 * i], sems[2 * i + 1]) for i, (src, dst) in enumerate(shapes)
        ]
        groups, later = packs[:2], packs[2:]
        for o in rest:
            groups[0].along(o)
        groups[0].first(0)

    @pl.when(me.stays)
    def _():
        for i in range(2):
            rows_to(tok, own, me.twin, 1, i).start()
            rows_to(tok, own, me.beside, 2, i).start()

    @pl.when(me.moves)
    def _():
        for i in range(2):
            rows_to(tok, me.z, me.opposite, 0, i).start()

    def swapped(i):
        @pl.when(me.moves)
        def _():
            rows_to(None, own, me.opposite, 0, i).wait_recv()
            rows_to(None, own, me.beside, 2, i).start()
            rows_to(None, own, me.twin, 1, i).start()

    if fused:
        w = w_qkv[...].astype(F32)
        p1[...] = pack_group(w, jnp.zeros((SLIVER, 128), F32), 1).astype(BF)
        g1_all[me.dp, me.z] = p1[...]
        po[...] = pack_out(w_out[...].astype(F32), tile_of(gain_m)).astype(BF)
        pm[...] = pack_mlp(w_in[:, 0, :].astype(F32), w_in[:, 1, :].astype(F32), w_down[...].astype(F32).T).astype(BF)
        here(po, po_all.at[me.dp, me.z], 4).start()
        here(pm, pm_all.at[me.dp, me.z], 5).start()
        for o in rest:
            groups[1].along(o)
        groups[1].first(0)
        groups[0].second(0)
        for o in rest:
            groups[0].first(o)
        swapped(0)
        for o in rest:
            groups[0].second(o)
        for o in rest:
            groups[1].first(o)
        for g in later:
            g.along(1)
            g.first(0)

    if not fused:
        swapped(0)
    swapped(1)

    @pl.when(me.stays)
    def _():
        here(tok, tok_all.at[own], 0).wait()

    here(tok_all.at[own], tok_own, 6).start()
    if fused:
        for g in later:
            g.along(2)
        for o in range(nz):
            groups[0].third(o)
        for o in range(nz):
            groups[0].finish(o)

    @pl.when(me.moves)
    def _():
        there(gout, gout_own, me.opposite, 4).start()

    here(cos_in, cos, 2).wait()
    spread_tables(cos, sine)

    def build(i, whole):
        def band_of(g, _):
            slabs = [unpack_group(whole[g, s].astype(F32)) for s in range(LINE)]
            band = pl.ds(pl.multiple_of(g * BAND, BAND), BAND)
            q, k, v0, v1, t = [jnp.concatenate([x[j] for x in slabs], 0) for j in range(5)]
            at = WIDTH * i
            wq[band, at : at + HALF] = k.astype(BF)
            wq[band, at + HALF : at + HALF + 256] = v0.astype(BF)
            wq[band, at + HALF + 256 : at + WIDTH] = v1.astype(BF)
            wq[band, 2 * WIDTH + HALF * i : 2 * WIDTH + HALF * i + HALF] = q.astype(BF)
            if i == 0:
                gcol[band, :] = t
            return 0

        lax.fori_loop(0, GROUPS, band_of, 0)

    def norm_chunk(c):
        def block(i, _):
            at = pl.ds(pl.multiple_of(i * 64, 64), 64)
            hat, _ = normed(tok_all[c, at, :].astype(F32))
            fb[c, at, :] = (hat * gain[0:1, :]).astype(BF)
            return 0

        lax.fori_loop(0, rows // 64, block, 0)
        here(fb.at[c], firsts.at[c], 8 + c).start()

    def queries(i):
        u = dot(fb[own], wq[:, 2 * WIDTH + HALF * i : 2 * WIDTH + HALF * i + HALF], NN)
        for j in range(3):
            tile = rope(u[:, 128 * j : 128 * j + 128], cos[own], sine[own])
            query[:, HALF * i + 128 * j : HALF * i + 128 * j + 128] = (tile * (SCALE * LOG2E)).astype(BF)

    def visits(steps):
        def visit(n, _):
            t, grp = lax.rem(n, nz), n // nz
            stay = jnp.where(t == 1, 1, jnp.where(t == 2, 3, 2))
            move = jnp.where(t == 1, 3, jnp.where(t == 2, 2, 1))
            turn = jnp.where(me.stays, stay, move)
            c = jnp.where(t == 0, own, own ^ turn)
            @pl.when((n > 0) & (n < nz))
            def _():
                for i in range(2):
                    rows_to(None, c, me.twin, jnp.where(turn == 1, 2, jnp.where(turn == 3, 1, 3)), i).wait_recv()

                    @pl.when(turn == 1)
                    def _(i=i):
                        rows_to(None, c, me.twin, 3, i).start()

                norm_chunk(c)

            for j in range(3):
                u = dot(fb[c], wq[:, tiles(WIDTH * grp + 256 * j, 256)], NN)
                for i in range(2):
                    tile = 2 * j + i
                    x = u[:, 128 * i : 128 * i + 128]
                    x = rope(x, cos[c], sine[c]) if tile < 3 else x
                    kvb[grp, c, :, 128 * tile : 128 * tile + 128] = x.astype(BF)
            here(kvb.at[grp, c], kv.at[grp, c], 8 + nz * (1 + grp) + c).start()
            jobs = [(i, h) for i in range(3) for h in range(2)]

            def score(i, h):
                q = query[:, tiles(HALF * grp + 128 * i, 128)]
                mask = (lane_iota() < 64) if h == 0 else (lane_iota() >= 64)
                return dot(kvb[grp, c, :, 128 * i : 128 * i + 128], jnp.where(mask, q, jnp.zeros_like(q)), NT)

            ready = [score(*j) for j in jobs[:2]]
            for m, (i, h) in enumerate(jobs):
                if h == 0:
                    vt = kvb[grp, c, :, HALF + 128 * i : HALF + 128 * i + 128].T
                s = ready[m]
                if m + 2 < len(jobs):
                    ready.append(score(*jobs[m + 2]))
                head = pl.ds(6 * grp + m, 1)
                band = tiles(64 * (6 * grp + m), 64)
                old = top[head, :]
                new = jnp.maximum(old, jnp.max(s, 0, keepdims=True))
                p = jnp.exp2(s - new)
                fade = jnp.exp2(old - new)
                top[head, :] = new
                lhs = jnp.concatenate([vt[h * 64 : h * 64 + 64], jnp.ones((16, rows), BF)], 0)
                oo = dot(lhs, p.astype(BF), NN)
                total[head, :] = total[head, :] * fade + oo[64:65]
                acc[band, :] = acc[band, :] * fade + oo[:64]
            for k, step in steps.items():

                @pl.when(n == k)
                def _(k=k, step=step):
                    for which, name, order in step:
                        for g in which:
                            for o in order:
                                getattr(g, name)(o)
                    if k == nz - 1:
                        build(1, g1_all)
                        here(wq, wqkv, 7).start()
                        queries(1)

            return 0

        lax.fori_loop(0, 2 * nz, visit, 0)

    build(0, g0_all)
    gain[...] = gcol[...].T[:8]
    norm_chunk(own)
    queries(0)
    acc[...] = jnp.zeros_like(acc)
    total[...] = jnp.zeros_like(total)
    top[...] = jnp.full_like(top, -1e30)
    one = groups[1:]
    visits({
        0: [(one, "second", every), (later, "first", (1,))],
        1: [(one, "third", every)],
        2: [(later, "relay", (2,)), (later, "first", (2,))],
        3: [(one, "finish", every), (later, "second", (0, 1))],
        4: [(later, "first", (3,))],
        5: [(later, "second", (2,))],
        6: [(later, "second", (3,))],
        7: [(later, "third", every)],
    })

    for hp in range(PAIRS):
        parts = [
            acc[128 * hp + 64 * h : 128 * hp + 64 * h + 64, :] / total[2 * hp + h : 2 * hp + h + 1, :] for h in range(2)
        ]
        mixed[:, 128 * hp : 128 * hp + 128] = jnp.concatenate(parts, 0).T.astype(BF)
    lse[...] = top[...] + jnp.log(jnp.maximum(total[...], 1e-30)) * LOG2E

    if fused:
        for g in later:
            for o in range(nz):
                g.finish(o)
        for g in packs:
            g.done()
        here(po, po_all.at[me.dp, me.z], 4).wait()
        here(pm, pm_all.at[me.dp, me.z], 5).wait()
    for i in range(2):
        for k in (1, 2, 3):
            rows_to(None, own, me.twin, k, i).wait_send()

    @pl.when(me.moves)
    def _():
        for i in range(2):
            rows_to(None, own, me.opposite, 0, i).wait_send()
        there(gout, gout_own, me.opposite, 4).wait()

    @pl.when(me.stays)
    def _():
        here(gout, gout_own, 1).wait()

    here(tok_all.at[own], tok_own, 6).wait()
    here(wq, wqkv, 7).wait()
    for c in range(nz):
        here(fb.at[c], firsts.at[c], 8 + c).wait()
        for grp in range(2):
            here(kvb.at[grp, c], kv.at[grp, c], 8 + nz * (1 + grp) + c).wait()


def front(tok, gout, weights, tables, nz, masks):
    rows = tok.shape[0]
    vmem, anyspace = pl.BlockSpec(memory_space=pltpu.VMEM), pl.BlockSpec(memory_space=pl.ANY)
    shape, vm = jax.ShapeDtypeStruct, pltpu.VMEM
    outs = [shape((rows, WIDTH), BF), shape((16, rows), F32), shape((rows, WIDTH), BF), shape((8, WIDTH), F32)]
    outs += [shape((rows, WIDTH), BF)] * 2
    outs += [shape((2, nz, rows, WIDTH), BF), shape((nz, rows, WIDTH), BF), shape((WIDTH, 3 * WIDTH), BF)]
    out_specs = [vmem] * 4 + [anyspace, vmem] + [anyspace] * 3
    scratch = [
        vm((nz, rows, WIDTH), BF),
        vm((2, nz, rows, WIDTH), BF),
        vm((nz, rows, WIDTH), BF),
        vm((WIDTH, 3 * WIDTH), BF),
        vm((nz, rows, 128), F32),
        vm((nz, rows, 128), F32),
        vm((WIDTH, 128), F32),
        vm((WIDTH, rows), F32),
        vm((16, rows), F32),
        vm((16, rows), F32),
        pltpu.SemaphoreType.DMA((9,)),
        pltpu.SemaphoreType.DMA((9,)),
        pltpu.SemaphoreType.DMA((8 + 3 * nz,)),
    ]
    if masks:
        grp, out, mlp = (2 * SLIVER, 640), (2 * SLIVER, 512), (BAND, 896)
        outs += [shape((GROUPS, nz) + out, BF), shape((GROUPS, nz) + mlp, BF)]
        out_specs += [anyspace] * 2
        scratch += [vm(x, BF) for x in (grp, grp, out, mlp)] + [vm((GROUPS, nz) + grp, BF)] * 2
        scratch += [pltpu.SemaphoreType.DMA((Gather.sems(nz),)) for _ in range(8)]
    return pl.pallas_call(
        functools.partial(front_kernel, nz, masks, rows),
        out_shape=outs,
        in_specs=[anyspace] * 2 + [vmem] * len(weights) + [anyspace],
        out_specs=out_specs,
        scratch_shapes=scratch,
        compiler_params=pltpu.CompilerParams(collective_id=0, has_side_effects=True, vmem_limit_bytes=60 << 20),
        cost_estimate=pl.CostEstimate(flops=14_000_000_000, bytes_accessed=40_000_000, transcendentals=13_000_000),
        name="front",
    )(tok, gout, *weights, tables)


def middle_kernel(rows, tok, mixed, gout, po_all, pm_in, out_own, gmid_own, gmixed, delta, po_g, pm_sums,
                  pm_all, pm_g, out, gmid, loc, wout, wg, wu, wd, gcol, gain, resid, hat, inv, second, hidden, ggate, gup, gsec, gattn, dwout):
    lane = lane_iota()

    def here(src, dst, k):
        return pltpu.make_async_copy(src, dst, loc.at[k])

    here(pm_in, pm_all, 0).start()

    def build(g, _):
        band = pl.ds(pl.multiple_of(g * BAND, BAND), BAND)
        slabs = [po_all[g, s].astype(F32) for s in range(LINE)]
        wout[band, :384] = jnp.concatenate([x[:SLIVER, :384] for x in slabs], 0).astype(BF)
        wout[band, 384:] = jnp.concatenate([x[SLIVER:, :384] for x in slabs], 0).astype(BF)
        gcol[band, :] = jnp.concatenate([x[:SLIVER, 384:] for x in slabs], 0)
        return 0

    def build_units(g, _):
        band = pl.ds(pl.multiple_of(g * BAND, BAND), BAND)
        for i, w in enumerate((wg, wu, wd)):
            tail = jnp.zeros((BAND, 128), F32)
            for s in range(LINE):
                w[band, MAIN * s : MAIN * s + MAIN] = pm_all[g, s, :, MAIN * i : MAIN * i + MAIN]
                rest = pm_all[g, s, :, 3 * MAIN :].astype(F32)
                turn = (REST * (s - i)) % 128
                rest = pltpu.roll(rest, turn, 1) if turn else rest
                tail = jnp.where((lane >= REST * s) & (lane < REST * (s + 1)), rest, tail)
            w[band, MAIN * LINE :] = tail.astype(BF)
        return 0

    lax.fori_loop(0, GROUPS, build, 0)
    gain[...] = gcol[...].T[:8]

    for j in range(3):
        at = slice(256 * j, 256 * j + 256)
        resid[:, at] = tok[:, at].astype(F32) + dot(mixed[...], wout[:, at], NN)

    def norm_block(i, _):
        at = pl.ds(pl.multiple_of(i * 64, 64), 64)
        h, r = normed(resid[at, :])
        hat[at, :] = h
        inv[at, :] = jnp.broadcast_to(r, (64, 128))
        second[at, :] = (h * gain[0:1, :]).astype(BF)
        return 0

    lax.fori_loop(0, rows // 64, norm_block, 0)
    here(pm_in, pm_all, 0).wait()
    lax.fori_loop(0, GROUPS, build_units, 0)

    def units(start, width):
        at = pl.ds(start, width)
        gate, up, gh = dot(second[...], wg[:, at], NN), dot(second[...], wu[:, at], NN), dot(gout[...], wd[:, at], NN)
        cdf = 0.5 + 0.5 * lax.erf(gate * math.sqrt(0.5))
        pdf = jnp.exp2(gate * gate * (-0.5 * LOG2E)) * (1.0 / math.sqrt(2.0 * math.pi))
        act = gate * cdf
        hidden[:, at] = (act * up).astype(BF)
        gup[:, at] = (gh * act).astype(BF)
        ggate[:, at] = (gh * up * (cdf + gate * pdf)).astype(BF)

    for start in range(0, UNITS, 256):
        units(start, min(256, UNITS - start))

    for j in range(3):
        at = slice(256 * j, 256 * j + 256)
        out[:, at] = (resid[:, at] + dot(hidden[...], wd[at, :], NT)).astype(BF)
        gsec[:, at] = dot(ggate[...], wg[at, :], NT) + dot(gup[...], wu[at, :], NT)

    here(out, out_own, 1).start()

    for j in range(2):
        at = slice(384 * j, 384 * j + 384)
        tails = []
        for i, (a, b) in enumerate(((second, ggate), (second, gup), (gout, hidden))):
            for s in range(LINE):
                x = dot(a[:, at], b[:, MAIN * s : MAIN * s + MAIN], TN).astype(BF)
                for g in range(4):
                    pm_g[4 * j + g, s, :, MAIN * i : MAIN * i + MAIN] = x[BAND * g : BAND * g + BAND]
            tails.append(dot(a[:, at], b[:, MAIN * LINE :], TN))
        for s in range(LINE):
            y = jnp.zeros((384, 128), F32)
            for i, tail in enumerate(tails):
                turn = (REST * (i - s)) % 128
                tail = pltpu.roll(tail, turn, 1) if turn else tail
                y = jnp.where((lane >= REST * i) & (lane < REST * (i + 1)), tail, y)
            y = y.astype(BF)
            for g in range(4):
                pm_g[4 * j + g, s, :, 3 * MAIN :] = y[BAND * g : BAND * g + BAND]
        here(pm_g.at[pl.ds(4 * j, 4)], pm_sums.at[pl.ds(4 * j, 4)], 3 + j).start()

    def back_block(i, dgain):
        at = pl.ds(pl.multiple_of(i * 64, 64), 64)
        dy, h = gsec[at, :], hat[at, :]
        gm = gout[at, :].astype(F32) + norm_back(dy, gain[0:1, :], h, inv[at, 0:1])
        gmid[at, :] = gm
        gattn[at, :] = gm.astype(BF)
        return dgain + jnp.sum(dy * h, 0, keepdims=True)

    dgain = lax.fori_loop(0, rows // 64, back_block, jnp.zeros((1, WIDTH), F32))

    here(gmid, gmid_own, 2).start()
    heads = lax.broadcasted_iota(jnp.int32, (16, 256), 0)
    for j in range(3):
        at = slice(256 * j, 256 * j + 256)
        gmx = dot(gattn[...], wout[at, :], NT).astype(BF)
        gmixed[:, at] = gmx
        prod = gmx.astype(F32) * mixed[:, at].astype(F32)
        high = prod.astype(BF)
        low = (prod - high.astype(F32)).astype(BF)
        pick = ((lax.broadcasted_iota(jnp.int32, (16, 256), 1) + 256 * j) // HEAD_DIM == heads).astype(BF)
        part = dot(pick, high, NT) + dot(pick, low, NT)
        delta[...] = part if j == 0 else delta[...] + part

    for j in range(2):
        at = slice(384 * j, 384 * j + 384)
        dwout[at, :] = dot(mixed[:, at], gattn[...], TN)
    row = lax.broadcasted_iota(jnp.int32, (128, WIDTH), 0)
    gcol[...] = jnp.where(row == 0, dgain, 0.0).T

    def pack_out(g, _):
        for s in range(LINE):
            at = pl.ds(pl.multiple_of(g * BAND + s * SLIVER, 8), SLIVER)
            x, c = dwout[at, :], gcol[at, :]
            po_g[g, s, :, :384] = jnp.concatenate([x[:, :384], x[:, 384:]], 0).astype(BF)
            po_g[g, s, :, 384:] = jnp.concatenate([c, jnp.zeros_like(c)], 0).astype(BF)
        return 0

    lax.fori_loop(0, GROUPS, pack_out, 0)

    here(out, out_own, 1).wait()
    here(gmid, gmid_own, 2).wait()
    for j in range(2):
        here(pm_g.at[pl.ds(4 * j, 4)], pm_sums.at[pl.ds(4 * j, 4)], 3 + j).wait()


def middle(tok, mixed, gout, po_all, pm_all):
    rows = tok.shape[0]
    shape, vm = jax.ShapeDtypeStruct, pltpu.VMEM
    vmem, anyspace = pl.BlockSpec(memory_space=pltpu.VMEM), pl.BlockSpec(memory_space=pl.ANY)
    return pl.pallas_call(
        functools.partial(middle_kernel, rows),
        out_shape=[
            shape((rows, WIDTH), BF),
            shape((rows, WIDTH), F32),
            shape((rows, WIDTH), BF),
            shape((16, rows), F32),
            shape(po_all.shape, BF),
            shape(pm_all.shape, BF),
        ],
        in_specs=[vmem] * 4 + [anyspace],
        out_specs=[anyspace, anyspace, vmem, vmem, vmem, anyspace],
        scratch_shapes=[
            vm(pm_all.shape, BF),
            vm(pm_all.shape, BF),
            vm((rows, WIDTH), BF),
            vm((rows, WIDTH), F32),
            pltpu.SemaphoreType.DMA((5,)),
            vm((WIDTH, WIDTH), BF),
            vm((WIDTH, UNITS), BF),
            vm((WIDTH, UNITS), BF),
            vm((WIDTH, UNITS), BF),
            vm((WIDTH, 128), F32),
            vm((8, WIDTH), F32),
            vm((rows, WIDTH), F32),
            vm((rows, WIDTH), F32),
            vm((rows, 128), F32),
            vm((rows, WIDTH), BF),
            vm((rows, UNITS), BF),
            vm((rows, UNITS), BF),
            vm((rows, UNITS), BF),
            vm((rows, WIDTH), F32),
            vm((rows, WIDTH), BF),
            vm((WIDTH, WIDTH), F32),
        ],
        compiler_params=pltpu.CompilerParams(vmem_limit_bytes=58 << 20),
        cost_estimate=pl.CostEstimate(flops=11_000_000_000, bytes_accessed=25_000_000, transcendentals=1_200_000),
        name="middle",
    )(tok, mixed, gout, po_all, pm_all)


class Reduce:
    COPIES = 10

    def __init__(self, src, total, cut, nz, masks, bufs, send, recv, loc=None):
        self.src, self.total, self.cut, self.nz, self.masks = src, total, cut, nz, masks
        self.near, self.side0, self.side1, self.far, *mine = bufs
        self.mine = mine[0] if mine else None
        self.send, self.recv, self.loc = send, recv, loc
        self.dp, self.z = lax.axis_index("dp"), lax.axis_index("seq")
        my, mx, mc = masks
        self.turns = (0, my, mx, my ^ mx)
        self.started = []

    @staticmethod
    def scratch(shape, nz, held):
        r, c = shape
        cut = CUTS[c]
        bufs = [
            pltpu.VMEM((4, nz, r, c), BF),
            pltpu.VMEM((3, nz, r, cut), BF),
            pltpu.VMEM((3, nz, r, c - cut), BF),
            pltpu.VMEM((nz - 1, r, c), BF),
        ]
        sems = [pltpu.SemaphoreType.DMA((Reduce.COPIES * nz + nz,))] * 2
        if not held:
            bufs += [pltpu.VMEM((4, nz, r, c), BF)]
            sems += [pltpu.SemaphoreType.DMA((4 * nz,))]
        return bufs, sems

    def begin(self, src, dst, device, k):
        remote(src, dst, self.send.at[k], self.recv.at[k], device).start()
        self.started.append((k, src.shape[-1]))

    def arrived(self, ref, k):
        remote(ref, ref, self.send.at[k], self.recv.at[k], {"dp": self.dp ^ self.masks[2]}).wait_recv()

    def seat(self, o):
        return self.z ^ LINKED[o]

    def held(self, i, s):
        return self.mine.at[i, s] if self.mine is not None else self.src.at[self.dp ^ self.turns[i], s]

    def local(self, i, o):
        s = self.seat(o)
        return pltpu.make_async_copy(self.src.at[self.dp ^ self.turns[i], s], self.mine.at[i, s], self.loc.at[4 * o + i])

    def zero(self, o):
        s, mc = self.seat(o), self.masks[2]
        for i in (3, 1, 2, 0):
            if self.mine is not None:
                self.local(i, o).start()
            self.begin(self.src.at[self.dp ^ mc ^ self.turns[i], s], self.near.at[i, s], {"dp": self.dp ^ mc}, self.COPIES * o + i)

    def add(self, ref, other):
        ref[...] = (ref[...].astype(F32) + other[...].astype(F32)).astype(BF)

    def p0(self, i, s):
        return self.held(i, s).at[:, pl.ds(0, self.cut)]

    def p1(self, i, s):
        return self.held(i, s).at[:, pl.ds(self.cut, self.src.shape[-1] - self.cut)]

    def one(self, o):
        my, mx, _ = self.masks
        s, k = self.seat(o), self.COPIES * o
        for i in (3, 1, 2, 0):
            if self.mine is not None:
                self.local(i, o).wait()
            self.arrived(self.near.at[i, s], k + i)
            self.add(self.held(i, s), self.near.at[i, s])
            if i == 3:
                self.begin(self.p0(3, s), self.side0.at[1, s], {"dp": self.dp ^ my}, k + 4)
                self.begin(self.p1(3, s), self.side1.at[1, s], {"dp": self.dp ^ mx}, k + 5)
            if i == 1:
                self.begin(self.p0(1, s), self.side0.at[0, s], {"dp": self.dp ^ my}, k + 6)
            if i == 2:
                self.begin(self.p1(2, s), self.side1.at[0, s], {"dp": self.dp ^ mx}, k + 7)

    def two(self, o):
        my, mx, _ = self.masks
        s, k = self.seat(o), self.COPIES * o
        self.arrived(self.side0.at[1, s], k + 4)
        self.add(self.p0(2, s), self.side0.at[1, s])
        self.begin(self.p0(2, s), self.side0.at[2, s], {"dp": self.dp ^ mx}, k + 8)
        self.arrived(self.side1.at[1, s], k + 5)
        self.add(self.p1(1, s), self.side1.at[1, s])
        self.begin(self.p1(1, s), self.side1.at[2, s], {"dp": self.dp ^ my}, k + 9)

    def three(self, o):
        s, k = self.seat(o), self.COPIES * o
        for ref, side, k1, k2 in ((self.p0(0, s), self.side0, k + 6, k + 8), (self.p1(0, s), self.side1, k + 7, k + 9)):
            self.arrived(side.at[0, s], k1)
            self.arrived(side.at[2, s], k2)
            ref[...] = (ref[...].astype(F32) + side[0, s].astype(F32) + side[2, s].astype(F32)).astype(BF)
        if o:
            self.begin(self.held(0, s), self.far.at[o - 1], {"seq": s}, self.COPIES * self.nz + o)

    def four(self):
        out = self.held(0, self.z)[...].astype(F32)
        for o in range(1, self.nz):
            self.arrived(self.far.at[o - 1], self.COPIES * self.nz + o)
            out = out + self.far[o - 1].astype(F32)
        self.total[...] = out

    def done(self):
        for k, width in self.started:
            whole = width == self.src.shape[-1]
            ref = self.near.at[0, 0] if whole else (self.side0 if k % self.COPIES in (4, 6, 8) else self.side1).at[0, 0]
            remote(ref, ref, self.send.at[k], self.recv.at[k], {"dp": self.dp ^ self.masks[2]}).wait_send()


def back_kernel(nz, masks, rows, *refs):
    fused = masks is not None
    (tok, gmid, out_own, query, kv, firsts, wqkv, gain, gmixed, lse, delta, cos_in), refs = refs[:12], refs[12:]
    if fused:
        (po_g, pm_g, gtok, out, s0, s1, so, sm), refs = refs[:8], refs[8:]
    else:
        (gtok, out, p0_g, p1_g), refs = refs[:4], refs[4:]
    (kvb, fb, ft, wq, cos, sine, dq, dqb, dkv, dx, dw, sent, landed, gown, gcol, send, recv, loc), refs = refs[:18], refs[18:]
    me = Place(nz)
    own = me.shard

    def here(src, dst, k):
        return pltpu.make_async_copy(src, dst, loc.at[k])

    def there(src, dst, device, k):
        return remote(src, dst, send.at[k], recv.at[k], device)

    def chunk(t):
        return jnp.where(t == 0, own ^ 2, jnp.where(t == 1, own ^ 1, jnp.where(t == 2, own ^ 3, own)))

    def fetch(n):
        return here(kv.at[n // nz, chunk(lax.rem(n, nz))], kvb.at[lax.rem(n, 2)], lax.rem(n, 2))

    def fetch_first(t):
        return here(firsts.at[chunk(t)], fb.at[lax.rem(t, 2)], 2 + lax.rem(t, 2))

    fetch(0).start()
    fetch_first(0).start()
    whole = [here(wqkv, wq, 4), here(cos_in, cos, 5)]
    for c in whole:
        c.start()
    me.greet(masks or (1,))
    jobs, sums = [], []
    if fused:
        (p0_g, p1_g), refs = refs[:2], refs[2:]
        for src, total in ((p0_g, s0), (p1_g, s1)):
            sums.append(Reduce(src, total, CUTS[src.shape[-1]], nz, masks, refs[:4], *refs[4:6]))
            refs = refs[6:]
        for src, total in ((po_g, so), (pm_g, sm)):
            jobs.append(Reduce(src, total, CUTS[src.shape[-1]], nz, masks, refs[:5], *refs[5:8]))
            refs = refs[8:]
    order = (3, 2, 1, 0)

    def advance(which, step):
        for j in which:
            for o in order:
                getattr(j, step)(o)

    def wave(which):
        for i in range(nz + 2):
            for k, step in enumerate(("one", "two", "three")):
                if 0 <= i - k < nz:
                    for j in which:
                        getattr(j, step)(order[i - k])

    advance(jobs, "zero")

    @pl.when(me.moves)
    def _():
        there(out_own, out, me.opposite, 3).start()

    @pl.when(me.stays)
    def _():
        here(out_own, out, 7).start()

    dq[...] = jnp.zeros_like(dq)
    for c in whole:
        c.wait()
    spread_tables(cos, sine)

    def visits(steps):
        def visit(n, _):
            t, grp = lax.rem(n, nz), n // nz
            c, slot = chunk(t), lax.rem(t, 2)
            fetch(n).wait()

            @pl.when(n < nz)
            def _():
                fetch_first(t).wait()

            @pl.when(n + 1 < 2 * nz)
            def _():
                fetch(n + 1).start()

            @pl.when(n + 1 < nz)
            def _():
                fetch_first(n + 1).start()

            band = pl.ds(pl.multiple_of(t * rows, rows), rows)
            todo = [(i, h) for i in range(3) for h in range(2)]

            def pick(ref, i, h):
                x = ref[:, tiles(HALF * grp + 128 * i, 128)]
                mask = (lane_iota() < 64) if h == 0 else (lane_iota() >= 64)
                return jnp.where(mask, x, jnp.zeros_like(x))

            def score(i, h):
                qh, gh = pick(query, i, h), pick(gmixed, i, h)
                k, v = kvb[slot, :, 128 * i : 128 * i + 128], kvb[slot, :, HALF + 128 * i : HALF + 128 * i + 128]
                return dot(k, qh, NT), dot(v, gh, NT), qh, gh

            ready = [score(*todo[0])]
            dk = dv = None
            for m, (i, h) in enumerate(todo):
                s, dp, qh, gh = ready[m]
                if m + 1 < len(todo):
                    ready.append(score(*todo[m + 1]))
                if h == 0:
                    kt = kvb[slot, :, 128 * i : 128 * i + 128].T
                head = pl.ds(6 * grp + m, 1)
                rows_of = tiles(64 * (6 * grp + m), 64)
                p = jnp.exp2(s - lse[head, :])
                ds = (p * (dp - delta[head, :])).astype(BF)
                a = dot(p.astype(BF), gh, NN)
                dv = a if h == 0 else dv + a
                a = dot(ds, qh, NN)
                dk = a if h == 0 else dk + a
                dq[rows_of, :] += dot(kt[h * 64 : h * 64 + 64], ds, NN)
                if h == 1:
                    at = WIDTH * grp + 128 * i
                    dkv[band, tiles(at, 128)] = rope_back(dk * (1.0 / LOG2E), cos[c], sine[c]).astype(BF)
                    dkv[band, tiles(at + HALF, 128)] = dv.astype(BF)

            @pl.when(n < nz)
            def _():
                for j in range(6):
                    ft[128 * j : 128 * j + 128, band] = fb[slot, :, 128 * j : 128 * j + 128].T
            @pl.when(n >= nz)
            def _():
                for j in range(3):
                    at = slice(256 * j, 256 * j + 256)
                    dx[:, at] = dot(dkv[band, :], wq[at, : 2 * WIDTH], NT)

                @pl.when(lax.rem(t, 2) == 0)
                def _():
                    sent[t] = dx[...].astype(BF)
                    there(sent.at[t], landed.at[t], me.twin, t).start()

                @pl.when(t == 1)
                def _():
                    there(sent.at[0], landed.at[0], me.twin, 0).wait_recv()
                    sent[1] = (dx[...] + landed[0].astype(F32)).astype(BF)
                    there(sent.at[1], landed.at[1], me.beside, 1).start()

            for k, step in steps.items():

                @pl.when(n == k)
                def _(k=k, step=step):
                    if k == nz - 1:
                        close(0)
                        weigh(0)
                        pack(0, p0_g)
                    for which, name in step:
                        advance(which, name)

            return 0

        lax.fori_loop(0, 2 * nz, visit, 0)

    def close(grp):
        for i in range(3 * grp, 3 * grp + 3):
            at = slice(128 * i, 128 * i + 128)
            dqb[:, at] = rope_back(dq[at, :].T * SCALE, cos[own], sine[own]).astype(BF)

    def weigh(grp):
        for r in (slice(0, HALF), slice(HALF, WIDTH)):
            for j in range(3):
                at = WIDTH * grp + 256 * j
                dw[r, HALF + 256 * j : HALF + 256 * j + 256] = dot(ft[r, :], dkv[:, at : at + 256], NN)
            dw[r, :HALF] = dot(ft[r, (nz - 1) * rows :], dqb[:, HALF * grp : HALF * grp + HALF], NN)

    def pack(grp, dst):
        def band_of(g, _):
            for s in range(LINE):
                at = pl.ds(pl.multiple_of(g * BAND + s * SLIVER, 8), SLIVER)
                q, k, v0, v1 = dw[at, :HALF], dw[at, HALF:WIDTH], dw[at, WIDTH : WIDTH + 256], dw[at, WIDTH + 256 :]
                tile = gcol[at, :] if grp else jnp.zeros((SLIVER, 128), F32)
                dst[g, s] = jnp.concatenate(
                    [jnp.concatenate([q, v0], 1), jnp.concatenate([k, v1, tile], 1)], 0
                ).astype(BF)
            return 0

        lax.fori_loop(0, GROUPS, band_of, 0)

    early = sums[:1]
    visits({
        0: [(jobs, "one")],
        3: [(early, "zero")],
        4: [(jobs, "two"), (early, "one")],
        6: [(jobs, "three")],
        7: [(early, "two"), (early, "three")],
    })
    close(1)
    for j in range(3):
        at = slice(256 * j, 256 * j + 256)
        dx[:, at] += dot(dqb[...], wq[at, 2 * WIDTH :], NT)
    there(sent.at[1], landed.at[1], me.beside, 1).wait_recv()
    there(sent.at[2], landed.at[2], me.twin, 2).wait_recv()

    def norm_block(i, dgain):
        at = pl.ds(pl.multiple_of(i * 64, 64), 64)
        dy = dx[at, :] + landed[1, at, :].astype(F32) + landed[2, at, :].astype(F32)
        h, r = normed(tok[at, :].astype(F32))
        gown[at, :] = (gmid[at, :] + norm_back(dy, gain[0:1, :], h, r)).astype(BF)
        return dgain + jnp.sum(dy * h, 0, keepdims=True)

    dgain = lax.fori_loop(0, rows // 64, norm_block, jnp.zeros((1, WIDTH), F32))

    @pl.when(me.moves)
    def _():
        there(gown, gtok, me.opposite, 4).start()

    @pl.when(me.stays)
    def _():
        here(gown, gtok, 8).start()

    row = lax.broadcasted_iota(jnp.int32, (128, WIDTH), 0)
    gcol[...] = jnp.where(row == 0, dgain, 0.0).T
    weigh(1)
    pack(1, p1_g)
    if fused:
        advance(sums[1:], "zero")
        wave(sums[1:])
        for j in jobs + sums:
            j.four()
        for j in jobs + sums:
            j.done()
    for k, device in ((0, me.twin), (1, me.beside), (2, me.twin)):
        there(sent.at[k], landed.at[k], device, k).wait_send()

    @pl.when(me.moves)
    def _():
        there(out_own, out, me.opposite, 3).wait()
        there(gown, gtok, me.opposite, 4).wait()

    @pl.when(me.stays)
    def _():
        here(out_own, out, 7).wait()
        here(gown, gtok, 8).wait()


def back(tok, gmid, out_own, query, kv, firsts, wqkv, gain, gmixed, lse, delta, tables, packs, nz, masks):
    rows = tok.shape[0]
    shape, vm = jax.ShapeDtypeStruct, pltpu.VMEM
    vmem, anyspace = pl.BlockSpec(memory_space=pltpu.VMEM), pl.BlockSpec(memory_space=pl.ANY)
    in_specs = [vmem, vmem, anyspace, vmem] + [anyspace] * 3 + [vmem] * 4 + [anyspace]
    slab = (2 * SLIVER, 640)
    outs, out_specs = [shape((rows, WIDTH), BF)] * 2, [vmem] * 2
    scratch = [
        vm((2, rows, WIDTH), BF),
        vm((2, rows, WIDTH), BF),
        vm((WIDTH, nz * rows), BF),
        vm((WIDTH, 3 * WIDTH), BF),
        vm((nz, rows, 128), F32),
        vm((nz, rows, 128), F32),
        vm((WIDTH, rows), F32),
        vm((rows, WIDTH), BF),
        vm((nz * rows, 2 * WIDTH), BF),
        vm((rows, WIDTH), F32),
        vm((WIDTH, 3 * HALF), F32),
        vm((3, rows, WIDTH), BF),
        vm((3, rows, WIDTH), BF),
        vm((rows, WIDTH), BF),
        vm((WIDTH, 128), F32),
        pltpu.SemaphoreType.DMA((5,)),
        pltpu.SemaphoreType.DMA((5,)),
        pltpu.SemaphoreType.DMA((9,)),
    ]
    if masks:
        in_specs += [anyspace] * 2
        outs += [shape(s, F32) for s in (slab, slab, packs[0].shape[-2:], packs[1].shape[-2:])]
        out_specs += [vmem] * 4
        scratch += [vm((GROUPS, LINE) + slab, BF)] * 2
        for s, held in ((slab, True), (slab, True), (packs[0].shape[-2:], False), (packs[1].shape[-2:], False)):
            bufs, sems = Reduce.scratch(s, nz, held)
            scratch += bufs + sems
    else:
        outs += [shape((GROUPS, LINE) + slab, BF)] * 2
        out_specs += [vmem] * 2
        packs = []
    return pl.pallas_call(
        functools.partial(back_kernel, nz, masks, rows),
        out_shape=outs,
        in_specs=in_specs,
        out_specs=out_specs,
        scratch_shapes=scratch,
        compiler_params=pltpu.CompilerParams(collective_id=1, has_side_effects=True, vmem_limit_bytes=62 << 20),
        cost_estimate=pl.CostEstimate(flops=24_000_000_000, bytes_accessed=40_000_000, transcendentals=13_000_000),
        name="back",
    )(tok, gmid, out_own, query, kv, firsts, wqkv, gain, gmixed, lse, delta, tables, *packs)


def finish_kernel(out, gtok, s0, s1, so, sm, out_o, gtok_o, qkv_o, w_out_o, gain_a_o, gain_m_o, w_in_o, down_o):
    out_o[...] = out[...]
    gtok_o[...] = gtok[...]
    for i, total in enumerate((s0, s1)):
        q, k, v0, v1, tile = unpack_group(total[...])
        for j, x in enumerate((q, k)):
            qkv_o[:, WIDTH * j + HALF * i : WIDTH * j + HALF * i + HALF] = x
        at = 2 * WIDTH + HALF * i
        qkv_o[:, at : at + 256] = v0
        qkv_o[:, at + 256 : at + HALF] = v1
    w_out_o[:, :HALF] = so[:SLIVER, :HALF]
    w_out_o[:, HALF:] = so[SLIVER:, :HALF]
    zeros = jnp.zeros((128 - SLIVER, 128), F32)
    for dst, col in ((gain_a_o, tile), (gain_m_o, so[:SLIVER, HALF:])):
        dst[...] = jnp.concatenate([col, zeros], 0).T[:1, :SLIVER]
    gate, up, down = unpack_mlp(sm[...])
    w_in_o[:, 0, :] = gate
    w_in_o[:, 1, :] = up
    down_o[...] = down.T


def finish(out, gtok, s0, s1, so, sm):
    shape = jax.ShapeDtypeStruct
    vmem = pl.BlockSpec(memory_space=pltpu.VMEM)
    return pl.pallas_call(
        finish_kernel,
        out_shape=[
            shape(out.shape, BF),
            shape(gtok.shape, BF),
            shape((SLIVER, 3 * WIDTH), F32),
            shape((SLIVER, WIDTH), F32),
            shape((1, SLIVER), F32),
            shape((1, SLIVER), F32),
            shape((BAND, 2, SHARE), F32),
            shape((SHARE, BAND), F32),
        ],
        in_specs=[vmem] * 6,
        out_specs=[vmem] * 8,
        compiler_params=pltpu.CompilerParams(vmem_limit_bytes=60 << 20),
        name="finish",
    )(out, gtok, s0, s1, so, sm)


def whole_packs(w_qkv, w_out, attn_gain, mlp_gain, w_in, w_down):
    both = ("dp", "seq")

    def shards_of(w):
        w = lax.all_gather(w, both, axis=0, tiled=True)
        return w.reshape(GROUPS * LINE, SLIVER, -1)

    def slabs(pack, w, gain):
        found = jax.vmap(pack)(w, jnp.pad(gain, ((0, 0), (0, 0), (0, 127))))
        return found.reshape((GROUPS, LINE) + found.shape[1:])

    qkv, gain_a, gain_m = shards_of(w_qkv), shards_of(attn_gain), shards_of(mlp_gain)
    groups = [slabs(lambda w, t, i=i: pack_group(w, t, i), qkv, gain_a) for i in range(2)]
    w_in, w_down = lax.all_gather(w_in, "dp", axis=0, tiled=True), lax.all_gather(w_down, "dp", axis=1, tiled=True)
    mlp = lax.all_gather(pack_mlp(w_in[:, 0], w_in[:, 1], w_down.T), "seq", axis=0, tiled=False)
    mlp = mlp.reshape(LINE, GROUPS, BAND, -1).transpose(1, 0, 2, 3)
    return groups, slabs(pack_out, shards_of(w_out), gain_m), mlp


def whole_sums(p0_g, p1_g, po_g, pm_g):
    both = ("dp", "seq")

    def scattered(x):
        return lax.psum_scatter(x.reshape(WIDTH, -1), both, scatter_dimension=0, tiled=True)

    parts = [jax.vmap(unpack_group)(p.reshape((GROUPS * LINE,) + p.shape[2:]).astype(F32)) for p in (p0_g, p1_g)]
    columns = [parts[0][0], parts[1][0], parts[0][1], parts[1][1], parts[0][2], parts[0][3], parts[1][2], parts[1][3]]
    g_qkv, gain_a = scattered(jnp.concatenate(columns, -1)), scattered(parts[1][4][..., :1])[:, 0]
    po = po_g.reshape(GROUPS * LINE, 2 * SLIVER, -1).astype(F32)
    g_out = scattered(jnp.concatenate([po[:, :SLIVER, :HALF], po[:, SLIVER:, :HALF]], -1))
    gain_m = scattered(po[:, :SLIVER, HALF : HALF + 1])[:, 0]
    mlp = pm_g.astype(F32).transpose(1, 0, 2, 3).reshape(LINE, WIDTH, -1)
    mlp = lax.psum_scatter(mlp, "seq", scatter_dimension=0, tiled=False)
    gate, up, down = unpack_mlp(lax.psum_scatter(mlp, "dp", scatter_dimension=0, tiled=True))
    return g_qkv, g_out, gain_a, gain_m, jnp.stack([gate, up], 1), down.T


def on_device(tokens, w_qkv, w_out, attn_gain, mlp_gain, w_in, w_down, grad_out, *, dp, nz):
    rows = tokens.shape[0]
    masks = (dp // 2, dp // 4, 1) if dp == GROUPS else None
    tables = jnp.asarray(rope_tables(nz * rows)).reshape(nz, rows, 128)
    if masks:
        weights = [w_qkv, w_out, attn_gain[None], mlp_gain[None], w_in, w_down]
        got = front(tokens, grad_out, weights, tables, nz, masks)
        po_all, pm_all = got[-2:]
    else:
        groups, po_all, pm_all = whole_packs(w_qkv, w_out, attn_gain, mlp_gain, w_in, w_down)
        got = front(tokens, grad_out, groups, tables, nz, None)
    mixed, lse, query, gain, tok_own, gout_own, kv, firsts, wqkv = got[:9]
    out_own, gmid, gmixed, delta, po_g, pm_g = middle(tok_own, mixed, gout_own, po_all, pm_all)
    found = back(tok_own, gmid, out_own, query, kv, firsts, wqkv, gain, gmixed, lse, delta, tables, [po_g, pm_g], nz, masks)
    gtok, out, *sums = found
    if not masks:
        return (out, gtok, *whole_sums(*sums, po_g, pm_g))
    out, gtok, g_qkv, g_out, gain_a, gain_m, g_in, g_down = finish(out, gtok, *sums)
    return out, gtok, g_qkv, g_out, gain_a[0], gain_m[0], g_in, g_down


def solution(mesh):
    both = P(("dp", "seq"), None)
    vector = P(("dp", "seq"))
    w_in, w_down = P("dp", None, "seq"), P("seq", "dp")
    step = functools.partial(on_device, dp=mesh.shape["dp"], nz=mesh.shape["seq"])
    return jax.shard_map(
        step,
        mesh=mesh,
        in_specs=(both, both, both, vector, vector, w_in, w_down, both),
        out_specs=(both, both, both, both, vector, vector, w_in, w_down),
        check_vma=False,
    )
```
